32 devices in a mesh: seq: 8 (over y, x, core), tp: 4 (over z).
Axes of the slice: x: 2, y: 2, z: 4, core: 2. Of those that a mesh axis runs over, the one named last changes fastest.
Arguments:
- block_input: bfloat16 [4, 4096, 1792], P(None, 'seq'), may hold values from -6 to 6
- gain_first: bfloat16 [1792], replicated, may hold values from 0.5 to 1.5
- frozen_mixer_weight: bfloat16 [1792, 16, 704], P(None, 'tp'), may hold values from -0.125 to 0.125
- conv_filter: bfloat16 [3, 1792], P(None, 'tp'), may hold values from -2.5 to 2.5
- frozen_output_weight: bfloat16 [1792, 1792], P('tp'), may hold values from -0.125 to 0.125
- gain_second: bfloat16 [1792], replicated, may hold values from 0.5 to 1.5
- frozen_gate_up_weight: bfloat16 [1792, 2, 4864], P(None, None, 'tp'), may hold values from -0.125 to 0.125
- frozen_down_weight: bfloat16 [4864, 1792], P('tp'), may hold values from -0.15625 to 0.15625
- mixer_left: bfloat16 [8, 1792, 16], replicated, may hold values from -0.125 to 0.125
- mixer_right: bfloat16 [8, 16, 16, 704], P(None, None, 'tp'), may hold values from -0.75 to 0.75
- output_left: bfloat16 [8, 1792, 16], P(None, 'tp'), may hold values from -0.125 to 0.125
- output_right: bfloat16 [8, 16, 1792], replicated, may hold values from -0.75 to 0.75
- gateup_left: bfloat16 [8, 1792, 16], replicated, may hold values from -0.125 to 0.125
- gateup_right: bfloat16 [8, 16, 2, 4864], P(None, None, None, 'tp'), may hold values from -0.75 to 0.75
- down_left: bfloat16 [8, 4864, 16], P(None, 'tp'), may hold values from -0.15625 to 0.15625
- down_right: bfloat16 [8, 16, 1792], replicated, may hold values from -0.75 to 0.75
- adapter_index: int32 [4], replicated, may hold values from 0 to 7, as said below
- seq_lengths: int32 [4], replicated, may hold values from 2048 to 4096, as said below
- out_cotangent: bfloat16 [4, 4096, 1792], P(None, 'seq'), may hold values from -6 to 6
Outputs:
- block_output: bfloat16 [4, 4096, 1792], P(None, 'seq')
- input_grad: bfloat16 [4, 4096, 1792], P(None, 'seq')
- grad_mixer_left: float32 [8, 1792, 16], replicated
- grad_mixer_right: float32 [8, 16, 16, 704], P(None, None, 'tp')
- grad_output_left: float32 [8, 1792, 16], P(None, 'tp')
- grad_output_right: float32 [8, 16, 1792], replicated
- grad_gateup_left: float32 [8, 1792, 16], replicated
- grad_gateup_right: float32 [8, 16, 2, 4864], P(None, None, None, 'tp')
- grad_down_left: float32 [8, 4864, 16], P(None, 'tp')
- grad_down_right: float32 [8, 16, 1792], replicated
The draws below stay inside these ranges and needn't reach their ends.
Inputs may be any that keep to these rules, and one draw needn't show every extreme that they name: `adapter_index`: different sequences use different adapters; one sequence uses adapter 8 - 1. `seq_lengths`: one sequence of every draw is full (4096); if there are two or more, another has 2048.
All inputs are finite; a program needn't handle non-finite values.
Results may differ from the reference program's by a relative error of at most 0.025.
Values may be sent and summed in bfloat16 or wider, within the bound.
A program may use at most 576 MiB of HBM per device.

```python
import jax
import jax.numpy as jnp
import numpy as np
from jax import lax

HEADS = 16
HD = 112
FD = 16
FF = 4864
R = 16
NA = 8
KW = 3
WIN = 64
SEQS = 4
D = 1792
HCOLS = 704
LEN = 4096


def draw_adapter_index(key, part):
    key = jax.random.fold_in(key, 11)
    order_key, slot_key = jax.random.split(key)
    order = jax.random.permutation(order_key, NA)
    picked = order[:SEQS]
    slot = jax.random.randint(slot_key, (), 0, SEQS)
    present = jnp.any(picked == NA - 1)
    forced = jnp.where(jnp.arange(SEQS) == slot, NA - 1, picked)
    return jnp.where(present, picked, forced).astype(jnp.int32)


def draw_seq_lengths(key, part):
    key = jax.random.fold_in(key, 7)
    first_key, second_key = jax.random.split(key)
    lengths = jax.random.randint(first_key, (SEQS,), LEN // 2, LEN + 1)
    full_one = jax.random.randint(second_key, (), 0, SEQS)
    half_one = (full_one + 1) % SEQS
    order = jnp.arange(SEQS)
    lengths = jnp.where(order == half_one, LEN // 2, lengths)
    lengths = jnp.where(order == full_one, LEN, lengths)
    return lengths.astype(jnp.int32)


def shard_levels(key, extent, cuts, least, high):
    loudness = 1.0
    for dim, blocks in cuts:
        heights = jax.random.uniform(jax.random.fold_in(jax.random.fold_in(key, 6), dim), (blocks,), jnp.float32, least / len(cuts), high / len(cuts))
        loudness = loudness * jnp.repeat(jnp.exp(heights), extent[dim] // blocks).reshape((-1,) + (1,) * (len(extent) - 1 - dim))
    return loudness


def bell_draw(own_key, shape, width, most, cuts=(), held_as=jnp.bfloat16):
    values = width * jax.random.normal(own_key, shape, jnp.float32)
    if cuts:
        values = values * shard_levels(own_key, shape, cuts, -0.22, 0.18)
    return jnp.clip(values, -most, most).astype(held_as)


def setup_inputs(seed: int = 0) -> dict:
    splits = jax.random.split(jax.random.key(seed), 20)
    return {
        "block_input": bell_draw(splits[0], (SEQS, LEN, D), 1.0, 6.0, ((1, 8),)),
        "gain_first": jnp.clip(1.0 + 0.1 * jax.random.normal(splits[1], (D,), jnp.float32), 0.5, 1.5).astype(jnp.bfloat16),
        "frozen_mixer_weight": bell_draw(splits[2], (D, HEADS, HCOLS), D ** -0.5, 0.125, ((1, 4),)),
        "conv_filter": bell_draw(splits[3], (KW, D), 0.5, 2.5, ((1, 4),)),
        "frozen_output_weight": bell_draw(splits[4], (D, D), D ** -0.5, 0.125, ((0, 4),)),
        "gain_second": jnp.clip(1.0 + 0.1 * jax.random.normal(splits[5], (D,), jnp.float32), 0.5, 1.5).astype(jnp.bfloat16),
        "frozen_gate_up_weight": bell_draw(splits[6], (D, 2, FF), D ** -0.5, 0.125, ((2, 4),)),
        "frozen_down_weight": bell_draw(splits[7], (FF, D), (FF // 4) ** -0.5, 0.15625, ((0, 4),)),
        "mixer_left": bell_draw(splits[8], (NA, D, R), D ** -0.5, 0.125),
        "mixer_right": bell_draw(splits[9], (NA, R, HEADS, HCOLS), (4 * R) ** -0.5, 0.75, ((2, 4),)),
        "output_left": bell_draw(splits[10], (NA, D, R), D ** -0.5, 0.125, ((1, 4),)),
        "output_right": bell_draw(splits[11], (NA, R, D), (4 * R) ** -0.5, 0.75),
        "gateup_left": bell_draw(splits[12], (NA, D, R), D ** -0.5, 0.125),
        "gateup_right": bell_draw(splits[13], (NA, R, 2, FF), (4 * R) ** -0.5, 0.75, ((3, 4),)),
        "down_left": bell_draw(splits[14], (NA, FF, R), (FF // 4) ** -0.5, 0.15625, ((1, 4),)),
        "down_right": bell_draw(splits[15], (NA, R, D), (4 * R) ** -0.5, 0.75),
        "adapter_index": draw_adapter_index(jax.random.fold_in(splits[19], 71), 0),
        "seq_lengths": draw_seq_lengths(jax.random.fold_in(splits[19], 71), 0),
        "out_cotangent": bell_draw(splits[18], (SEQS, LEN, D), 1.0, 6.0, ((1, 8),)),
    }


@jax.custom_vjp
def lower_precision(v):
    return lax.optimization_barrier(v.astype(jnp.bfloat16)).astype(jnp.float32)

@jax.custom_vjp
def low_back(v):
    return v

def low_keep(v):
    return (lower_precision(v), None)

def low_pass(kept, grad):
    return (grad,)

def back_keep(v):
    return (v, None)

def back_low(kept, grad):
    return (lower_precision(grad),)
lower_precision.defvjp(low_keep, low_pass)
low_back.defvjp(back_keep, back_low)
epsilon = 1e-05
masked = -1e+30
highest_precision = lax.Precision.HIGHEST

def taylor(vector):
    leading, trailing = np.triu_indices(vector.shape[-1])
    weights = np.where(leading == trailing, np.sqrt(0.5), 1.0).astype(np.float32)
    square_terms = vector[..., leading] * vector[..., trailing] * weights
    constant = jnp.ones(vector.shape[:-1] + (1,), jnp.float32)
    return jnp.concatenate([constant, vector, square_terms], -1)

def norm_rows(vector, gain_vector):
    return vector * lax.rsqrt(lax.optimization_barrier(jnp.mean(vector * vector, -1, keepdims=True)) + epsilon) * gain_vector

def linear_mix(feat_query, feat_key, values):
    sequences, length, head_count, head_width = values.shape
    block_rows = min(512, length)
    blocks = length // block_rows

    def split_blocks(tensor):
        return jnp.moveaxis(tensor.reshape((sequences, blocks, block_rows) + tensor.shape[2:]), 1, 0)
    causal = jnp.tril(jnp.ones((block_rows, block_rows), jnp.bool_))

    def one_block(carried, block_parts):
        block_query, block_keys, block_values = block_parts
        scores = jnp.einsum('slhf,smhf->shlm', block_query, block_keys, precision=highest_precision)
        scores = jnp.where(causal, scores, 0.0)
        result = jnp.einsum('shlm,smhd->slhd', scores, block_values, precision=highest_precision)
        result = result + jnp.einsum('slhf,shfd->slhd', block_query, carried, precision=highest_precision)
        carried = carried + jnp.einsum('smhf,smhd->shfd', block_keys, block_values, precision=highest_precision)
        return (carried, result)
    initial = jnp.zeros((sequences, head_count, feat_query.shape[-1], head_width), jnp.float32)
    final_state, results = lax.scan(jax.checkpoint(one_block), initial, (split_blocks(feat_query), split_blocks(feat_key), split_blocks(values)))
    return jnp.moveaxis(results, 0, 1).reshape(values.shape)

def window_mix(query, keys_all, values):
    sequences, length, head_count, head_width = values.shape
    block_rows = min(512, length)
    blocks = length // block_rows
    padding = ((0, 0), (WIN, 0), (0, 0), (0, 0))
    keys_padded = jnp.pad(keys_all, padding)
    values_padded = jnp.pad(values, padding)

    def one_block(block_number):
        offset_rows = (block_number * block_rows).astype(jnp.int32)
        block_query = lax.dynamic_slice_in_dim(query, offset_rows, block_rows, 1)
        block_keys = lax.dynamic_slice_in_dim(keys_padded, offset_rows, block_rows + WIN, 1)
        block_values = lax.dynamic_slice_in_dim(values_padded, offset_rows, block_rows + WIN, 1)
        query_pos = offset_rows + jnp.arange(block_rows, dtype=jnp.int32)
        key_pos = offset_rows - WIN + jnp.arange(block_rows + WIN, dtype=jnp.int32)
        allowed = (key_pos[None, :] >= 0) & (key_pos[None, :] <= query_pos[:, None]) & (key_pos[None, :] > query_pos[:, None] - WIN)
        scores = jnp.einsum('slhd,smhd->shlm', block_query, block_keys, precision=highest_precision) * head_width ** (-0.5)
        scores = jnp.where(allowed, low_back(scores), masked)
        largest = lax.optimization_barrier(jnp.max(scores, -1, keepdims=True))
        expo = jnp.exp(scores - largest)
        win_prob = expo / lax.optimization_barrier(jnp.sum(expo, -1, keepdims=True))
        return jnp.einsum('shlm,smhd->slhd', lower_precision(win_prob), block_values, precision=highest_precision)
    results = lax.map(jax.checkpoint(one_block), jnp.arange(blocks, dtype=jnp.int32))
    return jnp.moveaxis(results, 0, 1).reshape(values.shape)

def forward(xfull, adapters, frozen, onehot):
    frozen_mixer_weight, conv_filter, frozen_output_weight, frozen_gate_up_weight, frozen_down_weight, gain_first, gain_second = frozen

    def select(table):
        return jnp.einsum('se,e...->s...', onehot, table, precision=highest_precision)
    chosen = [select(table) for table in adapters]
    select_mixer_left, pick_mixer_right, select_output_left, select_output_right = chosen[:4]
    select_gate_up_left, pick_gateup_right, pick_down_left, select_down_right = chosen[4:]
    sequences, length, hidden_model_width = xfull.shape
    pre_mixer_norm = lower_precision(norm_rows(xfull, gain_first))
    mixer_adapter_rank = lower_precision(jnp.einsum('foc,fcn->fon', pre_mixer_norm, select_mixer_left, precision=highest_precision))
    projected_rows = jnp.einsum('tzm,mf->tzf', pre_mixer_norm, frozen_mixer_weight.reshape(hidden_model_width, -1), precision=highest_precision)
    projected_rows = projected_rows + jnp.einsum('slr,src->slc', mixer_adapter_rank, pick_mixer_right.reshape(sequences, R, -1), precision=highest_precision)
    projected_rows = low_back(projected_rows).reshape(sequences, length, HEADS, HCOLS)
    query_lin = projected_rows[..., :FD] * FD ** (-0.25)
    key_lin = projected_rows[..., FD:2 * FD] * FD ** (-0.25)
    column = 2 * FD
    pieces = [projected_rows[..., column + HD * number:column + HD * (number + 1)] for number in range(6)]
    value_lin, query_win, key_win, value_win, conv_input, conv_gate = pieces
    numerator = low_back(linear_mix(lower_precision(taylor(query_lin)), lower_precision(taylor(key_lin)), lower_precision(value_lin)))
    lin_out = numerator * lax.rsqrt(lax.optimization_barrier(jnp.mean(numerator * numerator, -1, keepdims=True)) + epsilon)
    win_out = low_back(window_mix(lower_precision(query_win), lower_precision(key_win), lower_precision(value_win)))
    conv_round = lower_precision(conv_input)
    conv_taps = conv_filter.reshape(KW, HEADS, HD)
    conv_out = conv_taps[0] * conv_round
    for offset in range(1, KW):
        shifted = jnp.pad(conv_round, ((0, 0), (offset, 0), (0, 0), (0, 0)))[:, :length]
        conv_out = conv_out + conv_taps[offset] * shifted
    conv_branch = conv_out * jax.nn.silu(conv_gate)
    mixer_result_rows = lower_precision((lin_out + win_out + conv_branch).reshape(sequences, length, hidden_model_width))
    output_adapter_rank = jnp.einsum('foc,fcn->fon', mixer_result_rows, select_output_left, precision=highest_precision)
    first_branch_path = jnp.einsum('ofz,zu->ofu', mixer_result_rows, frozen_output_weight, precision=highest_precision)
    first_branch_path = first_branch_path + jnp.einsum('fjt,ftg->fjg', output_adapter_rank, select_output_right, precision=highest_precision)
    middle = xfull + low_back(first_branch_path)
    pre_feed_norm = lower_precision(norm_rows(middle, gain_second))
    gate_adapter_rank = lower_precision(jnp.einsum('foc,fcn->fon', pre_feed_norm, select_gate_up_left, precision=highest_precision))
    gate_up_hidden = jnp.einsum('tzm,mf->tzf', pre_feed_norm, frozen_gate_up_weight.reshape(hidden_model_width, -1), precision=highest_precision)
    gate_up_hidden = gate_up_hidden + jnp.einsum('slr,src->slc', gate_adapter_rank, pick_gateup_right.reshape(sequences, R, -1), precision=highest_precision)
    gate_up_hidden = low_back(gate_up_hidden).reshape(sequences, length, 2, FF)
    hidden_activation = lower_precision(jax.nn.silu(gate_up_hidden[:, :, 0]) * gate_up_hidden[:, :, 1])
    down_adapter_rank = jnp.einsum('slf,sfr->slr', hidden_activation, pick_down_left, precision=highest_precision)
    second_branch_path = jnp.einsum('cuz,zo->cuo', hidden_activation, frozen_down_weight, precision=highest_precision)
    second_branch_path = second_branch_path + jnp.einsum('fjt,ftg->fjg', down_adapter_rank, select_down_right, precision=highest_precision)
    return middle + low_back(second_branch_path)

def reference(block_input, gain_first, frozen_mixer_weight, conv_filter, frozen_output_weight, gain_second, frozen_gate_up_weight, frozen_down_weight, mixer_left, mixer_right, output_left, output_right, gateup_left, gateup_right, down_left, down_right, adapter_index, seq_lengths, out_cotangent):
    frozen = tuple((tensor.astype(jnp.float32) for tensor in (frozen_mixer_weight, conv_filter, frozen_output_weight, frozen_gate_up_weight, frozen_down_weight, gain_first, gain_second)))
    adapters = tuple((tensor.astype(jnp.float32) for tensor in (mixer_left, mixer_right, output_left, output_right, gateup_left, gateup_right, down_left, down_right)))
    onehot = (adapter_index[:, None] == jnp.arange(NA, dtype=jnp.int32)[None, :]).astype(jnp.float32)

    def whole_block(xfull, *tables):
        return forward(xfull, tables, frozen, onehot)
    output, pullback = jax.vjp(whole_block, block_input.astype(jnp.float32), *adapters)
    positions = jnp.arange(LEN, dtype=jnp.int32)
    valid_mask = (positions[None, :] < seq_lengths[:, None]).astype(jnp.float32)
    gradients = pullback(out_cotangent.astype(jnp.float32) * valid_mask[:, :, None])
    return (output.astype(jnp.bfloat16), gradients[0].astype(jnp.bfloat16), gradients[1], gradients[2], gradients[3], gradients[4], gradients[5], gradients[6], gradients[7], gradients[8])
```

```python
import functools

import jax
import jax.numpy as jnp
import numpy as np
from jax import lax
from jax.experimental import pallas as pl
from jax.experimental.pallas import tpu as pltpu
from jax.sharding import Mesh
from jax.sharding import PartitionSpec as P

HD = 112
PD = 128
FD = 16
R = 16
NA = 8
KW = 3
WIN = 64
HCOLS = 704
SLOTS = 4
HEAD_PAD = 7 * PD
FEATS = 1 + FD + FD * (FD + 1) // 2
STATE = 160
CHUNK = 256
QB = 128

epsilon = 1e-05
masked = -1e30
f32 = jnp.float32
bf16 = jnp.bfloat16
ANY = pl.BlockSpec(memory_space=pl.ANY)


def nn(a, b):
    return lax.dot_general(a, b, (((1,), (0,)), ((), ())), preferred_element_type=f32)


def nt(a, b):
    return lax.dot_general(a, b, (((1,), (1,)), ((), ())), preferred_element_type=f32)


def tn(a, b):
    return lax.dot_general(a, b, (((0,), (0,)), ((), ())), preferred_element_type=f32)


def feature_tables():
    leading, trailing = np.triu_indices(FD)
    pick = np.zeros((PD, 1280), np.float32)
    bias = np.zeros((1, 512), np.float32)
    coef = np.zeros((1, 256), np.float32)
    bias[0, 0] = 1.0
    bias[0, 256 : 256 + 1 + FD] = 1.0
    coef[0, : 1 + FD] = 1.0
    coef[0, 1 + FD : FEATS] = np.where(leading == trailing, np.sqrt(0.5), 1.0)
    for base, row in ((0, 0), (512, FD)):
        for i in range(FD):
            pick[row + i, base + 1 + i] = 0.5
        for n, (i, j) in enumerate(zip(leading, trailing)):
            pick[row + i, base + 1 + FD + n] = 0.5
            pick[row + j, base + 256 + 1 + FD + n] = 0.5
    for i in range(FD):
        pick[FD + i, 1024 + i] = 0.25
        pick[i, 1152 + FD + i] = 0.25
    return pick, bias, coef


HEAD_SEGMENTS = [(0, 2 * FD, 0)] + [(2 * FD + HD * i, HD, PD * (i + 1)) for i in range(6)]
M_ROWS = HCOLS + HD
M_CUT = 2 * FD + 3 * HD


def place():
    j = lax.rem(lax.axis_index("chip"), 4)
    return j // 2, lax.rem(j, 2)


def run_copies(copies, sems, start):
    for number, (src, dst) in enumerate(copies):
        copy = pltpu.make_async_copy(src, dst, sems.at[start + number])
        copy.start()


def wait_copies(copies, sems, start):
    for number, (src, dst) in enumerate(copies):
        pltpu.make_async_copy(src, dst, sems.at[start + number]).wait()


def spread_pieces(refs, cut, rows, dest, base, width, offset_of):
    y, x = place()
    z_ref, x_ref, y_ref, da_ref, db_ref = refs
    copies = []
    for kind, yy, xx in (("z", y, x), ("x", y, 1 - x), ("y", 1 - y, x), ("d", 1 - y, 1 - x)):
        cols = pl.ds(pl.multiple_of(xx * width, PD), width)
        for first, count in rows:
            spans = [(first, count)]
            if kind == "d" and first < cut < first + count:
                spans = [(first, cut - first), (cut, first + count - cut)]
            for row, size in spans:
                if kind == "d":
                    src = da_ref if row < cut else db_ref
                    src = src.at[pl.ds(row if row < cut else row - cut, size)]
                else:
                    src = {"z": z_ref, "x": x_ref, "y": y_ref}[kind].at[pl.ds(row, size)]
                start = pl.multiple_of(base + offset_of(row, yy), 16)
                copies.append((src, dest.at[pl.ds(start, size), cols]))
    return copies


def mixer_offset(row, yy):
    for first, count, at in HEAD_SEGMENTS:
        if first <= row < first + count:
            return yy * HEAD_PAD + at + row - first
    return None


MIXER_ROWS = [(first, count) for first, count, _ in HEAD_SEGMENTS]


def mixer_copies(refs, own, dest, base):
    if own:
        core = lax.axis_index("core")
        copies = []
        for head in range(2):
            for first, count, at in HEAD_SEGMENTS:
                src = pl.multiple_of(2 * HCOLS * core + HCOLS * head + first, 16)
                copies.append(
                    (refs[0].at[pl.ds(src, count)], dest.at[pl.ds(base + HEAD_PAD * head + at, count)])
                )
        return copies
    return spread_pieces(refs, M_CUT, MIXER_ROWS, dest, base, dest.shape[1] // 2, mixer_offset)


def mixer_pads(dest, base):
    for head in range(2):
        for first, count, at in HEAD_SEGMENTS:
            start = base + HEAD_PAD * head + at + count
            dest[start : start + PD - count] = jnp.zeros((PD - count, dest.shape[1]), bf16)


def output_copies(refs, own, dest, base):
    if own:
        core = lax.axis_index("core")
        return [
            (
                refs[0].at[pl.ds(pl.multiple_of(2 * HD * core + HD * head, 16), HD)],
                dest.at[pl.ds(base + PD * head, HD)],
            )
            for head in range(2)
        ]
    return spread_pieces(
        refs, M_CUT, [(HCOLS, HD)], dest, base, dest.shape[1] // 2, lambda row, yy: yy * PD + row - HCOLS
    )


def output_pads(dest, base):
    for head in range(2):
        start = base + PD * head + HD
        dest[start : start + PD - HD] = jnp.zeros((PD - HD, dest.shape[1]), bf16)


def feed_cut(quarter):
    return quarter + (quarter // 2 + 15) // 16 * 16


def feed_copies(refs, own, dest, half, pad):
    if own:
        core = lax.axis_index("core")
        wg, wd = refs
        spots = [(wg, 0, 0), (wg, 2 * half, pad), (wd, 0, 2 * pad)]
        return [
            (
                ref.at[pl.ds(pl.multiple_of(half * core + first, 16), half)],
                dest.at[pl.ds(at, half)],
            )
            for ref, first, at in spots
        ]
    quarter = half // 2

    def offset_of(row, yy):
        return row // quarter * pad + yy * quarter + row % quarter

    rows = [(quarter * i, quarter) for i in range(3)]
    return spread_pieces(
        refs, feed_cut(quarter), rows, dest, 0, dest.shape[1] // 2, offset_of
    )


def feed_pads(dest, half, pad):
    for i in range(3):
        dest[pad * i + half : pad * (i + 1)] = jnp.zeros((pad - half, dest.shape[1]), bf16)


def features(picked, bias, coef, at):
    one = picked[:, at : at + 256] + bias[:, :256]
    two = picked[:, at + 256 : at + 512] + bias[:, 256:]
    return one, two, one * two * coef


class Table:
    def __init__(self, pad):
        sizes = (2 * HEAD_PAD, 2 * PD, 2 * pad, pad, 2 * PD)
        starts = np.cumsum((0,) + sizes)
        self.right, self.left, self.gate, self.down, self.taps = (
            slice(int(a), int(a) + n) for a, n in zip(starts, sizes)
        )
        self.edges = [int(a) for a in starts]


def params(mib, **more):
    return pltpu.CompilerParams(vmem_limit_bytes=mib * 2**20, **more)


def project_kernel(own, first, rank, table, pick, bias, coef, *rest):
    count = 1 if own else 5
    refs = rest[:count]
    proj, tails, state, weight, sems = rest[count:]
    copies = mixer_copies(refs, own, weight, 0)
    run_copies(copies, sems, 0)
    mixer_pads(weight, 0)
    wait_copies(copies, sems, 0)
    blocks = first.shape[0] // CHUNK
    for head in range(2):
        cols = pl.ds(HEAD_PAD * head, HEAD_PAD)

        def one(block, carry):
            rows = pl.ds(pl.multiple_of(block * CHUNK, CHUNK), CHUNK)
            result = nt(first[rows, :], weight[cols, :]) + nn(rank[rows, :], table[:, cols])
            rounded = result.astype(bf16)
            proj[rows, cols] = rounded
            picked = nn(rounded[:, :PD], pick[...][:, 512:1024])
            _, _, feat = features(picked, bias[...], coef[...], 0)
            return carry + tn(feat.astype(bf16), rounded[:, PD : 2 * PD])

        total = lax.fori_loop(0, blocks, one, jnp.zeros((256, PD), f32))
        state[head] = total[:STATE].astype(bf16)
        last = first.shape[0]
        at = HEAD_PAD * head
        tails[head, 0:WIN, 0:PD] = proj[last - WIN :, at + 3 * PD : at + 4 * PD]
        tails[head, 0:WIN, PD : 2 * PD] = proj[last - WIN :, at + 4 * PD : at + 5 * PD]
        tails[head, WIN : WIN + 16, 0:PD] = proj[last - 16 :, at + 5 * PD : at + 6 * PD]
        tails[head, WIN : WIN + 16, PD : 2 * PD] = jnp.zeros((16, PD), bf16)


def project(own, first, rank, table, tables, refs):
    rows, width = first.shape
    vm = pl.BlockSpec(memory_space=pltpu.VMEM)
    return pl.pallas_call(
        functools.partial(project_kernel, own),
        out_shape=(
            jax.ShapeDtypeStruct((rows, 2 * HEAD_PAD), bf16),
            jax.ShapeDtypeStruct((2, WIN + 16, 2 * PD), bf16),
            jax.ShapeDtypeStruct((2, STATE, PD), bf16),
        ),
        in_specs=[vm] * 6 + [ANY] * len(refs),
        out_specs=(vm, vm, vm),
        scratch_shapes=[pltpu.VMEM((2 * HEAD_PAD, width), bf16), pltpu.SemaphoreType.DMA((40,))],
        compiler_params=params(48),
        cost_estimate=pl.CostEstimate(
            flops=100_000_000, bytes_accessed=300_000, transcendentals=0
        ),
        name="project",
    )(first, rank, table, *tables, *refs)


def window_mask(number):
    query = lax.broadcasted_iota(jnp.int32, (QB, QB + WIN), 0)
    key = lax.broadcasted_iota(jnp.int32, (QB, QB + WIN), 1)
    allowed = (key > query) & (key <= query + WIN)
    if number == 0:
        lead = jnp.where(lax.axis_index("chip") > 0, 0, WIN)
        allowed = allowed & (key >= lead)
    return allowed


def window_prob(query, keys, number):
    scores = nt(query, keys) * HD ** (-0.5)
    scores = jnp.where(window_mask(number), scores, masked)
    largest = jnp.max(scores, -1, keepdims=True)
    expo = jnp.exp(scores - largest)
    return expo / jnp.sum(expo, -1, keepdims=True)


def causal_mask():
    row = lax.broadcasted_iota(jnp.int32, (CHUNK, CHUNK), 0)
    col = lax.broadcasted_iota(jnp.int32, (CHUNK, CHUNK), 1)
    return col <= row


def conv_of(conv, taps, start, count):
    result = taps[0:1] * conv[pl.ds(16 + start, count), :]
    for offset in range(1, KW):
        result = result + taps[offset : offset + 1] * conv[pl.ds(16 + start - offset, count), :]
    return result


def attend_kernel(spots, proj, tails, prior, table, pick, bias, coef, mixed, numer, keys, vals, conv):
    rows = proj.shape[0]
    keys[0:WIN, :] = tails[0, 0:WIN, 0:PD]
    vals[0:WIN, :] = tails[0, 0:WIN, PD : 2 * PD]
    conv[0:16, :] = tails[0, WIN : WIN + 16, 0:PD].astype(f32)
    keys[WIN:, :] = proj[:, 3 * PD : 4 * PD]
    vals[WIN:, :] = proj[:, 4 * PD : 5 * PD]
    conv[16:, :] = proj[:, 5 * PD : 6 * PD].astype(f32)
    tap = head_taps(spots, table)
    state = prior[0]
    causal = causal_mask()
    for chunk in range(rows // CHUNK):
        at = chunk * CHUNK
        span = slice(at, at + CHUNK)
        base = proj[span, 0:PD]
        value = proj[span, PD : 2 * PD]
        picked = nn(base, pick[:, :1152])
        _, _, feat_q = features(picked, bias[...], coef[...], 0)
        _, _, feat_k = features(picked, bias[...], coef[...], 512)
        score = nt(base, picked[:, 1024:1152].astype(bf16))
        weight = jnp.where(causal, 1.0 + score + 0.5 * score * score, 0.0).astype(bf16)
        total = nn(weight, value) + nn(feat_q.astype(bf16), state.astype(bf16))
        state = state + tn(feat_k.astype(bf16), value)
        parts = []
        for number in range(chunk * CHUNK // QB, (chunk + 1) * CHUNK // QB):
            query = proj[number * QB : (number + 1) * QB, 2 * PD : 3 * PD]
            prob = window_prob(query, keys[number * QB : number * QB + QB + WIN, :], number)
            parts.append(nn(prob.astype(bf16), vals[number * QB : number * QB + QB + WIN, :]))
        window = jnp.concatenate(parts, 0)
        scale = lax.rsqrt(jnp.sum(total * total, -1, keepdims=True) * (1.0 / HD) + epsilon)
        gate = proj[span, 6 * PD : 7 * PD].astype(f32)
        branch = conv_of(conv, tap, at, CHUNK) * (gate * jax.nn.sigmoid(gate))
        mixed[span, :] = (total * scale + window + branch).astype(bf16)
        numer[span, :] = total.astype(bf16)


def head_taps(spots, table):
    start = pl.multiple_of(spots.taps.start + PD * pl.program_id(0), PD)
    return table[:, pl.ds(start, PD)].astype(f32)


def attend(spots, proj, tails, prior, table, tables):
    rows = proj.shape[0]
    whole = lambda a: pl.BlockSpec(a.shape, lambda h: (0,) * a.ndim)
    return pl.pallas_call(
        functools.partial(attend_kernel, spots),
        grid=(2,),
        out_shape=(
            jax.ShapeDtypeStruct((rows, 2 * PD), bf16),
            jax.ShapeDtypeStruct((rows, 2 * PD), bf16),
        ),
        in_specs=[
            pl.BlockSpec((rows, HEAD_PAD), lambda h: (0, h)),
            pl.BlockSpec((1, WIN + 16, 2 * PD), lambda h: (h, 0, 0)),
            pl.BlockSpec((1, 256, PD), lambda h: (h, 0, 0)),
            whole(table),
        ]
        + [whole(t) for t in tables],
        out_specs=(
            pl.BlockSpec((rows, PD), lambda h: (0, h)),
            pl.BlockSpec((rows, PD), lambda h: (0, h)),
        ),
        scratch_shapes=[
            pltpu.VMEM((rows + WIN, PD), bf16),
            pltpu.VMEM((rows + WIN, PD), bf16),
            pltpu.VMEM((rows + 16, PD), f32),
        ],
        compiler_params=params(48),
        cost_estimate=pl.CostEstimate(
            flops=100_000_000, bytes_accessed=300_000, transcendentals=0
        ),
        name="attend",
    )(proj, tails, prior, table, *tables)


def mix_out_kernel(spots, *refs):
    mixed = refs[0:4]
    lefts = refs[4:8]
    right = refs[8]
    sources = refs[9 : 9 + 1 + 15]
    part, rank, weight, sems = refs[25:]
    groups = []
    for slot in range(SLOTS):
        pieces = sources[0:1] if slot == 0 else sources[1 + 5 * (slot - 1) : 1 + 5 * slot]
        groups.append(output_copies(pieces, slot == 0, weight, 2 * PD * slot))

    @pl.when(pl.program_id(0) == 0)
    def _():
        for slot in range(SLOTS):
            run_copies(groups[slot], sems, 8 * slot)
            output_pads(weight, 2 * PD * slot)
        for slot in range(SLOTS):
            wait_copies(groups[slot], sems, 8 * slot)

    total = jnp.zeros(part.shape, f32)
    rank_sum = jnp.zeros((part.shape[0], R), f32)
    for slot in range(SLOTS):
        total = total + nn(mixed[slot][...], weight[2 * PD * slot : 2 * PD * (slot + 1), :])
        rank_sum = rank_sum + nt(mixed[slot][...], lefts[slot][:, spots.left])
    total = total + nn(rank_sum.astype(bf16), right[...])
    part[...] = total.astype(bf16)
    rank[...] = rank_sum


def mix_out(spots, mixed, lefts, right, sources):
    rows = mixed[0].shape[0]
    width = right.shape[1]
    block = CHUNK
    steps = rows // block
    whole = lambda a: pl.BlockSpec(a.shape, lambda i: (0,) * a.ndim)
    return pl.pallas_call(
        functools.partial(mix_out_kernel, spots),
        grid=(steps,),
        out_shape=(
            jax.ShapeDtypeStruct((rows, width), bf16),
            jax.ShapeDtypeStruct((rows, R), f32),
        ),
        in_specs=[pl.BlockSpec((block, 2 * PD), lambda i: (i, 0))] * 4
        + [whole(a) for a in lefts]
        + [whole(right)]
        + [ANY] * len(sources),
        out_specs=(
            pl.BlockSpec((block, width), lambda i: (i, 0)),
            pl.BlockSpec((block, R), lambda i: (i, 0)),
        ),
        scratch_shapes=[pltpu.VMEM((SLOTS * 2 * PD, width), bf16), pltpu.SemaphoreType.DMA((32,))],
        compiler_params=params(48),
        cost_estimate=pl.CostEstimate(
            flops=100_000_000, bytes_accessed=300_000, transcendentals=0
        ),
        name="mix_out",
    )(*mixed, *lefts, right, *sources)


def feed_kernel(own, last, half, pad, spots, *refs):
    second, grad, grank, rgrad, table, dright, gleft = refs[:7]
    right, left = table.at[:, spots.gate], table.at[:, spots.down]
    count = 2 if own else 5
    refs = refs[7:]
    sources, refs = refs[:count], refs[count:]
    if not own:
        (down_in, back_in, ranks_in), refs = refs[:3], refs[3:]
    down_out, back_out, ranks_out, right_grad, left_grad, weight, sems = refs
    copies = feed_copies(sources, own, weight, half, pad)

    @pl.when(pl.program_id(0) == 0)
    def _():
        run_copies(copies, sems, 0)
        feed_pads(weight, half, pad)
        right_grad[...] = jnp.zeros(right_grad.shape, f32)
        left_grad[...] = jnp.zeros(left_grad.shape, f32)
        wait_copies(copies, sems, 0)

    gate_up = nt(second[...], weight[0 : 2 * pad, :]) + nn(grank[...], right[...])
    gate, up = gate_up[:, :pad], gate_up[:, pad:]
    sig = jax.nn.sigmoid(gate)
    act = gate * sig
    hidden = (act * up).astype(bf16)
    hidden_grad = nt(grad[...], weight[2 * pad :, :]) + nn(rgrad[...], left[...])
    gate_grad = hidden_grad * up * (sig * (1.0 + gate * (1.0 - sig)))
    both = jnp.concatenate([gate_grad.astype(bf16), (hidden_grad * act).astype(bf16)], 1)
    down = nn(hidden, weight[2 * pad :, :])
    back = nn(both, weight[0 : 2 * pad, :])
    down_rank = nt(hidden, left[...])
    back_rank = nt(both, right[...])
    if not own:
        down = down + down_in[...]
        back = back + back_in[...]
        down_rank = down_rank + ranks_in[:, :R]
        back_rank = back_rank + ranks_in[:, R:]
    ranks_out[:, :R] = down_rank
    ranks_out[:, R:] = back_rank
    if last:
        down = down + nn(down_rank.astype(bf16), dright[...])
        back = back + nn(back_rank.astype(bf16), gleft[...])
    down_out[...] = down.astype(down_out.dtype)
    back_out[...] = back.astype(back_out.dtype)
    right_grad[...] += tn(grank[...], both)
    left_grad[...] += tn(rgrad[...], hidden)


def feed(own, last, half, spots, second, grad, grank, rgrad, table, dright, gleft, sources, carry):
    rows, width = second.shape
    pad = spots.down.stop - spots.down.start
    block = CHUNK
    kind = bf16 if last else f32
    whole = lambda a: pl.BlockSpec(a.shape, lambda i: (0,) * a.ndim)
    wide = pl.BlockSpec((block, width), lambda i: (i, 0))
    thin = pl.BlockSpec((block, R), lambda i: (i, 0))
    pair = pl.BlockSpec((block, 2 * R), lambda i: (i, 0))
    return pl.pallas_call(
        functools.partial(feed_kernel, own, last, half, pad, spots),
        grid=(rows // block,),
        out_shape=(
            jax.ShapeDtypeStruct((rows, width), kind),
            jax.ShapeDtypeStruct((rows, width), kind),
            jax.ShapeDtypeStruct((rows, 2 * R), f32),
            jax.ShapeDtypeStruct((R, 2 * pad), f32),
            jax.ShapeDtypeStruct((R, pad), f32),
        ),
        in_specs=[wide, wide, thin, thin, whole(table), whole(dright), whole(gleft)]
        + [ANY] * len(sources)
        + ([] if own else [wide, wide, pair]),
        out_specs=(
            wide,
            wide,
            pair,
            pl.BlockSpec((R, 2 * pad), lambda i: (0, 0)),
            pl.BlockSpec((R, pad), lambda i: (0, 0)),
        ),
        scratch_shapes=[pltpu.VMEM((3 * pad, width), bf16), pltpu.SemaphoreType.DMA((16,))],
        compiler_params=params(56),
        cost_estimate=pl.CostEstimate(
            flops=100_000_000, bytes_accessed=300_000, transcendentals=0
        ),
        name="feed",
    )(second, grad, grank, rgrad, table, dright, gleft, *sources, *carry)


def turn_kernel(own, spots, *refs):
    mixer_up, orgrad, table, numer, mixed, base0, base1, head_rows, tails = refs[:9]
    left, taps = table.at[:, spots.left], table.at[:, spots.taps]
    pick, bias, coef = refs[9:12]
    count = 1 if own else 5
    sources = refs[12 : 12 + count]
    up_out, grad_out, state, lent, left_grad, weight, sems = refs[12 + count :]
    copies = output_copies(sources, own, weight, 0)
    run_copies(copies, sems, 0)
    output_pads(weight, 0)
    wait_copies(copies, sems, 0)
    rows = mixer_up.shape[0]

    def one(block, carry):
        span = pl.ds(pl.multiple_of(block * CHUNK, CHUNK), CHUNK)
        both = nt(mixer_up[span, :], weight[...]) + nn(orgrad[span, :], left[...])
        result = []
        for head in range(2):
            cols = slice(PD * head, PD * (head + 1))
            up = both[:, cols]
            total = numer[span, cols].astype(f32)
            scale = lax.rsqrt(jnp.sum(total * total, -1, keepdims=True) * (1.0 / HD) + epsilon)
            inner = jnp.sum(total * up, -1, keepdims=True) * (1.0 / HD)
            grad = (scale * up - total * (scale * scale * scale * inner)).astype(bf16)
            up_out[span, cols] = up.astype(bf16)
            grad_out[span, cols] = grad
            base = (base0 if head == 0 else base1)[span, :]
            _, _, feat = features(nn(base, pick[:, 0:512]), bias[...], coef[...], 0)
            result.append(carry[head] + tn(feat.astype(bf16), grad))
        result.append(carry[2] + tn(orgrad[span, :], mixed[span, :]))
        return tuple(result)

    zero = jnp.zeros((256, PD), f32)
    done = lax.fori_loop(
        0, rows // CHUNK, one, (zero, zero, jnp.zeros((R, 2 * PD), f32))
    )
    left_grad[...] = done[2]
    for head in range(2):
        state[head] = done[head][:STATE].astype(bf16)
        at = HEAD_PAD * head
        query = head_rows[:, at + 2 * PD : at + 3 * PD]
        keys = jnp.concatenate([tails[head, 0:WIN, 0:PD], head_rows[:, at + 3 * PD : at + 4 * PD]], 0)
        vals = jnp.concatenate(
            [tails[head, 0:WIN, PD : 2 * PD], head_rows[:, at + 4 * PD : at + 5 * PD]], 0
        )
        prob = window_prob(query, keys, 0)
        up = up_out[0:QB, PD * head : PD * (head + 1)]
        prob_grad = nt(up, vals)
        inner = jnp.sum(prob * prob_grad, -1, keepdims=True)
        score = (prob * (prob_grad - inner)).astype(bf16)
        lent[head, 0:WIN, 0:PD] = (tn(score, query)[:WIN] * HD ** (-0.5)).astype(bf16)
        lent[head, 0:WIN, PD : 2 * PD] = tn(prob.astype(bf16), up)[:WIN].astype(bf16)
        tap = taps[:, PD * head : PD * (head + 1)].astype(f32)
        gate = head_rows[0:16, at + 6 * PD : at + 7 * PD].astype(f32)
        flow = up_out[0:16, PD * head : PD * (head + 1)].astype(f32) * (gate * jax.nn.sigmoid(gate))
        row0 = tap[2:3] * flow[0:1]
        row1 = tap[1:2] * flow[0:1] + tap[2:3] * flow[1:2]
        index = lax.broadcasted_iota(jnp.int32, (16, PD), 0)
        lent[head, WIN : WIN + 16, 0:PD] = jnp.where(
            index == 14, row0, jnp.where(index == 15, row1, 0.0)
        ).astype(bf16)
        lent[head, WIN : WIN + 16, PD : 2 * PD] = jnp.zeros((16, PD), bf16)


def turn(own, spots, mixer_up, orgrad, table, numer, mixed, proj, tails, tables, sources):
    rows, width = mixer_up.shape
    whole = lambda a: pl.BlockSpec(a.shape, lambda i: (0,) * a.ndim)
    flat = lambda *shape: pl.BlockSpec(shape, lambda i: (0,) * len(shape))
    return pl.pallas_call(
        functools.partial(turn_kernel, own, spots),
        grid=(1,),
        out_shape=(
            jax.ShapeDtypeStruct((rows, 2 * PD), bf16),
            jax.ShapeDtypeStruct((rows, 2 * PD), bf16),
            jax.ShapeDtypeStruct((2, STATE, PD), bf16),
            jax.ShapeDtypeStruct((2, WIN + 16, 2 * PD), bf16),
            jax.ShapeDtypeStruct((R, 2 * PD), f32),
        ),
        in_specs=[
            whole(mixer_up),
            whole(orgrad),
            whole(table),
            whole(numer),
            whole(mixed),
            pl.BlockSpec((rows, PD), lambda i: (0, 0)),
            pl.BlockSpec((rows, PD), lambda i: (0, 7)),
            pl.BlockSpec((QB, 2 * HEAD_PAD), lambda i: (0, 0)),
            whole(tails),
        ]
        + [whole(t) for t in tables]
        + [ANY] * len(sources),
        out_specs=(
            flat(rows, 2 * PD),
            flat(rows, 2 * PD),
            flat(2, STATE, PD),
            flat(2, WIN + 16, 2 * PD),
            flat(R, 2 * PD),
        ),
        scratch_shapes=[pltpu.VMEM((2 * PD, width), bf16), pltpu.SemaphoreType.DMA((8,))],
        compiler_params=params(48),
        cost_estimate=pl.CostEstimate(
            flops=100_000_000, bytes_accessed=300_000, transcendentals=0
        ),
        name="turn",
    )(mixer_up, orgrad, table, numer, mixed, proj, proj, proj, tails, *tables, *sources)


def attend_back_kernel(
    spots, proj, tails, prior, later, lent, ups, grads, table, rank, pick, bias, coef,
    out, rank_grad, right_grad, keys, vals, conv, flow, dkeys, dvals, states
):
    rows = proj.shape[0]
    chunks = rows // CHUNK
    keys[0:WIN, :] = tails[0, 0:WIN, 0:PD]
    vals[0:WIN, :] = tails[0, 0:WIN, PD : 2 * PD]
    conv[0:16, :] = tails[0, WIN : WIN + 16, 0:PD].astype(f32)
    keys[WIN:, :] = proj[:, 3 * PD : 4 * PD]
    vals[WIN:, :] = proj[:, 4 * PD : 5 * PD]
    conv[16:, :] = proj[:, 5 * PD : 6 * PD].astype(f32)
    tap = head_taps(spots, table)
    right = table.at[:, pl.ds(pl.multiple_of(HEAD_PAD * pl.program_id(0), PD), HEAD_PAD)]
    dkeys[...] = jnp.zeros(dkeys.shape, f32)
    dvals[...] = jnp.zeros(dvals.shape, f32)
    dkeys[rows:, :] = lent[0, 0:WIN, 0:PD].astype(f32)
    dvals[rows:, :] = lent[0, 0:WIN, PD : 2 * PD].astype(f32)
    flow[rows:, :] = jnp.zeros((16, PD), f32)
    state = prior[0]
    for chunk in range(chunks):
        span = slice(chunk * CHUNK, (chunk + 1) * CHUNK)
        states[chunk] = state.astype(bf16)
        if chunk + 1 < chunks:
            _, _, feat = features(nn(proj[span, 0:PD], pick[:, 512:1024]), bias[...], coef[...], 0)
            state = state + tn(feat.astype(bf16), proj[span, PD : 2 * PD])
    follow = later[0]
    causal = causal_mask()
    coefs = coef[...]
    for chunk in range(chunks - 1, -1, -1):
        at = chunk * CHUNK
        span = slice(at, at + CHUNK)
        base = proj[span, 0:PD]
        value = proj[span, PD : 2 * PD]
        grad = grads[span, :]
        picked = nn(base, pick[...])
        q_one, q_two, feat_q = features(picked, bias[...], coefs, 0)
        k_one, k_two, feat_k = features(picked, bias[...], coefs, 512)
        key_low = picked[:, 1024:1152].astype(bf16)
        query_high = picked[:, 1152:1280].astype(bf16)
        score = nt(base, key_low)
        weight = jnp.where(causal, 1.0 + score + 0.5 * score * score, 0.0).astype(bf16)
        slope = jnp.where(causal, nt(grad, value) * (1.0 + score), 0.0).astype(bf16)
        follow_round = follow.astype(bf16)
        q_up = nt(grad, states[chunk]) * coefs
        k_up = nt(value, follow_round) * coefs
        low = nn(slope, key_low) + tn(slope, query_high)
        low = low + nt((q_up * q_two).astype(bf16), pick[:, 0:256])
        low = low + nt((q_up * q_one).astype(bf16), pick[:, 256:512])
        low = low + nt((k_up * k_two).astype(bf16), pick[:, 512:768])
        low = low + nt((k_up * k_one).astype(bf16), pick[:, 768:1024])
        out[span, 0:PD] = low.astype(bf16)
        out[span, PD : 2 * PD] = (
            tn(weight, grad) + nn(feat_k.astype(bf16), follow_round)
        ).astype(bf16)
        follow = follow + tn(feat_q.astype(bf16), grad)
        gate = proj[span, 6 * PD : 7 * PD].astype(f32)
        up = ups[span, :].astype(f32)
        sig = jax.nn.sigmoid(gate)
        flow[span, :] = up * gate * sig
        slope_gate = sig * (1.0 + gate * (1.0 - sig))
        out[span, 6 * PD : 7 * PD] = (up * conv_of(conv, tap, at, CHUNK) * slope_gate).astype(bf16)
    for number in range(rows // QB):
        span = slice(number * QB, (number + 1) * QB)
        band = slice(number * QB, number * QB + QB + WIN)
        query = proj[span, 2 * PD : 3 * PD]
        key = keys[band, :]
        prob = window_prob(query, key, number)
        up = ups[span, :]
        prob_grad = nt(up, vals[band, :])
        inner = jnp.sum(prob * prob_grad, -1, keepdims=True)
        score = (prob * (prob_grad - inner)).astype(bf16)
        out[span, 2 * PD : 3 * PD] = (nn(score, key) * HD ** (-0.5)).astype(bf16)
        dkeys[band, :] += tn(score, query) * HD ** (-0.5)
        dvals[band, :] += tn(prob.astype(bf16), up)
    out[:, 3 * PD : 4 * PD] = dkeys[WIN:, :].astype(bf16)
    out[:, 4 * PD : 5 * PD] = dvals[WIN:, :].astype(bf16)
    grad_in = tap[0:1] * flow[0:rows, :]
    for offset in range(1, KW):
        grad_in = grad_in + tap[offset : offset + 1] * flow[offset : offset + rows, :]
    out[:, 5 * PD : 6 * PD] = grad_in.astype(bf16)
    last = slice(rows - 16, rows)
    edge = grad_in[rows - 16 :, :] + lent[0, WIN : WIN + 16, 0:PD].astype(f32)
    out[last, 5 * PD : 6 * PD] = edge.astype(bf16)
    right_grad[...] = tn(rank[...], out[...])

    @pl.when(pl.program_id(0) == 0)
    def _():
        rank_grad[...] = nt(out[...], right[...])

    @pl.when(pl.program_id(0) > 0)
    def _():
        rank_grad[...] += nt(out[...], right[...])


def attend_back(spots, proj, tails, prior, later, lent, ups, grads, table, rank, tables):
    rows = proj.shape[0]
    whole = lambda a: pl.BlockSpec(a.shape, lambda h: (0,) * a.ndim)
    head = pl.BlockSpec((rows, HEAD_PAD), lambda h: (0, h))
    edge = pl.BlockSpec((1, WIN + 16, 2 * PD), lambda h: (h, 0, 0))
    state = pl.BlockSpec((1, 256, PD), lambda h: (h, 0, 0))
    column = pl.BlockSpec((rows, PD), lambda h: (0, h))
    return pl.pallas_call(
        functools.partial(attend_back_kernel, spots),
        grid=(2,),
        out_shape=(
            jax.ShapeDtypeStruct((rows, 2 * HEAD_PAD), bf16),
            jax.ShapeDtypeStruct((rows, R), f32),
            jax.ShapeDtypeStruct((R, 2 * HEAD_PAD), f32),
        ),
        in_specs=[head, edge, state, state, edge, column, column, whole(table), whole(rank)]
        + [whole(t) for t in tables],
        out_specs=(
            head,
            pl.BlockSpec((rows, R), lambda h: (0, 0)),
            pl.BlockSpec((R, HEAD_PAD), lambda h: (0, h)),
        ),
        scratch_shapes=[
            pltpu.VMEM((rows + WIN, PD), bf16),
            pltpu.VMEM((rows + WIN, PD), bf16),
            pltpu.VMEM((rows + 16, PD), f32),
            pltpu.VMEM((rows + 16, PD), f32),
            pltpu.VMEM((rows + WIN, PD), f32),
            pltpu.VMEM((rows + WIN, PD), f32),
            pltpu.VMEM((rows // CHUNK, 256, PD), bf16),
        ],
        compiler_params=params(48),
        cost_estimate=pl.CostEstimate(
            flops=100_000_000, bytes_accessed=300_000, transcendentals=0
        ),
        name="attend_back",
    )(proj, tails, prior, later, lent, ups, grads, table, rank, *tables)


def first_back_kernel(*refs):
    grads = refs[0:4]
    rank_grad, left = refs[4:6]
    sources = refs[6 : 6 + 16]
    part, weight, sems = refs[22:]
    groups = []
    size = 2 * HEAD_PAD
    for slot in range(SLOTS):
        pieces = sources[0:1] if slot == 0 else sources[1 + 5 * (slot - 1) : 1 + 5 * slot]
        groups.append(mixer_copies(pieces, slot == 0, weight, size * slot))
    begin = pl.program_id(0) == 0

    @pl.when(begin)
    def _():
        for slot in range(SLOTS):
            run_copies(groups[slot], sems, 40 * slot)
        for slot in range(SLOTS):
            mixer_pads(weight, size * slot)

    total = nn(rank_grad[...].astype(bf16), left[...])
    for slot in range(SLOTS):

        @pl.when(begin)
        def _():
            wait_copies(groups[slot], sems, 40 * slot)

        total = total + nn(grads[slot][...], weight[size * slot : size * (slot + 1), :])
    part[...] = total.astype(bf16)


def first_back(number, grads, rank_grad, left, sources):
    rows = rank_grad.shape[0]
    width = left.shape[1]
    block = rows // 4
    whole = lambda a: pl.BlockSpec(a.shape, lambda i: (0,) * a.ndim)
    size = 2 * HEAD_PAD
    return pl.pallas_call(
        first_back_kernel,
        grid=(2,),
        out_shape=jax.ShapeDtypeStruct((rows // 2, width), bf16),
        in_specs=[pl.BlockSpec((block, size), lambda i: (2 * i + number, 0))] * 4
        + [pl.BlockSpec((block, R), lambda i: (2 * i + number, 0)), whole(left)]
        + [ANY] * len(sources),
        out_specs=pl.BlockSpec((block, width), lambda i: (i, 0)),
        scratch_shapes=[pltpu.VMEM((SLOTS * size, width), bf16), pltpu.SemaphoreType.DMA((160,))],
        compiler_params=params(56),
        cost_estimate=pl.CostEstimate(
            flops=100_000_000, bytes_accessed=300_000, transcendentals=0
        ),
        name="first_back",
    )(*grads, rank_grad, left, *sources)


def norm_two_kernel(own, other, wide, gain, left, middle, second, rank):
    total = wide[...].astype(f32) + (own[...].astype(f32) + other[...].astype(f32))
    scale = lax.rsqrt(jnp.mean(total * total, -1, keepdims=True) + epsilon)
    rounded = (total * scale * gain[...]).astype(bf16)
    middle[...] = total
    second[...] = rounded
    rank[...] = nn(rounded, left[...]).astype(bf16)


def norm_two(own, other, wide, gain, left):
    rows, width = own.shape
    block = pl.BlockSpec((CHUNK, width), lambda i: (i, 0))
    whole = lambda a: pl.BlockSpec(a.shape, lambda i: (0,) * a.ndim)
    return pl.pallas_call(
        norm_two_kernel,
        grid=(rows // CHUNK,),
        out_shape=(
            jax.ShapeDtypeStruct((rows, width), f32),
            jax.ShapeDtypeStruct((rows, width), bf16),
            jax.ShapeDtypeStruct((rows, R), bf16),
        ),
        in_specs=[block, block, block, whole(gain), whole(left)],
        out_specs=(block, block, pl.BlockSpec((CHUNK, R), lambda i: (i, 0))),
        compiler_params=params(40),
        cost_estimate=pl.CostEstimate(
            flops=100_000_000, bytes_accessed=300_000, transcendentals=0
        ),
        name="norm_two",
    )(own, other, wide, gain, left)


def back_two_kernel(own, other, middle, upstream, gain, right, mixer_up, rgrad):
    vector = middle[...]
    scale = lax.rsqrt(jnp.mean(vector * vector, -1, keepdims=True) + epsilon)
    flow = gain[...] * (own[...].astype(f32) + other[...].astype(f32))
    inner = jnp.mean(vector * flow, -1, keepdims=True)
    total = upstream[...].astype(f32) + scale * flow - vector * (scale * scale * scale * inner)
    rounded = total.astype(bf16)
    mixer_up[...] = rounded
    rgrad[...] = nt(rounded, right[...]).astype(bf16)


def back_two(own, other, middle, upstream, gain, right):
    rows, width = own.shape
    block = pl.BlockSpec((CHUNK, width), lambda i: (i, 0))
    whole = lambda a: pl.BlockSpec(a.shape, lambda i: (0,) * a.ndim)
    return pl.pallas_call(
        back_two_kernel,
        grid=(rows // CHUNK,),
        out_shape=(
            jax.ShapeDtypeStruct((rows, width), bf16),
            jax.ShapeDtypeStruct((rows, R), bf16),
        ),
        in_specs=[block, block, block, block, whole(gain), whole(right)],
        out_specs=(block, pl.BlockSpec((CHUNK, R), lambda i: (i, 0))),
        compiler_params=params(40),
        cost_estimate=pl.CostEstimate(
            flops=100_000_000, bytes_accessed=300_000, transcendentals=0
        ),
        name="back_two",
    )(own, other, middle, upstream, gain, right)


def swap_core(array):
    return lax.ppermute(array, "core", [(0, 1), (1, 0)])


def swap_chip(array, bit):
    count = lax.axis_size("chip")
    return lax.ppermute(array, "chip", [(i, i ^ bit) for i in range(count)])


def swap_tp(array, bit):
    return lax.ppermute(array, "tp", [(i, i ^ bit) for i in range(4)])


def both_cores(own):
    other = swap_core(own)
    lead = lax.axis_index("core") == 0
    return jnp.concatenate([jnp.where(lead, own, other), jnp.where(lead, other, own)], 0)


def own_rows(array, core):
    half = array.shape[0] // 2
    return lax.dynamic_slice_in_dim(array, core * half, half, 0)


def hold_kernel(*refs):
    pass


def hold(*arrays, after=()):
    return pl.pallas_call(
        hold_kernel,
        out_shape=tuple(jax.ShapeDtypeStruct(a.shape, a.dtype) for a in arrays),
        in_specs=[ANY] * (len(arrays) + len(after)),
        out_specs=(ANY,) * len(arrays),
        input_output_aliases={i: i for i in range(len(arrays))},
        compiler_params=pltpu.CompilerParams(has_side_effects=True),
        name="hold",
    )(*arrays, *after)


def hop_xy(piece):
    return swap_chip(piece, 1), swap_chip(piece, 2)


def hop_diag(from_x, from_y, cut):
    return swap_chip(from_y[:cut], 1), swap_chip(from_x[cut:], 2)


def cross(array):
    return lax.ppermute(array, "tp", [(1, 2), (2, 1)])


def edge(array):
    return lax.ppermute(array, "tp", [(1, 0), (2, 3)])


def pick_inner(inner_array, edge_array):
    z = lax.axis_index("tp")
    return jnp.where((z == 1) | (z == 2), inner_array, edge_array)


def add_swapped(array, bit):
    other = swap_chip(array, bit)
    return (array.astype(f32) + other.astype(f32)).astype(array.dtype)


def add_rest(array):
    bit = 2
    while bit < lax.axis_size("chip"):
        array = add_swapped(array, bit)
        bit *= 2
    return array


def neighbour_chip(array, by):
    count = lax.axis_size("chip")
    pairs = [(i, i + by) for i in range(count) if 0 <= i + by < count]
    return lax.ppermute(array, "chip", pairs)


def carried(states, backward):
    if backward and lax.axis_size("chip") == 4:
        return tuple(swap_chip(states, bit) for bit in (1, 2, 3))
    return (lax.all_gather(states, "chip"),)


def carried_sum(parts, backward):
    chip = lax.axis_index("chip")
    if len(parts) > 1:
        total = 0.0
        for bit, part in zip((1, 2, 3), parts):
            other = chip ^ bit
            ahead = (other > chip) if backward else (other < chip)
            total = total + jnp.where(ahead, part.astype(f32), 0.0)
    else:
        index = jnp.arange(lax.axis_size("chip"), dtype=jnp.int32)
        ahead = (index > chip) if backward else (index < chip)
        total = jnp.sum(jnp.where(ahead[:, None, None, None], parts[0].astype(f32), 0.0), 0)
    return jnp.pad(total, ((0, 0), (0, 256 - STATE), (0, 0)))


def stack_tp(parts):
    z = lax.axis_index("tp")
    result = jnp.zeros((SLOTS,) + parts[0].shape, parts[0].dtype)
    for slot, part in enumerate(parts):
        result = lax.dynamic_update_index_in_dim(result, part, z ^ slot, 0)
    return result


def pad_heads(table):
    lead = table.shape[:-2]
    heads = table.shape[-2]
    zero = [(0, 0)] * (len(lead) + 1)
    low = jnp.pad(table[..., : 2 * FD], zero + [(0, PD - 2 * FD)])
    high = table[..., 2 * FD :].reshape(lead + (heads, 6, HD))
    high = jnp.pad(high, zero + [(0, 0), (0, PD - HD)]).reshape(lead + (heads, 6 * PD))
    return jnp.concatenate([low, high], -1).reshape(lead + (heads * HEAD_PAD,))


def trim_heads(table):
    lead = table.shape[:-1]
    table = table.reshape(lead + (2, 7, PD))
    low = table[..., 0, : 2 * FD]
    high = table[..., 1:, :HD].reshape(lead + (2, 6 * HD))
    return jnp.concatenate([low, high], -1)


def pad_last(table, size):
    return jnp.pad(table, [(0, 0)] * (table.ndim - 1) + [(0, size - table.shape[-1])])


def norm_rows(vector, gain_vector):
    row_scale = lax.rsqrt(jnp.mean(vector * vector, -1, keepdims=True) + epsilon)
    return (vector * row_scale * gain_vector, row_scale)


def norm_back(vector, row_scale, gain_vector, upstream):
    inner_mean = jnp.mean(vector * gain_vector * upstream, -1, keepdims=True)
    return (
        row_scale * gain_vector * upstream - vector * row_scale * row_scale * row_scale * inner_mean
    )


def body(
    block_input,
    gain_first,
    frozen_mixer_weight,
    conv_filter,
    frozen_output_weight,
    gain_second,
    frozen_gate_up_weight,
    frozen_down_weight,
    mixer_left,
    mixer_right,
    output_left,
    output_right,
    gateup_left,
    gateup_right,
    down_left,
    down_right,
    adapter_index,
    seq_lengths,
    out_cotangent,
):
    chip = lax.axis_index("chip")
    core = lax.axis_index("core")
    z = lax.axis_index("tp")
    y, x = place()
    sequences, length, width = block_input.shape
    rows = 2 * length
    heads_here = frozen_mixer_weight.shape[1]
    ff_here = frozen_down_weight.shape[0]
    half = ff_here // 2
    pad = (half + PD - 1) // PD * PD
    quarter = half // 2

    pick, bias, coef = feature_tables()
    tables = (jnp.asarray(pick, bf16), jnp.asarray(bias), jnp.asarray(coef))

    w_mix = jnp.transpose(frozen_mixer_weight, (1, 2, 0)).reshape(heads_here * HCOLS, width)
    w_gate = jnp.transpose(frozen_gate_up_weight, (1, 2, 0)).reshape(2 * ff_here, width)
    w_out = frozen_output_weight
    w_down = frozen_down_weight
    side = width // 2

    def cut(matrix, start, count):
        return lax.dynamic_slice(matrix, (start, x * side), (count, side))

    mixer_piece = jnp.concatenate(
        [
            cut(w_mix, 2 * HCOLS * core + HCOLS * y, HCOLS),
            cut(w_out, 2 * HD * core + HD * y, HD),
        ],
        0,
    )
    feed_piece = jnp.concatenate(
        [
            cut(w_gate, half * core + quarter * y, quarter),
            cut(w_gate, ff_here + half * core + quarter * y, quarter),
            cut(w_down, half * core + quarter * y, quarter),
        ],
        0,
    )
    slot_seq = z ^ jnp.arange(SLOTS, dtype=jnp.int32)
    slot_adapter = jnp.sum(
        jnp.where(slot_seq[:, None] == jnp.arange(SLOTS)[None, :], adapter_index[None, :], 0), 1
    )
    onehot = slot_adapter[:, None] == jnp.arange(NA, dtype=jnp.int32)[None, :]

    def select(table):
        return jnp.einsum(
            "se,e...->s...", onehot.astype(bf16), table, preferred_element_type=f32
        ).astype(bf16)

    mine = slot_adapter[0]
    my_mixer_left = lax.dynamic_index_in_dim(mixer_left, mine, 0, False)
    my_output_right = lax.dynamic_index_in_dim(output_right, mine, 0, False)
    my_gateup_left = lax.dynamic_index_in_dim(gateup_left, mine, 0, False)
    my_down_right = lax.dynamic_index_in_dim(down_right, mine, 0, False)
    right_table = pad_heads(
        select(lax.dynamic_slice_in_dim(mixer_right, 2 * core, 2, 2))
    )
    out_table = lax.dynamic_slice_in_dim(jnp.swapaxes(output_left, 1, 2), 2 * HD * core, 2 * HD, 2)
    out_table = pad_last(select(out_table).reshape(SLOTS, R, 2, HD), PD).reshape(SLOTS, R, 2 * PD)
    gate_table = lax.dynamic_slice_in_dim(gateup_right, half * core, half, 3)
    gate_table = pad_last(select(gate_table), pad).reshape(SLOTS, R, 2 * pad)
    down_table = lax.dynamic_slice_in_dim(jnp.swapaxes(down_left, 1, 2), half * core, half, 2)
    down_table = pad_last(select(down_table), pad)
    taps = lax.dynamic_slice_in_dim(conv_filter, 2 * HD * core, 2 * HD, 1)
    taps = pad_last(taps.reshape(KW, 2, HD), PD).reshape(KW, 2 * PD)
    taps = jnp.broadcast_to(jnp.pad(taps, ((0, R - KW), (0, 0))), (SLOTS, R, 2 * PD))
    packed = jnp.concatenate([right_table, out_table, gate_table, down_table, taps], 2)
    spots = Table(pad)

    gain_one = gain_first.astype(f32)
    gain_two = gain_second.astype(f32)[None, :]
    own_input = lax.dynamic_index_in_dim(block_input, z, 0, False)
    own_cotangent = lax.dynamic_index_in_dim(out_cotangent, z, 0, False)
    my_length = lax.dynamic_index_in_dim(seq_lengths, z, 0, False)
    upstream_own = jnp.where(
        (((chip * 2 + core) * length + jnp.arange(length, dtype=jnp.int32)) < my_length)[:, None],
        own_cotangent,
        0.0,
    ).astype(bf16)

    e_m, c_m = swap_tp(mixer_piece, 1), cross(mixer_piece)
    both_input = both_cores(own_input)
    first = norm_rows(both_input.astype(f32), gain_one)[0].astype(bf16)
    mixer_rank = nn(first, my_mixer_left).astype(bf16)
    e_m, c_m, mixer_rank, packed = hold(e_m, c_m, mixer_rank, packed)

    projs, tails, states = [], [], []
    borrowed, prior, mixed, numer = [None] * SLOTS, [None] * SLOTS, [], []
    slots = [packed[0], None, None, None]

    def attend_slot(slot):
        out = attend(spots, projs[slot], borrowed[slot], prior[slot], slots[slot], tables)
        for kept, value in zip((mixed, numer), out):
            kept.append(value)

    def project_slot(slot, refs):
        out = project(slot == 0, first, mixer_rank, slots[slot], tables, refs)
        for kept, value in zip((projs, tails, states), out):
            kept.append(value)

    def exchange(slot):
        edges_here = jnp.concatenate(tails[slot : slot + 2], 0).reshape(4, 2 * (WIN + 16), PD)
        states_here = jnp.concatenate(states[slot : slot + 2], 0)
        return lax.all_gather(jnp.concatenate([states_here, edges_here], 1), "chip")

    def use_exchange(slot, gathered):
        total = carried_sum((gathered[:, :, :STATE],), False)
        before = lax.dynamic_index_in_dim(gathered, jnp.maximum(chip - 1, 0), 0, False)
        before = jnp.where(chip > 0, before[:, STATE:], 0.0).astype(bf16)
        before = before.reshape(4, WIN + 16, 2 * PD)
        borrowed[slot], borrowed[slot + 1] = before[:2], before[2:]
        prior[slot], prior[slot + 1] = total[:2], total[2:]

    x1, y1 = hop_xy(e_m)
    c2_m, f_m = cross(e_m), edge(c_m)
    table1 = swap_tp(packed[1], 1)
    project_slot(0, (w_mix,))
    slot2 = pick_inner(c2_m, f_m)
    x1, y1, slot2, c2_m, c_m, tails[0], states[0], table1, feed_piece, packed = hold(
        x1, y1, slot2, c2_m, c_m, tails[0], states[0], table1, feed_piece, packed
    )
    slots[1] = table1
    d1 = hop_diag(x1, y1, M_CUT)
    x2, y2 = hop_xy(slot2)
    f2_m = edge(c2_m)
    table2, table3 = swap_tp(packed[2], 2), swap_tp(packed[3], 3)
    slot3 = pick_inner(c_m, f2_m)
    x2, y2, slot3, feed_piece, table2, table3, *d1 = hold(
        x2, y2, slot3, feed_piece, table2, table3, *d1
    )
    slots[2], slots[3] = table2, table3
    d2 = hop_diag(x2, y2, M_CUT)
    x3, y3 = hop_xy(slot3)
    e_f = swap_tp(feed_piece, 1)
    set1 = (e_m, x1, y1, *d1)
    project_slot(1, set1)
    x3, y3, e_f, tails[0], tails[1], states[0], states[1], upstream_own, *d2 = hold(
        x3, y3, e_f, tails[0], tails[1], states[0], states[1], upstream_own, *d2
    )
    d3 = hop_diag(x3, y3, M_CUT)
    c_f = cross(feed_piece)
    exchanged = exchange(0)
    set2 = (slot2, x2, y2, *d2)
    project_slot(2, set2)
    upstream = both_cores(upstream_own)
    down_rgrad = nt(upstream, my_down_right).astype(bf16)
    c_f, states[2], down_rgrad, *d3 = hold(c_f, states[2], down_rgrad, *d3)
    fx1, fy1 = hop_xy(e_f)
    c2_f, f_f = cross(e_f), edge(c_f)
    set3 = (slot3, x3, y3, *d3)
    project_slot(3, set3)
    fslot2 = pick_inner(c2_f, f_f)
    fx1, fy1, fslot2, c2_f, c_f, tails[3], states[2], states[3], exchanged = hold(
        fx1, fy1, fslot2, c2_f, c_f, tails[3], states[2], states[3], exchanged
    )
    use_exchange(0, exchanged)
    fd1 = hop_diag(fx1, fy1, feed_cut(quarter))
    fx2, fy2 = hop_xy(fslot2)
    f2_f = edge(c2_f)
    exchanged = exchange(2)
    attend_slot(0)
    attend_slot(1)
    fslot3 = pick_inner(c_f, f2_f)
    fx2, fy2, fslot3, mixed[0], mixed[1], exchanged, *fd1 = hold(
        fx2, fy2, fslot3, mixed[0], mixed[1], exchanged, *fd1
    )
    use_exchange(2, exchanged)
    fd2 = hop_diag(fx2, fy2, feed_cut(quarter))
    fx3, fy3 = hop_xy(fslot3)
    attend_slot(2)
    attend_slot(3)
    sets = list(set1) + list(set2) + list(set3)
    out_part, out_rank = mix_out(spots, mixed, slots, my_output_right, [w_out] + sets)
    other_part = swap_core(out_part)
    middle, second, gate_rank = norm_two(out_part, other_part, both_input, gain_two, my_gateup_left)
    weights_feed = [
        (w_gate, w_down),
        (e_f, fx1, fy1, *fd1),
        None,
        None,
    ]

    gateup_left_t = my_gateup_left.T
    carry = ()
    gate_grads, down_grads = [], []
    for slot in range(SLOTS):
        out = feed(
            slot == 0,
            slot == SLOTS - 1,
            half,
            spots,
            second,
            upstream,
            gate_rank,
            down_rgrad,
            slots[slot],
            my_down_right,
            gateup_left_t,
            weights_feed[slot],
            carry,
        )
        carry = list(out[:3])
        if slot == 0:
            fx3, fy3, carry[2], *fd2 = hold(fx3, fy3, carry[2], *fd2)
            weights_feed[2] = (fslot2, fx2, fy2, *fd2)
            fd3 = hop_diag(fx3, fy3, feed_cut(quarter))
        if slot == 1:
            carry[2], *fd3 = hold(carry[2], *fd3)
            weights_feed[3] = (fslot3, fx3, fy3, *fd3)
        gate_grads.append(out[3])
        down_grads.append(out[4])
    down_part, back_part, ranks = carry
    down_rank, gateup_rgrad = ranks[:, :R].astype(bf16), ranks[:, R:].astype(bf16)
    other_back = swap_core(back_part)
    other_down = swap_core(own_rows(down_part, 1 - core))
    own_down = own_rows(down_part, core).astype(f32)
    own_output = own_rows(middle, core) + (own_down + other_down.astype(f32))
    own_output = own_output.astype(bf16)
    mixer_up, output_rgrad = back_two(
        back_part, other_back, middle, upstream, gain_two, my_output_right
    )

    ups, grads, back_states, lent, left_grads = [], [], [], [], []

    def back_exchange(slot):
        edges_here = jnp.concatenate(lent[slot : slot + 2], 0)
        states_here = jnp.concatenate(back_states[slot : slot + 2], 0)
        return (neighbour_chip(edges_here, -1),) + carried(states_here, True)

    weights_out = [(w_out,), set1, set2, set3]
    for slot in range(SLOTS):
        out = turn(
            slot == 0,
            spots,
            mixer_up,
            output_rgrad,
            slots[slot],
            numer[slot],
            mixed[slot],
            projs[slot],
            borrowed[slot],
            tables,
            weights_out[slot],
        )
        for kept, value in zip((ups, grads, back_states, lent, left_grads), out):
            kept.append(value)
        if slot == 1:
            *both, own_output = hold(*lent, *back_states, own_output)
            lent, back_states = both[:2], both[2:]
            block_output = lax.all_gather(own_output, "tp")
            crossing = back_exchange(0)
    lent[2], lent[3], back_states[2], back_states[3], *crossing = hold(
        *lent[2:], *back_states[2:], *crossing
    )

    def back_slot(slot, returned, later):
        pair = slice(slot % 2 * 2, slot % 2 * 2 + 2)
        return attend_back(
            spots,
            projs[slot],
            borrowed[slot],
            prior[slot],
            later[pair],
            returned[pair],
            ups[slot],
            grads[slot],
            slots[slot],
            mixer_rank,
            tables,
        )

    returned, later = crossing[0], carried_sum(crossing[1:], True)
    crossing = back_exchange(2)
    backs = [back_slot(0, returned, later), back_slot(1, returned, later)]
    early_rank = backs[0][1] + backs[1][1]
    shared = jnp.stack(
        [
            tn(out_rank.astype(bf16), mixer_up),
            tn(gateup_rgrad, second),
            tn(down_rank, upstream),
        ]
    )
    owned = jnp.stack(
        [jnp.concatenate([left_grads[i], gate_grads[i], down_grads[i]], 1) for i in range(SLOTS)]
    ).astype(bf16)
    shared, owned, early_rank, *crossing = hold(shared, owned, early_rank, *crossing)
    returned, later = crossing[0], carried_sum(crossing[1:], True)
    shared_x, owned_x = swap_chip(shared, 1), swap_chip(owned, 1)
    backs = backs + [back_slot(2, returned, later), back_slot(3, returned, later)]
    rank_grad = early_rank + backs[2][1] + backs[3][1]
    rank_grad, shared_x, owned_x = hold(rank_grad, shared_x, owned_x)

    def join(array, other):
        return (array.astype(f32) + other.astype(f32)).astype(array.dtype)

    def by_core(own, other):
        lead = core == 0
        return jnp.stack([jnp.where(lead, own, other), jnp.where(lead, other, own)])

    def slots_of(owned, shared):
        flat = shared.reshape(-1)
        size = owned.size // SLOTS
        sent = [jnp.concatenate([owned[k].reshape(-1), flat.astype(bf16)]) for k in range(SLOTS)]
        got = [sent[0]] + [swap_tp(sent[bit], bit) for bit in (1, 2, 3)]
        return got, lambda got: (
            jnp.stack([g[:size].reshape(owned.shape[1:]) for g in got]).astype(f32),
            [g[size:].reshape(shared.shape).astype(f32) for g in got],
        )

    shared, owned = join(shared, shared_x), join(owned, owned_x)
    shared, owned = add_rest(shared), add_rest(owned)
    mixer_all = jnp.concatenate(
        [
            jnp.stack([back[2] for back in backs]),
            tn(rank_grad.astype(bf16), first)[None],
        ],
        0,
    ).astype(bf16)
    proj_grads = [back[0] for back in backs]
    left_t = my_mixer_left.T
    flat_mix = [w_mix] + sets
    part_a = first_back(0, proj_grads, rank_grad, left_t, flat_mix)
    part_a, rank_grad, mixer_all, shared, owned = hold(
        part_a, rank_grad, mixer_all, shared, owned, after=(block_output,)
    )
    block = length // 2

    def finish(part, number):
        here = lax.dynamic_slice_in_dim(part, core * block, block, 0)
        there = lax.dynamic_slice_in_dim(part, (1 - core) * block, block, 0)
        total = here.astype(f32) + swap_core(there).astype(f32)
        wide = own_input[number * block : (number + 1) * block].astype(f32)
        scale_one = lax.rsqrt(jnp.mean(wide * wide, -1, keepdims=True) + epsilon)
        straight = lax.dynamic_slice_in_dim(
            mixer_up, core * length + number * block, block, 0
        ).astype(f32)
        return (straight + norm_back(wide, scale_one, gain_one, total)).astype(bf16)

    done_a = finish(part_a, 0)
    e_a, c_a = swap_tp(done_a, 1), cross(done_a)
    mixer_x = swap_chip(mixer_all, 1)
    shared_core, owned_core = swap_core(shared), swap_core(owned)
    part_b = first_back(1, proj_grads, rank_grad, left_t, flat_mix)
    e_a, c_a, part_b, mixer_x, shared_core, owned_core = hold(
        e_a, c_a, part_b, mixer_x, shared_core, owned_core
    )
    done_b = finish(part_b, 1)
    c2_a, f_a = cross(e_a), edge(c_a)
    e_b, c_b = swap_tp(done_b, 1), cross(done_b)
    mixer_all = add_rest(join(mixer_all, mixer_x))
    shared = shared + shared_core
    owned = jnp.swapaxes(by_core(owned, owned_core), 0, 1)
    c2_a, f_a, e_b, c_b, mixer_all, shared, owned = hold(
        c2_a, f_a, e_b, c_b, mixer_all, shared, owned
    )
    f2_a, c2_b, f_b = edge(c2_a), cross(e_b), edge(c_b)
    mixer_core = swap_core(mixer_all)
    f2_a, c2_b, f_b, mixer_core, shared, owned = hold(f2_a, c2_b, f_b, mixer_core, shared, owned)
    f2_b = edge(c2_b)
    mixer_owned = jnp.swapaxes(by_core(mixer_all[:SLOTS], mixer_core[:SLOTS]), 0, 1)
    mixer_shared = mixer_all[SLOTS].astype(f32) + mixer_core[SLOTS].astype(f32)
    early, split_early = slots_of(owned, shared)
    late, split_late = slots_of(mixer_owned, mixer_shared)
    owned, shared = split_early(early)
    right_sum, mixer_shared = split_late(late)
    z_a = [done_a, e_a, pick_inner(c2_a, f_a), pick_inner(c_a, f2_a)]
    z_b = [done_b, e_b, pick_inner(c2_b, f_b), pick_inner(c_b, f2_b)]
    input_grad = jnp.zeros(block_input.shape, bf16)
    for number, parts in enumerate((z_a, z_b)):
        for slot, part in enumerate(parts):
            input_grad = lax.dynamic_update_slice(
                input_grad, part[None], (z ^ slot, number * block, 0)
            )

    slot_hot = onehot.astype(f32)

    def spread(hot, parts):
        shape = (NA,) + (1,) * parts[0].ndim
        return sum(hot[i].reshape(shape) * parts[i][None] for i in range(SLOTS))

    grad_mixer_left = jnp.swapaxes(spread(slot_hot, mixer_shared), 1, 2)
    grad_output_right = spread(slot_hot, [s[0] for s in shared])
    grad_gateup_left = jnp.swapaxes(spread(slot_hot, [s[1] for s in shared]), 1, 2)
    grad_down_right = spread(slot_hot, [s[2] for s in shared])
    first_edge = 2 * HEAD_PAD
    edges = [edge_at - first_edge for edge_at in spots.edges]
    b, c, d = [owned[..., edges[i] : edges[i + 1]] for i in (1, 2, 3)]
    a = jnp.moveaxis(trim_heads(right_sum), 1, 2).reshape(SLOTS, R, heads_here, HCOLS)
    grad_mixer_right = spread(slot_hot, a)
    b = b.reshape(SLOTS, 2, R, 2, PD)[..., :HD]
    b = jnp.moveaxis(b, 1, 2).reshape(SLOTS, R, heads_here * HD)
    grad_output_left = jnp.swapaxes(spread(slot_hot, b), 1, 2)
    c = c.reshape(SLOTS, 2, R, 2, pad)[..., :half]
    c = jnp.moveaxis(c, 1, 3).reshape(SLOTS, R, 2, ff_here)
    grad_gateup_right = spread(slot_hot, c)
    d = jnp.moveaxis(d[..., :half], 1, 2).reshape(SLOTS, R, ff_here)
    grad_down_left = jnp.swapaxes(spread(slot_hot, d), 1, 2)
    return (
        block_output,
        input_grad,
        grad_mixer_left,
        grad_mixer_right,
        grad_output_left,
        grad_output_right,
        grad_gateup_left,
        grad_gateup_right,
        grad_down_left,
        grad_down_right,
    )


def solution(mesh):
    seq, tp = mesh.devices.shape
    fine = Mesh(mesh.devices.reshape(seq // 2, 2, tp), ("chip", "core", "tp"))
    where = ("chip", "core")
    return jax.shard_map(
        body,
        mesh=fine,
        in_specs=(
            P(None, where, None),
            P(),
            P(None, "tp", None),
            P(None, "tp"),
            P("tp", None),
            P(),
            P(None, None, "tp"),
            P("tp", None),
            P(),
            P(None, None, "tp", None),
            P(None, "tp", None),
            P(),
            P(),
            P(None, None, None, "tp"),
            P(None, "tp", None),
            P(),
            P(),
            P(),
            P(None, where, None),
        ),
        out_specs=(
            P(None, where, None),
            P(None, where, None),
            P(),
            P(None, None, "tp", None),
            P(None, "tp", None),
            P(),
            P(),
            P(None, None, None, "tp"),
            P(None, "tp", None),
            P(),
        ),
        check_vma=False,
    )
```

```python
import functools

import jax
import jax.numpy as jnp
import numpy as np
from jax import lax
from jax.experimental import pallas as pl
from jax.experimental.pallas import tpu as pltpu
from jax.sharding import Mesh
from jax.sharding import PartitionSpec as P

HD = 112
PD = 128
FD = 16
R = 16
NA = 8
KW = 3
WIN = 64
HCOLS = 704
SLOTS = 4
HEAD_PAD = 7 * PD
FEATS = 1 + FD + FD * (FD + 1) // 2
STATE = 160
CHUNK = 256
QB = 128

epsilon = 1e-05
masked = -1e30
f32 = jnp.float32
bf16 = jnp.bfloat16
ANY = pl.BlockSpec(memory_space=pl.ANY)


def nn(a, b):
    return lax.dot_general(a, b, (((1,), (0,)), ((), ())), preferred_element_type=f32)


def nt(a, b):
    return lax.dot_general(a, b, (((1,), (1,)), ((), ())), preferred_element_type=f32)


def tn(a, b):
    return lax.dot_general(a, b, (((0,), (0,)), ((), ())), preferred_element_type=f32)


def feature_tables():
    leading, trailing = np.triu_indices(FD)
    pick = np.zeros((PD, 1280), np.float32)
    bias = np.zeros((1, 512), np.float32)
    coef = np.zeros((1, 256), np.float32)
    bias[0, 0] = 1.0
    bias[0, 256 : 256 + 1 + FD] = 1.0
    coef[0, : 1 + FD] = 1.0
    coef[0, 1 + FD : FEATS] = np.where(leading == trailing, np.sqrt(0.5), 1.0)
    for base, row in ((0, 0), (512, FD)):
        for i in range(FD):
            pick[row + i, base + 1 + i] = 0.5
        for n, (i, j) in enumerate(zip(leading, trailing)):
            pick[row + i, base + 1 + FD + n] = 0.5
            pick[row + j, base + 256 + 1 + FD + n] = 0.5
    for i in range(FD):
        pick[FD + i, 1024 + i] = 0.25
        pick[i, 1152 + FD + i] = 0.25
    return pick, bias, coef


HEAD_SEGMENTS = [(0, 2 * FD, 0)] + [(2 * FD + HD * i, HD, PD * (i + 1)) for i in range(6)]
M_ROWS = HCOLS + HD
M_CUT = 2 * FD + 3 * HD


def place():
    j = lax.rem(lax.axis_index("chip"), 4)
    return j // 2, lax.rem(j, 2)


def run_copies(copies, sems, start):
    for number, (src, dst) in enumerate(copies):
        copy = pltpu.make_async_copy(src, dst, sems.at[start + number])
        copy.start()


def wait_copies(copies, sems, start):
    for number, (src, dst) in enumerate(copies):
        pltpu.make_async_copy(src, dst, sems.at[start + number]).wait()


def spread_pieces(refs, cut, rows, dest, base, width, offset_of):
    y, x = place()
    z_ref, x_ref, y_ref, da_ref, db_ref = refs
    copies = []
    for kind, yy, xx in (("z", y, x), ("x", y, 1 - x), ("y", 1 - y, x), ("d", 1 - y, 1 - x)):
        cols = pl.ds(pl.multiple_of(xx * width, PD), width)
        for first, count in rows:
            spans = [(first, count)]
            if kind == "d" and first < cut < first + count:
                spans = [(first, cut - first), (cut, first + count - cut)]
            for row, size in spans:
                if kind == "d":
                    src = da_ref if row < cut else db_ref
                    src = src.at[pl.ds(row if row < cut else row - cut, size)]
                else:
                    src = {"z": z_ref, "x": x_ref, "y": y_ref}[kind].at[pl.ds(row, size)]
                start = pl.multiple_of(base + offset_of(row, yy), 16)
                copies.append((src, dest.at[pl.ds(start, size), cols]))
    return copies


def mixer_offset(row, yy):
    for first, count, at in HEAD_SEGMENTS:
        if first <= row < first + count:
            return yy * HEAD_PAD + at + row - first
    return None


MIXER_ROWS = [(first, count) for first, count, _ in HEAD_SEGMENTS]


def mixer_copies(refs, own, dest, base):
    if own:
        core = lax.axis_index("core")
        copies = []
        for head in range(2):
            for first, count, at in HEAD_SEGMENTS:
                src = pl.multiple_of(2 * HCOLS * core + HCOLS * head + first, 16)
                copies.append(
                    (refs[0].at[pl.ds(src, count)], dest.at[pl.ds(base + HEAD_PAD * head + at, count)])
                )
        return copies
    return spread_pieces(refs, M_CUT, MIXER_ROWS, dest, base, dest.shape[1] // 2, mixer_offset)


def mixer_pads(dest, base):
    for head in range(2):
        for first, count, at in HEAD_SEGMENTS:
            start = base + HEAD_PAD * head + at + count
            dest[start : start + PD - count] = jnp.zeros((PD - count, dest.shape[1]), bf16)


def output_copies(refs, own, dest, base):
    if own:
        core = lax.axis_index("core")
        return [
            (
                refs[0].at[pl.ds(pl.multiple_of(2 * HD * core + HD * head, 16), HD)],
                dest.at[pl.ds(base + PD * head, HD)],
            )
            for head in range(2)
        ]
    return spread_pieces(
        refs, M_CUT, [(HCOLS, HD)], dest, base, dest.shape[1] // 2, lambda row, yy: yy * PD + row - HCOLS
    )


def output_pads(dest, base):
    for head in range(2):
        start = base + PD * head + HD
        dest[start : start + PD - HD] = jnp.zeros((PD - HD, dest.shape[1]), bf16)


def feed_cut(quarter):
    return quarter + (quarter // 2 + 15) // 16 * 16


def feed_copies(refs, own, dest, half, pad):
    if own:
        core = lax.axis_index("core")
        wg, wd = refs
        spots = [(wg, 0, 0), (wg, 2 * half, pad), (wd, 0, 2 * pad)]
        return [
            (
                ref.at[pl.ds(pl.multiple_of(half * core + first, 16), half)],
                dest.at[pl.ds(at, half)],
            )
            for ref, first, at in spots
        ]
    quarter = half // 2

    def offset_of(row, yy):
        return row // quarter * pad + yy * quarter + row % quarter

    rows = [(quarter * i, quarter) for i in range(3)]
    return spread_pieces(
        refs, feed_cut(quarter), rows, dest, 0, dest.shape[1] // 2, offset_of
    )


def feed_pads(dest, half, pad):
    for i in range(3):
        dest[pad * i + half : pad * (i + 1)] = jnp.zeros((pad - half, dest.shape[1]), bf16)


def features(picked, bias, coef, at):
    one = picked[:, at : at + 256] + bias[:, :256]
    two = picked[:, at + 256 : at + 512] + bias[:, 256:]
    return one, two, one * two * coef


class Table:
    def __init__(self, pad):
        sizes = (2 * HEAD_PAD, 2 * PD, 2 * pad, pad, 2 * PD)
        starts = np.cumsum((0,) + sizes)
        self.right, self.left, self.gate, self.down, self.taps = (
            slice(int(a), int(a) + n) for a, n in zip(starts, sizes)
        )
        self.edges = [int(a) for a in starts]


def params(mib, **more):
    return pltpu.CompilerParams(vmem_limit_bytes=mib * 2**20, **more)


def project_kernel(own, first, rank, table, pick, bias, coef, *rest):
    count = 1 if own else 5
    refs = rest[:count]
    proj, tails, state, weight, sems = rest[count:]
    copies = mixer_copies(refs, own, weight, 0)
    run_copies(copies, sems, 0)
    mixer_pads(weight, 0)
    wait_copies(copies, sems, 0)
    blocks = first.shape[0] // CHUNK
    for head in range(2):
        cols = pl.ds(HEAD_PAD * head, HEAD_PAD)

        def one(block, carry):
            rows = pl.ds(pl.multiple_of(block * CHUNK, CHUNK), CHUNK)
            result = nt(first[rows, :], weight[cols, :]) + nn(rank[rows, :], table[:, cols])
            rounded = result.astype(bf16)
            proj[rows, cols] = rounded
            picked = nn(rounded[:, :PD], pick[...][:, 512:1024])
            _, _, feat = features(picked, bias[...], coef[...], 0)
            return carry + tn(feat.astype(bf16), rounded[:, PD : 2 * PD])

        total = lax.fori_loop(0, blocks, one, jnp.zeros((256, PD), f32))
        state[head] = total[:STATE].astype(bf16)
        last = first.shape[0]
        at = HEAD_PAD * head
        tails[head, 0:WIN, 0:PD] = proj[last - WIN :, at + 3 * PD : at + 4 * PD]
        tails[head, 0:WIN, PD : 2 * PD] = proj[last - WIN :, at + 4 * PD : at + 5 * PD]
        tails[head, WIN : WIN + 16, 0:PD] = proj[last - 16 :, at + 5 * PD : at + 6 * PD]
        tails[head, WIN : WIN + 16, PD : 2 * PD] = jnp.zeros((16, PD), bf16)


def project(own, first, rank, table, tables, refs):
    rows, width = first.shape
    vm = pl.BlockSpec(memory_space=pltpu.VMEM)
    return pl.pallas_call(
        functools.partial(project_kernel, own),
        out_shape=(
            jax.ShapeDtypeStruct((rows, 2 * HEAD_PAD), bf16),
            jax.ShapeDtypeStruct((2, WIN + 16, 2 * PD), bf16),
            jax.ShapeDtypeStruct((2, STATE, PD), bf16),
        ),
        in_specs=[vm] * 6 + [ANY] * len(refs),
        out_specs=(vm, vm, vm),
        scratch_shapes=[pltpu.VMEM((2 * HEAD_PAD, width), bf16), pltpu.SemaphoreType.DMA((40,))],
        compiler_params=params(48),
        cost_estimate=pl.CostEstimate(
            flops=100_000_000, bytes_accessed=300_000, transcendentals=0
        ),
        name="project",
    )(first, rank, table, *tables, *refs)


def window_mask(number):
    query = lax.broadcasted_iota(jnp.int32, (QB, QB + WIN), 0)
    key = lax.broadcasted_iota(jnp.int32, (QB, QB + WIN), 1)
    allowed = (key > query) & (key <= query + WIN)
    if number == 0:
        lead = jnp.where(lax.axis_index("chip") > 0, 0, WIN)
        allowed = allowed & (key >= lead)
    return allowed


def window_prob(query, keys, number):
    scores = nt(query, keys) * HD ** (-0.5)
    scores = jnp.where(window_mask(number), scores, masked)
    largest = jnp.max(scores, -1, keepdims=True)
    expo = jnp.exp(scores - largest)
    return expo / jnp.sum(expo, -1, keepdims=True)


def causal_mask():
    row = lax.broadcasted_iota(jnp.int32, (CHUNK, CHUNK), 0)
    col = lax.broadcasted_iota(jnp.int32, (CHUNK, CHUNK), 1)
    return col <= row


def conv_of(conv, taps, start, count):
    result = taps[0:1] * conv[pl.ds(16 + start, count), :]
    for offset in range(1, KW):
        result = result + taps[offset : offset + 1] * conv[pl.ds(16 + start - offset, count), :]
    return result


def attend_kernel(spots, proj, tails, prior, table, pick, bias, coef, mixed, numer, keys, vals, conv):
    rows = proj.shape[0]
    keys[0:WIN, :] = tails[0, 0:WIN, 0:PD]
    vals[0:WIN, :] = tails[0, 0:WIN, PD : 2 * PD]
    conv[0:16, :] = tails[0, WIN : WIN + 16, 0:PD].astype(f32)
    keys[WIN:, :] = proj[:, 3 * PD : 4 * PD]
    vals[WIN:, :] = proj[:, 4 * PD : 5 * PD]
    conv[16:, :] = proj[:, 5 * PD : 6 * PD].astype(f32)
    tap = head_taps(spots, table)
    state = whole_state(prior[0])
    causal = causal_mask()
    for chunk in range(rows // CHUNK):
        at = chunk * CHUNK
        span = slice(at, at + CHUNK)
        base = proj[span, 0:PD]
        value = proj[span, PD : 2 * PD]
        picked = nn(base, pick[:, :1152])
        _, _, feat_q = features(picked, bias[...], coef[...], 0)
        _, _, feat_k = features(picked, bias[...], coef[...], 512)
        score = nt(base, picked[:, 1024:1152].astype(bf16))
        weight = jnp.where(causal, 1.0 + score + 0.5 * score * score, 0.0).astype(bf16)
        total = nn(weight, value) + nn(feat_q.astype(bf16), state.astype(bf16))
        state = state + tn(feat_k.astype(bf16), value)
        parts = []
        for number in range(chunk * CHUNK // QB, (chunk + 1) * CHUNK // QB):
            query = proj[number * QB : (number + 1) * QB, 2 * PD : 3 * PD]
            prob = window_prob(query, keys[number * QB : number * QB + QB + WIN, :], number)
            parts.append(nn(prob.astype(bf16), vals[number * QB : number * QB + QB + WIN, :]))
        window = jnp.concatenate(parts, 0)
        scale = lax.rsqrt(jnp.sum(total * total, -1, keepdims=True) * (1.0 / HD) + epsilon)
        gate = proj[span, 6 * PD : 7 * PD].astype(f32)
        branch = conv_of(conv, tap, at, CHUNK) * (gate * jax.nn.sigmoid(gate))
        mixed[span, :] = (total * scale + window + branch).astype(bf16)
        numer[span, :] = total.astype(bf16)


def whole_state(state):
    return jnp.concatenate([state, jnp.zeros((256 - STATE, PD), f32)], 0)


def head_taps(spots, table):
    start = pl.multiple_of(spots.taps.start + PD * pl.program_id(0), PD)
    return table[:, pl.ds(start, PD)].astype(f32)


def attend(spots, number, proj, tails, prior, table, tables):
    rows = proj.shape[0]
    whole = lambda a: pl.BlockSpec(a.shape, lambda h: (0,) * a.ndim)
    return pl.pallas_call(
        functools.partial(attend_kernel, spots),
        grid=(2,),
        out_shape=(
            jax.ShapeDtypeStruct((rows, 2 * PD), bf16),
            jax.ShapeDtypeStruct((rows, 2 * PD), bf16),
        ),
        in_specs=[
            pl.BlockSpec((rows, HEAD_PAD), lambda h: (0, h)),
            pl.BlockSpec((1, WIN + 16, 2 * PD), lambda h: (2 * number + h, 0, 0)),
            pl.BlockSpec((1, STATE, PD), lambda h: (2 * number + h, 0, 0)),
            whole(table),
        ]
        + [whole(t) for t in tables],
        out_specs=(
            pl.BlockSpec((rows, PD), lambda h: (0, h)),
            pl.BlockSpec((rows, PD), lambda h: (0, h)),
        ),
        scratch_shapes=[
            pltpu.VMEM((rows + WIN, PD), bf16),
            pltpu.VMEM((rows + WIN, PD), bf16),
            pltpu.VMEM((rows + 16, PD), f32),
        ],
        compiler_params=params(48),
        cost_estimate=pl.CostEstimate(
            flops=100_000_000, bytes_accessed=300_000, transcendentals=0
        ),
        name="attend",
    )(proj, tails, prior, table, *tables)


def mix_out_kernel(spots, *refs):
    mixed = refs[0:4]
    lefts = refs[4:8]
    right = refs[8]
    sources = refs[9 : 9 + 1 + 15]
    part, rank, kept, weight, sems = refs[25:]
    groups = []
    for slot in range(SLOTS):
        pieces = sources[0:1] if slot == 0 else sources[1 + 5 * (slot - 1) : 1 + 5 * slot]
        groups.append(output_copies(pieces, slot == 0, weight, 2 * PD * slot))

    @pl.when(pl.program_id(0) == 0)
    def _():
        for slot in range(SLOTS):
            run_copies(groups[slot], sems, 8 * slot)
            output_pads(weight, 2 * PD * slot)
        for slot in range(SLOTS):
            wait_copies(groups[slot], sems, 8 * slot)

    total = jnp.zeros(part.shape, f32)
    rank_sum = jnp.zeros((part.shape[0], R), f32)
    for slot in range(SLOTS):
        total = total + nn(mixed[slot][...], weight[2 * PD * slot : 2 * PD * (slot + 1), :])
        rank_sum = rank_sum + nt(mixed[slot][...], lefts[slot][:, spots.left])
    total = total + nn(rank_sum.astype(bf16), right[...])
    part[...] = total.astype(bf16)
    rank[...] = rank_sum
    rows = kept.shape[0]
    kept[...] = weight[pl.ds(pl.multiple_of(pl.program_id(0) * rows, rows), rows), :]


def mix_out(spots, mixed, lefts, right, sources):
    rows = mixed[0].shape[0]
    width = right.shape[1]
    block = CHUNK
    steps = rows // block
    whole = lambda a: pl.BlockSpec(a.shape, lambda i: (0,) * a.ndim)
    return pl.pallas_call(
        functools.partial(mix_out_kernel, spots),
        grid=(steps,),
        out_shape=(
            jax.ShapeDtypeStruct((rows, width), bf16),
            jax.ShapeDtypeStruct((rows, R), f32),
            jax.ShapeDtypeStruct((SLOTS * 2 * PD, width), bf16),
        ),
        in_specs=[pl.BlockSpec((block, 2 * PD), lambda i: (i, 0))] * 4
        + [whole(a) for a in lefts]
        + [whole(right)]
        + [ANY] * len(sources),
        out_specs=(
            pl.BlockSpec((block, width), lambda i: (i, 0)),
            pl.BlockSpec((block, R), lambda i: (i, 0)),
            pl.BlockSpec((SLOTS * 2 * PD // steps, width), lambda i: (i, 0)),
        ),
        scratch_shapes=[pltpu.VMEM((SLOTS * 2 * PD, width), bf16), pltpu.SemaphoreType.DMA((32,))],
        compiler_params=params(48),
        cost_estimate=pl.CostEstimate(
            flops=100_000_000, bytes_accessed=300_000, transcendentals=0
        ),
        name="mix_out",
    )(*mixed, *lefts, right, *sources)


def feed_kernel(slots, last, half, pad, spots, *refs):
    count = len(slots)
    fresh = slots[0] == 0
    second, grad, grank, rgrad, dright, gleft = refs[:6]
    tables, refs = refs[6 : 6 + count], refs[6 + count :]
    groups = []
    sources = []
    for slot in slots:
        size = 2 if slot == 0 else 5
        sources.append(refs[:size])
        refs = refs[size:]
    if not fresh:
        (down_in, back_in, ranks_in), refs = refs[:3], refs[3:]
    down_out, back_out, ranks_out = refs[:3]
    right_outs, left_outs = refs[3 : 3 + count], refs[3 + count : 3 + 2 * count]
    weights, sems, *sums = refs[3 + 2 * count :]
    right_grads, left_grads = sums[:count], sums[count:]
    for n, slot in enumerate(slots):
        part = weights.at[3 * pad * n : 3 * pad * (n + 1)]
        groups.append(feed_copies(sources[n], slot == 0, part, half, pad))
    begin = pl.program_id(0) == 0

    @pl.when(begin)
    def _():
        for n in range(count):
            run_copies(groups[n], sems, 16 * n)
        for n in range(count):
            feed_pads(weights.at[3 * pad * n : 3 * pad * (n + 1)], half, pad)
            right_grads[n][...] = jnp.zeros(right_grads[n].shape, f32)
            left_grads[n][...] = jnp.zeros(left_grads[n].shape, f32)

    down = jnp.zeros(down_out.shape, f32) if fresh else down_in[...]
    back = jnp.zeros(back_out.shape, f32) if fresh else back_in[...]
    down_rank = jnp.zeros((down.shape[0], R), f32) if fresh else ranks_in[:, :R]
    back_rank = jnp.zeros((down.shape[0], R), f32) if fresh else ranks_in[:, R:]
    for n in range(count):

        @pl.when(begin)
        def _():
            wait_copies(groups[n], sems, 16 * n)

        at = 3 * pad * n
        right, left = tables[n][:, spots.gate], tables[n][:, spots.down]
        gate_up = nt(second[...], weights[at : at + 2 * pad, :]) + nn(grank[...], right)
        gate, up = gate_up[:, :pad], gate_up[:, pad:]
        hidden_grad = nt(grad[...], weights[at + 2 * pad : at + 3 * pad, :]) + nn(rgrad[...], left)
        sig = jax.nn.sigmoid(gate)
        act = gate * sig
        hidden = (act * up).astype(bf16)
        gate_grad = hidden_grad * up * (sig * (1.0 + gate * (1.0 - sig)))
        both = jnp.concatenate([gate_grad.astype(bf16), (hidden_grad * act).astype(bf16)], 1)
        down = down + nn(hidden, weights[at + 2 * pad : at + 3 * pad, :])
        back = back + nn(both, weights[at : at + 2 * pad, :])
        down_rank = down_rank + nt(hidden, left)
        back_rank = back_rank + nt(both, right)
        right_grads[n][...] += tn(grank[...], both)
        left_grads[n][...] += tn(rgrad[...], hidden)
    ranks_out[:, :R] = down_rank
    ranks_out[:, R:] = back_rank
    if last:
        down = down + nn(down_rank.astype(bf16), dright[...])
        back = back + nn(back_rank.astype(bf16), gleft[...])
    down_out[...] = down.astype(down_out.dtype)
    back_out[...] = back.astype(back_out.dtype)

    @pl.when(pl.program_id(0) == pl.num_programs(0) - 1)
    def _():
        for out, total in zip(right_outs + left_outs, right_grads + left_grads):
            out[...] = total[...].astype(bf16)


def feed(slots, last, half, spots, second, grad, grank, rgrad, dright, gleft, tables, sources, carry):
    rows, width = second.shape
    pad = spots.down.stop - spots.down.start
    count = len(slots)
    block = CHUNK
    kind = bf16 if last else f32
    whole = lambda a: pl.BlockSpec(a.shape, lambda i: (0,) * a.ndim)
    wide = pl.BlockSpec((block, width), lambda i: (i, 0))
    thin = pl.BlockSpec((block, R), lambda i: (i, 0))
    pair = pl.BlockSpec((block, 2 * R), lambda i: (i, 0))
    flat = sum([list(s) for s in sources], [])
    out = pl.pallas_call(
        functools.partial(feed_kernel, slots, last, half, pad, spots),
        grid=(rows // block,),
        out_shape=(
            jax.ShapeDtypeStruct((rows, width), kind),
            jax.ShapeDtypeStruct((rows, width), kind),
            jax.ShapeDtypeStruct((rows, 2 * R), f32),
        )
        + (jax.ShapeDtypeStruct((R, 2 * pad), bf16),) * count
        + (jax.ShapeDtypeStruct((R, pad), bf16),) * count,
        in_specs=[wide, wide, thin, thin, whole(dright), whole(gleft)]
        + [whole(t) for t in tables]
        + [ANY] * len(flat)
        + ([wide, wide, pair] if carry else []),
        out_specs=(wide, wide, pair)
        + (pl.BlockSpec((R, 2 * pad), lambda i: (0, 0)),) * count
        + (pl.BlockSpec((R, pad), lambda i: (0, 0)),) * count,
        scratch_shapes=[
            pltpu.VMEM((3 * pad * count, width), bf16),
            pltpu.SemaphoreType.DMA((16 * count,)),
        ]
        + [pltpu.VMEM((R, 2 * pad), f32)] * count
        + [pltpu.VMEM((R, pad), f32)] * count,
        compiler_params=params(58),
        cost_estimate=pl.CostEstimate(
            flops=100_000_000, bytes_accessed=300_000, transcendentals=0
        ),
        name="feed",
    )(second, grad, grank, rgrad, dright, gleft, *tables, *flat, *carry)
    return list(out[:3]), list(out[3 : 3 + count]), list(out[3 + count :])


def turn_kernel(spots, *refs):
    mixer_up, orgrad, weight = refs[:3]
    tables, numers, mixeds = refs[3:5], refs[5:7], refs[7:9]
    bases, heads, tails = refs[9:13], refs[13:15], refs[15]
    pick, bias, coef = refs[16:19]
    up_out, grad_out, state, lent, left_out, total_state, left0, left1 = refs[19:]
    step = pl.program_id(0)

    @pl.when(step == 0)
    def _():
        total_state[...] = jnp.zeros(total_state.shape, f32)
        left0[...] = jnp.zeros(left0.shape, f32)
        left1[...] = jnp.zeros(left1.shape, f32)

    both = nt(mixer_up[...], weight[...])
    for n, left_grad in enumerate((left0, left1)):
        table = tables[n]
        flow = both[:, 2 * PD * n : 2 * PD * (n + 1)] + nn(orgrad[...], table[:, spots.left])
        left_grad[...] += tn(orgrad[...], mixeds[n][...])
        for head in range(2):
            cols = slice(PD * head, PD * (head + 1))
            wide = slice(PD * (2 * n + head), PD * (2 * n + head + 1))
            up = flow[:, cols]
            total = numers[n][:, cols].astype(f32)
            scale = lax.rsqrt(jnp.sum(total * total, -1, keepdims=True) * (1.0 / HD) + epsilon)
            inner = jnp.sum(total * up, -1, keepdims=True) * (1.0 / HD)
            grad = (scale * up - total * (scale * scale * scale * inner)).astype(bf16)
            up_out[:, wide] = up.astype(bf16)
            grad_out[:, wide] = grad
            picked = nn(bases[2 * n + head][...], pick[:, 0:512])
            _, _, feat = features(picked, bias[...], coef[...], 0)
            total_state[2 * n + head] += tn(feat.astype(bf16), grad)

    @pl.when(step == pl.num_programs(0) - 1)
    def _():
        state[...] = total_state[:, :STATE, :].astype(bf16)
        left_out[0] = left0[...].astype(bf16)
        left_out[1] = left1[...].astype(bf16)

    @pl.when(step == 0)
    def _():
        for n in range(2):
            for head in range(2):
                give_back(
                    spots, tables[n], heads[n], tails.at[2 * n + head], up_out, lent.at[2 * n + head], n, head
                )


def give_back(spots, table, rows, tails, up_out, lent, n, head):
    at = HEAD_PAD * head
    wide = slice(PD * (2 * n + head), PD * (2 * n + head + 1))
    query = rows[:, at + 2 * PD : at + 3 * PD]
    keys = jnp.concatenate([tails[0:WIN, 0:PD], rows[:, at + 3 * PD : at + 4 * PD]], 0)
    vals = jnp.concatenate([tails[0:WIN, PD : 2 * PD], rows[:, at + 4 * PD : at + 5 * PD]], 0)
    prob = window_prob(query, keys, 0)
    up = up_out[0:QB, wide]
    prob_grad = nt(up, vals)
    inner = jnp.sum(prob * prob_grad, -1, keepdims=True)
    score = (prob * (prob_grad - inner)).astype(bf16)
    lent[0:WIN, 0:PD] = (tn(score, query)[:WIN] * HD ** (-0.5)).astype(bf16)
    lent[0:WIN, PD : 2 * PD] = tn(prob.astype(bf16), up)[:WIN].astype(bf16)
    start = spots.taps.start + PD * head
    tap = table[:, start : start + PD].astype(f32)
    gate = rows[0:16, at + 6 * PD : at + 7 * PD].astype(f32)
    flow = up_out[0:16, wide].astype(f32) * (gate * jax.nn.sigmoid(gate))
    row0 = tap[2:3] * flow[0:1]
    row1 = tap[1:2] * flow[0:1] + tap[2:3] * flow[1:2]
    index = lax.broadcasted_iota(jnp.int32, (16, PD), 0)
    edge_rows = jnp.where(index == 14, row0, jnp.where(index == 15, row1, 0.0))
    lent[WIN : WIN + 16, 0:PD] = edge_rows.astype(bf16)
    lent[WIN : WIN + 16, PD : 2 * PD] = jnp.zeros((16, PD), bf16)


def turn(pair, spots, mixer_up, orgrad, weight, slot_tables, numer, mixed, projs, tails, tables):
    rows, width = mixer_up.shape
    whole = lambda a: pl.BlockSpec(a.shape, lambda i: (0,) * a.ndim)
    flat = lambda *shape: pl.BlockSpec(shape, lambda i: (0,) * len(shape))
    tall = lambda cols, at: pl.BlockSpec((CHUNK, cols), lambda i: (i, at))
    return pl.pallas_call(
        functools.partial(turn_kernel, spots),
        grid=(rows // CHUNK,),
        out_shape=(
            jax.ShapeDtypeStruct((rows, 4 * PD), bf16),
            jax.ShapeDtypeStruct((rows, 4 * PD), bf16),
            jax.ShapeDtypeStruct((4, STATE, PD), bf16),
            jax.ShapeDtypeStruct((4, WIN + 16, 2 * PD), bf16),
            jax.ShapeDtypeStruct((2, R, 2 * PD), bf16),
        ),
        in_specs=[
            tall(width, 0),
            tall(R, 0),
            pl.BlockSpec((4 * PD, width), lambda i: (pair, 0)),
        ]
        + [whole(t) for t in slot_tables]
        + [tall(2 * PD, 0)] * 4
        + [tall(PD, 0), tall(PD, 7)] * 2
        + [pl.BlockSpec((QB, 2 * HEAD_PAD), lambda i: (0, 0))] * 2
        + [whole(tails)]
        + [whole(t) for t in tables],
        out_specs=(
            tall(4 * PD, 0),
            tall(4 * PD, 0),
            flat(4, STATE, PD),
            flat(4, WIN + 16, 2 * PD),
            flat(2, R, 2 * PD),
        ),
        scratch_shapes=[pltpu.VMEM((4, 256, PD), f32)] + [pltpu.VMEM((R, 2 * PD), f32)] * 2,
        compiler_params=params(48),
        cost_estimate=pl.CostEstimate(
            flops=100_000_000, bytes_accessed=300_000, transcendentals=0
        ),
        name="turn",
    )(
        mixer_up, orgrad, weight, *slot_tables, *numer, *mixed,
        projs[0], projs[0], projs[1], projs[1], *projs, tails, *tables,
    )


def attend_back_kernel(
    spots, proj, tails, prior, later, lent, ups, grads, table, rank, pick, bias, coef,
    out, rank_grad, right_grad, keys, vals, conv, flow, dkeys, dvals, states
):
    rows = proj.shape[0]
    chunks = rows // CHUNK
    keys[0:WIN, :] = tails[0, 0:WIN, 0:PD]
    vals[0:WIN, :] = tails[0, 0:WIN, PD : 2 * PD]
    conv[0:16, :] = tails[0, WIN : WIN + 16, 0:PD].astype(f32)
    keys[WIN:, :] = proj[:, 3 * PD : 4 * PD]
    vals[WIN:, :] = proj[:, 4 * PD : 5 * PD]
    conv[16:, :] = proj[:, 5 * PD : 6 * PD].astype(f32)
    tap = head_taps(spots, table)
    right = table.at[:, pl.ds(pl.multiple_of(HEAD_PAD * pl.program_id(0), PD), HEAD_PAD)]
    dkeys[...] = jnp.zeros(dkeys.shape, f32)
    dvals[...] = jnp.zeros(dvals.shape, f32)
    dkeys[rows:, :] = lent[0, 0:WIN, 0:PD].astype(f32)
    dvals[rows:, :] = lent[0, 0:WIN, PD : 2 * PD].astype(f32)
    flow[rows:, :] = jnp.zeros((16, PD), f32)
    state = whole_state(prior[0])
    for chunk in range(chunks):
        span = slice(chunk * CHUNK, (chunk + 1) * CHUNK)
        states[chunk] = state.astype(bf16)
        if chunk + 1 < chunks:
            _, _, feat = features(nn(proj[span, 0:PD], pick[:, 512:1024]), bias[...], coef[...], 0)
            state = state + tn(feat.astype(bf16), proj[span, PD : 2 * PD])
    follow = whole_state(later[0])
    causal = causal_mask()
    coefs = coef[...]
    for chunk in range(chunks - 1, -1, -1):
        at = chunk * CHUNK
        span = slice(at, at + CHUNK)
        base = proj[span, 0:PD]
        value = proj[span, PD : 2 * PD]
        grad = grads[span, :]
        picked = nn(base, pick[...])
        q_one, q_two, feat_q = features(picked, bias[...], coefs, 0)
        k_one, k_two, feat_k = features(picked, bias[...], coefs, 512)
        key_low = picked[:, 1024:1152].astype(bf16)
        query_high = picked[:, 1152:1280].astype(bf16)
        score = nt(base, key_low)
        weight = jnp.where(causal, 1.0 + score + 0.5 * score * score, 0.0).astype(bf16)
        slope = jnp.where(causal, nt(grad, value) * (1.0 + score), 0.0).astype(bf16)
        follow_round = follow.astype(bf16)
        q_up = nt(grad, states[chunk]) * coefs
        k_up = nt(value, follow_round) * coefs
        low = nn(slope, key_low) + tn(slope, query_high)
        low = low + nt((q_up * q_two).astype(bf16), pick[:, 0:256])
        low = low + nt((q_up * q_one).astype(bf16), pick[:, 256:512])
        low = low + nt((k_up * k_two).astype(bf16), pick[:, 512:768])
        low = low + nt((k_up * k_one).astype(bf16), pick[:, 768:1024])
        out[span, 0:PD] = low.astype(bf16)
        out[span, PD : 2 * PD] = (
            tn(weight, grad) + nn(feat_k.astype(bf16), follow_round)
        ).astype(bf16)
        follow = follow + tn(feat_q.astype(bf16), grad)
        gate = proj[span, 6 * PD : 7 * PD].astype(f32)
        up = ups[span, :].astype(f32)
        sig = jax.nn.sigmoid(gate)
        flow[span, :] = up * gate * sig
        slope_gate = sig * (1.0 + gate * (1.0 - sig))
        out[span, 6 * PD : 7 * PD] = (up * conv_of(conv, tap, at, CHUNK) * slope_gate).astype(bf16)
    for number in range(rows // QB):
        span = slice(number * QB, (number + 1) * QB)
        band = slice(number * QB, number * QB + QB + WIN)
        query = proj[span, 2 * PD : 3 * PD]
        key = keys[band, :]
        prob = window_prob(query, key, number)
        up = ups[span, :]
        prob_grad = nt(up, vals[band, :])
        inner = jnp.sum(prob * prob_grad, -1, keepdims=True)
        score = (prob * (prob_grad - inner)).astype(bf16)
        out[span, 2 * PD : 3 * PD] = (nn(score, key) * HD ** (-0.5)).astype(bf16)
        dkeys[band, :] += tn(score, query) * HD ** (-0.5)
        dvals[band, :] += tn(prob.astype(bf16), up)
    out[:, 3 * PD : 4 * PD] = dkeys[WIN:, :].astype(bf16)
    out[:, 4 * PD : 5 * PD] = dvals[WIN:, :].astype(bf16)
    grad_in = tap[0:1] * flow[0:rows, :]
    for offset in range(1, KW):
        grad_in = grad_in + tap[offset : offset + 1] * flow[offset : offset + rows, :]
    out[:, 5 * PD : 6 * PD] = grad_in.astype(bf16)
    last = slice(rows - 16, rows)
    edge = grad_in[rows - 16 :, :] + lent[0, WIN : WIN + 16, 0:PD].astype(f32)
    out[last, 5 * PD : 6 * PD] = edge.astype(bf16)
    right_grad[...] = tn(rank[...], out[...]).astype(bf16)

    @pl.when(pl.program_id(0) == 0)
    def _():
        rank_grad[...] = nt(out[...], right[...])

    @pl.when(pl.program_id(0) > 0)
    def _():
        rank_grad[...] += nt(out[...], right[...])


def attend_back(spots, number, proj, tails, prior, later, lent, ups, grads, table, rank, tables):
    rows = proj.shape[0]
    whole = lambda a: pl.BlockSpec(a.shape, lambda h: (0,) * a.ndim)
    head = pl.BlockSpec((rows, HEAD_PAD), lambda h: (0, h))
    edge = pl.BlockSpec((1, WIN + 16, 2 * PD), lambda h: (2 * number + h, 0, 0))
    state = pl.BlockSpec((1, STATE, PD), lambda h: (2 * number + h, 0, 0))
    column = pl.BlockSpec((rows, PD), lambda h: (0, 2 * number + h))
    return pl.pallas_call(
        functools.partial(attend_back_kernel, spots),
        grid=(2,),
        out_shape=(
            jax.ShapeDtypeStruct((rows, 2 * HEAD_PAD), bf16),
            jax.ShapeDtypeStruct((rows, R), f32),
            jax.ShapeDtypeStruct((R, 2 * HEAD_PAD), bf16),
        ),
        in_specs=[head, edge, state, state, edge, column, column, whole(table), whole(rank)]
        + [whole(t) for t in tables],
        out_specs=(
            head,
            pl.BlockSpec((rows, R), lambda h: (0, 0)),
            pl.BlockSpec((R, HEAD_PAD), lambda h: (0, h)),
        ),
        scratch_shapes=[
            pltpu.VMEM((rows + WIN, PD), bf16),
            pltpu.VMEM((rows + WIN, PD), bf16),
            pltpu.VMEM((rows + 16, PD), f32),
            pltpu.VMEM((rows + 16, PD), f32),
            pltpu.VMEM((rows + WIN, PD), f32),
            pltpu.VMEM((rows + WIN, PD), f32),
            pltpu.VMEM((rows // CHUNK, 256, PD), bf16),
        ],
        compiler_params=params(48),
        cost_estimate=pl.CostEstimate(
            flops=100_000_000, bytes_accessed=300_000, transcendentals=0
        ),
        name="attend_back",
    )(proj, tails, prior, later, lent, ups, grads, table, rank, *tables)


def first_back_kernel(*refs):
    grads = refs[0:4]
    rank_grad, left = refs[4:6]
    sources = refs[6 : 6 + 16]
    part, weight, sems = refs[22:]
    groups = []
    size = 2 * HEAD_PAD
    for slot in range(SLOTS):
        pieces = sources[0:1] if slot == 0 else sources[1 + 5 * (slot - 1) : 1 + 5 * slot]
        groups.append(mixer_copies(pieces, slot == 0, weight, size * slot))
    begin = pl.program_id(0) == 0

    @pl.when(begin)
    def _():
        for slot in range(SLOTS):
            run_copies(groups[slot], sems, 40 * slot)
        for slot in range(SLOTS):
            mixer_pads(weight, size * slot)

    total = nn(rank_grad[...].astype(bf16), left[...])
    for slot in range(SLOTS):

        @pl.when(begin)
        def _():
            wait_copies(groups[slot], sems, 40 * slot)

        total = total + nn(grads[slot][...], weight[size * slot : size * (slot + 1), :])
    part[...] = total.astype(bf16)


def first_back(number, grads, rank_grad, left, sources):
    rows = rank_grad.shape[0]
    width = left.shape[1]
    block = rows // 4
    whole = lambda a: pl.BlockSpec(a.shape, lambda i: (0,) * a.ndim)
    size = 2 * HEAD_PAD
    return pl.pallas_call(
        first_back_kernel,
        grid=(2,),
        out_shape=jax.ShapeDtypeStruct((rows // 2, width), bf16),
        in_specs=[pl.BlockSpec((block, size), lambda i: (2 * i + number, 0))] * 4
        + [pl.BlockSpec((block, R), lambda i: (2 * i + number, 0)), whole(left)]
        + [ANY] * len(sources),
        out_specs=pl.BlockSpec((block, width), lambda i: (i, 0)),
        scratch_shapes=[pltpu.VMEM((SLOTS * size, width), bf16), pltpu.SemaphoreType.DMA((160,))],
        compiler_params=params(56),
        cost_estimate=pl.CostEstimate(
            flops=100_000_000, bytes_accessed=300_000, transcendentals=0
        ),
        name="first_back",
    )(*grads, rank_grad, left, *sources)


def norm_two_kernel(own, other, wide, gain, left, middle, second, rank):
    total = wide[...].astype(f32) + (own[...].astype(f32) + other[...].astype(f32))
    scale = lax.rsqrt(jnp.mean(total * total, -1, keepdims=True) + epsilon)
    rounded = (total * scale * gain[...]).astype(bf16)
    middle[...] = total
    second[...] = rounded
    rank[...] = nn(rounded, left[...]).astype(bf16)


def norm_two(own, other, wide, gain, left):
    rows, width = own.shape
    block = pl.BlockSpec((CHUNK, width), lambda i: (i, 0))
    whole = lambda a: pl.BlockSpec(a.shape, lambda i: (0,) * a.ndim)
    return pl.pallas_call(
        norm_two_kernel,
        grid=(rows // CHUNK,),
        out_shape=(
            jax.ShapeDtypeStruct((rows, width), f32),
            jax.ShapeDtypeStruct((rows, width), bf16),
            jax.ShapeDtypeStruct((rows, R), bf16),
        ),
        in_specs=[block, block, block, whole(gain), whole(left)],
        out_specs=(block, block, pl.BlockSpec((CHUNK, R), lambda i: (i, 0))),
        compiler_params=params(40),
        cost_estimate=pl.CostEstimate(
            flops=100_000_000, bytes_accessed=300_000, transcendentals=0
        ),
        name="norm_two",
    )(own, other, wide, gain, left)


def back_two_kernel(own, other, middle, upstream, gain, right, mixer_up, rgrad):
    vector = middle[...]
    scale = lax.rsqrt(jnp.mean(vector * vector, -1, keepdims=True) + epsilon)
    flow = gain[...] * (own[...].astype(f32) + other[...].astype(f32))
    inner = jnp.mean(vector * flow, -1, keepdims=True)
    total = upstream[...].astype(f32) + scale * flow - vector * (scale * scale * scale * inner)
    rounded = total.astype(bf16)
    mixer_up[...] = rounded
    rgrad[...] = nt(rounded, right[...]).astype(bf16)


def back_two(own, other, middle, upstream, gain, right):
    rows, width = own.shape
    block = pl.BlockSpec((CHUNK, width), lambda i: (i, 0))
    whole = lambda a: pl.BlockSpec(a.shape, lambda i: (0,) * a.ndim)
    return pl.pallas_call(
        back_two_kernel,
        grid=(rows // CHUNK,),
        out_shape=(
            jax.ShapeDtypeStruct((rows, width), bf16),
            jax.ShapeDtypeStruct((rows, R), bf16),
        ),
        in_specs=[block, block, block, block, whole(gain), whole(right)],
        out_specs=(block, pl.BlockSpec((CHUNK, R), lambda i: (i, 0))),
        compiler_params=params(40),
        cost_estimate=pl.CostEstimate(
            flops=100_000_000, bytes_accessed=300_000, transcendentals=0
        ),
        name="back_two",
    )(own, other, middle, upstream, gain, right)


def weighted(hot, parts):
    expert = pl.program_id(0)
    total = hot[expert, 0] * parts[0].astype(f32)
    for slot in range(1, SLOTS):
        total = total + hot[expert, slot] * parts[slot].astype(f32)
    return total


def by_core(flag, mine, other, base):
    lead = flag[0] > 0
    one, two = mine[:, :base], other[:, :base]
    return jnp.where(lead, one, two), jnp.where(lead, two, one)


def early_kernel(half, pad, hot, flag, mine, other, *outs):
    right, gate_left, down_right, out_left, gate_right, down_left = outs
    width = right.shape[2]
    base = 2 * PD + 3 * pad
    own, sibling = weighted(hot, mine), weighted(hot, other)
    for n, ref in enumerate((right, gate_left, down_right)):
        cols = slice(base + width * n, base + width * (n + 1))
        ref[0] = own[:, cols] + sibling[:, cols]
    cores = by_core(flag, own, sibling, base)
    out_left[0] = jnp.concatenate(
        [part[:, PD * h : PD * h + HD] for part in cores for h in range(2)], 1
    )
    for g in range(2):
        at = 2 * PD + pad * g
        gate_right[0, :, g, :] = jnp.concatenate([part[:, at : at + half] for part in cores], 1)
    at = 2 * PD + 2 * pad
    down_left[0] = jnp.concatenate([part[:, at : at + half] for part in cores], 1)


def late_kernel(hot, flag, mine, other, right, left):
    width = left.shape[2]
    base = 2 * HEAD_PAD
    own, sibling = weighted(hot, mine), weighted(hot, other)
    left[0] = own[:, base : base + width] + sibling[:, base : base + width]
    for core, part in enumerate(by_core(flag, own, sibling, base)):
        for head in range(2):
            at = HEAD_PAD * head
            right[0, :, 2 * core + head, :] = jnp.concatenate(
                [part[:, at + place_at : at + place_at + size] for _, size, place_at in HEAD_SEGMENTS], 1
            )


def tables_of(kernel, shapes, name, hot, flag, mine, other):
    whole = lambda a: pl.BlockSpec(a.shape, lambda e: (0,) * a.ndim)
    smem = pl.BlockSpec(memory_space=pltpu.SMEM)
    spot = lambda rank: lambda e: (e,) + (0,) * (rank - 1)
    return pl.pallas_call(
        kernel,
        grid=(NA,),
        out_shape=[jax.ShapeDtypeStruct((NA,) + shape, f32) for shape in shapes],
        in_specs=[smem, smem, whole(mine), whole(other)],
        out_specs=[pl.BlockSpec((1,) + shape, spot(len(shape) + 1)) for shape in shapes],
        compiler_params=params(40),
        cost_estimate=pl.CostEstimate(
            flops=100_000_000, bytes_accessed=300_000, transcendentals=0
        ),
        name=name,
    )(hot, flag, mine, other)


def swap_core(array):
    return lax.ppermute(array, "core", [(0, 1), (1, 0)])


def swap_chip(array, bit):
    count = lax.axis_size("chip")
    return lax.ppermute(array, "chip", [(i, i ^ bit) for i in range(count)])


def swap_tp(array, bit):
    return lax.ppermute(array, "tp", [(i, i ^ bit) for i in range(4)])


def both_cores(own):
    other = swap_core(own)
    lead = lax.axis_index("core") == 0
    return jnp.concatenate([jnp.where(lead, own, other), jnp.where(lead, other, own)], 0)


def own_rows(array, core):
    half = array.shape[0] // 2
    return lax.dynamic_slice_in_dim(array, core * half, half, 0)


def hold_kernel(*refs):
    pass


def hold(*arrays, after=()):
    return pl.pallas_call(
        hold_kernel,
        out_shape=tuple(jax.ShapeDtypeStruct(a.shape, a.dtype) for a in arrays),
        in_specs=[ANY] * (len(arrays) + len(after)),
        out_specs=(ANY,) * len(arrays),
        input_output_aliases={i: i for i in range(len(arrays))},
        compiler_params=pltpu.CompilerParams(has_side_effects=True),
        name="hold",
    )(*arrays, *after)


def hop_xy(piece):
    return swap_chip(piece, 1), swap_chip(piece, 2)


def hop_diag(from_x, from_y, cut):
    return swap_chip(from_y[:cut], 1), swap_chip(from_x[cut:], 2)


def cross(array):
    return lax.ppermute(array, "tp", [(1, 2), (2, 1)])


def edge(array):
    return lax.ppermute(array, "tp", [(1, 0), (2, 3)])


def pick_inner(inner_array, edge_array):
    z = lax.axis_index("tp")
    return jnp.where((z == 1) | (z == 2), inner_array, edge_array)


def add_swapped(array, bit):
    other = swap_chip(array, bit)
    return (array.astype(f32) + other.astype(f32)).astype(array.dtype)


def add_rest(array):
    bit = 2
    while bit < lax.axis_size("chip"):
        array = add_swapped(array, bit)
        bit *= 2
    return array


def neighbour_chip(array, by):
    count = lax.axis_size("chip")
    pairs = [(i, i + by) for i in range(count) if 0 <= i + by < count]
    return lax.ppermute(array, "chip", pairs)


def swap_states(packed):
    if lax.axis_size("chip") == 4:
        return tuple(swap_chip(packed, bit) for bit in (1, 2, 3))
    return (lax.all_gather(packed, "chip"),)


def use_states(parts, backward):
    chip = lax.axis_index("chip")
    count = lax.axis_size("chip")
    if len(parts) > 1:
        total = 0.0
        for bit, part in zip((1, 2, 3), parts):
            other = chip ^ bit
            ahead = (other > chip) if backward else (other < chip)
            total = total + jnp.where(ahead, part[:, :STATE].astype(f32), 0.0)
        near = jnp.where(lax.rem(chip, 2) == (0 if backward else 1), parts[0], parts[2])
    else:
        index = jnp.arange(count, dtype=jnp.int32)
        ahead = (index > chip) if backward else (index < chip)
        states = parts[0][:, :, :STATE].astype(f32)
        total = jnp.sum(jnp.where(ahead[:, None, None, None], states, 0.0), 0)
        at = jnp.minimum(chip + 1, count - 1) if backward else jnp.maximum(chip - 1, 0)
        near = lax.dynamic_index_in_dim(parts[0], at, 0, False)
    inside = (chip < count - 1) if backward else (chip > 0)
    rows = jnp.where(inside, near[:, STATE:], 0.0).astype(bf16)
    rows = rows.reshape(near.shape[0], WIN + 16, 2 * PD)
    return total, rows


def pack_states(states, rows):
    return jnp.concatenate([states, rows.reshape(rows.shape[0], 2 * (WIN + 16), PD)], 1)


def copy_kernel(source, dest):
    dest[...] = source[...]


def copy_of(array):
    block = pl.BlockSpec((1,) + array.shape[1:], lambda i: (i, 0, 0))
    return pl.pallas_call(
        copy_kernel,
        grid=(array.shape[0],),
        out_shape=jax.ShapeDtypeStruct(array.shape, array.dtype),
        in_specs=[block],
        out_specs=block,
        compiler_params=params(32),
        cost_estimate=pl.CostEstimate(
            flops=100_000_000, bytes_accessed=300_000, transcendentals=0
        ),
        name="copy_of",
    )(array)


def stack_tp(parts):
    z = lax.axis_index("tp")
    result = jnp.zeros((SLOTS,) + parts[0].shape, parts[0].dtype)
    for slot, part in enumerate(parts):
        result = lax.dynamic_update_index_in_dim(result, part, z ^ slot, 0)
    return result


def pad_heads(table):
    lead = table.shape[:-2]
    heads = table.shape[-2]
    zero = [(0, 0)] * (len(lead) + 1)
    low = jnp.pad(table[..., : 2 * FD], zero + [(0, PD - 2 * FD)])
    high = table[..., 2 * FD :].reshape(lead + (heads, 6, HD))
    high = jnp.pad(high, zero + [(0, 0), (0, PD - HD)]).reshape(lead + (heads, 6 * PD))
    return jnp.concatenate([low, high], -1).reshape(lead + (heads * HEAD_PAD,))


def pad_last(table, size):
    return jnp.pad(table, [(0, 0)] * (table.ndim - 1) + [(0, size - table.shape[-1])])


def norm_rows(vector, gain_vector):
    row_scale = lax.rsqrt(jnp.mean(vector * vector, -1, keepdims=True) + epsilon)
    return (vector * row_scale * gain_vector, row_scale)


def norm_back(vector, row_scale, gain_vector, upstream):
    inner_mean = jnp.mean(vector * gain_vector * upstream, -1, keepdims=True)
    return (
        row_scale * gain_vector * upstream - vector * row_scale * row_scale * row_scale * inner_mean
    )


def body(
    block_input,
    gain_first,
    frozen_mixer_weight,
    conv_filter,
    frozen_output_weight,
    gain_second,
    frozen_gate_up_weight,
    frozen_down_weight,
    mixer_left,
    mixer_right,
    output_left,
    output_right,
    gateup_left,
    gateup_right,
    down_left,
    down_right,
    adapter_index,
    seq_lengths,
    out_cotangent,
):
    chip = lax.axis_index("chip")
    core = lax.axis_index("core")
    z = lax.axis_index("tp")
    y, x = place()
    sequences, length, width = block_input.shape
    rows = 2 * length
    heads_here = frozen_mixer_weight.shape[1]
    ff_here = frozen_down_weight.shape[0]
    half = ff_here // 2
    pad = (half + PD - 1) // PD * PD
    quarter = half // 2

    pick, bias, coef = feature_tables()
    tables = (jnp.asarray(pick, bf16), jnp.asarray(bias), jnp.asarray(coef))

    w_mix = jnp.transpose(frozen_mixer_weight, (1, 2, 0)).reshape(heads_here * HCOLS, width)
    w_gate = jnp.transpose(frozen_gate_up_weight, (1, 2, 0)).reshape(2 * ff_here, width)
    w_out = frozen_output_weight
    w_down = frozen_down_weight
    side = width // 2

    def cut(matrix, start, count):
        return lax.dynamic_slice(matrix, (start, x * side), (count, side))

    mixer_piece = jnp.concatenate(
        [
            cut(w_mix, 2 * HCOLS * core + HCOLS * y, HCOLS),
            cut(w_out, 2 * HD * core + HD * y, HD),
        ],
        0,
    )
    feed_piece = jnp.concatenate(
        [
            cut(w_gate, half * core + quarter * y, quarter),
            cut(w_gate, ff_here + half * core + quarter * y, quarter),
            cut(w_down, half * core + quarter * y, quarter),
        ],
        0,
    )
    slot_seq = z ^ jnp.arange(SLOTS, dtype=jnp.int32)
    slot_adapter = jnp.sum(
        jnp.where(slot_seq[:, None] == jnp.arange(SLOTS)[None, :], adapter_index[None, :], 0), 1
    )
    onehot = slot_adapter[:, None] == jnp.arange(NA, dtype=jnp.int32)[None, :]

    def select(table):
        return jnp.einsum(
            "se,e...->s...", onehot.astype(bf16), table, preferred_element_type=f32
        ).astype(bf16)

    mine = slot_adapter[0]
    my_mixer_left = lax.dynamic_index_in_dim(mixer_left, mine, 0, False)
    my_output_right = lax.dynamic_index_in_dim(output_right, mine, 0, False)
    my_gateup_left = lax.dynamic_index_in_dim(gateup_left, mine, 0, False)
    my_down_right = lax.dynamic_index_in_dim(down_right, mine, 0, False)
    right_table = pad_heads(
        select(lax.dynamic_slice_in_dim(mixer_right, 2 * core, 2, 2))
    )
    out_table = lax.dynamic_slice_in_dim(jnp.swapaxes(output_left, 1, 2), 2 * HD * core, 2 * HD, 2)
    out_table = pad_last(select(out_table).reshape(SLOTS, R, 2, HD), PD).reshape(SLOTS, R, 2 * PD)
    gate_table = lax.dynamic_slice_in_dim(gateup_right, half * core, half, 3)
    gate_table = pad_last(select(gate_table), pad).reshape(SLOTS, R, 2 * pad)
    down_table = lax.dynamic_slice_in_dim(jnp.swapaxes(down_left, 1, 2), half * core, half, 2)
    down_table = pad_last(select(down_table), pad)
    taps = lax.dynamic_slice_in_dim(conv_filter, 2 * HD * core, 2 * HD, 1)
    taps = pad_last(taps.reshape(KW, 2, HD), PD).reshape(KW, 2 * PD)
    taps = jnp.broadcast_to(jnp.pad(taps, ((0, R - KW), (0, 0))), (SLOTS, R, 2 * PD))
    packed = jnp.concatenate([right_table, out_table, gate_table, down_table, taps], 2)
    spots = Table(pad)

    gain_one = gain_first.astype(f32)
    gain_two = gain_second.astype(f32)[None, :]
    own_input = lax.dynamic_index_in_dim(block_input, z, 0, False)
    own_cotangent = lax.dynamic_index_in_dim(out_cotangent, z, 0, False)
    my_length = lax.dynamic_index_in_dim(seq_lengths, z, 0, False)
    upstream_own = jnp.where(
        (((chip * 2 + core) * length + jnp.arange(length, dtype=jnp.int32)) < my_length)[:, None],
        own_cotangent,
        0.0,
    ).astype(bf16)

    e_m, c_m = swap_tp(mixer_piece, 1), cross(mixer_piece)
    both_input = both_cores(own_input)
    first = norm_rows(both_input.astype(f32), gain_one)[0].astype(bf16)
    mixer_rank = nn(first, my_mixer_left).astype(bf16)
    e_m, c_m, mixer_rank, packed, both_input = hold(e_m, c_m, mixer_rank, packed, both_input)

    projs, tails, states = [], [], []
    borrowed, prior, mixed, numer = [None, None], [None, None], [], []
    slots = [packed[0], None, None, None]

    def attend_slot(slot):
        pair, n = slot // 2, slot % 2
        out = attend(spots, n, projs[slot], borrowed[pair], prior[pair], slots[slot], tables)
        for kept, value in zip((mixed, numer), out):
            kept.append(value)

    def project_slot(slot, refs):
        out = project(slot == 0, first, mixer_rank, slots[slot], tables, refs)
        for kept, value in zip((projs, tails, states), out):
            kept.append(value)

    def exchange(slot):
        rows_here = jnp.concatenate(tails[slot : slot + 2], 0)
        states_here = jnp.concatenate(states[slot : slot + 2], 0)
        return lax.all_gather(pack_states(states_here, rows_here), "chip")

    def use_exchange(slot, gathered):
        prior[slot // 2], borrowed[slot // 2] = use_states((gathered,), False)

    x1, y1 = hop_xy(e_m)
    c2_m, f_m = cross(e_m), edge(c_m)
    table1 = swap_tp(packed[1], 1)
    project_slot(0, (w_mix,))
    slot2 = pick_inner(c2_m, f_m)
    x1, y1, slot2, c2_m, c_m, tails[0], states[0], table1, feed_piece, packed = hold(
        x1, y1, slot2, c2_m, c_m, tails[0], states[0], table1, feed_piece, packed
    )
    slots[1] = table1
    d1 = hop_diag(x1, y1, M_CUT)
    x2, y2 = hop_xy(slot2)
    f2_m = edge(c2_m)
    table2, table3 = swap_tp(packed[2], 2), swap_tp(packed[3], 3)
    slot3 = pick_inner(c_m, f2_m)
    x2, y2, slot3, feed_piece, table2, table3, *d1 = hold(
        x2, y2, slot3, feed_piece, table2, table3, *d1
    )
    slots[2], slots[3] = table2, table3
    d2 = hop_diag(x2, y2, M_CUT)
    x3, y3 = hop_xy(slot3)
    e_f = swap_tp(feed_piece, 1)
    set1 = (e_m, x1, y1, *d1)
    project_slot(1, set1)
    x3, y3, e_f, tails[0], tails[1], states[0], states[1], upstream_own, *d2 = hold(
        x3, y3, e_f, tails[0], tails[1], states[0], states[1], upstream_own, *d2
    )
    d3 = hop_diag(x3, y3, M_CUT)
    c_f = cross(feed_piece)
    exchanged = exchange(0)
    set2 = (slot2, x2, y2, *d2)
    project_slot(2, set2)
    use_exchange(0, exchanged)
    d3_a, d3_b, c_f, states[2], upstream_own, prior[0], borrowed[0] = hold(
        *d3, c_f, states[2], upstream_own, prior[0], borrowed[0]
    )
    fx1, fy1 = hop_xy(e_f)
    c2_f, f_f = cross(e_f), edge(c_f)
    set3 = (slot3, x3, y3, d3_a, d3_b)
    project_slot(3, set3)
    fslot2 = pick_inner(c2_f, f_f)
    fx1, fy1, fslot2, c2_f, c_f, prior[0], tails[3], states[3] = hold(
        fx1, fy1, fslot2, c2_f, c_f, prior[0], tails[3], states[3]
    )
    fd1 = hop_diag(fx1, fy1, feed_cut(quarter))
    f2_f = edge(c2_f)
    exchanged = exchange(2)
    attend_slot(0)
    attend_slot(1)
    upstream = both_cores(upstream_own)
    down_rgrad = nt(upstream, my_down_right).astype(bf16)
    mixed[0], mixed[1], down_rgrad, upstream, fslot2, exchanged, *fd1 = hold(
        mixed[0], mixed[1], down_rgrad, upstream, fslot2, exchanged, *fd1
    )
    fx2, fy2 = hop_xy(fslot2)
    use_exchange(2, exchanged)
    attend_slot(2)
    attend_slot(3)
    fslot3 = pick_inner(c_f, f2_f)
    sets = list(set1) + list(set2) + list(set3)
    out_part, out_rank, out_weight = mix_out(spots, mixed, slots, my_output_right, [w_out] + sets)
    fx2, fy2, fslot3, out_part = hold(fx2, fy2, fslot3, out_part)

    other_part = swap_core(out_part)
    middle, second, gate_rank = norm_two(out_part, other_part, both_input, gain_two, my_gateup_left)
    gateup_left_t = my_gateup_left.T

    def feed_slots(which, sources, carry):
        return feed(
            which,
            which[-1] == SLOTS - 1,
            half,
            spots,
            second,
            upstream,
            gate_rank,
            down_rgrad,
            my_down_right,
            gateup_left_t,
            [slots[k] for k in which],
            sources,
            carry,
        )

    fd2 = hop_diag(fx2, fy2, feed_cut(quarter))
    fx3, fy3 = hop_xy(fslot3)
    carry, gate_grads, down_grads = feed_slots(
        (0, 1), [(w_gate, w_down), (e_f, fx1, fy1, *fd1)], []
    )
    fx3, fy3, carry[2], *fd2 = hold(fx3, fy3, carry[2], *fd2)
    fd3 = hop_diag(fx3, fy3, feed_cut(quarter))
    carry, more_gates, more_downs = feed_slots((2,), [(fslot2, fx2, fy2, *fd2)], carry)
    gate_grads, down_grads = gate_grads + more_gates, down_grads + more_downs
    carry[2], *fd3 = hold(carry[2], *fd3)
    carry, more_gates, more_downs = feed_slots((3,), [(fslot3, fx3, fy3, *fd3)], carry)
    gate_grads, down_grads = gate_grads + more_gates, down_grads + more_downs
    down_part, back_part, ranks = carry
    other_back = swap_core(back_part)
    mixer_up, output_rgrad = back_two(
        back_part, other_back, middle, upstream, gain_two, my_output_right
    )

    output_rgrad, down_part, middle, ranks = hold(output_rgrad, down_part, middle, ranks)
    other_down = swap_core(own_rows(down_part, 1 - core))
    own_down = own_rows(down_part, core).astype(f32)
    own_output = own_rows(middle, core) + (own_down + other_down.astype(f32))
    own_output = own_output.astype(bf16)

    def turn_pair(pair):
        both = slice(2 * pair, 2 * pair + 2)
        return turn(
            pair,
            spots,
            mixer_up,
            output_rgrad,
            out_weight,
            slots[both],
            numer[both],
            mixed[both],
            projs[both],
            borrowed[pair],
            tables,
        )

    up0, grad0, states0, lent0, left_grads0 = turn_pair(0)
    states0, lent0, own_output = hold(states0, lent0, own_output)
    packed0 = pack_states(states0, lent0)
    block_output = lax.all_gather(own_output, "tp")
    crossing = swap_states(packed0)
    up1, grad1, states1, lent1, left_grads1 = turn_pair(1)
    left_grads = [left_grads0[0], left_grads0[1], left_grads1[0], left_grads1[1]]
    states1, lent1, ranks, out_rank, *crossing = hold(states1, lent1, ranks, out_rank, *crossing)
    packed1 = pack_states(states1, lent1)
    down_rank, gateup_rgrad = ranks[:, :R].astype(bf16), ranks[:, R:].astype(bf16)
    backs = []

    def back_slots(pair, which, later, returned):
        for n in which:
            slot = 2 * pair + n
            backs.append(
                attend_back(
                    spots,
                    n,
                    projs[slot],
                    borrowed[pair],
                    prior[pair],
                    later,
                    returned,
                    (up0, up1)[pair],
                    (grad0, grad1)[pair],
                    slots[slot],
                    mixer_rank,
                    tables,
                )
            )

    def join(array, other):
        return (array.astype(f32) + other.astype(f32)).astype(array.dtype)

    next_crossing = swap_states(packed1)
    back_slots(0, (0, 1), *use_states(crossing, True))
    early_rank = backs[0][1] + backs[1][1]
    shared = jnp.stack(
        [
            tn(out_rank.astype(bf16), mixer_up),
            tn(gateup_rgrad, second),
            tn(down_rank, upstream),
        ]
    )
    owned = jnp.stack(
        [jnp.concatenate([left_grads[i], gate_grads[i], down_grads[i]], 1) for i in range(SLOTS)]
    )
    early_rank, shared, owned, *crossing = hold(early_rank, shared, owned, *next_crossing)
    shared_x, owned_x = swap_chip(shared, 1), swap_chip(owned, 1)
    later, returned = use_states(crossing, True)
    back_slots(1, (0,), later, returned)
    early_rank = early_rank + backs[2][1]
    early_rank, later, shared_x, owned_x = hold(early_rank, later, shared_x, owned_x)
    shared, owned = add_rest(join(shared, shared_x)), add_rest(join(owned, owned_x))
    back_slots(1, (1,), later, returned)
    rank_grad = early_rank + backs[3][1]
    rank_grad, shared, owned = hold(rank_grad, shared, owned)

    def packs_of(owned, shared):
        flat = jnp.concatenate(list(shared), 1).astype(bf16)
        return [jnp.concatenate([owned[k], flat], 1) for k in range(SLOTS)]

    mixer_all = jnp.concatenate(
        [
            jnp.stack([back[2] for back in backs]),
            tn(rank_grad.astype(bf16), first)[None].astype(bf16),
        ],
        0,
    )
    mixer_x = swap_chip(mixer_all, 1)
    early = packs_of(owned, shared)
    early = [early[0]] + [swap_tp(early[bit], bit) for bit in (1, 2, 3)]
    proj_grads = [back[0] for back in backs]
    left_t = my_mixer_left.T
    flat_mix = [w_mix] + sets
    part_a = first_back(0, proj_grads, rank_grad, left_t, flat_mix)
    part_a, rank_grad, mixer_x, *early = hold(
        part_a, rank_grad, mixer_x, *early, after=(block_output,)
    )
    early = jnp.stack(early)
    mixer_all = join(mixer_all, mixer_x)
    block = length // 2

    def finish(part, number):
        here = lax.dynamic_slice_in_dim(part, core * block, block, 0)
        there = lax.dynamic_slice_in_dim(part, (1 - core) * block, block, 0)
        total = here.astype(f32) + swap_core(there).astype(f32)
        wide = own_input[number * block : (number + 1) * block].astype(f32)
        scale_one = lax.rsqrt(jnp.mean(wide * wide, -1, keepdims=True) + epsilon)
        straight = lax.dynamic_slice_in_dim(
            mixer_up, core * length + number * block, block, 0
        ).astype(f32)
        return (straight + norm_back(wide, scale_one, gain_one, total)).astype(bf16)

    done_a = finish(part_a, 0)
    e_a, c_a = swap_tp(done_a, 1), cross(done_a)
    mixer_all = add_rest(mixer_all)
    early_other = swap_core(early)
    part_b = first_back(1, proj_grads, rank_grad, left_t, flat_mix)
    e_a, c_a, part_b, mixer_all, early_other = hold(e_a, c_a, part_b, mixer_all, early_other)
    c2_a, f_a = cross(e_a), edge(c_a)
    done_b = finish(part_b, 1)
    done_b, early, early_other, mixer_all = hold(done_b, early, early_other, mixer_all)
    e_b, c_b = swap_tp(done_b, 1), cross(done_b)
    late = packs_of(mixer_all[:SLOTS], mixer_all[SLOTS:])
    late1 = swap_tp(late[1], 1)
    hot = jnp.swapaxes(onehot, 0, 1).astype(f32)
    flag = jnp.reshape(core == 0, (1,)).astype(jnp.int32)
    early_tables = tables_of(
        functools.partial(early_kernel, half, pad),
        [(R, width)] * 3 + [(R, heads_here * HD), (R, 2, ff_here), (R, ff_here)],
        "early_tables",
        hot,
        flag,
        early,
        early_other,
    )
    (
        c2_a, f_a, e_b, c_b, late1, late[2], late[3], done_a, done_b, e_a, block_output
    ) = hold(
        c2_a, f_a, e_b, c_b, late1, late[2], late[3], done_a, done_b, e_a, block_output,
        after=early_tables,
    )
    f2_a, c2_b, f_b = edge(c2_a), cross(e_b), edge(c_b)
    late2, late3 = swap_tp(late[2], 2), swap_tp(late[3], 3)

    block_output = copy_of(block_output)
    input_grad = jnp.zeros(block_input.shape, bf16)

    def put(whole, part, slot, number):
        return lax.dynamic_update_slice(whole, part[None], (z ^ slot, number * block, 0))

    input_grad = put(input_grad, done_a, 0, 0)
    input_grad = put(input_grad, done_b, 0, 1)
    input_grad = put(input_grad, e_a, 1, 0)
    input_grad = put(input_grad, e_b, 1, 1)
    input_grad = put(input_grad, pick_inner(c2_a, f_a), 2, 0)
    f2_a, c2_b, f_b, late2, late3, input_grad = hold(
        f2_a, c2_b, f_b, late2, late3, input_grad, after=(block_output,)
    )
    f2_b = edge(c2_b)
    late = jnp.stack([late[0], late1, late2, late3])
    grad_mixer_right, grad_mixer_left = tables_of(
        late_kernel,
        [(R, heads_here, HCOLS), (R, width)],
        "late_tables",
        hot,
        flag,
        late,
        swap_core(late),
    )
    input_grad = put(input_grad, pick_inner(c_a, f2_a), 3, 0)
    input_grad = put(input_grad, pick_inner(c2_b, f_b), 2, 1)
    input_grad = put(input_grad, pick_inner(c_b, f2_b), 3, 1)
    grad_output_right, grad_gateup_left, grad_down_right = early_tables[:3]
    grad_output_left, grad_gateup_right, grad_down_left = early_tables[3:]
    return (
        block_output,
        input_grad,
        jnp.swapaxes(grad_mixer_left, 1, 2),
        grad_mixer_right,
        jnp.swapaxes(grad_output_left, 1, 2),
        grad_output_right,
        jnp.swapaxes(grad_gateup_left, 1, 2),
        grad_gateup_right,
        jnp.swapaxes(grad_down_left, 1, 2),
        grad_down_right,
    )


def solution(mesh):
    seq, tp = mesh.devices.shape
    fine = Mesh(mesh.devices.reshape(seq // 2, 2, tp), ("chip", "core", "tp"))
    where = ("chip", "core")
    return jax.shard_map(
        body,
        mesh=fine,
        in_specs=(
            P(None, where, None),
            P(),
            P(None, "tp", None),
            P(None, "tp"),
            P("tp", None),
            P(),
            P(None, None, "tp"),
            P("tp", None),
            P(),
            P(None, None, "tp", None),
            P(None, "tp", None),
            P(),
            P(),
            P(None, None, None, "tp"),
            P(None, "tp", None),
            P(),
            P(),
            P(),
            P(None, where, None),
        ),
        out_specs=(
            P(None, where, None),
            P(None, where, None),
            P(),
            P(None, None, "tp", None),
            P(None, "tp", None),
            P(),
            P(),
            P(None, None, None, "tp"),
            P(None, "tp", None),
            P(),
        ),
        check_vma=False,
    )
```

```python
import functools

import jax
import jax.numpy as jnp
import numpy as np
from jax import lax
from jax.experimental import pallas as pl
from jax.experimental.pallas import tpu as pltpu
from jax.sharding import Mesh
from jax.sharding import PartitionSpec as P

HD = 112
PD = 128
FD = 16
R = 16
NA = 8
KW = 3
WIN = 64
HCOLS = 704
SLOTS = 4
HEAD_PAD = 7 * PD
STATE = 160
CHUNK = 256
QB = 128
BACK_QB = 256
PACK = STATE + 2 * WIN + 32

epsilon = 1e-05
masked = -1e30
f32 = jnp.float32
bf16 = jnp.bfloat16
ANY = pl.BlockSpec(memory_space=pl.ANY)


def nn(a, b):
    return lax.dot_general(a, b, (((1,), (0,)), ((), ())), preferred_element_type=f32)


def nt(a, b):
    return lax.dot_general(a, b, (((1,), (1,)), ((), ())), preferred_element_type=f32)


def tn(a, b):
    return lax.dot_general(a, b, (((0,), (0,)), ((), ())), preferred_element_type=f32)


def feature_tables():
    leading, trailing = np.triu_indices(FD)
    pick = np.zeros((PD, 1280), np.float32)
    for base, row in ((0, 0), (512, FD)):
        pick[PD - 1, base] = 1.0
        pick[PD - 1, base + 256 : base + 256 + 1 + FD] = 1.0
        for i in range(FD):
            pick[row + i, base + 1 + i] = 0.5
        for n, (i, j) in enumerate(zip(leading, trailing)):
            pick[row + i, base + 1 + FD + n] = 0.25 if i == j and base == 0 else 0.5
            pick[row + j, base + 256 + 1 + FD + n] = 0.5
    for i in range(FD):
        pick[FD + i, 1024 + i] = 0.25
        pick[i, 1152 + FD + i] = 0.25
    return pick


HEAD_SEGMENTS = [(0, 2 * FD, 0)] + [(2 * FD + HD * i, HD, PD * (i + 1)) for i in range(6)]
M_ROWS = HCOLS + HD
M_CUT = 2 * FD + 3 * HD


def place():
    j = lax.rem(lax.axis_index("chip"), 4)
    return j // 2, lax.rem(j, 2)


def run_copies(copies, sems, start):
    for number, (src, dst) in enumerate(copies):
        copy = pltpu.make_async_copy(src, dst, sems.at[start + number])
        copy.start()


def wait_copies(copies, sems, start):
    for number, (src, dst) in enumerate(copies):
        pltpu.make_async_copy(src, dst, sems.at[start + number]).wait()


def spread_pieces(refs, cut, rows, dest, base, width, offset_of):
    y, x = place()
    z_ref, x_ref, y_ref, da_ref, db_ref = refs
    copies = []
    for kind, yy, xx in (("z", y, x), ("x", y, 1 - x), ("y", 1 - y, x), ("d", 1 - y, 1 - x)):
        cols = pl.ds(pl.multiple_of(xx * width, PD), width)
        for first, count in rows:
            spans = [(first, count)]
            if kind == "d" and first < cut < first + count:
                spans = [(first, cut - first), (cut, first + count - cut)]
            for row, size in spans:
                if kind == "d":
                    src = da_ref if row < cut else db_ref
                    src = src.at[pl.ds(row if row < cut else row - cut, size)]
                else:
                    src = {"z": z_ref, "x": x_ref, "y": y_ref}[kind].at[pl.ds(row, size)]
                start = pl.multiple_of(base + offset_of(row, yy), 16)
                copies.append((src, dest.at[pl.ds(start, size), cols]))
    return copies


def mixer_offset(row, yy):
    for first, count, at in HEAD_SEGMENTS:
        if first <= row < first + count:
            return yy * HEAD_PAD + at + row - first
    return None


MIXER_ROWS = [(first, count) for first, count, _ in HEAD_SEGMENTS]


def mixer_copies(refs, own, dest, base):
    if own:
        core = lax.axis_index("core")
        copies = []
        for head in range(2):
            for first, count, at in HEAD_SEGMENTS:
                src = pl.multiple_of(2 * HCOLS * core + HCOLS * head + first, 16)
                copies.append(
                    (refs[0].at[pl.ds(src, count)], dest.at[pl.ds(base + HEAD_PAD * head + at, count)])
                )
        return copies
    return spread_pieces(refs, M_CUT, MIXER_ROWS, dest, base, dest.shape[1] // 2, mixer_offset)


def mixer_pads(dest, base):
    for head in range(2):
        for first, count, at in HEAD_SEGMENTS:
            start = base + HEAD_PAD * head + at + count
            dest[start : start + PD - count] = jnp.zeros((PD - count, dest.shape[1]), bf16)


def output_copies(refs, own, dest, base):
    if own:
        core = lax.axis_index("core")
        return [
            (
                refs[0].at[pl.ds(pl.multiple_of(2 * HD * core + HD * head, 16), HD)],
                dest.at[pl.ds(base + PD * head, HD)],
            )
            for head in range(2)
        ]
    return spread_pieces(
        refs, M_CUT, [(HCOLS, HD)], dest, base, dest.shape[1] // 2, lambda row, yy: yy * PD + row - HCOLS
    )


def output_pads(dest, base):
    for head in range(2):
        start = base + PD * head + HD
        dest[start : start + PD - HD] = jnp.zeros((PD - HD, dest.shape[1]), bf16)


def feed_cut(quarter):
    return quarter + (quarter // 2 + 15) // 16 * 16


def feed_copies(refs, own, dest, half, pad):
    if own:
        core = lax.axis_index("core")
        wg, wd = refs
        spots = [(wg, 0, 0), (wg, 2 * half, pad), (wd, 0, 2 * pad)]
        return [
            (
                ref.at[pl.ds(pl.multiple_of(half * core + first, 16), half)],
                dest.at[pl.ds(at, half)],
            )
            for ref, first, at in spots
        ]
    quarter = half // 2

    def offset_of(row, yy):
        return row // quarter * pad + yy * quarter + row % quarter

    rows = [(quarter * i, quarter) for i in range(3)]
    return spread_pieces(
        refs, feed_cut(quarter), rows, dest, 0, dest.shape[1] // 2, offset_of
    )


def feed_pads(dest, half, pad):
    for i in range(3):
        dest[pad * i + half : pad * (i + 1)] = jnp.zeros((pad - half, dest.shape[1]), bf16)


def features(picked, at):
    one = picked[:, at : at + 256]
    two = picked[:, at + 256 : at + 512]
    return one, two, (one * two).astype(bf16)


class Table:
    def __init__(self, pad):
        sizes = (2 * HEAD_PAD, 2 * PD, 2 * pad, pad, 2 * PD)
        starts = np.cumsum((0,) + sizes)
        self.right, self.left, self.gate, self.down, self.taps = (
            slice(int(a), int(a) + n) for a, n in zip(starts, sizes)
        )
        self.edges = [int(a) for a in starts]


def params(mib, **more):
    return pltpu.CompilerParams(vmem_limit_bytes=mib * 2**20, **more)


def project_kernel(own, first, rank, table, pick, *rest):
    count = 1 if own else 5
    refs = rest[:count]
    proj, packed, weight, sems = rest[count:]
    copies = mixer_copies(refs, own, weight, 0)
    run_copies(copies, sems, 0)
    mixer_pads(weight, 0)
    wait_copies(copies, sems, 0)
    blocks = first.shape[0] // CHUNK
    for head in range(2):
        cols = pl.ds(HEAD_PAD * head, HEAD_PAD)

        def one(block, carry):
            rows = pl.ds(pl.multiple_of(block * CHUNK, CHUNK), CHUNK)
            result = nt(first[rows, :], weight[cols, :]) + nn(rank[rows, :], table[:, cols])
            rounded = result.astype(bf16)
            lane = lax.broadcasted_iota(jnp.int32, (CHUNK, PD), 1)
            base = jnp.where(lane == PD - 1, 1.0, result[:, :PD]).astype(bf16)
            proj[rows, cols] = rounded
            proj[rows, HEAD_PAD * head : HEAD_PAD * head + PD] = base
            _, _, feat = features(nn(base, pick[:, 512:1024]), 0)
            return carry + tn(feat, rounded[:, PD : 2 * PD])

        total = lax.fori_loop(0, blocks, one, jnp.zeros((256, PD), f32))
        packed[head, 0:STATE] = total[:STATE].astype(bf16)
        last = first.shape[0]
        at = HEAD_PAD * head
        packed[head, STATE : STATE + WIN] = proj[last - WIN :, at + 3 * PD : at + 4 * PD]
        packed[head, STATE + WIN : STATE + 2 * WIN] = proj[last - WIN :, at + 4 * PD : at + 5 * PD]
        packed[head, PACK - 32 : PACK - 16] = proj[last - 16 :, at + 5 * PD : at + 6 * PD]
        packed[head, PACK - 16 : PACK] = jnp.zeros((16, PD), bf16)


def project(own, first, rank, table, tables, refs):
    rows, width = first.shape
    vm = pl.BlockSpec(memory_space=pltpu.VMEM)
    return pl.pallas_call(
        functools.partial(project_kernel, own),
        out_shape=(
            jax.ShapeDtypeStruct((rows, 2 * HEAD_PAD), bf16),
            jax.ShapeDtypeStruct((2, PACK, PD), bf16),
        ),
        in_specs=[vm] * 4 + [ANY] * len(refs),
        out_specs=(vm, vm),
        scratch_shapes=[pltpu.VMEM((2 * HEAD_PAD, width), bf16), pltpu.SemaphoreType.DMA((40,))],
        compiler_params=params(48),
        cost_estimate=pl.CostEstimate(
            flops=100_000_000, bytes_accessed=300_000, transcendentals=0
        ),
        name="project",
    )(first, rank, table, *tables, *refs)


def window_masks(count):
    query = lax.broadcasted_iota(jnp.int32, (count, count + WIN), 0)
    key = lax.broadcasted_iota(jnp.int32, (count, count + WIN), 1)
    others = (key > query) & (key <= query + WIN)
    lead = jnp.where(lax.axis_index("chip") > 0, 0, WIN)
    return others & (key >= lead), others


def window_prob(query, keys, allowed):
    scores = nt(query, keys) * HD ** (-0.5)
    scores = jnp.where(allowed, scores, masked)
    largest = jnp.max(scores, -1, keepdims=True)
    expo = jnp.exp(scores - largest)
    return expo * (1.0 / jnp.sum(expo, -1, keepdims=True))


def causal_mask():
    row = lax.broadcasted_iota(jnp.int32, (CHUNK, CHUNK), 0)
    col = lax.broadcasted_iota(jnp.int32, (CHUNK, CHUNK), 1)
    return col <= row


def conv_of(conv, taps, start, count):
    result = taps[0:1] * conv[pl.ds(16 + start, count), :]
    for offset in range(1, KW):
        result = result + taps[offset : offset + 1] * conv[pl.ds(16 + start - offset, count), :]
    return result


def attend_kernel(spots, proj, tails, prior, table, pick, mixed, numer, states, keys, vals, conv):
    rows = proj.shape[0]
    keys[0:WIN, :] = tails[0, 0:WIN]
    vals[0:WIN, :] = tails[0, WIN : 2 * WIN]
    conv[0:16, :] = tails[0, 2 * WIN : 2 * WIN + 16].astype(f32)
    keys[WIN:, :] = proj[:, 3 * PD : 4 * PD]
    vals[WIN:, :] = proj[:, 4 * PD : 5 * PD]
    conv[16:, :] = proj[:, 5 * PD : 6 * PD].astype(f32)
    tap = head_taps(spots, table)
    state = whole_state(prior[0])
    causal = causal_mask()
    first_mask, mask = window_masks(QB)
    for chunk in range(rows // CHUNK):
        states[0, chunk] = state.astype(bf16)
        at = chunk * CHUNK
        span = slice(at, at + CHUNK)
        base = proj[span, 0:PD]
        value = proj[span, PD : 2 * PD]
        picked = nn(base, pick[:, :1152])
        _, _, feat_q = features(picked, 0)
        score = nt(base, picked[:, 1024:1152].astype(bf16))
        weight = jnp.where(causal, 1.0 + score + 0.5 * score * score, 0.0).astype(bf16)
        total = nn(weight, value) + nn(feat_q, state.astype(bf16))
        if at + CHUNK < rows:
            _, _, feat_k = features(picked, 512)
            state = state + tn(feat_k, value)
        parts = []
        for number in range(chunk * CHUNK // QB, (chunk + 1) * CHUNK // QB):
            query = proj[number * QB : (number + 1) * QB, 2 * PD : 3 * PD]
            allowed = mask if number else first_mask
            prob = window_prob(query, keys[number * QB : number * QB + QB + WIN, :], allowed)
            parts.append(nn(prob.astype(bf16), vals[number * QB : number * QB + QB + WIN, :]))
        window = jnp.concatenate(parts, 0)
        scale = lax.rsqrt(jnp.sum(total * total, -1, keepdims=True) * (1.0 / HD) + epsilon)
        gate = proj[span, 6 * PD : 7 * PD].astype(f32)
        branch = conv_of(conv, tap, at, CHUNK) * (gate * jax.nn.sigmoid(gate))
        mixed[span, :] = (total * scale + window + branch).astype(bf16)
        numer[span, :] = total.astype(bf16)


def whole_state(state):
    return jnp.concatenate([state, jnp.zeros((256 - STATE, PD), f32)], 0)


def head_taps(spots, table):
    start = pl.multiple_of(spots.taps.start + PD * pl.program_id(0), PD)
    return table[:, pl.ds(start, PD)].astype(f32)


def attend(spots, number, proj, tails, prior, table, tables):
    rows = proj.shape[0]
    whole = lambda a: pl.BlockSpec(a.shape, lambda h: (0,) * a.ndim)
    return pl.pallas_call(
        functools.partial(attend_kernel, spots),
        grid=(2,),
        out_shape=(
            jax.ShapeDtypeStruct((rows, 2 * PD), bf16),
            jax.ShapeDtypeStruct((rows, 2 * PD), bf16),
            jax.ShapeDtypeStruct((2, rows // CHUNK, 256, PD), bf16),
        ),
        in_specs=[
            pl.BlockSpec((rows, HEAD_PAD), lambda h: (0, h)),
            pl.BlockSpec((1, PACK - STATE, PD), lambda h: (2 * number + h, 0, 0)),
            pl.BlockSpec((1, STATE, PD), lambda h: (2 * number + h, 0, 0)),
            whole(table),
        ]
        + [whole(t) for t in tables],
        out_specs=(
            pl.BlockSpec((rows, PD), lambda h: (0, h)),
            pl.BlockSpec((rows, PD), lambda h: (0, h)),
            pl.BlockSpec((1, rows // CHUNK, 256, PD), lambda h: (h, 0, 0, 0)),
        ),
        scratch_shapes=[
            pltpu.VMEM((rows + WIN, PD), bf16),
            pltpu.VMEM((rows + WIN, PD), bf16),
            pltpu.VMEM((rows + 16, PD), f32),
        ],
        compiler_params=params(48),
        cost_estimate=pl.CostEstimate(
            flops=100_000_000, bytes_accessed=300_000, transcendentals=0
        ),
        name="attend",
    )(proj, tails, prior, table, *tables)


def mix_out_kernel(spots, *refs):
    mixed = refs[0:4]
    lefts = refs[4:8]
    right = refs[8]
    sources = refs[9 : 9 + 1 + 15]
    part, rank, kept, weight, sems = refs[25:]
    groups = []
    for slot in range(SLOTS):
        pieces = sources[0:1] if slot == 0 else sources[1 + 5 * (slot - 1) : 1 + 5 * slot]
        groups.append(output_copies(pieces, slot == 0, weight, 2 * PD * slot))

    @pl.when(pl.program_id(0) == 0)
    def _():
        for slot in range(SLOTS):
            run_copies(groups[slot], sems, 8 * slot)
            output_pads(weight, 2 * PD * slot)
        for slot in range(SLOTS):
            wait_copies(groups[slot], sems, 8 * slot)

    total = jnp.zeros(part.shape, f32)
    rank_sum = jnp.zeros((part.shape[0], R), f32)
    for slot in range(SLOTS):
        total = total + nn(mixed[slot][...], weight[2 * PD * slot : 2 * PD * (slot + 1), :])
        rank_sum = rank_sum + nt(mixed[slot][...], lefts[slot][:, spots.left])
    total = total + nn(rank_sum.astype(bf16), right[...])
    part[...] = total.astype(bf16)
    rank[...] = rank_sum
    rows = kept.shape[0]
    kept[...] = weight[pl.ds(pl.multiple_of(pl.program_id(0) * rows, rows), rows), :]


def mix_out(spots, mixed, lefts, right, sources):
    rows = mixed[0].shape[0]
    width = right.shape[1]
    block = CHUNK
    steps = rows // block
    whole = lambda a: pl.BlockSpec(a.shape, lambda i: (0,) * a.ndim)
    return pl.pallas_call(
        functools.partial(mix_out_kernel, spots),
        grid=(steps,),
        out_shape=(
            jax.ShapeDtypeStruct((rows, width), bf16),
            jax.ShapeDtypeStruct((rows, R), f32),
            jax.ShapeDtypeStruct((SLOTS * 2 * PD, width), bf16),
        ),
        in_specs=[pl.BlockSpec((block, 2 * PD), lambda i: (i, 0))] * 4
        + [whole(a) for a in lefts]
        + [whole(right)]
        + [ANY] * len(sources),
        out_specs=(
            pl.BlockSpec((block, width), lambda i: (i, 0)),
            pl.BlockSpec((block, R), lambda i: (i, 0)),
            pl.BlockSpec((SLOTS * 2 * PD // steps, width), lambda i: (i, 0)),
        ),
        scratch_shapes=[pltpu.VMEM((SLOTS * 2 * PD, width), bf16), pltpu.SemaphoreType.DMA((32,))],
        compiler_params=params(48),
        cost_estimate=pl.CostEstimate(
            flops=100_000_000, bytes_accessed=300_000, transcendentals=0
        ),
        name="mix_out",
    )(*mixed, *lefts, right, *sources)


def feed_kernel(slots, last, half, pad, spots, *refs):
    count = len(slots)
    fresh = slots[0] == 0
    second, grad, grank, rgrad, dright, gleft = refs[:6]
    tables, refs = refs[6 : 6 + count], refs[6 + count :]
    groups = []
    sources = []
    for slot in slots:
        size = 2 if slot == 0 else 5
        sources.append(refs[:size])
        refs = refs[size:]
    if not fresh:
        (down_in, back_in, ranks_in), refs = refs[:3], refs[3:]
    down_out, back_out, ranks_out = refs[:3]
    right_outs, left_outs = refs[3 : 3 + count], refs[3 + count : 3 + 2 * count]
    weights, sems, *sums = refs[3 + 2 * count :]
    right_grads, left_grads = sums[:count], sums[count:]
    for n, slot in enumerate(slots):
        part = weights.at[3 * pad * n : 3 * pad * (n + 1)]
        groups.append(feed_copies(sources[n], slot == 0, part, half, pad))
    begin = pl.program_id(0) == 0

    @pl.when(begin)
    def _():
        for n in range(count):
            run_copies(groups[n], sems, 16 * n)
        for n in range(count):
            feed_pads(weights.at[3 * pad * n : 3 * pad * (n + 1)], half, pad)
            right_grads[n][...] = jnp.zeros(right_grads[n].shape, f32)
            left_grads[n][...] = jnp.zeros(left_grads[n].shape, f32)

    down = jnp.zeros(down_out.shape, f32) if fresh else down_in[...]
    back = jnp.zeros(back_out.shape, f32) if fresh else back_in[...]
    down_rank = jnp.zeros((down.shape[0], R), f32) if fresh else ranks_in[:, :R]
    back_rank = jnp.zeros((down.shape[0], R), f32) if fresh else ranks_in[:, R:]
    for n in range(count):

        @pl.when(begin)
        def _():
            wait_copies(groups[n], sems, 16 * n)

        at = 3 * pad * n
        right, left = tables[n][:, spots.gate], tables[n][:, spots.down]
        gate_up = nt(second[...], weights[at : at + 2 * pad, :]) + nn(grank[...], right)
        gate, up = gate_up[:, :pad], gate_up[:, pad:]
        hidden_grad = nt(grad[...], weights[at + 2 * pad : at + 3 * pad, :]) + nn(rgrad[...], left)
        sig = jax.nn.sigmoid(gate)
        act = gate * sig
        hidden = (act * up).astype(bf16)
        gate_grad = hidden_grad * up * (sig * (1.0 + gate * (1.0 - sig)))
        both = jnp.concatenate([gate_grad.astype(bf16), (hidden_grad * act).astype(bf16)], 1)
        down = down + nn(hidden, weights[at + 2 * pad : at + 3 * pad, :])
        back = back + nn(both, weights[at : at + 2 * pad, :])
        down_rank = down_rank + nt(hidden, left)
        back_rank = back_rank + nt(both, right)
        right_grads[n][...] += tn(grank[...], both)
        left_grads[n][...] += tn(rgrad[...], hidden)
    ranks_out[:, :R] = down_rank
    ranks_out[:, R:] = back_rank
    if last:
        down = down + nn(down_rank.astype(bf16), dright[...])
        back = back + nn(back_rank.astype(bf16), gleft[...])
    down_out[...] = down.astype(down_out.dtype)
    back_out[...] = back.astype(back_out.dtype)

    @pl.when(pl.program_id(0) == pl.num_programs(0) - 1)
    def _():
        for out, total in zip(right_outs + left_outs, right_grads + left_grads):
            out[...] = total[...].astype(bf16)


def feed(slots, last, half, spots, second, grad, grank, rgrad, dright, gleft, tables, sources, carry):
    rows, width = second.shape
    pad = spots.down.stop - spots.down.start
    count = len(slots)
    block = CHUNK
    kind = bf16 if last else f32
    whole = lambda a: pl.BlockSpec(a.shape, lambda i: (0,) * a.ndim)
    wide = pl.BlockSpec((block, width), lambda i: (i, 0))
    thin = pl.BlockSpec((block, R), lambda i: (i, 0))
    pair = pl.BlockSpec((block, 2 * R), lambda i: (i, 0))
    flat = sum([list(s) for s in sources], [])
    out = pl.pallas_call(
        functools.partial(feed_kernel, slots, last, half, pad, spots),
        grid=(rows // block,),
        out_shape=(
            jax.ShapeDtypeStruct((rows, width), kind),
            jax.ShapeDtypeStruct((rows, width), kind),
            jax.ShapeDtypeStruct((rows, 2 * R), f32),
        )
        + (jax.ShapeDtypeStruct((R, 2 * pad), bf16),) * count
        + (jax.ShapeDtypeStruct((R, pad), bf16),) * count,
        in_specs=[wide, wide, thin, thin, whole(dright), whole(gleft)]
        + [whole(t) for t in tables]
        + [ANY] * len(flat)
        + ([wide, wide, pair] if carry else []),
        out_specs=(wide, wide, pair)
        + (pl.BlockSpec((R, 2 * pad), lambda i: (0, 0)),) * count
        + (pl.BlockSpec((R, pad), lambda i: (0, 0)),) * count,
        scratch_shapes=[
            pltpu.VMEM((3 * pad * count, width), bf16),
            pltpu.SemaphoreType.DMA((16 * count,)),
        ]
        + [pltpu.VMEM((R, 2 * pad), f32)] * count
        + [pltpu.VMEM((R, pad), f32)] * count,
        compiler_params=params(58),
        cost_estimate=pl.CostEstimate(
            flops=100_000_000, bytes_accessed=300_000, transcendentals=0
        ),
        name="feed",
    )(second, grad, grank, rgrad, dright, gleft, *tables, *flat, *carry)
    return list(out[:3]), list(out[3 : 3 + count]), list(out[3 + count :])


def turn_kernel(spots, *refs):
    mixer_up, orgrad, weight = refs[:3]
    tables, numers, mixeds = refs[3:5], refs[5:7], refs[7:9]
    bases, heads, tails = refs[9:13], refs[13:15], refs[15]
    pick = refs[16]
    up_out, grad_out, packed, left_out, total_state, left0, left1 = refs[17:]
    step = pl.program_id(0)

    @pl.when(step == 0)
    def _():
        total_state[...] = jnp.zeros(total_state.shape, f32)
        left0[...] = jnp.zeros(left0.shape, f32)
        left1[...] = jnp.zeros(left1.shape, f32)

    both = nt(mixer_up[...], weight[...])
    for n, left_grad in enumerate((left0, left1)):
        table = tables[n]
        flow = both[:, 2 * PD * n : 2 * PD * (n + 1)] + nn(orgrad[...], table[:, spots.left])
        left_grad[...] += tn(orgrad[...], mixeds[n][...])
        for head in range(2):
            cols = slice(PD * head, PD * (head + 1))
            wide = slice(PD * (2 * n + head), PD * (2 * n + head + 1))
            up = flow[:, cols]
            total = numers[n][:, cols].astype(f32)
            scale = lax.rsqrt(jnp.sum(total * total, -1, keepdims=True) * (1.0 / HD) + epsilon)
            inner = jnp.sum(total * up, -1, keepdims=True) * (1.0 / HD)
            grad = (scale * up - total * (scale * scale * scale * inner)).astype(bf16)
            up_out[:, wide] = up.astype(bf16)
            grad_out[:, wide] = grad
            _, _, feat = features(nn(bases[2 * n + head][...], pick[:, 0:512]), 0)
            total_state[2 * n + head] += tn(feat, grad)

    @pl.when(step == pl.num_programs(0) - 1)
    def _():
        packed[:, 0:STATE, :] = total_state[:, :STATE, :].astype(bf16)
        left_out[0] = left0[...].astype(bf16)
        left_out[1] = left1[...].astype(bf16)

    @pl.when(step == 0)
    def _():
        for n in range(2):
            for head in range(2):
                give_back(
                    spots, tables[n], heads[n], tails.at[2 * n + head], up_out, packed.at[2 * n + head], n, head
                )


def give_back(spots, table, rows, tails, up_out, lent, n, head):
    at = HEAD_PAD * head
    wide = slice(PD * (2 * n + head), PD * (2 * n + head + 1))
    query = rows[:, at + 2 * PD : at + 3 * PD]
    keys = jnp.concatenate([tails[0:WIN, :], rows[:, at + 3 * PD : at + 4 * PD]], 0)
    vals = jnp.concatenate([tails[WIN : 2 * WIN, :], rows[:, at + 4 * PD : at + 5 * PD]], 0)
    prob = window_prob(query, keys, window_masks(QB)[0])
    up = up_out[0:QB, wide]
    prob_grad = nt(up, vals)
    inner = jnp.sum(prob * prob_grad, -1, keepdims=True)
    score = (prob * (prob_grad - inner)).astype(bf16)
    lent[STATE : STATE + WIN, :] = (tn(score, query)[:WIN] * HD ** (-0.5)).astype(bf16)
    lent[STATE + WIN : STATE + 2 * WIN, :] = tn(prob.astype(bf16), up)[:WIN].astype(bf16)
    start = spots.taps.start + PD * head
    tap = table[:, start : start + PD].astype(f32)
    gate = rows[0:16, at + 6 * PD : at + 7 * PD].astype(f32)
    flow = up_out[0:16, wide].astype(f32) * (gate * jax.nn.sigmoid(gate))
    row0 = tap[2:3] * flow[0:1]
    row1 = tap[1:2] * flow[0:1] + tap[2:3] * flow[1:2]
    index = lax.broadcasted_iota(jnp.int32, (16, PD), 0)
    edge_rows = jnp.where(index == 14, row0, jnp.where(index == 15, row1, 0.0))
    lent[PACK - 32 : PACK - 16, :] = edge_rows.astype(bf16)
    lent[PACK - 16 : PACK, :] = jnp.zeros((16, PD), bf16)


def turn(pair, spots, mixer_up, orgrad, weight, slot_tables, numer, mixed, projs, tails, tables):
    rows, width = mixer_up.shape
    whole = lambda a: pl.BlockSpec(a.shape, lambda i: (0,) * a.ndim)
    flat = lambda *shape: pl.BlockSpec(shape, lambda i: (0,) * len(shape))
    tall = lambda cols, at: pl.BlockSpec((CHUNK, cols), lambda i: (i, at))
    return pl.pallas_call(
        functools.partial(turn_kernel, spots),
        grid=(rows // CHUNK,),
        out_shape=(
            jax.ShapeDtypeStruct((rows, 4 * PD), bf16),
            jax.ShapeDtypeStruct((rows, 4 * PD), bf16),
            jax.ShapeDtypeStruct((4, PACK, PD), bf16),
            jax.ShapeDtypeStruct((2, R, 2 * PD), bf16),
        ),
        in_specs=[
            tall(width, 0),
            tall(R, 0),
            pl.BlockSpec((4 * PD, width), lambda i: (pair, 0)),
        ]
        + [whole(t) for t in slot_tables]
        + [tall(2 * PD, 0)] * 4
        + [tall(PD, 0), tall(PD, 7)] * 2
        + [pl.BlockSpec((QB, 2 * HEAD_PAD), lambda i: (0, 0))] * 2
        + [whole(tails)]
        + [whole(t) for t in tables],
        out_specs=(
            tall(4 * PD, 0),
            tall(4 * PD, 0),
            flat(4, PACK, PD),
            flat(2, R, 2 * PD),
        ),
        scratch_shapes=[pltpu.VMEM((4, 256, PD), f32)] + [pltpu.VMEM((R, 2 * PD), f32)] * 2,
        compiler_params=params(48),
        cost_estimate=pl.CostEstimate(
            flops=100_000_000, bytes_accessed=300_000, transcendentals=0
        ),
        name="turn",
    )(
        mixer_up, orgrad, weight, *slot_tables, *numer, *mixed,
        projs[0], projs[0], projs[1], projs[1], *projs, tails, *tables,
    )


def window_back(proj, keys, vals, ups, out, number, allowed, held):
    start = number * BACK_QB
    span = slice(start, start + BACK_QB)
    band = slice(start, start + BACK_QB + WIN)
    query = proj[span, 2 * PD : 3 * PD]
    key = keys[band, :]
    prob = window_prob(query, key, allowed)
    up = ups[span, :]
    prob_grad = nt(up, vals[band, :])
    inner = jnp.sum(prob * prob_grad, -1, keepdims=True)
    score = (prob * (prob_grad - inner)).astype(bf16)
    out[span, 2 * PD : 3 * PD] = (nn(score, key) * HD ** (-0.5)).astype(bf16)
    dkey = tn(score, query) * HD ** (-0.5)
    dval = tn(prob.astype(bf16), up)
    for piece, new, more in ((3, dkey, held[0]), (4, dval, held[1])):
        cols = slice(piece * PD, (piece + 1) * PD)
        out[start : start + BACK_QB - WIN, cols] = new[WIN:BACK_QB].astype(bf16)
        out[start + BACK_QB - WIN : start + BACK_QB, cols] = (new[BACK_QB:] + more).astype(bf16)
    return dkey[:WIN], dval[:WIN]


def attend_back_kernel(
    spots, proj, tails, states, later, lent, ups, grads, table, rank, pick,
    out, rank_grad, right_grad, keys, vals, conv, flow
):
    rows = proj.shape[0]
    chunks = rows // CHUNK
    keys[0:WIN, :] = tails[0, 0:WIN]
    vals[0:WIN, :] = tails[0, WIN : 2 * WIN]
    conv[0:16, :] = tails[0, 2 * WIN : 2 * WIN + 16].astype(f32)
    keys[WIN:, :] = proj[:, 3 * PD : 4 * PD]
    vals[WIN:, :] = proj[:, 4 * PD : 5 * PD]
    conv[16:, :] = proj[:, 5 * PD : 6 * PD].astype(f32)
    tap = head_taps(spots, table)
    right = table.at[:, pl.ds(pl.multiple_of(HEAD_PAD * pl.program_id(0), PD), HEAD_PAD)]
    flow[rows:, :] = jnp.zeros((16, PD), f32)
    follow = whole_state(later[0])
    causal = causal_mask()
    first_mask, mask = window_masks(BACK_QB)
    held = (lent[0, 0:WIN].astype(f32), lent[0, WIN : 2 * WIN].astype(f32))
    for chunk in range(chunks - 1, -1, -1):
        at = chunk * CHUNK
        span = slice(at, at + CHUNK)
        base = proj[span, 0:PD]
        value = proj[span, PD : 2 * PD]
        grad = grads[span, :]
        picked = nn(base, pick[...])
        q_one, q_two, feat_q = features(picked, 0)
        k_one, k_two, feat_k = features(picked, 512)
        key_low = picked[:, 1024:1152].astype(bf16)
        query_high = picked[:, 1152:1280].astype(bf16)
        score = nt(base, key_low)
        weight = jnp.where(causal, 1.0 + score + 0.5 * score * score, 0.0).astype(bf16)
        slope = jnp.where(causal, nt(grad, value) * (1.0 + score), 0.0).astype(bf16)
        follow_round = follow.astype(bf16)
        q_up = nt(grad, states[0, chunk])
        k_up = nt(value, follow_round)
        inside = [q_up * q_two, q_up * q_one, k_up * k_two, k_up * k_one]
        inside = jnp.concatenate([part.astype(bf16) for part in inside], 1)
        low = nn(slope, key_low) + tn(slope, query_high) + nt(inside, pick[:, :1024])
        out[span, 0:PD] = low.astype(bf16)
        out[span, PD : 2 * PD] = (tn(weight, grad) + nn(feat_k, follow_round)).astype(bf16)
        if chunk:
            follow = follow + tn(feat_q, grad)
        gate = proj[span, 6 * PD : 7 * PD].astype(f32)
        up = ups[span, :].astype(f32)
        sig = jax.nn.sigmoid(gate)
        act = gate * sig
        flow[span, :] = up * act
        for number in range((at + CHUNK) // BACK_QB - 1, at // BACK_QB - 1, -1):
            held = window_back(
                proj, keys, vals, ups, out, number, mask if number else first_mask, held
            )
        slope_gate = sig + act * (1.0 - sig)
        out[span, 6 * PD : 7 * PD] = (up * conv_of(conv, tap, at, CHUNK) * slope_gate).astype(bf16)
    grad_in = tap[0:1] * flow[0:rows, :]
    for offset in range(1, KW):
        grad_in = grad_in + tap[offset : offset + 1] * flow[offset : offset + rows, :]
    out[:, 5 * PD : 6 * PD] = grad_in.astype(bf16)
    last = slice(rows - 16, rows)
    edge = grad_in[rows - 16 :, :] + lent[0, 2 * WIN : 2 * WIN + 16].astype(f32)
    out[last, 5 * PD : 6 * PD] = edge.astype(bf16)
    right_grad[...] = tn(rank[...], out[...]).astype(bf16)

    @pl.when(pl.program_id(0) == 0)
    def _():
        rank_grad[...] = nt(out[...], right[...])

    @pl.when(pl.program_id(0) > 0)
    def _():
        rank_grad[...] += nt(out[...], right[...])


def attend_back(spots, number, proj, tails, states, later, lent, ups, grads, table, rank, tables):
    rows = proj.shape[0]
    whole = lambda a: pl.BlockSpec(a.shape, lambda h: (0,) * a.ndim)
    head = pl.BlockSpec((rows, HEAD_PAD), lambda h: (0, h))
    edge = pl.BlockSpec((1, PACK - STATE, PD), lambda h: (2 * number + h, 0, 0))
    state = pl.BlockSpec((1, STATE, PD), lambda h: (2 * number + h, 0, 0))
    column = pl.BlockSpec((rows, PD), lambda h: (0, 2 * number + h))
    return pl.pallas_call(
        functools.partial(attend_back_kernel, spots),
        grid=(2,),
        out_shape=(
            jax.ShapeDtypeStruct((rows, 2 * HEAD_PAD), bf16),
            jax.ShapeDtypeStruct((rows, R), f32),
            jax.ShapeDtypeStruct((R, 2 * HEAD_PAD), bf16),
        ),
        in_specs=[
            head,
            edge,
            pl.BlockSpec((1, rows // CHUNK, 256, PD), lambda h: (h, 0, 0, 0)),
            state,
            edge,
            column,
            column,
            whole(table),
            whole(rank),
        ]
        + [whole(t) for t in tables],
        out_specs=(
            head,
            pl.BlockSpec((rows, R), lambda h: (0, 0)),
            pl.BlockSpec((R, HEAD_PAD), lambda h: (0, h)),
        ),
        scratch_shapes=[
            pltpu.VMEM((rows + WIN, PD), bf16),
            pltpu.VMEM((rows + WIN, PD), bf16),
            pltpu.VMEM((rows + 16, PD), f32),
            pltpu.VMEM((rows + 16, PD), f32),
        ],
        compiler_params=params(48),
        cost_estimate=pl.CostEstimate(
            flops=100_000_000, bytes_accessed=300_000, transcendentals=0
        ),
        name="attend_back",
    )(proj, tails, states, later, lent, ups, grads, table, rank, *tables)


def first_back_kernel(*refs):
    grads = refs[0:4]
    rank_grad, left = refs[4:6]
    sources = refs[6 : 6 + 16]
    part, weight, sems = refs[22:]
    groups = []
    size = 2 * HEAD_PAD
    for slot in range(SLOTS):
        pieces = sources[0:1] if slot == 0 else sources[1 + 5 * (slot - 1) : 1 + 5 * slot]
        groups.append(mixer_copies(pieces, slot == 0, weight, size * slot))
    begin = pl.program_id(0) == 0

    @pl.when(begin)
    def _():
        for slot in range(SLOTS):
            run_copies(groups[slot], sems, 40 * slot)
        for slot in range(SLOTS):
            mixer_pads(weight, size * slot)

    total = nn(rank_grad[...].astype(bf16), left[...])
    for slot in range(SLOTS):

        @pl.when(begin)
        def _():
            wait_copies(groups[slot], sems, 40 * slot)

        total = total + nn(grads[slot][...], weight[size * slot : size * (slot + 1), :])
    part[...] = total.astype(bf16)


def first_back(number, grads, rank_grad, left, sources):
    rows = rank_grad.shape[0]
    width = left.shape[1]
    block = rows // 4
    whole = lambda a: pl.BlockSpec(a.shape, lambda i: (0,) * a.ndim)
    size = 2 * HEAD_PAD
    return pl.pallas_call(
        first_back_kernel,
        grid=(2,),
        out_shape=jax.ShapeDtypeStruct((rows // 2, width), bf16),
        in_specs=[pl.BlockSpec((block, size), lambda i: (2 * i + number, 0))] * 4
        + [pl.BlockSpec((block, R), lambda i: (2 * i + number, 0)), whole(left)]
        + [ANY] * len(sources),
        out_specs=pl.BlockSpec((block, width), lambda i: (i, 0)),
        scratch_shapes=[pltpu.VMEM((SLOTS * size, width), bf16), pltpu.SemaphoreType.DMA((160,))],
        compiler_params=params(56),
        cost_estimate=pl.CostEstimate(
            flops=100_000_000, bytes_accessed=300_000, transcendentals=0
        ),
        name="first_back",
    )(*grads, rank_grad, left, *sources)


def norm_two_kernel(own, other, wide, gain, left, middle, second, rank):
    total = wide[...].astype(f32) + (own[...].astype(f32) + other[...].astype(f32))
    scale = lax.rsqrt(jnp.mean(total * total, -1, keepdims=True) + epsilon)
    rounded = (total * scale * gain[...]).astype(bf16)
    middle[...] = total
    second[...] = rounded
    rank[...] = nn(rounded, left[...]).astype(bf16)


def norm_two(own, other, wide, gain, left):
    rows, width = own.shape
    block = pl.BlockSpec((CHUNK, width), lambda i: (i, 0))
    whole = lambda a: pl.BlockSpec(a.shape, lambda i: (0,) * a.ndim)
    return pl.pallas_call(
        norm_two_kernel,
        grid=(rows // CHUNK,),
        out_shape=(
            jax.ShapeDtypeStruct((rows, width), f32),
            jax.ShapeDtypeStruct((rows, width), bf16),
            jax.ShapeDtypeStruct((rows, R), bf16),
        ),
        in_specs=[block, block, block, whole(gain), whole(left)],
        out_specs=(block, block, pl.BlockSpec((CHUNK, R), lambda i: (i, 0))),
        compiler_params=params(40),
        cost_estimate=pl.CostEstimate(
            flops=100_000_000, bytes_accessed=300_000, transcendentals=0
        ),
        name="norm_two",
    )(own, other, wide, gain, left)


def back_two_kernel(own, other, middle, upstream, gain, right, mixer_up, rgrad):
    vector = middle[...]
    scale = lax.rsqrt(jnp.mean(vector * vector, -1, keepdims=True) + epsilon)
    flow = gain[...] * (own[...].astype(f32) + other[...].astype(f32))
    inner = jnp.mean(vector * flow, -1, keepdims=True)
    total = upstream[...].astype(f32) + scale * flow - vector * (scale * scale * scale * inner)
    rounded = total.astype(bf16)
    mixer_up[...] = rounded
    rgrad[...] = nt(rounded, right[...]).astype(bf16)


def back_two(own, other, middle, upstream, gain, right):
    rows, width = own.shape
    block = pl.BlockSpec((CHUNK, width), lambda i: (i, 0))
    whole = lambda a: pl.BlockSpec(a.shape, lambda i: (0,) * a.ndim)
    return pl.pallas_call(
        back_two_kernel,
        grid=(rows // CHUNK,),
        out_shape=(
            jax.ShapeDtypeStruct((rows, width), bf16),
            jax.ShapeDtypeStruct((rows, R), bf16),
        ),
        in_specs=[block, block, block, block, whole(gain), whole(right)],
        out_specs=(block, pl.BlockSpec((CHUNK, R), lambda i: (i, 0))),
        compiler_params=params(40),
        cost_estimate=pl.CostEstimate(
            flops=100_000_000, bytes_accessed=300_000, transcendentals=0
        ),
        name="back_two",
    )(own, other, middle, upstream, gain, right)


def weighted(hot, parts):
    expert = pl.program_id(0)
    total = hot[expert, 0] * parts[0].astype(f32)
    for slot in range(1, SLOTS):
        total = total + hot[expert, slot] * parts[slot].astype(f32)
    return total


def by_core(flag, mine, other, base):
    lead = flag[0] > 0
    one, two = mine[:, :base], other[:, :base]
    return jnp.where(lead, one, two), jnp.where(lead, two, one)


def early_kernel(half, pad, hot, flag, mine, other, *outs):
    right, gate_left, down_right, out_left, gate_right, down_left = outs
    width = right.shape[2]
    base = 2 * PD + 3 * pad
    own, sibling = weighted(hot, mine), weighted(hot, other)
    for n, ref in enumerate((right, gate_left, down_right)):
        cols = slice(base + width * n, base + width * (n + 1))
        ref[0] = own[:, cols] + sibling[:, cols]
    cores = by_core(flag, own, sibling, base)
    out_left[0] = jnp.concatenate(
        [part[:, PD * h : PD * h + HD] for part in cores for h in range(2)], 1
    )
    for g in range(2):
        at = 2 * PD + pad * g
        gate_right[0, :, g, :] = jnp.concatenate([part[:, at : at + half] for part in cores], 1)
    at = 2 * PD + 2 * pad
    down_left[0] = jnp.concatenate([part[:, at : at + half] for part in cores], 1)


def late_kernel(hot, flag, mine, other, right, left):
    width = left.shape[2]
    base = 2 * HEAD_PAD
    own, sibling = weighted(hot, mine), weighted(hot, other)
    left[0] = own[:, base : base + width] + sibling[:, base : base + width]
    for core, part in enumerate(by_core(flag, own, sibling, base)):
        for head in range(2):
            at = HEAD_PAD * head
            right[0, :, 2 * core + head, :] = jnp.concatenate(
                [part[:, at + place_at : at + place_at + size] for _, size, place_at in HEAD_SEGMENTS], 1
            )


def tables_of(kernel, shapes, name, hot, flag, mine, other):
    whole = lambda a: pl.BlockSpec(a.shape, lambda e: (0,) * a.ndim)
    smem = pl.BlockSpec(memory_space=pltpu.SMEM)
    spot = lambda rank: lambda e: (e,) + (0,) * (rank - 1)
    return pl.pallas_call(
        kernel,
        grid=(NA,),
        out_shape=[jax.ShapeDtypeStruct((NA,) + shape, f32) for shape in shapes],
        in_specs=[smem, smem, whole(mine), whole(other)],
        out_specs=[pl.BlockSpec((1,) + shape, spot(len(shape) + 1)) for shape in shapes],
        compiler_params=params(40),
        cost_estimate=pl.CostEstimate(
            flops=100_000_000, bytes_accessed=300_000, transcendentals=0
        ),
        name=name,
    )(hot, flag, mine, other)


def swap_core(array):
    return lax.ppermute(array, "core", [(0, 1), (1, 0)])


def swap_chip(array, bit):
    count = lax.axis_size("chip")
    return lax.ppermute(array, "chip", [(i, i ^ bit) for i in range(count)])


def swap_tp(array, bit):
    return lax.ppermute(array, "tp", [(i, i ^ bit) for i in range(4)])


def both_cores(own):
    return order_cores(own, swap_core(own))


def order_cores(own, other):
    lead = lax.axis_index("core") == 0
    return jnp.concatenate([jnp.where(lead, own, other), jnp.where(lead, other, own)], 0)


def own_rows(array, core):
    half = array.shape[0] // 2
    return lax.dynamic_slice_in_dim(array, core * half, half, 0)


def hold_kernel(*refs):
    pass


def hold(*arrays, after=()):
    return pl.pallas_call(
        hold_kernel,
        out_shape=tuple(jax.ShapeDtypeStruct(a.shape, a.dtype) for a in arrays),
        in_specs=[ANY] * (len(arrays) + len(after)),
        out_specs=(ANY,) * len(arrays),
        input_output_aliases={i: i for i in range(len(arrays))},
        compiler_params=pltpu.CompilerParams(has_side_effects=True),
        name="hold",
    )(*arrays, *after)


def hop_xy(piece):
    return swap_chip(piece, 1), swap_chip(piece, 2)


def hop_diag(from_x, from_y, cut):
    return swap_chip(from_y[:cut], 1), swap_chip(from_x[cut:], 2)


def cross(array):
    return lax.ppermute(array, "tp", [(1, 2), (2, 1)])


def edge(array):
    return lax.ppermute(array, "tp", [(1, 0), (2, 3)])


def pick_inner(inner_array, edge_array):
    z = lax.axis_index("tp")
    return jnp.where((z == 1) | (z == 2), inner_array, edge_array)


def add_swapped(array, bit):
    other = swap_chip(array, bit)
    return (array.astype(f32) + other.astype(f32)).astype(array.dtype)


def add_rest(array):
    bit = 2
    while bit < lax.axis_size("chip"):
        array = add_swapped(array, bit)
        bit *= 2
    return array


def neighbour_chip(array, by):
    count = lax.axis_size("chip")
    pairs = [(i, i + by) for i in range(count) if 0 <= i + by < count]
    return lax.ppermute(array, "chip", pairs)


def swap_states(packed):
    if lax.axis_size("chip") == 4:
        return tuple(swap_chip(packed, bit) for bit in (1, 2, 3))
    return (lax.all_gather(packed, "chip"),)


def use_states(parts, backward):
    chip = lax.axis_index("chip")
    count = lax.axis_size("chip")
    if len(parts) > 1:
        total = 0.0
        for bit, part in zip((1, 2, 3), parts):
            other = chip ^ bit
            ahead = (other > chip) if backward else (other < chip)
            total = total + jnp.where(ahead, part[:, :STATE].astype(f32), 0.0)
        near = jnp.where(lax.rem(chip, 2) == (0 if backward else 1), parts[0], parts[2])
    else:
        index = jnp.arange(count, dtype=jnp.int32)
        ahead = (index > chip) if backward else (index < chip)
        states = parts[0][:, :, :STATE].astype(f32)
        total = jnp.sum(jnp.where(ahead[:, None, None, None], states, 0.0), 0)
        at = jnp.minimum(chip + 1, count - 1) if backward else jnp.maximum(chip - 1, 0)
        near = lax.dynamic_index_in_dim(parts[0], at, 0, False)
    inside = (chip < count - 1) if backward else (chip > 0)
    return total, jnp.where(inside, near[:, STATE:], 0.0).astype(bf16)


def copy_kernel(source, dest):
    dest[...] = source[...]


def copy_of(array):
    block = pl.BlockSpec((1,) + array.shape[1:], lambda i: (i, 0, 0))
    return pl.pallas_call(
        copy_kernel,
        grid=(array.shape[0],),
        out_shape=jax.ShapeDtypeStruct(array.shape, array.dtype),
        in_specs=[block],
        out_specs=block,
        compiler_params=params(32),
        cost_estimate=pl.CostEstimate(
            flops=100_000_000, bytes_accessed=300_000, transcendentals=0
        ),
        name="copy_of",
    )(array)


def stack_tp(parts):
    z = lax.axis_index("tp")
    result = jnp.zeros((SLOTS,) + parts[0].shape, parts[0].dtype)
    for slot, part in enumerate(parts):
        result = lax.dynamic_update_index_in_dim(result, part, z ^ slot, 0)
    return result


def pad_heads(table):
    lead = table.shape[:-2]
    heads = table.shape[-2]
    zero = [(0, 0)] * (len(lead) + 1)
    low = jnp.pad(table[..., : 2 * FD], zero + [(0, PD - 2 * FD)])
    high = table[..., 2 * FD :].reshape(lead + (heads, 6, HD))
    high = jnp.pad(high, zero + [(0, 0), (0, PD - HD)]).reshape(lead + (heads, 6 * PD))
    return jnp.concatenate([low, high], -1).reshape(lead + (heads * HEAD_PAD,))


def pad_last(table, size):
    return jnp.pad(table, [(0, 0)] * (table.ndim - 1) + [(0, size - table.shape[-1])])


def norm_rows(vector, gain_vector):
    row_scale = lax.rsqrt(jnp.mean(vector * vector, -1, keepdims=True) + epsilon)
    return (vector * row_scale * gain_vector, row_scale)


def norm_back(vector, row_scale, gain_vector, upstream):
    inner_mean = jnp.mean(vector * gain_vector * upstream, -1, keepdims=True)
    return (
        row_scale * gain_vector * upstream - vector * row_scale * row_scale * row_scale * inner_mean
    )


def body(
    block_input,
    gain_first,
    frozen_mixer_weight,
    conv_filter,
    frozen_output_weight,
    gain_second,
    frozen_gate_up_weight,
    frozen_down_weight,
    mixer_left,
    mixer_right,
    output_left,
    output_right,
    gateup_left,
    gateup_right,
    down_left,
    down_right,
    adapter_index,
    seq_lengths,
    out_cotangent,
):
    chip = lax.axis_index("chip")
    core = lax.axis_index("core")
    z = lax.axis_index("tp")
    y, x = place()
    sequences, length, width = block_input.shape
    rows = 2 * length
    heads_here = frozen_mixer_weight.shape[1]
    ff_here = frozen_down_weight.shape[0]
    half = ff_here // 2
    pad = (half + PD - 1) // PD * PD
    quarter = half // 2

    tables = (jnp.asarray(feature_tables(), bf16),)

    w_mix = jnp.transpose(frozen_mixer_weight, (1, 2, 0)).reshape(heads_here * HCOLS, width)
    w_gate = jnp.transpose(frozen_gate_up_weight, (1, 2, 0)).reshape(2 * ff_here, width)
    w_out = frozen_output_weight
    w_down = frozen_down_weight
    side = width // 2

    def cut(matrix, start, count):
        return lax.dynamic_slice(matrix, (start, x * side), (count, side))

    mixer_piece = jnp.concatenate(
        [
            cut(w_mix, 2 * HCOLS * core + HCOLS * y, HCOLS),
            cut(w_out, 2 * HD * core + HD * y, HD),
        ],
        0,
    )
    feed_piece = jnp.concatenate(
        [
            cut(w_gate, half * core + quarter * y, quarter),
            cut(w_gate, ff_here + half * core + quarter * y, quarter),
            cut(w_down, half * core + quarter * y, quarter),
        ],
        0,
    )
    slot_seq = z ^ jnp.arange(SLOTS, dtype=jnp.int32)
    slot_adapter = jnp.sum(
        jnp.where(slot_seq[:, None] == jnp.arange(SLOTS)[None, :], adapter_index[None, :], 0), 1
    )
    onehot = slot_adapter[:, None] == jnp.arange(NA, dtype=jnp.int32)[None, :]

    def select(table):
        return jnp.einsum(
            "se,e...->s...", onehot.astype(bf16), table, preferred_element_type=f32
        ).astype(bf16)

    mine = slot_adapter[0]
    my_mixer_left = lax.dynamic_index_in_dim(mixer_left, mine, 0, False)
    my_output_right = lax.dynamic_index_in_dim(output_right, mine, 0, False)
    my_gateup_left = lax.dynamic_index_in_dim(gateup_left, mine, 0, False)
    my_down_right = lax.dynamic_index_in_dim(down_right, mine, 0, False)
    right_table = pad_heads(
        select(lax.dynamic_slice_in_dim(mixer_right, 2 * core, 2, 2))
    )
    out_table = lax.dynamic_slice_in_dim(jnp.swapaxes(output_left, 1, 2), 2 * HD * core, 2 * HD, 2)
    out_table = pad_last(select(out_table).reshape(SLOTS, R, 2, HD), PD).reshape(SLOTS, R, 2 * PD)
    gate_table = lax.dynamic_slice_in_dim(gateup_right, half * core, half, 3)
    gate_table = pad_last(select(gate_table), pad).reshape(SLOTS, R, 2 * pad)
    down_table = lax.dynamic_slice_in_dim(jnp.swapaxes(down_left, 1, 2), half * core, half, 2)
    down_table = pad_last(select(down_table), pad)
    taps = lax.dynamic_slice_in_dim(conv_filter, 2 * HD * core, 2 * HD, 1)
    taps = pad_last(taps.reshape(KW, 2, HD), PD).reshape(KW, 2 * PD)
    taps = jnp.broadcast_to(jnp.pad(taps, ((0, R - KW), (0, 0))), (SLOTS, R, 2 * PD))
    packed = jnp.concatenate([right_table, out_table, gate_table, down_table, taps], 2)
    spots = Table(pad)

    gain_one = gain_first.astype(f32)
    gain_two = gain_second.astype(f32)[None, :]
    own_input = lax.dynamic_index_in_dim(block_input, z, 0, False)
    own_cotangent = lax.dynamic_index_in_dim(out_cotangent, z, 0, False)
    my_length = lax.dynamic_index_in_dim(seq_lengths, z, 0, False)
    upstream_own = jnp.where(
        (((chip * 2 + core) * length + jnp.arange(length, dtype=jnp.int32)) < my_length)[:, None],
        own_cotangent,
        0.0,
    ).astype(bf16)

    e_m, c_m = swap_tp(mixer_piece, 1), cross(mixer_piece)
    both_input = both_cores(own_input)
    first = norm_rows(both_input.astype(f32), gain_one)[0].astype(bf16)
    mixer_rank = nn(first, my_mixer_left).astype(bf16)
    upstream_other = swap_core(upstream_own)
    upstream_own, upstream_other, e_m, c_m, mixer_rank, packed, both_input = hold(
        upstream_own, upstream_other, e_m, c_m, mixer_rank, packed, both_input
    )

    projs, packs = [], []
    borrowed, prior, mixed, numer, chunk_states = [None, None], [None, None], [], [], []
    slots = [packed[0], None, None, None]

    def attend_slot(slot):
        pair, n = slot // 2, slot % 2
        out = attend(spots, n, projs[slot], borrowed[pair], prior[pair], slots[slot], tables)
        for kept, value in zip((mixed, numer, chunk_states), out):
            kept.append(value)

    def project_slot(slot, refs):
        out = project(slot == 0, first, mixer_rank, slots[slot], tables, refs)
        for kept, value in zip((projs, packs), out):
            kept.append(value)

    x1, y1 = hop_xy(e_m)
    c2_m, f_m = cross(e_m), edge(c_m)
    table1 = swap_tp(packed[1], 1)
    project_slot(0, (w_mix,))
    slot2 = pick_inner(c2_m, f_m)
    x1, y1, slot2, c2_m, c_m, packs[0], table1, feed_piece, packed = hold(
        x1, y1, slot2, c2_m, c_m, packs[0], table1, feed_piece, packed
    )
    slots[1] = table1
    d1 = hop_diag(x1, y1, M_CUT)
    x2, y2 = hop_xy(slot2)
    f2_m = edge(c2_m)
    table2, table3 = swap_tp(packed[2], 2), swap_tp(packed[3], 3)
    upstream = order_cores(upstream_own, upstream_other)
    down_rgrad = nt(upstream, my_down_right).astype(bf16)
    slot3 = pick_inner(c_m, f2_m)
    x2, y2, slot3, feed_piece, table2, table3, upstream, down_rgrad, *d1 = hold(
        x2, y2, slot3, feed_piece, table2, table3, upstream, down_rgrad, *d1
    )
    slots[2], slots[3] = table2, table3
    d2 = hop_diag(x2, y2, M_CUT)
    x3, y3 = hop_xy(slot3)
    e_f = swap_tp(feed_piece, 1)
    set1 = (e_m, x1, y1, *d1)
    project_slot(1, set1)
    x3, y3, e_f, packs[0], packs[1], *d2 = hold(x3, y3, e_f, packs[0], packs[1], *d2)
    d3 = hop_diag(x3, y3, M_CUT)
    c_f = cross(feed_piece)
    gathered = lax.all_gather(jnp.concatenate(packs[:2], 0), "chip")
    set2 = (slot2, x2, y2, *d2)
    project_slot(2, set2)
    prior[0], borrowed[0] = use_states((gathered,), False)
    d3_a, d3_b, c_f, packs[2], prior[0], borrowed[0] = hold(
        *d3, c_f, packs[2], prior[0], borrowed[0]
    )
    fx1, fy1 = hop_xy(e_f)
    c2_f, f_f = cross(e_f), edge(c_f)
    set3 = (slot3, x3, y3, d3_a, d3_b)
    project_slot(3, set3)
    fslot2 = pick_inner(c2_f, f_f)
    fx1, fy1, fslot2, c2_f, c_f, packs[2], packs[3] = hold(
        fx1, fy1, fslot2, c2_f, c_f, packs[2], packs[3]
    )
    crossing = swap_states(jnp.concatenate(packs[2:], 0))
    attend_slot(0)
    attend_slot(1)
    fd1 = hop_diag(fx1, fy1, feed_cut(quarter))
    mixed[0], mixed[1], fslot2, c2_f, fd1_a, fd1_b, *crossing = hold(
        mixed[0], mixed[1], fslot2, c2_f, *fd1, *crossing
    )
    fd1 = (fd1_a, fd1_b)
    fx2, fy2 = hop_xy(fslot2)
    f2_f = edge(c2_f)
    prior[1], borrowed[1] = use_states(crossing, False)
    attend_slot(2)
    attend_slot(3)
    fslot3 = pick_inner(c_f, f2_f)
    sets = list(set1) + list(set2) + list(set3)
    out_part, out_rank, out_weight = mix_out(spots, mixed, slots, my_output_right, [w_out] + sets)
    fx2, fy2, out_part, fslot3 = hold(fx2, fy2, out_part, fslot3)
    other_part = swap_core(out_part)
    middle, second, gate_rank = norm_two(out_part, other_part, both_input, gain_two, my_gateup_left)

    gateup_left_t = my_gateup_left.T

    def feed_slots(which, sources, carry):
        return feed(
            which,
            which[-1] == SLOTS - 1,
            half,
            spots,
            second,
            upstream,
            gate_rank,
            down_rgrad,
            my_down_right,
            gateup_left_t,
            [slots[k] for k in which],
            sources,
            carry,
        )

    fd2 = hop_diag(fx2, fy2, feed_cut(quarter))
    fx3, fy3 = hop_xy(fslot3)
    carry, gate_grads, down_grads = feed_slots(
        (0, 1), [(w_gate, w_down), (e_f, fx1, fy1, *fd1)], []
    )
    fx3, fy3, carry[2], *fd2 = hold(fx3, fy3, carry[2], *fd2)
    fd3 = hop_diag(fx3, fy3, feed_cut(quarter))
    carry, more_gates, more_downs = feed_slots((2,), [(fslot2, fx2, fy2, *fd2)], carry)
    gate_grads, down_grads = gate_grads + more_gates, down_grads + more_downs
    carry[2], *fd3 = hold(carry[2], *fd3)
    carry, more_gates, more_downs = feed_slots((3,), [(fslot3, fx3, fy3, *fd3)], carry)
    gate_grads, down_grads = gate_grads + more_gates, down_grads + more_downs
    down_part, back_part, ranks = carry
    other_back = swap_core(back_part)
    mixer_up, output_rgrad = back_two(
        back_part, other_back, middle, upstream, gain_two, my_output_right
    )

    output_rgrad, down_part, middle = hold(output_rgrad, down_part, middle)
    other_down = swap_core(own_rows(down_part, 1 - core))
    own_down = own_rows(down_part, core).astype(f32)
    own_output = own_rows(middle, core) + (own_down + other_down.astype(f32))
    output_rgrad, own_output = hold(output_rgrad, own_output.astype(bf16))
    block_output = lax.all_gather(own_output, "tp")

    def turn_pair(pair):
        both = slice(2 * pair, 2 * pair + 2)
        return turn(
            pair,
            spots,
            mixer_up,
            output_rgrad,
            out_weight,
            slots[both],
            numer[both],
            mixed[both],
            projs[both],
            borrowed[pair],
            tables,
        )

    up0, grad0, packed0, left_grads0 = turn_pair(0)
    up1, grad1, packed1, left_grads1 = turn_pair(1)
    packed0, packed1, left_grads1, ranks, out_rank = hold(
        packed0, packed1, left_grads1, ranks, out_rank
    )
    crossing = swap_states(packed0)
    left_grads = [left_grads0[0], left_grads0[1], left_grads1[0], left_grads1[1]]
    down_rank, gateup_rgrad = ranks[:, :R].astype(bf16), ranks[:, R:].astype(bf16)
    shared = jnp.stack(
        [
            tn(out_rank.astype(bf16), mixer_up),
            tn(gateup_rgrad, second),
            tn(down_rank, upstream),
        ]
    )
    owned = jnp.stack(
        [jnp.concatenate([left_grads[i], gate_grads[i], down_grads[i]], 1) for i in range(SLOTS)]
    )
    packed1, shared, owned, *crossing = hold(packed1, shared, owned, *crossing)
    backs = []

    def back_slots(pair, which, later, returned):
        for n in which:
            slot = 2 * pair + n
            backs.append(
                attend_back(
                    spots,
                    n,
                    projs[slot],
                    borrowed[pair],
                    chunk_states[slot],
                    later,
                    returned,
                    (up0, up1)[pair],
                    (grad0, grad1)[pair],
                    slots[slot],
                    mixer_rank,
                    tables,
                )
            )

    def join(array, other):
        return (array.astype(f32) + other.astype(f32)).astype(array.dtype)

    def packs_of(owned, shared):
        flat = jnp.concatenate(list(shared), 1).astype(bf16)
        return [jnp.concatenate([owned[k], flat], 1) for k in range(SLOTS)]

    next_crossing = swap_states(packed1)
    back_slots(0, (0, 1), *use_states(crossing, True))
    early_rank = backs[0][1] + backs[1][1]
    shared_x, owned_x = swap_chip(shared, 1), swap_chip(owned, 1)
    early_rank, shared_x, owned_x, *crossing = hold(
        early_rank, shared_x, owned_x, *next_crossing
    )
    shared, owned = add_rest(join(shared, shared_x)), add_rest(join(owned, owned_x))
    later, returned = use_states(crossing, True)
    back_slots(1, (0,), later, returned)
    early_rank = early_rank + backs[2][1]
    early_rank, later, shared, owned = hold(early_rank, later, shared, owned)
    early = packs_of(owned, shared)
    early = [early[0]] + [swap_tp(early[bit], bit) for bit in (1, 2, 3)]
    back_slots(1, (1,), later, returned)
    rank_grad = early_rank + backs[3][1]
    rank_grad, *early = hold(rank_grad, *early)
    early = jnp.stack(early)
    early_other = swap_core(early)

    mixer_all = jnp.concatenate(
        [
            jnp.stack([back[2] for back in backs]),
            tn(rank_grad.astype(bf16), first)[None].astype(bf16),
        ],
        0,
    )
    mixer_x = swap_chip(mixer_all, 1)
    proj_grads = [back[0] for back in backs]
    left_t = my_mixer_left.T
    flat_mix = [w_mix] + sets
    part_a = first_back(0, proj_grads, rank_grad, left_t, flat_mix)
    part_a, rank_grad, mixer_x, early, early_other = hold(
        part_a, rank_grad, mixer_x, early, early_other, after=(block_output,)
    )
    mixer_all = join(mixer_all, mixer_x)
    block = length // 2

    def finish(part, number):
        here = lax.dynamic_slice_in_dim(part, core * block, block, 0)
        there = lax.dynamic_slice_in_dim(part, (1 - core) * block, block, 0)
        total = here.astype(f32) + swap_core(there).astype(f32)
        wide = own_input[number * block : (number + 1) * block].astype(f32)
        scale_one = lax.rsqrt(jnp.mean(wide * wide, -1, keepdims=True) + epsilon)
        straight = lax.dynamic_slice_in_dim(
            mixer_up, core * length + number * block, block, 0
        ).astype(f32)
        return (straight + norm_back(wide, scale_one, gain_one, total)).astype(bf16)

    done_a = finish(part_a, 0)
    e_a, c_a = swap_tp(done_a, 1), cross(done_a)
    mixer_all = add_rest(mixer_all)
    part_b = first_back(1, proj_grads, rank_grad, left_t, flat_mix)
    e_a, c_a, part_b, mixer_all = hold(e_a, c_a, part_b, mixer_all)
    c2_a, f_a = cross(e_a), edge(c_a)
    done_b = finish(part_b, 1)
    done_b, early, early_other, mixer_all = hold(done_b, early, early_other, mixer_all)
    e_b, c_b = swap_tp(done_b, 1), cross(done_b)
    late = packs_of(mixer_all[:SLOTS], mixer_all[SLOTS:])
    late1 = swap_tp(late[1], 1)
    hot = jnp.swapaxes(onehot, 0, 1).astype(f32)
    flag = jnp.reshape(core == 0, (1,)).astype(jnp.int32)
    early_tables = tables_of(
        functools.partial(early_kernel, half, pad),
        [(R, width)] * 3 + [(R, heads_here * HD), (R, 2, ff_here), (R, ff_here)],
        "early_tables",
        hot,
        flag,
        early,
        early_other,
    )
    (
        c2_a, f_a, e_b, c_b, late1, late[2], late[3], done_a, done_b, e_a, block_output
    ) = hold(
        c2_a, f_a, e_b, c_b, late1, late[2], late[3], done_a, done_b, e_a, block_output,
        after=early_tables,
    )
    f2_a, c2_b, f_b = edge(c2_a), cross(e_b), edge(c_b)
    late2, late3 = swap_tp(late[2], 2), swap_tp(late[3], 3)

    block_output = copy_of(block_output)
    input_grad = jnp.zeros(block_input.shape, bf16)

    def put(whole, part, slot, number):
        return lax.dynamic_update_slice(whole, part[None], (z ^ slot, number * block, 0))

    input_grad = put(input_grad, done_a, 0, 0)
    input_grad = put(input_grad, done_b, 0, 1)
    input_grad = put(input_grad, e_a, 1, 0)
    input_grad = put(input_grad, e_b, 1, 1)
    input_grad = put(input_grad, pick_inner(c2_a, f_a), 2, 0)
    f2_a, c2_b, f_b, late2, late3, input_grad = hold(
        f2_a, c2_b, f_b, late2, late3, input_grad, after=(block_output,)
    )
    f2_b = edge(c2_b)
    late = jnp.stack([late[0], late1, late2, late3])
    grad_mixer_right, grad_mixer_left = tables_of(
        late_kernel,
        [(R, heads_here, HCOLS), (R, width)],
        "late_tables",
        hot,
        flag,
        late,
        swap_core(late),
    )
    input_grad = put(input_grad, pick_inner(c_a, f2_a), 3, 0)
    input_grad = put(input_grad, pick_inner(c2_b, f_b), 2, 1)
    input_grad = put(input_grad, pick_inner(c_b, f2_b), 3, 1)
    grad_output_right, grad_gateup_left, grad_down_right = early_tables[:3]
    grad_output_left, grad_gateup_right, grad_down_left = early_tables[3:]
    return (
        block_output,
        input_grad,
        jnp.swapaxes(grad_mixer_left, 1, 2),
        grad_mixer_right,
        jnp.swapaxes(grad_output_left, 1, 2),
        grad_output_right,
        jnp.swapaxes(grad_gateup_left, 1, 2),
        grad_gateup_right,
        jnp.swapaxes(grad_down_left, 1, 2),
        grad_down_right,
    )


def solution(mesh):
    seq, tp = mesh.devices.shape
    fine = Mesh(mesh.devices.reshape(seq // 2, 2, tp), ("chip", "core", "tp"))
    where = ("chip", "core")
    return jax.shard_map(
        body,
        mesh=fine,
        in_specs=(
            P(None, where, None),
            P(),
            P(None, "tp", None),
            P(None, "tp"),
            P("tp", None),
            P(),
            P(None, None, "tp"),
            P("tp", None),
            P(),
            P(None, None, "tp", None),
            P(None, "tp", None),
            P(),
            P(),
            P(None, None, None, "tp"),
            P(None, "tp", None),
            P(),
            P(),
            P(),
            P(None, where, None),
        ),
        out_specs=(
            P(None, where, None),
            P(None, where, None),
            P(),
            P(None, None, "tp", None),
            P(None, "tp", None),
            P(),
            P(),
            P(None, None, None, "tp"),
            P(None, "tp", None),
            P(),
        ),
        check_vma=False,
    )
```

```python
import functools

import jax
import jax.numpy as jnp
import numpy as np
from jax import lax
from jax.experimental import pallas as pl
from jax.experimental.pallas import tpu as pltpu
from jax.sharding import Mesh
from jax.sharding import PartitionSpec as P

HD = 112
PD = 128
FD = 16
R = 16
NA = 8
KW = 3
WIN = 64
HCOLS = 704
SLOTS = 4
HEAD_PAD = 7 * PD
STATE = 160
CHUNK = 256
QB = 128
BACK_QB = 256
BACK_CHUNK = 512
PACK = STATE + 2 * WIN + 32

epsilon = 1e-05
masked = -1e30
f32 = jnp.float32
bf16 = jnp.bfloat16
ANY = pl.BlockSpec(memory_space=pl.ANY)


def nn(a, b):
    return lax.dot_general(a, b, (((1,), (0,)), ((), ())), preferred_element_type=f32)


def nt(a, b):
    return lax.dot_general(a, b, (((1,), (1,)), ((), ())), preferred_element_type=f32)


def tn(a, b):
    return lax.dot_general(a, b, (((0,), (0,)), ((), ())), preferred_element_type=f32)


def feature_tables():
    leading, trailing = np.triu_indices(FD)
    pick = np.zeros((PD, 1280), np.float32)
    for base, row in ((0, 0), (512, FD)):
        pick[PD - 1, base] = 1.0
        pick[PD - 1, base + 256 : base + 256 + 1 + FD] = 1.0
        for i in range(FD):
            pick[row + i, base + 1 + i] = 0.5
        for n, (i, j) in enumerate(zip(leading, trailing)):
            pick[row + i, base + 1 + FD + n] = 0.25 if i == j and base == 0 else 0.5
            pick[row + j, base + 256 + 1 + FD + n] = 0.5
    for i in range(FD):
        pick[FD + i, 1024 + i] = 0.25
        pick[i, 1152 + FD + i] = 0.25
    return pick


HEAD_SEGMENTS = [(0, 2 * FD, 0)] + [(2 * FD + HD * i, HD, PD * (i + 1)) for i in range(6)]
M_ROWS = HCOLS + HD
M_CUT = 2 * FD + 3 * HD


def place():
    j = lax.rem(lax.axis_index("chip"), 4)
    return j // 2, lax.rem(j, 2)


def run_copies(copies, sems, start):
    for number, (src, dst) in enumerate(copies):
        copy = pltpu.make_async_copy(src, dst, sems.at[start + number])
        copy.start()


def wait_copies(copies, sems, start):
    for number, (src, dst) in enumerate(copies):
        pltpu.make_async_copy(src, dst, sems.at[start + number]).wait()


def spread_pieces(refs, cut, rows, dest, base, width, offset_of):
    y, x = place()
    z_ref, x_ref, y_ref, da_ref, db_ref = refs
    copies = []
    for kind, yy, xx in (("z", y, x), ("x", y, 1 - x), ("y", 1 - y, x), ("d", 1 - y, 1 - x)):
        cols = pl.ds(pl.multiple_of(xx * width, PD), width)
        for first, count in rows:
            spans = [(first, count)]
            if kind == "d" and first < cut < first + count:
                spans = [(first, cut - first), (cut, first + count - cut)]
            for row, size in spans:
                if kind == "d":
                    src = da_ref if row < cut else db_ref
                    src = src.at[pl.ds(row if row < cut else row - cut, size)]
                else:
                    src = {"z": z_ref, "x": x_ref, "y": y_ref}[kind].at[pl.ds(row, size)]
                start = pl.multiple_of(base + offset_of(row, yy), 16)
                copies.append((src, dest.at[pl.ds(start, size), cols]))
    return copies


def mixer_offset(row, yy):
    for first, count, at in HEAD_SEGMENTS:
        if first <= row < first + count:
            return yy * HEAD_PAD + at + row - first
    return None


MIXER_ROWS = [(first, count) for first, count, _ in HEAD_SEGMENTS]


def mixer_copies(refs, own, dest, base):
    if own:
        core = lax.axis_index("core")
        copies = []
        for head in range(2):
            for first, count, at in HEAD_SEGMENTS:
                src = pl.multiple_of(2 * HCOLS * core + HCOLS * head + first, 16)
                copies.append(
                    (refs[0].at[pl.ds(src, count)], dest.at[pl.ds(base + HEAD_PAD * head + at, count)])
                )
        return copies
    return spread_pieces(refs, M_CUT, MIXER_ROWS, dest, base, dest.shape[1] // 2, mixer_offset)


def mixer_pads(dest, base):
    for head in range(2):
        for first, count, at in HEAD_SEGMENTS:
            start = base + HEAD_PAD * head + at + count
            dest[start : start + PD - count] = jnp.zeros((PD - count, dest.shape[1]), bf16)


def output_copies(refs, own, dest, base):
    if own:
        core = lax.axis_index("core")
        return [
            (
                refs[0].at[pl.ds(pl.multiple_of(2 * HD * core + HD * head, 16), HD)],
                dest.at[pl.ds(base + PD * head, HD)],
            )
            for head in range(2)
        ]
    return spread_pieces(
        refs, M_CUT, [(HCOLS, HD)], dest, base, dest.shape[1] // 2, lambda row, yy: yy * PD + row - HCOLS
    )


def output_pads(dest, base):
    for head in range(2):
        start = base + PD * head + HD
        dest[start : start + PD - HD] = jnp.zeros((PD - HD, dest.shape[1]), bf16)


def feed_cut(quarter):
    return quarter + (quarter // 2 + 15) // 16 * 16


def feed_copies(refs, own, dest, half, pad):
    if own:
        core = lax.axis_index("core")
        wg, wd = refs
        spots = [(wg, 0, 0), (wg, 2 * half, pad), (wd, 0, 2 * pad)]
        return [
            (
                ref.at[pl.ds(pl.multiple_of(half * core + first, 16), half)],
                dest.at[pl.ds(at, half)],
            )
            for ref, first, at in spots
        ]
    quarter = half // 2

    def offset_of(row, yy):
        return row // quarter * pad + yy * quarter + row % quarter

    rows = [(quarter * i, quarter) for i in range(3)]
    return spread_pieces(
        refs, feed_cut(quarter), rows, dest, 0, dest.shape[1] // 2, offset_of
    )


def feed_pads(dest, half, pad):
    for i in range(3):
        dest[pad * i + half : pad * (i + 1)] = jnp.zeros((pad - half, dest.shape[1]), bf16)


def features(picked, at):
    one = picked[:, at : at + 256]
    two = picked[:, at + 256 : at + 512]
    return one, two, (one * two).astype(bf16)


class Table:
    def __init__(self, pad):
        sizes = (2 * HEAD_PAD, 2 * PD, 2 * pad, pad, 2 * PD)
        starts = np.cumsum((0,) + sizes)
        self.right, self.left, self.gate, self.down, self.taps = (
            slice(int(a), int(a) + n) for a, n in zip(starts, sizes)
        )
        self.edges = [int(a) for a in starts]


def params(mib, **more):
    return pltpu.CompilerParams(vmem_limit_bytes=mib * 2**20, **more)


def project_kernel(own, first, rank, table, pick, *rest):
    count = 1 if own else 5
    refs = rest[:count]
    proj, packed, weight, sems = rest[count:]
    copies = mixer_copies(refs, own, weight, 0)
    run_copies(copies, sems, 0)
    mixer_pads(weight, 0)
    wait_copies(copies, sems, 0)
    blocks = first.shape[0] // CHUNK
    for head in range(2):
        cols = pl.ds(HEAD_PAD * head, HEAD_PAD)

        def one(block, carry):
            rows = pl.ds(pl.multiple_of(block * CHUNK, CHUNK), CHUNK)
            result = nt(first[rows, :], weight[cols, :]) + nn(rank[rows, :], table[:, cols])
            rounded = result.astype(bf16)
            lane = lax.broadcasted_iota(jnp.int32, (CHUNK, PD), 1)
            base = jnp.where(lane == PD - 1, 1.0, result[:, :PD]).astype(bf16)
            proj[rows, cols] = rounded
            proj[rows, HEAD_PAD * head : HEAD_PAD * head + PD] = base
            _, _, feat = features(nn(base, pick[:, 512:1024]), 0)
            return carry + tn(feat, rounded[:, PD : 2 * PD])

        total = lax.fori_loop(0, blocks, one, jnp.zeros((256, PD), f32))
        packed[head, 0:STATE] = total[:STATE].astype(bf16)
        last = first.shape[0]
        at = HEAD_PAD * head
        packed[head, STATE : STATE + WIN] = proj[last - WIN :, at + 3 * PD : at + 4 * PD]
        packed[head, STATE + WIN : STATE + 2 * WIN] = proj[last - WIN :, at + 4 * PD : at + 5 * PD]
        packed[head, PACK - 32 : PACK - 16] = proj[last - 16 :, at + 5 * PD : at + 6 * PD]
        packed[head, PACK - 16 : PACK] = jnp.zeros((16, PD), bf16)


def project(own, first, rank, table, tables, refs):
    rows, width = first.shape
    vm = pl.BlockSpec(memory_space=pltpu.VMEM)
    return pl.pallas_call(
        functools.partial(project_kernel, own),
        out_shape=(
            jax.ShapeDtypeStruct((rows, 2 * HEAD_PAD), bf16),
            jax.ShapeDtypeStruct((2, PACK, PD), bf16),
        ),
        in_specs=[vm] * 4 + [ANY] * len(refs),
        out_specs=(vm, vm),
        scratch_shapes=[pltpu.VMEM((2 * HEAD_PAD, width), bf16), pltpu.SemaphoreType.DMA((40,))],
        compiler_params=params(48),
        cost_estimate=pl.CostEstimate(
            flops=100_000_000, bytes_accessed=300_000, transcendentals=0
        ),
        name="project",
    )(first, rank, table, *tables, *refs)


def window_masks(count):
    query = lax.broadcasted_iota(jnp.int32, (count, count + WIN), 0)
    key = lax.broadcasted_iota(jnp.int32, (count, count + WIN), 1)
    others = (key > query) & (key <= query + WIN)
    lead = jnp.where(lax.axis_index("chip") > 0, 0, WIN)
    return others & (key >= lead), others


def window_prob(query, keys, allowed):
    scores = nt(query, keys) * HD ** (-0.5)
    scores = jnp.where(allowed, scores, masked)
    largest = jnp.max(scores, -1, keepdims=True)
    expo = jnp.exp(scores - largest)
    return expo * (1.0 / jnp.sum(expo, -1, keepdims=True))


def causal_mask(size):
    row = lax.broadcasted_iota(jnp.int32, (size, size), 0)
    col = lax.broadcasted_iota(jnp.int32, (size, size), 1)
    return col <= row


def conv_of(conv, taps, start, count):
    result = taps[0:1] * conv[pl.ds(16 + start, count), :]
    for offset in range(1, KW):
        result = result + taps[offset : offset + 1] * conv[pl.ds(16 + start - offset, count), :]
    return result


def attend_kernel(spots, proj, tails, prior, table, pick, mixed, numer, states, keys, vals, conv):
    rows = proj.shape[0]
    keys[0:WIN, :] = tails[0, 0:WIN]
    vals[0:WIN, :] = tails[0, WIN : 2 * WIN]
    conv[0:16, :] = tails[0, 2 * WIN : 2 * WIN + 16].astype(f32)
    keys[WIN:, :] = proj[:, 3 * PD : 4 * PD]
    vals[WIN:, :] = proj[:, 4 * PD : 5 * PD]
    conv[16:, :] = proj[:, 5 * PD : 6 * PD].astype(f32)
    tap = head_taps(spots, table)
    state = whole_state(prior[0])
    causal = causal_mask(CHUNK)
    first_mask, mask = window_masks(QB)
    for chunk in range(rows // CHUNK):
        states[0, chunk] = state.astype(bf16)
        at = chunk * CHUNK
        span = slice(at, at + CHUNK)
        base = proj[span, 0:PD]
        value = proj[span, PD : 2 * PD]
        picked = nn(base, pick[:, :1152])
        _, _, feat_q = features(picked, 0)
        score = nt(base, picked[:, 1024:1152].astype(bf16))
        weight = jnp.where(causal, 1.0 + score + 0.5 * score * score, 0.0).astype(bf16)
        total = nn(weight, value) + nn(feat_q, state.astype(bf16))
        if at + CHUNK < rows:
            _, _, feat_k = features(picked, 512)
            state = state + tn(feat_k, value)
        parts = []
        for number in range(chunk * CHUNK // QB, (chunk + 1) * CHUNK // QB):
            query = proj[number * QB : (number + 1) * QB, 2 * PD : 3 * PD]
            allowed = mask if number else first_mask
            prob = window_prob(query, keys[number * QB : number * QB + QB + WIN, :], allowed)
            parts.append(nn(prob.astype(bf16), vals[number * QB : number * QB + QB + WIN, :]))
        window = jnp.concatenate(parts, 0)
        scale = lax.rsqrt(jnp.sum(total * total, -1, keepdims=True) * (1.0 / HD) + epsilon)
        gate = proj[span, 6 * PD : 7 * PD].astype(f32)
        branch = conv_of(conv, tap, at, CHUNK) * (gate * jax.nn.sigmoid(gate))
        mixed[span, :] = (total * scale + window + branch).astype(bf16)
        numer[span, :] = total.astype(bf16)


def whole_state(state):
    return jnp.concatenate([state, jnp.zeros((256 - STATE, PD), f32)], 0)


def head_taps(spots, table):
    start = pl.multiple_of(spots.taps.start + PD * pl.program_id(0), PD)
    return table[:, pl.ds(start, PD)].astype(f32)


def attend(spots, number, proj, tails, prior, table, tables):
    rows = proj.shape[0]
    whole = lambda a: pl.BlockSpec(a.shape, lambda h: (0,) * a.ndim)
    return pl.pallas_call(
        functools.partial(attend_kernel, spots),
        grid=(2,),
        out_shape=(
            jax.ShapeDtypeStruct((rows, 2 * PD), bf16),
            jax.ShapeDtypeStruct((rows, 2 * PD), bf16),
            jax.ShapeDtypeStruct((2, rows // CHUNK, 256, PD), bf16),
        ),
        in_specs=[
            pl.BlockSpec((rows, HEAD_PAD), lambda h: (0, h)),
            pl.BlockSpec((1, PACK - STATE, PD), lambda h: (2 * number + h, 0, 0)),
            pl.BlockSpec((1, STATE, PD), lambda h: (2 * number + h, 0, 0)),
            whole(table),
        ]
        + [whole(t) for t in tables],
        out_specs=(
            pl.BlockSpec((rows, PD), lambda h: (0, h)),
            pl.BlockSpec((rows, PD), lambda h: (0, h)),
            pl.BlockSpec((1, rows // CHUNK, 256, PD), lambda h: (h, 0, 0, 0)),
        ),
        scratch_shapes=[
            pltpu.VMEM((rows + WIN, PD), bf16),
            pltpu.VMEM((rows + WIN, PD), bf16),
            pltpu.VMEM((rows + 16, PD), f32),
        ],
        compiler_params=params(48),
        cost_estimate=pl.CostEstimate(
            flops=100_000_000, bytes_accessed=300_000, transcendentals=0
        ),
        name="attend",
    )(proj, tails, prior, table, *tables)


def mix_out_kernel(spots, *refs):
    mixed = refs[0:4]
    lefts = refs[4:8]
    right = refs[8]
    sources = refs[9 : 9 + 1 + 15]
    part, rank, kept, weight, sems = refs[25:]
    groups = []
    for slot in range(SLOTS):
        pieces = sources[0:1] if slot == 0 else sources[1 + 5 * (slot - 1) : 1 + 5 * slot]
        groups.append(output_copies(pieces, slot == 0, weight, 2 * PD * slot))

    @pl.when(pl.program_id(0) == 0)
    def _():
        for slot in range(SLOTS):
            run_copies(groups[slot], sems, 8 * slot)
            output_pads(weight, 2 * PD * slot)
        for slot in range(SLOTS):
            wait_copies(groups[slot], sems, 8 * slot)

    total = jnp.zeros(part.shape, f32)
    rank_sum = jnp.zeros((part.shape[0], R), f32)
    for slot in range(SLOTS):
        total = total + nn(mixed[slot][...], weight[2 * PD * slot : 2 * PD * (slot + 1), :])
        rank_sum = rank_sum + nt(mixed[slot][...], lefts[slot][:, spots.left])
    total = total + nn(rank_sum.astype(bf16), right[...])
    part[...] = total.astype(bf16)
    rank[...] = rank_sum
    rows = kept.shape[0]
    kept[...] = weight[pl.ds(pl.multiple_of(pl.program_id(0) * rows, rows), rows), :]


def mix_out(spots, mixed, lefts, right, sources):
    rows = mixed[0].shape[0]
    width = right.shape[1]
    block = CHUNK
    steps = rows // block
    whole = lambda a: pl.BlockSpec(a.shape, lambda i: (0,) * a.ndim)
    return pl.pallas_call(
        functools.partial(mix_out_kernel, spots),
        grid=(steps,),
        out_shape=(
            jax.ShapeDtypeStruct((rows, width), bf16),
            jax.ShapeDtypeStruct((rows, R), f32),
            jax.ShapeDtypeStruct((SLOTS * 2 * PD, width), bf16),
        ),
        in_specs=[pl.BlockSpec((block, 2 * PD), lambda i: (i, 0))] * 4
        + [whole(a) for a in lefts]
        + [whole(right)]
        + [ANY] * len(sources),
        out_specs=(
            pl.BlockSpec((block, width), lambda i: (i, 0)),
            pl.BlockSpec((block, R), lambda i: (i, 0)),
            pl.BlockSpec((SLOTS * 2 * PD // steps, width), lambda i: (i, 0)),
        ),
        scratch_shapes=[pltpu.VMEM((SLOTS * 2 * PD, width), bf16), pltpu.SemaphoreType.DMA((32,))],
        compiler_params=params(48),
        cost_estimate=pl.CostEstimate(
            flops=100_000_000, bytes_accessed=300_000, transcendentals=0
        ),
        name="mix_out",
    )(*mixed, *lefts, right, *sources)


def feed_kernel(slots, last, half, pad, spots, *refs):
    count = len(slots)
    fresh = slots[0] == 0
    second, grad, grank, rgrad, dright, gleft = refs[:6]
    tables, refs = refs[6 : 6 + count], refs[6 + count :]
    groups = []
    sources = []
    for slot in slots:
        size = 2 if slot == 0 else 5
        sources.append(refs[:size])
        refs = refs[size:]
    if not fresh:
        (down_in, back_in, ranks_in), refs = refs[:3], refs[3:]
    down_out, back_out, ranks_out = refs[:3]
    right_outs, left_outs = refs[3 : 3 + count], refs[3 + count : 3 + 2 * count]
    weights, sems, *sums = refs[3 + 2 * count :]
    right_grads, left_grads = sums[:count], sums[count:]
    for n, slot in enumerate(slots):
        part = weights.at[3 * pad * n : 3 * pad * (n + 1)]
        groups.append(feed_copies(sources[n], slot == 0, part, half, pad))
    begin = pl.program_id(0) == 0

    @pl.when(begin)
    def _():
        for n in range(count):
            run_copies(groups[n], sems, 16 * n)
        for n in range(count):
            feed_pads(weights.at[3 * pad * n : 3 * pad * (n + 1)], half, pad)
            right_grads[n][...] = jnp.zeros(right_grads[n].shape, f32)
            left_grads[n][...] = jnp.zeros(left_grads[n].shape, f32)

    down = jnp.zeros(down_out.shape, f32) if fresh else down_in[...]
    back = jnp.zeros(back_out.shape, f32) if fresh else back_in[...]
    down_rank = jnp.zeros((down.shape[0], R), f32) if fresh else ranks_in[:, :R]
    back_rank = jnp.zeros((down.shape[0], R), f32) if fresh else ranks_in[:, R:]
    for n in range(count):

        @pl.when(begin)
        def _():
            wait_copies(groups[n], sems, 16 * n)

        at = 3 * pad * n
        right, left = tables[n][:, spots.gate], tables[n][:, spots.down]
        gate_up = nt(second[...], weights[at : at + 2 * pad, :]) + nn(grank[...], right)
        gate, up = gate_up[:, :pad], gate_up[:, pad:]
        hidden_grad = nt(grad[...], weights[at + 2 * pad : at + 3 * pad, :]) + nn(rgrad[...], left)
        sig = jax.nn.sigmoid(gate)
        act = gate * sig
        hidden = (act * up).astype(bf16)
        gate_grad = hidden_grad * up * (sig * (1.0 + gate * (1.0 - sig)))
        both = jnp.concatenate([gate_grad.astype(bf16), (hidden_grad * act).astype(bf16)], 1)
        down = down + nn(hidden, weights[at + 2 * pad : at + 3 * pad, :])
        back = back + nn(both, weights[at : at + 2 * pad, :])
        down_rank = down_rank + nt(hidden, left)
        back_rank = back_rank + nt(both, right)
        right_grads[n][...] += tn(grank[...], both)
        left_grads[n][...] += tn(rgrad[...], hidden)
    ranks_out[:, :R] = down_rank
    ranks_out[:, R:] = back_rank
    if last:
        down = down + nn(down_rank.astype(bf16), dright[...])
        back = back + nn(back_rank.astype(bf16), gleft[...])
    down_out[...] = down.astype(down_out.dtype)
    back_out[...] = back.astype(back_out.dtype)

    @pl.when(pl.program_id(0) == pl.num_programs(0) - 1)
    def _():
        for out, total in zip(right_outs + left_outs, right_grads + left_grads):
            out[...] = total[...].astype(bf16)


def feed(slots, last, half, spots, second, grad, grank, rgrad, dright, gleft, tables, sources, carry):
    rows, width = second.shape
    pad = spots.down.stop - spots.down.start
    count = len(slots)
    block = CHUNK
    kind = bf16 if last else f32
    whole = lambda a: pl.BlockSpec(a.shape, lambda i: (0,) * a.ndim)
    wide = pl.BlockSpec((block, width), lambda i: (i, 0))
    thin = pl.BlockSpec((block, R), lambda i: (i, 0))
    pair = pl.BlockSpec((block, 2 * R), lambda i: (i, 0))
    flat = sum([list(s) for s in sources], [])
    out = pl.pallas_call(
        functools.partial(feed_kernel, slots, last, half, pad, spots),
        grid=(rows // block,),
        out_shape=(
            jax.ShapeDtypeStruct((rows, width), kind),
            jax.ShapeDtypeStruct((rows, width), kind),
            jax.ShapeDtypeStruct((rows, 2 * R), f32),
        )
        + (jax.ShapeDtypeStruct((R, 2 * pad), bf16),) * count
        + (jax.ShapeDtypeStruct((R, pad), bf16),) * count,
        in_specs=[wide, wide, thin, thin, whole(dright), whole(gleft)]
        + [whole(t) for t in tables]
        + [ANY] * len(flat)
        + ([wide, wide, pair] if carry else []),
        out_specs=(wide, wide, pair)
        + (pl.BlockSpec((R, 2 * pad), lambda i: (0, 0)),) * count
        + (pl.BlockSpec((R, pad), lambda i: (0, 0)),) * count,
        scratch_shapes=[
            pltpu.VMEM((3 * pad * count, width), bf16),
            pltpu.SemaphoreType.DMA((16 * count,)),
        ]
        + [pltpu.VMEM((R, 2 * pad), f32)] * count
        + [pltpu.VMEM((R, pad), f32)] * count,
        compiler_params=params(58),
        cost_estimate=pl.CostEstimate(
            flops=100_000_000, bytes_accessed=300_000, transcendentals=0
        ),
        name="feed",
    )(second, grad, grank, rgrad, dright, gleft, *tables, *flat, *carry)
    return list(out[:3]), list(out[3 : 3 + count]), list(out[3 + count :])


def turn_kernel(spots, *refs):
    mixer_up, orgrad, weight = refs[:3]
    tables, numers, mixeds, bases, heads, tails = (
        refs[3:7], refs[7:11], refs[11:15], refs[15:23], refs[23:27], refs[27:29]
    )
    pick = refs[29]
    up_out, grad_out, packs, left_out, total_state, left_sums = (
        refs[30], refs[31], refs[32:34], refs[34], refs[35], refs[36]
    )
    step = pl.program_id(0)

    @pl.when(step == 0)
    def _():
        total_state[...] = jnp.zeros(total_state.shape, f32)
        left_sums[...] = jnp.zeros(left_sums.shape, f32)

    both = nt(mixer_up[...], weight[...])
    for n in range(SLOTS):
        table = tables[n]
        flow = both[:, 2 * PD * n : 2 * PD * (n + 1)] + nn(orgrad[...], table[:, spots.left])
        left_sums[n] += tn(orgrad[...], mixeds[n][...])
        for head in range(2):
            cols = slice(PD * head, PD * (head + 1))
            wide = slice(PD * (2 * n + head), PD * (2 * n + head + 1))
            up = flow[:, cols]
            total = numers[n][:, cols].astype(f32)
            scale = lax.rsqrt(jnp.sum(total * total, -1, keepdims=True) * (1.0 / HD) + epsilon)
            inner = jnp.sum(total * up, -1, keepdims=True) * (1.0 / HD)
            grad = (scale * up - total * (scale * scale * scale * inner)).astype(bf16)
            up_out[:, wide] = up.astype(bf16)
            grad_out[:, wide] = grad
            _, _, feat = features(nn(bases[2 * n + head][...], pick[:, 0:512]), 0)
            total_state[2 * n + head] += tn(feat, grad)

    @pl.when(step == pl.num_programs(0) - 1)
    def _():
        for pair in range(2):
            packs[pair][:, 0:STATE, :] = total_state[4 * pair : 4 * pair + 4, :STATE, :].astype(bf16)
        left_out[...] = left_sums[...].astype(bf16)

    @pl.when(step == 0)
    def _():
        for n in range(SLOTS):
            for head in range(2):
                at = n % 2 * 2 + head
                rows = tails[n // 2].at[at]
                give_back(spots, tables[n], heads[n], rows, up_out, packs[n // 2].at[at], n, head)


def give_back(spots, table, rows, tails, up_out, lent, n, head):
    at = HEAD_PAD * head
    wide = slice(PD * (2 * n + head), PD * (2 * n + head + 1))
    query = rows[:, at + 2 * PD : at + 3 * PD]
    keys = jnp.concatenate([tails[0:WIN, :], rows[:, at + 3 * PD : at + 4 * PD]], 0)
    vals = jnp.concatenate([tails[WIN : 2 * WIN, :], rows[:, at + 4 * PD : at + 5 * PD]], 0)
    prob = window_prob(query, keys, window_masks(QB)[0])
    up = up_out[0:QB, wide]
    prob_grad = nt(up, vals)
    inner = jnp.sum(prob * prob_grad, -1, keepdims=True)
    score = (prob * (prob_grad - inner)).astype(bf16)
    lent[STATE : STATE + WIN, :] = (tn(score, query)[:WIN] * HD ** (-0.5)).astype(bf16)
    lent[STATE + WIN : STATE + 2 * WIN, :] = tn(prob.astype(bf16), up)[:WIN].astype(bf16)
    start = spots.taps.start + PD * head
    tap = table[:, start : start + PD].astype(f32)
    gate = rows[0:16, at + 6 * PD : at + 7 * PD].astype(f32)
    flow = up_out[0:16, wide].astype(f32) * (gate * jax.nn.sigmoid(gate))
    row0 = tap[2:3] * flow[0:1]
    row1 = tap[1:2] * flow[0:1] + tap[2:3] * flow[1:2]
    index = lax.broadcasted_iota(jnp.int32, (16, PD), 0)
    edge_rows = jnp.where(index == 14, row0, jnp.where(index == 15, row1, 0.0))
    lent[PACK - 32 : PACK - 16, :] = edge_rows.astype(bf16)
    lent[PACK - 16 : PACK, :] = jnp.zeros((16, PD), bf16)


def turn(spots, mixer_up, orgrad, weight, slot_tables, numer, mixed, projs, tails, tables):
    rows, width = mixer_up.shape
    whole = lambda a: pl.BlockSpec(a.shape, lambda i: (0,) * a.ndim)
    flat = lambda *shape: pl.BlockSpec(shape, lambda i: (0,) * len(shape))
    tall = lambda cols, at: pl.BlockSpec((CHUNK, cols), lambda i: (i, at))
    heads = 2 * SLOTS
    return pl.pallas_call(
        functools.partial(turn_kernel, spots),
        grid=(rows // CHUNK,),
        out_shape=(
            jax.ShapeDtypeStruct((rows, heads * PD), bf16),
            jax.ShapeDtypeStruct((rows, heads * PD), bf16),
            jax.ShapeDtypeStruct((4, PACK, PD), bf16),
            jax.ShapeDtypeStruct((4, PACK, PD), bf16),
            jax.ShapeDtypeStruct((SLOTS, R, 2 * PD), bf16),
        ),
        in_specs=[tall(width, 0), tall(R, 0), whole(weight)]
        + [whole(t) for t in slot_tables]
        + [tall(2 * PD, 0)] * 8
        + [tall(PD, 0), tall(PD, 7)] * SLOTS
        + [flat(QB, 2 * HEAD_PAD)] * SLOTS
        + [whole(t) for t in tails]
        + [whole(t) for t in tables],
        out_specs=(
            tall(heads * PD, 0),
            tall(heads * PD, 0),
            flat(4, PACK, PD),
            flat(4, PACK, PD),
            flat(SLOTS, R, 2 * PD),
        ),
        scratch_shapes=[pltpu.VMEM((heads, 256, PD), f32), pltpu.VMEM((SLOTS, R, 2 * PD), f32)],
        compiler_params=params(48),
        cost_estimate=pl.CostEstimate(
            flops=100_000_000, bytes_accessed=300_000, transcendentals=0
        ),
        name="turn",
    )(
        mixer_up, orgrad, weight, *slot_tables, *numer, *mixed,
        *[proj for proj in projs for _ in range(2)], *projs, *tails, *tables,
    )


def window_back(proj, keys, vals, ups, out, number, allowed, held):
    start = number * BACK_QB
    span = slice(start, start + BACK_QB)
    band = slice(start, start + BACK_QB + WIN)
    query = proj[span, 2 * PD : 3 * PD]
    key = keys[band, :]
    prob = window_prob(query, key, allowed)
    up = ups[span, :]
    prob_grad = nt(up, vals[band, :])
    inner = jnp.sum(prob * prob_grad, -1, keepdims=True)
    score = (prob * (prob_grad - inner)).astype(bf16)
    out[span, 2 * PD : 3 * PD] = (nn(score, key) * HD ** (-0.5)).astype(bf16)
    dkey = tn(score, query) * HD ** (-0.5)
    dval = tn(prob.astype(bf16), up)
    for piece, new, more in ((3, dkey, held[0]), (4, dval, held[1])):
        cols = slice(piece * PD, (piece + 1) * PD)
        out[start : start + BACK_QB - WIN, cols] = new[WIN:BACK_QB].astype(bf16)
        out[start + BACK_QB - WIN : start + BACK_QB, cols] = (new[BACK_QB:] + more).astype(bf16)
    return dkey[:WIN], dval[:WIN]


def attend_back_kernel(
    spots, proj, tails, states, later, lent, ups, grads, table, rank, pick,
    out, rank_grad, right_grad, keys, vals, conv, flow
):
    rows = proj.shape[0]
    chunks = rows // BACK_CHUNK
    keys[0:WIN, :] = tails[0, 0:WIN]
    vals[0:WIN, :] = tails[0, WIN : 2 * WIN]
    conv[0:16, :] = tails[0, 2 * WIN : 2 * WIN + 16].astype(f32)
    keys[WIN:, :] = proj[:, 3 * PD : 4 * PD]
    vals[WIN:, :] = proj[:, 4 * PD : 5 * PD]
    conv[16:, :] = proj[:, 5 * PD : 6 * PD].astype(f32)
    tap = head_taps(spots, table)
    right = table.at[:, pl.ds(pl.multiple_of(HEAD_PAD * pl.program_id(0), PD), HEAD_PAD)]
    flow[rows:, :] = jnp.zeros((16, PD), f32)
    follow = whole_state(later[0])
    causal = causal_mask(BACK_CHUNK)
    first_mask, mask = window_masks(BACK_QB)
    held = (lent[0, 0:WIN].astype(f32), lent[0, WIN : 2 * WIN].astype(f32))
    for chunk in range(chunks - 1, -1, -1):
        at = chunk * BACK_CHUNK
        span = slice(at, at + BACK_CHUNK)
        base = proj[span, 0:PD]
        value = proj[span, PD : 2 * PD]
        grad = grads[span, :]
        picked = nn(base, pick[...])
        q_one, q_two, feat_q = features(picked, 0)
        k_one, k_two, feat_k = features(picked, 512)
        key_low = picked[:, 1024:1152].astype(bf16)
        query_high = picked[:, 1152:1280].astype(bf16)
        score = nt(base, key_low)
        weight = jnp.where(causal, 1.0 + score + 0.5 * score * score, 0.0).astype(bf16)
        slope = jnp.where(causal, nt(grad, value) * (1.0 + score), 0.0).astype(bf16)
        follow_round = follow.astype(bf16)
        q_up = nt(grad, states[0, chunk * (BACK_CHUNK // CHUNK)])
        k_up = nt(value, follow_round)
        inside = [q_up * q_two, q_up * q_one, k_up * k_two, k_up * k_one]
        inside = jnp.concatenate([part.astype(bf16) for part in inside], 1)
        low = nn(slope, key_low) + tn(slope, query_high) + nt(inside, pick[:, :1024])
        out[span, 0:PD] = low.astype(bf16)
        out[span, PD : 2 * PD] = (tn(weight, grad) + nn(feat_k, follow_round)).astype(bf16)
        if chunk:
            follow = follow + tn(feat_q, grad)
        gate = proj[span, 6 * PD : 7 * PD].astype(f32)
        up = ups[span, :].astype(f32)
        sig = jax.nn.sigmoid(gate)
        act = gate * sig
        flow[span, :] = up * act
        for number in range((at + BACK_CHUNK) // BACK_QB - 1, at // BACK_QB - 1, -1):
            held = window_back(
                proj, keys, vals, ups, out, number, mask if number else first_mask, held
            )
        slope_gate = sig + act * (1.0 - sig)
        out[span, 6 * PD : 7 * PD] = (up * conv_of(conv, tap, at, BACK_CHUNK) * slope_gate).astype(bf16)
    grad_in = tap[0:1] * flow[0:rows, :]
    for offset in range(1, KW):
        grad_in = grad_in + tap[offset : offset + 1] * flow[offset : offset + rows, :]
    out[:, 5 * PD : 6 * PD] = grad_in.astype(bf16)
    last = slice(rows - 16, rows)
    edge = grad_in[rows - 16 :, :] + lent[0, 2 * WIN : 2 * WIN + 16].astype(f32)
    out[last, 5 * PD : 6 * PD] = edge.astype(bf16)
    right_grad[...] = tn(rank[...], out[...]).astype(bf16)

    @pl.when(pl.program_id(0) == 0)
    def _():
        rank_grad[...] = nt(out[...], right[...])

    @pl.when(pl.program_id(0) > 0)
    def _():
        rank_grad[...] += nt(out[...], right[...])


def attend_back(spots, slot, proj, tails, states, later, lent, ups, grads, table, rank, tables):
    rows = proj.shape[0]
    number = slot % 2
    whole = lambda a: pl.BlockSpec(a.shape, lambda h: (0,) * a.ndim)
    head = pl.BlockSpec((rows, HEAD_PAD), lambda h: (0, h))
    edge = pl.BlockSpec((1, PACK - STATE, PD), lambda h: (2 * number + h, 0, 0))
    state = pl.BlockSpec((1, STATE, PD), lambda h: (2 * number + h, 0, 0))
    column = pl.BlockSpec((rows, PD), lambda h: (0, 2 * slot + h))
    return pl.pallas_call(
        functools.partial(attend_back_kernel, spots),
        grid=(2,),
        out_shape=(
            jax.ShapeDtypeStruct((rows, 2 * HEAD_PAD), bf16),
            jax.ShapeDtypeStruct((rows, R), f32),
            jax.ShapeDtypeStruct((R, 2 * HEAD_PAD), bf16),
        ),
        in_specs=[
            head,
            edge,
            pl.BlockSpec((1, rows // CHUNK, 256, PD), lambda h: (h, 0, 0, 0)),
            state,
            edge,
            column,
            column,
            whole(table),
            whole(rank),
        ]
        + [whole(t) for t in tables],
        out_specs=(
            head,
            pl.BlockSpec((rows, R), lambda h: (0, 0)),
            pl.BlockSpec((R, HEAD_PAD), lambda h: (0, h)),
        ),
        scratch_shapes=[
            pltpu.VMEM((rows + WIN, PD), bf16),
            pltpu.VMEM((rows + WIN, PD), bf16),
            pltpu.VMEM((rows + 16, PD), f32),
            pltpu.VMEM((rows + 16, PD), f32),
        ],
        compiler_params=params(48),
        cost_estimate=pl.CostEstimate(
            flops=100_000_000, bytes_accessed=300_000, transcendentals=0
        ),
        name="attend_back",
    )(proj, tails, states, later, lent, ups, grads, table, rank, *tables)


def first_back_kernel(*refs):
    grads = refs[0:4]
    rank_grad, left = refs[4:6]
    sources = refs[6 : 6 + 16]
    part, weight, sems = refs[22:]
    groups = []
    size = 2 * HEAD_PAD
    for slot in range(SLOTS):
        pieces = sources[0:1] if slot == 0 else sources[1 + 5 * (slot - 1) : 1 + 5 * slot]
        groups.append(mixer_copies(pieces, slot == 0, weight, size * slot))
    begin = pl.program_id(0) == 0

    @pl.when(begin)
    def _():
        for slot in range(SLOTS):
            run_copies(groups[slot], sems, 40 * slot)
        for slot in range(SLOTS):
            mixer_pads(weight, size * slot)

    total = nn(rank_grad[0].astype(bf16), left[...])
    for slot in range(SLOTS):

        @pl.when(begin)
        def _():
            wait_copies(groups[slot], sems, 40 * slot)

        total = total + nn(grads[slot][0], weight[size * slot : size * (slot + 1), :])
    part[0] = total.astype(bf16)


def first_back(start, count, grads, rank_grad, left, sources):
    cores, _, size = grads[0].shape
    width = left.shape[1]
    whole = lambda a: pl.BlockSpec(a.shape, lambda i: (0,) * a.ndim)
    span = lambda cols: pl.BlockSpec((1, count, cols), lambda i: (i, start // count, 0))
    return pl.pallas_call(
        first_back_kernel,
        grid=(cores,),
        out_shape=jax.ShapeDtypeStruct((cores, count, width), bf16),
        in_specs=[span(size)] * 4 + [span(R), whole(left)] + [ANY] * len(sources),
        out_specs=pl.BlockSpec((1, count, width), lambda i: (i, 0, 0)),
        scratch_shapes=[pltpu.VMEM((SLOTS * size, width), bf16), pltpu.SemaphoreType.DMA((160,))],
        compiler_params=params(56),
        cost_estimate=pl.CostEstimate(
            flops=100_000_000, bytes_accessed=300_000, transcendentals=0
        ),
        name="first_back",
    )(*grads, rank_grad, left, *sources)


def norm_two_kernel(own, other, wide, gain, left, middle, second, rank):
    total = wide[...].astype(f32) + (own[...].astype(f32) + other[...].astype(f32))
    scale = lax.rsqrt(jnp.mean(total * total, -1, keepdims=True) + epsilon)
    rounded = (total * scale * gain[...]).astype(bf16)
    middle[...] = total
    second[...] = rounded
    rank[...] = nn(rounded, left[...]).astype(bf16)


def norm_two(own, other, wide, gain, left):
    rows, width = own.shape
    block = pl.BlockSpec((CHUNK, width), lambda i: (i, 0))
    whole = lambda a: pl.BlockSpec(a.shape, lambda i: (0,) * a.ndim)
    return pl.pallas_call(
        norm_two_kernel,
        grid=(rows // CHUNK,),
        out_shape=(
            jax.ShapeDtypeStruct((rows, width), f32),
            jax.ShapeDtypeStruct((rows, width), bf16),
            jax.ShapeDtypeStruct((rows, R), bf16),
        ),
        in_specs=[block, block, block, whole(gain), whole(left)],
        out_specs=(block, block, pl.BlockSpec((CHUNK, R), lambda i: (i, 0))),
        compiler_params=params(40),
        cost_estimate=pl.CostEstimate(
            flops=100_000_000, bytes_accessed=300_000, transcendentals=0
        ),
        name="norm_two",
    )(own, other, wide, gain, left)


def back_two_kernel(own, other, middle, upstream, gain, right, mixer_up, rgrad):
    vector = middle[...]
    scale = lax.rsqrt(jnp.mean(vector * vector, -1, keepdims=True) + epsilon)
    flow = gain[...] * (own[...].astype(f32) + other[...].astype(f32))
    inner = jnp.mean(vector * flow, -1, keepdims=True)
    total = upstream[...].astype(f32) + scale * flow - vector * (scale * scale * scale * inner)
    rounded = total.astype(bf16)
    mixer_up[...] = rounded
    rgrad[...] = nt(rounded, right[...]).astype(bf16)


def back_two(own, other, middle, upstream, gain, right):
    rows, width = own.shape
    block = pl.BlockSpec((CHUNK, width), lambda i: (i, 0))
    whole = lambda a: pl.BlockSpec(a.shape, lambda i: (0,) * a.ndim)
    return pl.pallas_call(
        back_two_kernel,
        grid=(rows // CHUNK,),
        out_shape=(
            jax.ShapeDtypeStruct((rows, width), bf16),
            jax.ShapeDtypeStruct((rows, R), bf16),
        ),
        in_specs=[block, block, block, block, whole(gain), whole(right)],
        out_specs=(block, pl.BlockSpec((CHUNK, R), lambda i: (i, 0))),
        compiler_params=params(40),
        cost_estimate=pl.CostEstimate(
            flops=100_000_000, bytes_accessed=300_000, transcendentals=0
        ),
        name="back_two",
    )(own, other, middle, upstream, gain, right)


def weighted(hot, parts):
    expert = pl.program_id(0)
    total = hot[expert, 0] * parts[0].astype(f32)
    for slot in range(1, SLOTS):
        total = total + hot[expert, slot] * parts[slot].astype(f32)
    return total


def by_core(flag, mine, other, base):
    lead = flag[0] > 0
    one, two = mine[:, :base], other[:, :base]
    return jnp.where(lead, one, two), jnp.where(lead, two, one)


def early_kernel(half, pad, hot, flag, mine, other, *outs):
    right, gate_left, down_right, out_left, gate_right, down_left = outs
    width = right.shape[2]
    base = 2 * PD + 3 * pad
    own, sibling = weighted(hot, mine), weighted(hot, other)
    for n, ref in enumerate((right, gate_left, down_right)):
        cols = slice(base + width * n, base + width * (n + 1))
        ref[0] = own[:, cols] + sibling[:, cols]
    cores = by_core(flag, own, sibling, base)
    out_left[0] = jnp.concatenate(
        [part[:, PD * h : PD * h + HD] for part in cores for h in range(2)], 1
    )
    for g in range(2):
        at = 2 * PD + pad * g
        gate_right[0, :, g, :] = jnp.concatenate([part[:, at : at + half] for part in cores], 1)
    at = 2 * PD + 2 * pad
    down_left[0] = jnp.concatenate([part[:, at : at + half] for part in cores], 1)


def late_kernel(hot, flag, mine, other, right, left):
    width = left.shape[2]
    base = 2 * HEAD_PAD
    own, sibling = weighted(hot, mine), weighted(hot, other)
    left[0] = own[:, base : base + width] + sibling[:, base : base + width]
    for core, part in enumerate(by_core(flag, own, sibling, base)):
        for head in range(2):
            at = HEAD_PAD * head
            right[0, :, 2 * core + head, :] = jnp.concatenate(
                [part[:, at + place_at : at + place_at + size] for _, size, place_at in HEAD_SEGMENTS], 1
            )


def tables_of(kernel, shapes, name, hot, flag, mine, other):
    whole = lambda a: pl.BlockSpec(a.shape, lambda e: (0,) * a.ndim)
    smem = pl.BlockSpec(memory_space=pltpu.SMEM)
    spot = lambda rank: lambda e: (e,) + (0,) * (rank - 1)
    return pl.pallas_call(
        kernel,
        grid=(NA,),
        out_shape=[jax.ShapeDtypeStruct((NA,) + shape, f32) for shape in shapes],
        in_specs=[smem, smem, whole(mine), whole(other)],
        out_specs=[pl.BlockSpec((1,) + shape, spot(len(shape) + 1)) for shape in shapes],
        compiler_params=params(40),
        cost_estimate=pl.CostEstimate(
            flops=100_000_000, bytes_accessed=300_000, transcendentals=0
        ),
        name=name,
    )(hot, flag, mine, other)


def swap_core(array):
    return lax.ppermute(array, "core", [(0, 1), (1, 0)])


def swap_chip(array, bit):
    count = lax.axis_size("chip")
    return lax.ppermute(array, "chip", [(i, i ^ bit) for i in range(count)])


def swap_tp(array, bit):
    return lax.ppermute(array, "tp", [(i, i ^ bit) for i in range(4)])


def both_cores(own):
    return order_cores(own, swap_core(own))


def order_cores(own, other):
    lead = lax.axis_index("core") == 0
    return jnp.concatenate([jnp.where(lead, own, other), jnp.where(lead, other, own)], 0)


def own_rows(array, core):
    half = array.shape[0] // 2
    return lax.dynamic_slice_in_dim(array, core * half, half, 0)


def hold_kernel(*refs):
    pass


def hold(*arrays, after=()):
    return pl.pallas_call(
        hold_kernel,
        out_shape=tuple(jax.ShapeDtypeStruct(a.shape, a.dtype) for a in arrays),
        in_specs=[ANY] * (len(arrays) + len(after)),
        out_specs=(ANY,) * len(arrays),
        input_output_aliases={i: i for i in range(len(arrays))},
        compiler_params=pltpu.CompilerParams(has_side_effects=True),
        name="hold",
    )(*arrays, *after)


def hop_xy(piece):
    return swap_chip(piece, 1), swap_chip(piece, 2)


def hop_diag(from_x, from_y, cut):
    return swap_chip(from_y[:cut], 1), swap_chip(from_x[cut:], 2)


def cross(array):
    return lax.ppermute(array, "tp", [(1, 2), (2, 1)])


def edge(array):
    return lax.ppermute(array, "tp", [(1, 0), (2, 3)])


def pick_inner(inner_array, edge_array):
    z = lax.axis_index("tp")
    return jnp.where((z == 1) | (z == 2), inner_array, edge_array)


def add_swapped(array, bit):
    other = swap_chip(array, bit)
    return (array.astype(f32) + other.astype(f32)).astype(array.dtype)


def add_rest(array):
    bit = 2
    while bit < lax.axis_size("chip"):
        array = add_swapped(array, bit)
        bit *= 2
    return array


def plane_parts(array):
    if lax.axis_size("chip") == 4:
        return [swap_chip(array, bit) for bit in (1, 2, 3)]
    return [add_rest(add_swapped(array, 1))]


def plane_sum(array, parts):
    if len(parts) == 1:
        return parts[0]
    total = array.astype(f32)
    for part in parts:
        total = total + part.astype(f32)
    return total.astype(array.dtype)


def swap_states(packed):
    if lax.axis_size("chip") == 4:
        return tuple(swap_chip(packed, bit) for bit in (1, 2, 3))
    return (lax.all_gather(packed, "chip"),)


def use_states(parts, backward):
    chip = lax.axis_index("chip")
    count = lax.axis_size("chip")
    if len(parts) > 1:
        total = 0.0
        for bit, part in zip((1, 2, 3), parts):
            other = chip ^ bit
            ahead = (other > chip) if backward else (other < chip)
            total = total + jnp.where(ahead, part[:, :STATE].astype(f32), 0.0)
        near = jnp.where(lax.rem(chip, 2) == (0 if backward else 1), parts[0], parts[2])
    else:
        index = jnp.arange(count, dtype=jnp.int32)
        ahead = (index > chip) if backward else (index < chip)
        states = parts[0][:, :, :STATE].astype(f32)
        total = jnp.sum(jnp.where(ahead[:, None, None, None], states, 0.0), 0)
        at = jnp.minimum(chip + 1, count - 1) if backward else jnp.maximum(chip - 1, 0)
        near = lax.dynamic_index_in_dim(parts[0], at, 0, False)
    inside = (chip < count - 1) if backward else (chip > 0)
    return total, jnp.where(inside, near[:, STATE:], 0.0).astype(bf16)


def copy_kernel(source, dest):
    dest[...] = source[...]


def copy_of(array):
    block = pl.BlockSpec((1,) + array.shape[1:], lambda i: (i, 0, 0))
    return pl.pallas_call(
        copy_kernel,
        grid=(array.shape[0],),
        out_shape=jax.ShapeDtypeStruct(array.shape, array.dtype),
        in_specs=[block],
        out_specs=block,
        compiler_params=params(32),
        cost_estimate=pl.CostEstimate(
            flops=100_000_000, bytes_accessed=300_000, transcendentals=0
        ),
        name="copy_of",
    )(array)


def stack_tp(parts):
    z = lax.axis_index("tp")
    result = jnp.zeros((SLOTS,) + parts[0].shape, parts[0].dtype)
    for slot, part in enumerate(parts):
        result = lax.dynamic_update_index_in_dim(result, part, z ^ slot, 0)
    return result


def pad_heads(table):
    lead = table.shape[:-2]
    heads = table.shape[-2]
    zero = [(0, 0)] * (len(lead) + 1)
    low = jnp.pad(table[..., : 2 * FD], zero + [(0, PD - 2 * FD)])
    high = table[..., 2 * FD :].reshape(lead + (heads, 6, HD))
    high = jnp.pad(high, zero + [(0, 0), (0, PD - HD)]).reshape(lead + (heads, 6 * PD))
    return jnp.concatenate([low, high], -1).reshape(lead + (heads * HEAD_PAD,))


def pad_last(table, size):
    return jnp.pad(table, [(0, 0)] * (table.ndim - 1) + [(0, size - table.shape[-1])])


def norm_rows(vector, gain_vector):
    row_scale = lax.rsqrt(jnp.mean(vector * vector, -1, keepdims=True) + epsilon)
    return (vector * row_scale * gain_vector, row_scale)


def norm_back(vector, row_scale, gain_vector, upstream):
    inner_mean = jnp.mean(vector * gain_vector * upstream, -1, keepdims=True)
    return (
        row_scale * gain_vector * upstream - vector * row_scale * row_scale * row_scale * inner_mean
    )


def body(
    block_input,
    gain_first,
    frozen_mixer_weight,
    conv_filter,
    frozen_output_weight,
    gain_second,
    frozen_gate_up_weight,
    frozen_down_weight,
    mixer_left,
    mixer_right,
    output_left,
    output_right,
    gateup_left,
    gateup_right,
    down_left,
    down_right,
    adapter_index,
    seq_lengths,
    out_cotangent,
):
    chip = lax.axis_index("chip")
    core = lax.axis_index("core")
    z = lax.axis_index("tp")
    y, x = place()
    sequences, length, width = block_input.shape
    rows = 2 * length
    heads_here = frozen_mixer_weight.shape[1]
    ff_here = frozen_down_weight.shape[0]
    half = ff_here // 2
    pad = (half + PD - 1) // PD * PD
    quarter = half // 2

    tables = (jnp.asarray(feature_tables(), bf16),)

    w_mix = jnp.transpose(frozen_mixer_weight, (1, 2, 0)).reshape(heads_here * HCOLS, width)
    w_gate = jnp.transpose(frozen_gate_up_weight, (1, 2, 0)).reshape(2 * ff_here, width)
    w_out = frozen_output_weight
    w_down = frozen_down_weight
    side = width // 2

    def cut(matrix, start, count):
        return lax.dynamic_slice(matrix, (start, x * side), (count, side))

    mixer_piece = jnp.concatenate(
        [
            cut(w_mix, 2 * HCOLS * core + HCOLS * y, HCOLS),
            cut(w_out, 2 * HD * core + HD * y, HD),
        ],
        0,
    )
    feed_piece = jnp.concatenate(
        [
            cut(w_gate, half * core + quarter * y, quarter),
            cut(w_gate, ff_here + half * core + quarter * y, quarter),
            cut(w_down, half * core + quarter * y, quarter),
        ],
        0,
    )
    slot_seq = z ^ jnp.arange(SLOTS, dtype=jnp.int32)
    slot_adapter = jnp.sum(
        jnp.where(slot_seq[:, None] == jnp.arange(SLOTS)[None, :], adapter_index[None, :], 0), 1
    )
    onehot = slot_adapter[:, None] == jnp.arange(NA, dtype=jnp.int32)[None, :]

    def select(table):
        return jnp.einsum(
            "se,e...->s...", onehot.astype(bf16), table, preferred_element_type=f32
        ).astype(bf16)

    mine = slot_adapter[0]
    my_mixer_left = lax.dynamic_index_in_dim(mixer_left, mine, 0, False)
    my_output_right = lax.dynamic_index_in_dim(output_right, mine, 0, False)
    my_gateup_left = lax.dynamic_index_in_dim(gateup_left, mine, 0, False)
    my_down_right = lax.dynamic_index_in_dim(down_right, mine, 0, False)
    right_table = pad_heads(
        select(lax.dynamic_slice_in_dim(mixer_right, 2 * core, 2, 2))
    )
    out_table = lax.dynamic_slice_in_dim(jnp.swapaxes(output_left, 1, 2), 2 * HD * core, 2 * HD, 2)
    out_table = pad_last(select(out_table).reshape(SLOTS, R, 2, HD), PD).reshape(SLOTS, R, 2 * PD)
    gate_table = lax.dynamic_slice_in_dim(gateup_right, half * core, half, 3)
    gate_table = pad_last(select(gate_table), pad).reshape(SLOTS, R, 2 * pad)
    down_table = lax.dynamic_slice_in_dim(jnp.swapaxes(down_left, 1, 2), half * core, half, 2)
    down_table = pad_last(select(down_table), pad)
    taps = lax.dynamic_slice_in_dim(conv_filter, 2 * HD * core, 2 * HD, 1)
    taps = pad_last(taps.reshape(KW, 2, HD), PD).reshape(KW, 2 * PD)
    taps = jnp.broadcast_to(jnp.pad(taps, ((0, R - KW), (0, 0))), (SLOTS, R, 2 * PD))
    packed = jnp.concatenate([right_table, out_table, gate_table, down_table, taps], 2)
    spots = Table(pad)

    gain_one = gain_first.astype(f32)
    gain_two = gain_second.astype(f32)[None, :]
    own_input = lax.dynamic_index_in_dim(block_input, z, 0, False)
    own_cotangent = lax.dynamic_index_in_dim(out_cotangent, z, 0, False)
    my_length = lax.dynamic_index_in_dim(seq_lengths, z, 0, False)
    upstream_own = jnp.where(
        (((chip * 2 + core) * length + jnp.arange(length, dtype=jnp.int32)) < my_length)[:, None],
        own_cotangent,
        0.0,
    ).astype(bf16)

    e_m, c_m = swap_tp(mixer_piece, 1), cross(mixer_piece)
    both_input = both_cores(own_input)
    first = norm_rows(both_input.astype(f32), gain_one)[0].astype(bf16)
    mixer_rank = nn(first, my_mixer_left).astype(bf16)
    upstream_other = swap_core(upstream_own)
    upstream_own, upstream_other, e_m, c_m, mixer_rank, packed, both_input = hold(
        upstream_own, upstream_other, e_m, c_m, mixer_rank, packed, both_input
    )

    projs, packs = [], []
    borrowed, prior, mixed, numer, chunk_states = [None, None], [None, None], [], [], []
    slots = [packed[0], None, None, None]

    def attend_slot(slot):
        pair, n = slot // 2, slot % 2
        out = attend(spots, n, projs[slot], borrowed[pair], prior[pair], slots[slot], tables)
        for kept, value in zip((mixed, numer, chunk_states), out):
            kept.append(value)

    def project_slot(slot, refs):
        out = project(slot == 0, first, mixer_rank, slots[slot], tables, refs)
        for kept, value in zip((projs, packs), out):
            kept.append(value)

    x1, y1 = hop_xy(e_m)
    c2_m, f_m = cross(e_m), edge(c_m)
    table1 = swap_tp(packed[1], 1)
    project_slot(0, (w_mix,))
    slot2 = pick_inner(c2_m, f_m)
    x1, y1, slot2, c2_m, c_m, packs[0], table1, feed_piece, packed = hold(
        x1, y1, slot2, c2_m, c_m, packs[0], table1, feed_piece, packed
    )
    slots[1] = table1
    d1 = hop_diag(x1, y1, M_CUT)
    x2, y2 = hop_xy(slot2)
    f2_m = edge(c2_m)
    table2, table3 = swap_tp(packed[2], 2), swap_tp(packed[3], 3)
    upstream = order_cores(upstream_own, upstream_other)
    down_rgrad = nt(upstream, my_down_right).astype(bf16)
    slot3 = pick_inner(c_m, f2_m)
    x2, y2, slot3, feed_piece, table2, table3, upstream, down_rgrad, *d1 = hold(
        x2, y2, slot3, feed_piece, table2, table3, upstream, down_rgrad, *d1
    )
    slots[2], slots[3] = table2, table3
    d2 = hop_diag(x2, y2, M_CUT)
    x3, y3 = hop_xy(slot3)
    e_f = swap_tp(feed_piece, 1)
    set1 = (e_m, x1, y1, *d1)
    project_slot(1, set1)
    x3, y3, e_f, packs[0], packs[1], *d2 = hold(x3, y3, e_f, packs[0], packs[1], *d2)
    d3 = hop_diag(x3, y3, M_CUT)
    c_f = cross(feed_piece)
    gathered = lax.all_gather(jnp.concatenate(packs[:2], 0), "chip")
    set2 = (slot2, x2, y2, *d2)
    project_slot(2, set2)
    prior[0], borrowed[0] = use_states((gathered,), False)
    d3_a, d3_b, c_f, packs[2], prior[0], borrowed[0] = hold(
        *d3, c_f, packs[2], prior[0], borrowed[0]
    )
    fx1, fy1 = hop_xy(e_f)
    c2_f, f_f = cross(e_f), edge(c_f)
    set3 = (slot3, x3, y3, d3_a, d3_b)
    project_slot(3, set3)
    fslot2 = pick_inner(c2_f, f_f)
    fx1, fy1, fslot2, c2_f, c_f, packs[2], packs[3] = hold(
        fx1, fy1, fslot2, c2_f, c_f, packs[2], packs[3]
    )
    crossing = swap_states(jnp.concatenate(packs[2:], 0))
    attend_slot(0)
    attend_slot(1)
    fd1 = hop_diag(fx1, fy1, feed_cut(quarter))
    mixed[0], mixed[1], fslot2, c2_f, fd1_a, fd1_b, *crossing = hold(
        mixed[0], mixed[1], fslot2, c2_f, *fd1, *crossing
    )
    fd1 = (fd1_a, fd1_b)
    fx2, fy2 = hop_xy(fslot2)
    f2_f = edge(c2_f)
    prior[1], borrowed[1] = use_states(crossing, False)
    attend_slot(2)
    attend_slot(3)
    fslot3 = pick_inner(c_f, f2_f)
    sets = list(set1) + list(set2) + list(set3)
    out_part, out_rank, out_weight = mix_out(spots, mixed, slots, my_output_right, [w_out] + sets)
    fx2, fy2, out_part, fslot3 = hold(fx2, fy2, out_part, fslot3)
    other_part = swap_core(out_part)
    middle, second, gate_rank = norm_two(out_part, other_part, both_input, gain_two, my_gateup_left)

    gateup_left_t = my_gateup_left.T

    def feed_slots(which, sources, carry):
        return feed(
            which,
            which[-1] == SLOTS - 1,
            half,
            spots,
            second,
            upstream,
            gate_rank,
            down_rgrad,
            my_down_right,
            gateup_left_t,
            [slots[k] for k in which],
            sources,
            carry,
        )

    fd2 = hop_diag(fx2, fy2, feed_cut(quarter))
    fx3, fy3 = hop_xy(fslot3)
    carry, gate_grads, down_grads = feed_slots(
        (0, 1), [(w_gate, w_down), (e_f, fx1, fy1, *fd1)], []
    )
    fx3, fy3, carry[2], *fd2 = hold(fx3, fy3, carry[2], *fd2)
    fd3 = hop_diag(fx3, fy3, feed_cut(quarter))
    carry, more_gates, more_downs = feed_slots((2,), [(fslot2, fx2, fy2, *fd2)], carry)
    gate_grads, down_grads = gate_grads + more_gates, down_grads + more_downs
    carry[2], *fd3 = hold(carry[2], *fd3)
    carry, more_gates, more_downs = feed_slots((3,), [(fslot3, fx3, fy3, *fd3)], carry)
    gate_grads, down_grads = gate_grads + more_gates, down_grads + more_downs
    down_part, back_part, ranks = carry
    other_back = swap_core(back_part)
    other_down = swap_core(own_rows(down_part, 1 - core))
    mixer_up, output_rgrad = back_two(
        back_part, other_back, middle, upstream, gain_two, my_output_right
    )

    own_down = own_rows(down_part, core).astype(f32)
    own_output = (own_rows(middle, core) + (own_down + other_down.astype(f32))).astype(bf16)
    own_output, output_rgrad = hold(own_output, output_rgrad)
    block_output = lax.all_gather(own_output, "tp")

    ups, grads, packed0, packed1, left_grads = turn(
        spots, mixer_up, output_rgrad, out_weight, slots, numer, mixed, projs, borrowed, tables
    )
    packed0, packed1, left_grads, ranks, out_rank = hold(
        packed0, packed1, left_grads, ranks, out_rank
    )
    crossing = swap_states(packed0)
    down_rank, gateup_rgrad = ranks[:, :R].astype(bf16), ranks[:, R:].astype(bf16)
    shared = jnp.stack(
        [
            tn(out_rank.astype(bf16), mixer_up),
            tn(gateup_rgrad, second),
            tn(down_rank, upstream),
        ]
    )
    owned = jnp.stack(
        [jnp.concatenate([left_grads[i], gate_grads[i], down_grads[i]], 1) for i in range(SLOTS)]
    )
    packed1, shared, owned, *crossing = hold(packed1, shared, owned, *crossing)
    backs = []

    def back_slots(pair, which, later, returned):
        for n in which:
            slot = 2 * pair + n
            backs.append(
                attend_back(
                    spots,
                    slot,
                    projs[slot],
                    borrowed[pair],
                    chunk_states[slot],
                    later,
                    returned,
                    ups,
                    grads,
                    slots[slot],
                    mixer_rank,
                    tables,
                )
            )

    def join(array, other):
        return (array.astype(f32) + other.astype(f32)).astype(array.dtype)

    def packs_of(owned, shared):
        flat = jnp.concatenate(list(shared), 1).astype(bf16)
        return [jnp.concatenate([owned[k], flat], 1) for k in range(SLOTS)]

    next_crossing = swap_states(packed1)
    back_slots(0, (0, 1), *use_states(crossing, True))
    early_rank = backs[0][1] + backs[1][1]
    shared_x, owned_x = swap_chip(shared, 1), swap_chip(owned, 1)
    early_rank, shared_x, owned_x, *crossing = hold(
        early_rank, shared_x, owned_x, *next_crossing
    )
    shared, owned = add_rest(join(shared, shared_x)), add_rest(join(owned, owned_x))
    later, returned = use_states(crossing, True)
    back_slots(1, (0,), later, returned)
    early_rank = early_rank + backs[2][1]
    early_rank, later, shared, owned = hold(early_rank, later, shared, owned)
    early = packs_of(owned, shared)
    early = [early[0]] + [swap_tp(early[bit], bit) for bit in (1, 2, 3)]
    back_slots(1, (1,), later, returned)
    rank_grad = early_rank + backs[3][1]
    rank_grad, *early = hold(rank_grad, *early)
    early = jnp.stack(early)
    early_other = swap_core(early)

    mixer_all = jnp.concatenate(
        [
            jnp.stack([back[2] for back in backs]),
            tn(rank_grad.astype(bf16), first)[None].astype(bf16),
        ],
        0,
    )
    mixer_x = plane_parts(mixer_all)
    proj_grads = [back[0].reshape(2, length, 2 * HEAD_PAD) for back in backs]
    left_t = my_mixer_left.T
    flat_mix = [w_mix] + sets
    count_a = length // 2
    count_b = length - count_a
    rank_rows = rank_grad.reshape(2, length, R)
    part_a = first_back(0, count_a, proj_grads, rank_rows, left_t, flat_mix)
    part_a, rank_rows, early, early_other, *mixer_x = hold(
        part_a, rank_rows, early, early_other, *mixer_x, after=(block_output,)
    )
    mixer_all = plane_sum(mixer_all, mixer_x)

    def finish(part, start, count):
        here = lax.dynamic_index_in_dim(part, core, 0, False)
        there = lax.dynamic_index_in_dim(part, 1 - core, 0, False)
        total = here.astype(f32) + swap_core(there).astype(f32)
        wide = own_input[start : start + count].astype(f32)
        scale_one = lax.rsqrt(jnp.mean(wide * wide, -1, keepdims=True) + epsilon)
        straight = lax.dynamic_slice_in_dim(
            mixer_up, core * length + start, count, 0
        ).astype(f32)
        return (straight + norm_back(wide, scale_one, gain_one, total)).astype(bf16)

    done_a = finish(part_a, 0, count_a)
    e_a, c_a = swap_tp(done_a, 1), cross(done_a)
    late = packs_of(mixer_all[:SLOTS], mixer_all[SLOTS:])
    late = [late[0]] + [swap_tp(late[bit], bit) for bit in (1, 2, 3)]
    part_b = first_back(count_a, count_b, proj_grads, rank_rows, left_t, flat_mix)
    e_a, c_a, part_b, *late = hold(e_a, c_a, part_b, *late)
    late = jnp.stack(late)
    c2_a, f_a = cross(e_a), edge(c_a)
    done_b = finish(part_b, count_a, count_b)
    done_b, early, early_other, late, block_output = hold(
        done_b, early, early_other, late, block_output
    )
    block_output = copy_of(block_output)
    e_b, c_b = swap_tp(done_b, 1), cross(done_b)
    late_other = swap_core(late)
    hot = jnp.swapaxes(onehot, 0, 1).astype(f32)
    flag = jnp.reshape(core == 0, (1,)).astype(jnp.int32)
    early_tables = tables_of(
        functools.partial(early_kernel, half, pad),
        [(R, width)] * 3 + [(R, heads_here * HD), (R, 2, ff_here), (R, ff_here)],
        "early_tables",
        hot,
        flag,
        early,
        early_other,
    )
    (
        c2_a, f_a, e_b, c_b, late, late_other, done_a, done_b, e_a
    ) = hold(
        c2_a, f_a, e_b, c_b, late, late_other, done_a, done_b, e_a,
        after=(*early_tables, block_output),
    )
    f2_a, c2_b, f_b = edge(c2_a), cross(e_b), edge(c_b)

    input_grad = jnp.zeros(block_input.shape, bf16)

    def put(whole, part, slot, number):
        return lax.dynamic_update_slice(whole, part[None], (z ^ slot, number * count_a, 0))

    input_grad = put(input_grad, done_a, 0, 0)
    input_grad = put(input_grad, done_b, 0, 1)
    input_grad = put(input_grad, e_a, 1, 0)
    input_grad = put(input_grad, e_b, 1, 1)
    input_grad = put(input_grad, pick_inner(c2_a, f_a), 2, 0)
    grad_mixer_right, grad_mixer_left = tables_of(
        late_kernel,
        [(R, heads_here, HCOLS), (R, width)],
        "late_tables",
        hot,
        flag,
        late,
        late_other,
    )
    f2_a, c2_b, f_b, input_grad = hold(
        f2_a, c2_b, f_b, input_grad, after=(grad_mixer_right, grad_mixer_left)
    )
    f2_b = edge(c2_b)
    input_grad = put(input_grad, pick_inner(c_a, f2_a), 3, 0)
    input_grad = put(input_grad, pick_inner(c2_b, f_b), 2, 1)
    input_grad = put(input_grad, pick_inner(c_b, f2_b), 3, 1)
    grad_output_right, grad_gateup_left, grad_down_right = early_tables[:3]
    grad_output_left, grad_gateup_right, grad_down_left = early_tables[3:]
    return (
        block_output,
        input_grad,
        jnp.swapaxes(grad_mixer_left, 1, 2),
        grad_mixer_right,
        jnp.swapaxes(grad_output_left, 1, 2),
        grad_output_right,
        jnp.swapaxes(grad_gateup_left, 1, 2),
        grad_gateup_right,
        jnp.swapaxes(grad_down_left, 1, 2),
        grad_down_right,
    )


def solution(mesh):
    seq, tp = mesh.devices.shape
    fine = Mesh(mesh.devices.reshape(seq // 2, 2, tp), ("chip", "core", "tp"))
    where = ("chip", "core")
    return jax.shard_map(
        body,
        mesh=fine,
        in_specs=(
            P(None, where, None),
            P(),
            P(None, "tp", None),
            P(None, "tp"),
            P("tp", None),
            P(),
            P(None, None, "tp"),
            P("tp", None),
            P(),
            P(None, None, "tp", None),
            P(None, "tp", None),
            P(),
            P(),
            P(None, None, None, "tp"),
            P(None, "tp", None),
            P(),
            P(),
            P(),
            P(None, where, None),
        ),
        out_specs=(
            P(None, where, None),
            P(None, where, None),
            P(),
            P(None, None, "tp", None),
            P(None, "tp", None),
            P(),
            P(),
            P(None, None, None, "tp"),
            P(None, "tp", None),
            P(),
        ),
        check_vma=False,
    )
```

```python
import functools

import jax
import jax.numpy as jnp
import numpy as np
from jax import lax
from jax.experimental import pallas as pl
from jax.experimental.pallas import tpu as pltpu
from jax.sharding import Mesh
from jax.sharding import PartitionSpec as P

HD = 112
PD = 128
FD = 16
R = 16
NA = 8
KW = 3
WIN = 64
HCOLS = 704
SLOTS = 4
HEAD_PAD = 7 * PD
STATE = 160
CHUNK = 256
TURN = 1024
QB = 128
BACK_QB = 256
BACK_CHUNK = 512
PACK = STATE + 2 * WIN + 32

epsilon = 1e-05
masked = -1e30
f32 = jnp.float32
bf16 = jnp.bfloat16
ANY = pl.BlockSpec(memory_space=pl.ANY)


def nn(a, b):
    return lax.dot_general(a, b, (((1,), (0,)), ((), ())), preferred_element_type=f32)


def nt(a, b):
    return lax.dot_general(a, b, (((1,), (1,)), ((), ())), preferred_element_type=f32)


def tn(a, b):
    return lax.dot_general(a, b, (((0,), (0,)), ((), ())), preferred_element_type=f32)


def feature_tables():
    leading, trailing = np.triu_indices(FD)
    pick = np.zeros((PD, 1280), np.float32)
    for base, row in ((0, 0), (512, FD)):
        pick[PD - 1, base] = 1.0
        pick[PD - 1, base + 256 : base + 256 + 1 + FD] = 1.0
        for i in range(FD):
            pick[row + i, base + 1 + i] = 0.5
        for n, (i, j) in enumerate(zip(leading, trailing)):
            pick[row + i, base + 1 + FD + n] = 0.25 if i == j and base == 0 else 0.5
            pick[row + j, base + 256 + 1 + FD + n] = 0.5
    for i in range(FD):
        pick[FD + i, 1024 + i] = 0.25
        pick[i, 1152 + FD + i] = 0.25
    return pick


HEAD_SEGMENTS = [(0, 2 * FD, 0)] + [(2 * FD + HD * i, HD, PD * (i + 1)) for i in range(6)]
M_ROWS = HCOLS + HD
M_CUT = 2 * FD + 3 * HD


def place():
    j = lax.rem(lax.axis_index("chip"), 4)
    return j // 2, lax.rem(j, 2)


def run_copies(copies, sems, start):
    for number, (src, dst) in enumerate(copies):
        copy = pltpu.make_async_copy(src, dst, sems.at[start + number])
        copy.start()


def wait_copies(copies, sems, start):
    for number, (src, dst) in enumerate(copies):
        pltpu.make_async_copy(src, dst, sems.at[start + number]).wait()


def spread_pieces(refs, cut, rows, dest, base, width, offset_of):
    y, x = place()
    z_ref, x_ref, y_ref, da_ref, db_ref = refs
    copies = []
    for kind, yy, xx in (("z", y, x), ("x", y, 1 - x), ("y", 1 - y, x), ("d", 1 - y, 1 - x)):
        cols = pl.ds(pl.multiple_of(xx * width, PD), width)
        for first, count in rows:
            spans = [(first, count)]
            if kind == "d" and first < cut < first + count:
                spans = [(first, cut - first), (cut, first + count - cut)]
            for row, size in spans:
                if kind == "d":
                    src = da_ref if row < cut else db_ref
                    src = src.at[pl.ds(row if row < cut else row - cut, size)]
                else:
                    src = {"z": z_ref, "x": x_ref, "y": y_ref}[kind].at[pl.ds(row, size)]
                start = pl.multiple_of(base + offset_of(row, yy), 16)
                copies.append((src, dest.at[pl.ds(start, size), cols]))
    return copies


def mixer_offset(row, yy):
    for first, count, at in HEAD_SEGMENTS:
        if first <= row < first + count:
            return yy * HEAD_PAD + at + row - first
    return None


MIXER_ROWS = [(first, count) for first, count, _ in HEAD_SEGMENTS]


def mixer_copies(refs, own, dest, base):
    if own:
        core = lax.axis_index("core")
        copies = []
        for head in range(2):
            for first, count, at in HEAD_SEGMENTS:
                src = pl.multiple_of(2 * HCOLS * core + HCOLS * head + first, 16)
                copies.append(
                    (refs[0].at[pl.ds(src, count)], dest.at[pl.ds(base + HEAD_PAD * head + at, count)])
                )
        return copies
    return spread_pieces(refs, M_CUT, MIXER_ROWS, dest, base, dest.shape[1] // 2, mixer_offset)


def mixer_pads(dest, base):
    for head in range(2):
        for first, count, at in HEAD_SEGMENTS:
            start = base + HEAD_PAD * head + at + count
            dest[start : start + PD - count] = jnp.zeros((PD - count, dest.shape[1]), bf16)


def output_copies(refs, own, dest, base):
    if own:
        core = lax.axis_index("core")
        return [
            (
                refs[0].at[pl.ds(pl.multiple_of(2 * HD * core + HD * head, 16), HD)],
                dest.at[pl.ds(base + PD * head, HD)],
            )
            for head in range(2)
        ]
    return spread_pieces(
        refs, M_CUT, [(HCOLS, HD)], dest, base, dest.shape[1] // 2, lambda row, yy: yy * PD + row - HCOLS
    )


def output_pads(dest, base):
    for head in range(2):
        start = base + PD * head + HD
        dest[start : start + PD - HD] = jnp.zeros((PD - HD, dest.shape[1]), bf16)


def feed_cut(quarter):
    return quarter + (quarter // 2 + 15) // 16 * 16


def feed_copies(refs, own, dest, half, pad):
    if own:
        core = lax.axis_index("core")
        wg, wd = refs
        spots = [(wg, 0, 0), (wg, 2 * half, pad), (wd, 0, 2 * pad)]
        return [
            (
                ref.at[pl.ds(pl.multiple_of(half * core + first, 16), half)],
                dest.at[pl.ds(at, half)],
            )
            for ref, first, at in spots
        ]
    quarter = half // 2

    def offset_of(row, yy):
        return row // quarter * pad + yy * quarter + row % quarter

    rows = [(quarter * i, quarter) for i in range(3)]
    return spread_pieces(
        refs, feed_cut(quarter), rows, dest, 0, dest.shape[1] // 2, offset_of
    )


def feed_pads(dest, half, pad):
    for i in range(3):
        dest[pad * i + half : pad * (i + 1)] = jnp.zeros((pad - half, dest.shape[1]), bf16)


def features(picked, at):
    one = picked[:, at : at + 256]
    two = picked[:, at + 256 : at + 512]
    return one, two, (one * two).astype(bf16)


class Table:
    def __init__(self, pad):
        sizes = (2 * HEAD_PAD, 2 * PD, 2 * pad, pad, 2 * PD)
        starts = np.cumsum((0,) + sizes)
        self.right, self.left, self.gate, self.down, self.taps = (
            slice(int(a), int(a) + n) for a, n in zip(starts, sizes)
        )
        self.edges = [int(a) for a in starts]


def params(mib, **more):
    return pltpu.CompilerParams(vmem_limit_bytes=mib * 2**20, **more)


def project_kernel(own, first, rank, table, pick, *rest):
    count = 1 if own else 5
    refs = rest[:count]
    proj, packed, weight, sems = rest[count:]
    copies = mixer_copies(refs, own, weight, 0)
    run_copies(copies, sems, 0)
    mixer_pads(weight, 0)
    wait_copies(copies, sems, 0)
    blocks = first.shape[0] // CHUNK
    for head in range(2):
        cols = pl.ds(HEAD_PAD * head, HEAD_PAD)

        def one(block, carry):
            rows = pl.ds(pl.multiple_of(block * CHUNK, CHUNK), CHUNK)
            result = nt(first[rows, :], weight[cols, :]) + nn(rank[rows, :], table[:, cols])
            rounded = result.astype(bf16)
            lane = lax.broadcasted_iota(jnp.int32, (CHUNK, PD), 1)
            base = jnp.where(lane == PD - 1, 1.0, result[:, :PD]).astype(bf16)
            proj[rows, cols] = rounded
            proj[rows, HEAD_PAD * head : HEAD_PAD * head + PD] = base
            _, _, feat = features(nn(base, pick[:, 512:1024]), 0)
            return carry + tn(feat, rounded[:, PD : 2 * PD])

        total = lax.fori_loop(0, blocks, one, jnp.zeros((256, PD), f32))
        packed[head, 0:STATE] = total[:STATE].astype(bf16)
        last = first.shape[0]
        at = HEAD_PAD * head
        packed[head, STATE : STATE + WIN] = proj[last - WIN :, at + 3 * PD : at + 4 * PD]
        packed[head, STATE + WIN : STATE + 2 * WIN] = proj[last - WIN :, at + 4 * PD : at + 5 * PD]
        packed[head, PACK - 32 : PACK - 16] = proj[last - 16 :, at + 5 * PD : at + 6 * PD]
        packed[head, PACK - 16 : PACK] = jnp.zeros((16, PD), bf16)


def project(own, first, rank, table, tables, refs):
    rows, width = first.shape
    vm = pl.BlockSpec(memory_space=pltpu.VMEM)
    return pl.pallas_call(
        functools.partial(project_kernel, own),
        out_shape=(
            jax.ShapeDtypeStruct((rows, 2 * HEAD_PAD), bf16),
            jax.ShapeDtypeStruct((2, PACK, PD), bf16),
            jax.ShapeDtypeStruct((2 * HEAD_PAD, width), bf16),
        ),
        in_specs=[vm] * 4 + [ANY] * len(refs),
        out_specs=(vm, vm, vm),
        scratch_shapes=[pltpu.SemaphoreType.DMA((40,))],
        compiler_params=params(48),
        cost_estimate=pl.CostEstimate(
            flops=100_000_000, bytes_accessed=300_000, transcendentals=0
        ),
        name="project",
    )(first, rank, table, *tables, *refs)


def window_masks(count):
    query = lax.broadcasted_iota(jnp.int32, (count, count + WIN), 0)
    key = lax.broadcasted_iota(jnp.int32, (count, count + WIN), 1)
    others = (key > query) & (key <= query + WIN)
    lead = jnp.where(lax.axis_index("chip") > 0, 0, WIN)
    return others & (key >= lead), others


def window_prob(query, keys, allowed):
    scores = nt(query, keys) * HD ** (-0.5)
    scores = jnp.where(allowed, scores, masked)
    largest = jnp.max(scores, -1, keepdims=True)
    expo = jnp.exp(scores - largest)
    return expo * (1.0 / jnp.sum(expo, -1, keepdims=True))


def causal_mask(size):
    row = lax.broadcasted_iota(jnp.int32, (size, size), 0)
    col = lax.broadcasted_iota(jnp.int32, (size, size), 1)
    return col <= row


def conv_of(conv, taps, start, count):
    result = taps[0:1] * conv[pl.ds(16 + start, count), :]
    for offset in range(1, KW):
        result = result + taps[offset : offset + 1] * conv[pl.ds(16 + start - offset, count), :]
    return result


def attend_kernel(spots, proj, tails, prior, table, pick, mixed, numer, states, keys, vals, conv):
    rows = proj.shape[0]
    keys[0:WIN, :] = tails[0, 0:WIN]
    vals[0:WIN, :] = tails[0, WIN : 2 * WIN]
    conv[0:16, :] = tails[0, 2 * WIN : 2 * WIN + 16].astype(f32)
    keys[WIN:, :] = proj[:, 3 * PD : 4 * PD]
    vals[WIN:, :] = proj[:, 4 * PD : 5 * PD]
    conv[16:, :] = proj[:, 5 * PD : 6 * PD].astype(f32)
    tap = head_taps(spots, table)
    state = whole_state(prior[0])
    causal = causal_mask(CHUNK)
    first_mask, mask = window_masks(QB)
    for chunk in range(rows // CHUNK):
        states[0, chunk] = state.astype(bf16)
        at = chunk * CHUNK
        span = slice(at, at + CHUNK)
        base = proj[span, 0:PD]
        value = proj[span, PD : 2 * PD]
        picked = nn(base, pick[:, :1152])
        _, _, feat_q = features(picked, 0)
        score = nt(base, picked[:, 1024:1152].astype(bf16))
        weight = jnp.where(causal, 1.0 + score + 0.5 * score * score, 0.0).astype(bf16)
        total = nn(weight, value) + nn(feat_q, state.astype(bf16))
        if at + CHUNK < rows:
            _, _, feat_k = features(picked, 512)
            state = state + tn(feat_k, value)
        parts = []
        for number in range(chunk * CHUNK // QB, (chunk + 1) * CHUNK // QB):
            query = proj[number * QB : (number + 1) * QB, 2 * PD : 3 * PD]
            allowed = mask if number else first_mask
            prob = window_prob(query, keys[number * QB : number * QB + QB + WIN, :], allowed)
            parts.append(nn(prob.astype(bf16), vals[number * QB : number * QB + QB + WIN, :]))
        window = jnp.concatenate(parts, 0)
        scale = lax.rsqrt(jnp.sum(total * total, -1, keepdims=True) * (1.0 / HD) + epsilon)
        gate = proj[span, 6 * PD : 7 * PD].astype(f32)
        branch = conv_of(conv, tap, at, CHUNK) * (gate * jax.nn.sigmoid(gate))
        mixed[span, :] = (total * scale + window + branch).astype(bf16)
        numer[span, :] = total.astype(bf16)


def whole_state(state):
    return jnp.concatenate([state, jnp.zeros((256 - STATE, PD), f32)], 0)


def head_taps(spots, table):
    start = pl.multiple_of(spots.taps.start + PD * pl.program_id(0), PD)
    return table[:, pl.ds(start, PD)].astype(f32)


def attend(spots, number, proj, tails, prior, table, tables):
    rows = proj.shape[0]
    whole = lambda a: pl.BlockSpec(a.shape, lambda h: (0,) * a.ndim)
    return pl.pallas_call(
        functools.partial(attend_kernel, spots),
        grid=(2,),
        out_shape=(
            jax.ShapeDtypeStruct((rows, 2 * PD), bf16),
            jax.ShapeDtypeStruct((rows, 2 * PD), bf16),
            jax.ShapeDtypeStruct((2, rows // CHUNK, 256, PD), bf16),
        ),
        in_specs=[
            pl.BlockSpec((rows, HEAD_PAD), lambda h: (0, h)),
            pl.BlockSpec((1, PACK - STATE, PD), lambda h: (2 * number + h, 0, 0)),
            pl.BlockSpec((1, STATE, PD), lambda h: (2 * number + h, 0, 0)),
            whole(table),
        ]
        + [whole(t) for t in tables],
        out_specs=(
            pl.BlockSpec((rows, PD), lambda h: (0, h)),
            pl.BlockSpec((rows, PD), lambda h: (0, h)),
            pl.BlockSpec((1, rows // CHUNK, 256, PD), lambda h: (h, 0, 0, 0)),
        ),
        scratch_shapes=[
            pltpu.VMEM((rows + WIN, PD), bf16),
            pltpu.VMEM((rows + WIN, PD), bf16),
            pltpu.VMEM((rows + 16, PD), f32),
        ],
        compiler_params=params(48),
        cost_estimate=pl.CostEstimate(
            flops=100_000_000, bytes_accessed=300_000, transcendentals=0
        ),
        name="attend",
    )(proj, tails, prior, table, *tables)


def mix_out_kernel(spots, *refs):
    mixed = refs[0:4]
    lefts = refs[4:8]
    right = refs[8]
    sources = refs[9 : 9 + 1 + 15]
    part, rank, kept, weight, sems = refs[25:]
    groups = []
    for slot in range(SLOTS):
        pieces = sources[0:1] if slot == 0 else sources[1 + 5 * (slot - 1) : 1 + 5 * slot]
        groups.append(output_copies(pieces, slot == 0, weight, 2 * PD * slot))

    @pl.when(pl.program_id(0) == 0)
    def _():
        for slot in range(SLOTS):
            run_copies(groups[slot], sems, 8 * slot)
            output_pads(weight, 2 * PD * slot)
        for slot in range(SLOTS):
            wait_copies(groups[slot], sems, 8 * slot)

    total = jnp.zeros(part.shape, f32)
    rank_sum = jnp.zeros((part.shape[0], R), f32)
    for slot in range(SLOTS):
        total = total + nn(mixed[slot][...], weight[2 * PD * slot : 2 * PD * (slot + 1), :])
        rank_sum = rank_sum + nt(mixed[slot][...], lefts[slot][:, spots.left])
    total = total + nn(rank_sum.astype(bf16), right[...])
    part[...] = total.astype(bf16)
    rank[...] = rank_sum
    rows = kept.shape[0]
    kept[...] = weight[pl.ds(pl.multiple_of(pl.program_id(0) * rows, rows), rows), :]


def mix_out(spots, mixed, lefts, right, sources):
    rows = mixed[0].shape[0]
    width = right.shape[1]
    block = CHUNK
    steps = rows // block
    whole = lambda a: pl.BlockSpec(a.shape, lambda i: (0,) * a.ndim)
    return pl.pallas_call(
        functools.partial(mix_out_kernel, spots),
        grid=(steps,),
        out_shape=(
            jax.ShapeDtypeStruct((rows, width), bf16),
            jax.ShapeDtypeStruct((rows, R), f32),
            jax.ShapeDtypeStruct((SLOTS * 2 * PD, width), bf16),
        ),
        in_specs=[pl.BlockSpec((block, 2 * PD), lambda i: (i, 0))] * 4
        + [whole(a) for a in lefts]
        + [whole(right)]
        + [ANY] * len(sources),
        out_specs=(
            pl.BlockSpec((block, width), lambda i: (i, 0)),
            pl.BlockSpec((block, R), lambda i: (i, 0)),
            pl.BlockSpec((SLOTS * 2 * PD // steps, width), lambda i: (i, 0)),
        ),
        scratch_shapes=[pltpu.VMEM((SLOTS * 2 * PD, width), bf16), pltpu.SemaphoreType.DMA((32,))],
        compiler_params=params(48),
        cost_estimate=pl.CostEstimate(
            flops=100_000_000, bytes_accessed=300_000, transcendentals=0
        ),
        name="mix_out",
    )(*mixed, *lefts, right, *sources)


def feed_kernel(slots, last, half, pad, spots, *refs):
    count = len(slots)
    fresh = slots[0] == 0
    second, grad, grank, rgrad, dright, gleft = refs[:6]
    tables, refs = refs[6 : 6 + count], refs[6 + count :]
    groups = []
    sources = []
    for slot in slots:
        size = 2 if slot == 0 else 5
        sources.append(refs[:size])
        refs = refs[size:]
    if not fresh:
        (down_in, back_in, ranks_in), refs = refs[:3], refs[3:]
    down_out, back_out, ranks_out = refs[:3]
    right_outs, left_outs = refs[3 : 3 + count], refs[3 + count : 3 + 2 * count]
    weights, sems, *sums = refs[3 + 2 * count :]
    right_grads, left_grads = sums[:count], sums[count:]
    for n, slot in enumerate(slots):
        part = weights.at[3 * pad * n : 3 * pad * (n + 1)]
        groups.append(feed_copies(sources[n], slot == 0, part, half, pad))
    begin = pl.program_id(0) == 0

    @pl.when(begin)
    def _():
        for n in range(count):
            run_copies(groups[n], sems, 16 * n)
        for n in range(count):
            feed_pads(weights.at[3 * pad * n : 3 * pad * (n + 1)], half, pad)
            right_grads[n][...] = jnp.zeros(right_grads[n].shape, f32)
            left_grads[n][...] = jnp.zeros(left_grads[n].shape, f32)

    down = jnp.zeros(down_out.shape, f32) if fresh else down_in[...]
    back = jnp.zeros(back_out.shape, f32) if fresh else back_in[...]
    down_rank = jnp.zeros((down.shape[0], R), f32) if fresh else ranks_in[:, :R]
    back_rank = jnp.zeros((down.shape[0], R), f32) if fresh else ranks_in[:, R:]
    for n in range(count):

        @pl.when(begin)
        def _():
            wait_copies(groups[n], sems, 16 * n)

        at = 3 * pad * n
        right, left = tables[n][:, spots.gate], tables[n][:, spots.down]
        gate_up = nt(second[...], weights[at : at + 2 * pad, :]) + nn(grank[...], right)
        gate, up = gate_up[:, :pad], gate_up[:, pad:]
        hidden_grad = nt(grad[...], weights[at + 2 * pad : at + 3 * pad, :]) + nn(rgrad[...], left)
        sig = jax.nn.sigmoid(gate)
        act = gate * sig
        hidden = (act * up).astype(bf16)
        gate_grad = hidden_grad * up * (sig * (1.0 + gate * (1.0 - sig)))
        both = jnp.concatenate([gate_grad.astype(bf16), (hidden_grad * act).astype(bf16)], 1)
        down = down + nn(hidden, weights[at + 2 * pad : at + 3 * pad, :])
        back = back + nn(both, weights[at : at + 2 * pad, :])
        down_rank = down_rank + nt(hidden, left)
        back_rank = back_rank + nt(both, right)
        right_grads[n][...] += tn(grank[...], both)
        left_grads[n][...] += tn(rgrad[...], hidden)
    ranks_out[:, :R] = down_rank
    ranks_out[:, R:] = back_rank
    if last:
        down = down + nn(down_rank.astype(bf16), dright[...])
        back = back + nn(back_rank.astype(bf16), gleft[...])
    down_out[...] = down.astype(down_out.dtype)
    back_out[...] = back.astype(back_out.dtype)

    @pl.when(pl.program_id(0) == pl.num_programs(0) - 1)
    def _():
        for out, total in zip(right_outs + left_outs, right_grads + left_grads):
            out[...] = total[...].astype(bf16)


def feed(slots, last, half, spots, second, grad, grank, rgrad, dright, gleft, tables, sources, carry):
    rows, width = second.shape
    pad = spots.down.stop - spots.down.start
    count = len(slots)
    block = CHUNK
    kind = bf16 if last else f32
    whole = lambda a: pl.BlockSpec(a.shape, lambda i: (0,) * a.ndim)
    wide = pl.BlockSpec((block, width), lambda i: (i, 0))
    thin = pl.BlockSpec((block, R), lambda i: (i, 0))
    pair = pl.BlockSpec((block, 2 * R), lambda i: (i, 0))
    flat = sum([list(s) for s in sources], [])
    out = pl.pallas_call(
        functools.partial(feed_kernel, slots, last, half, pad, spots),
        grid=(rows // block,),
        out_shape=(
            jax.ShapeDtypeStruct((rows, width), kind),
            jax.ShapeDtypeStruct((rows, width), kind),
            jax.ShapeDtypeStruct((rows, 2 * R), f32),
        )
        + (jax.ShapeDtypeStruct((R, 2 * pad), bf16),) * count
        + (jax.ShapeDtypeStruct((R, pad), bf16),) * count,
        in_specs=[wide, wide, thin, thin, whole(dright), whole(gleft)]
        + [whole(t) for t in tables]
        + [ANY] * len(flat)
        + ([wide, wide, pair] if carry else []),
        out_specs=(wide, wide, pair)
        + (pl.BlockSpec((R, 2 * pad), lambda i: (0, 0)),) * count
        + (pl.BlockSpec((R, pad), lambda i: (0, 0)),) * count,
        scratch_shapes=[
            pltpu.VMEM((3 * pad * count, width), bf16),
            pltpu.SemaphoreType.DMA((16 * count,)),
        ]
        + [pltpu.VMEM((R, 2 * pad), f32)] * count
        + [pltpu.VMEM((R, pad), f32)] * count,
        compiler_params=params(58),
        cost_estimate=pl.CostEstimate(
            flops=100_000_000, bytes_accessed=300_000, transcendentals=0
        ),
        name="feed",
    )(second, grad, grank, rgrad, dright, gleft, *tables, *flat, *carry)
    return list(out[:3]), list(out[3 : 3 + count]), list(out[3 + count :])


def turn_kernel(spots, *refs):
    mixer_up, orgrad, weight = refs[:3]
    tables, numers, mixeds, bases, heads, tails = (
        refs[3:7], refs[7:11], refs[11:15], refs[15:23], refs[23:27], refs[27:29]
    )
    pick = refs[29]
    up_out, grad_out, packs, left_out, total_state, left_sums = (
        refs[30], refs[31], refs[32:34], refs[34], refs[35], refs[36]
    )
    step = pl.program_id(0)

    @pl.when(step == 0)
    def _():
        total_state[...] = jnp.zeros(total_state.shape, f32)
        left_sums[...] = jnp.zeros(left_sums.shape, f32)

    both = nt(mixer_up[...], weight[...])
    for n in range(SLOTS):
        table = tables[n]
        flow = both[:, 2 * PD * n : 2 * PD * (n + 1)] + nn(orgrad[...], table[:, spots.left])
        left_sums[n] += tn(orgrad[...], mixeds[n][...])
        for head in range(2):
            cols = slice(PD * head, PD * (head + 1))
            wide = slice(PD * (2 * n + head), PD * (2 * n + head + 1))
            up = flow[:, cols]
            total = numers[n][:, cols].astype(f32)
            scale = lax.rsqrt(jnp.sum(total * total, -1, keepdims=True) * (1.0 / HD) + epsilon)
            inner = jnp.sum(total * up, -1, keepdims=True) * (1.0 / HD)
            grad = (scale * up - total * (scale * scale * scale * inner)).astype(bf16)
            up_out[:, wide] = up.astype(bf16)
            grad_out[:, wide] = grad
            _, _, feat = features(nn(bases[2 * n + head][...], pick[:, 0:512]), 0)
            total_state[2 * n + head] += tn(feat, grad)

    @pl.when(step == pl.num_programs(0) - 1)
    def _():
        for pair in range(2):
            packs[pair][:, 0:STATE, :] = total_state[4 * pair : 4 * pair + 4, :STATE, :].astype(bf16)
        left_out[...] = left_sums[...].astype(bf16)

    @pl.when(step == 0)
    def _():
        for n in range(SLOTS):
            for head in range(2):
                at = n % 2 * 2 + head
                rows = tails[n // 2].at[at]
                give_back(spots, tables[n], heads[n], rows, up_out, packs[n // 2].at[at], n, head)


def give_back(spots, table, rows, tails, up_out, lent, n, head):
    at = HEAD_PAD * head
    wide = slice(PD * (2 * n + head), PD * (2 * n + head + 1))
    query = rows[:, at + 2 * PD : at + 3 * PD]
    keys = jnp.concatenate([tails[0:WIN, :], rows[:, at + 3 * PD : at + 4 * PD]], 0)
    vals = jnp.concatenate([tails[WIN : 2 * WIN, :], rows[:, at + 4 * PD : at + 5 * PD]], 0)
    prob = window_prob(query, keys, window_masks(QB)[0])
    up = up_out[0:QB, wide]
    prob_grad = nt(up, vals)
    inner = jnp.sum(prob * prob_grad, -1, keepdims=True)
    score = (prob * (prob_grad - inner)).astype(bf16)
    lent[STATE : STATE + WIN, :] = (tn(score, query)[:WIN] * HD ** (-0.5)).astype(bf16)
    lent[STATE + WIN : STATE + 2 * WIN, :] = tn(prob.astype(bf16), up)[:WIN].astype(bf16)
    start = spots.taps.start + PD * head
    tap = table[:, start : start + PD].astype(f32)
    gate = rows[0:16, at + 6 * PD : at + 7 * PD].astype(f32)
    flow = up_out[0:16, wide].astype(f32) * (gate * jax.nn.sigmoid(gate))
    row0 = tap[2:3] * flow[0:1]
    row1 = tap[1:2] * flow[0:1] + tap[2:3] * flow[1:2]
    index = lax.broadcasted_iota(jnp.int32, (16, PD), 0)
    edge_rows = jnp.where(index == 14, row0, jnp.where(index == 15, row1, 0.0))
    lent[PACK - 32 : PACK - 16, :] = edge_rows.astype(bf16)
    lent[PACK - 16 : PACK, :] = jnp.zeros((16, PD), bf16)


def turn(spots, mixer_up, orgrad, weight, slot_tables, numer, mixed, projs, tails, tables):
    rows, width = mixer_up.shape
    whole = lambda a: pl.BlockSpec(a.shape, lambda i: (0,) * a.ndim)
    flat = lambda *shape: pl.BlockSpec(shape, lambda i: (0,) * len(shape))
    tall = lambda cols, at: pl.BlockSpec((TURN, cols), lambda i: (i, at))
    heads = 2 * SLOTS
    return pl.pallas_call(
        functools.partial(turn_kernel, spots),
        grid=(rows // TURN,),
        out_shape=(
            jax.ShapeDtypeStruct((rows, heads * PD), bf16),
            jax.ShapeDtypeStruct((rows, heads * PD), bf16),
            jax.ShapeDtypeStruct((4, PACK, PD), bf16),
            jax.ShapeDtypeStruct((4, PACK, PD), bf16),
            jax.ShapeDtypeStruct((SLOTS, R, 2 * PD), bf16),
        ),
        in_specs=[tall(width, 0), tall(R, 0), whole(weight)]
        + [whole(t) for t in slot_tables]
        + [tall(2 * PD, 0)] * 8
        + [tall(PD, 0), tall(PD, 7)] * SLOTS
        + [flat(QB, 2 * HEAD_PAD)] * SLOTS
        + [whole(t) for t in tails]
        + [whole(t) for t in tables],
        out_specs=(
            tall(heads * PD, 0),
            tall(heads * PD, 0),
            flat(4, PACK, PD),
            flat(4, PACK, PD),
            flat(SLOTS, R, 2 * PD),
        ),
        scratch_shapes=[pltpu.VMEM((heads, 256, PD), f32), pltpu.VMEM((SLOTS, R, 2 * PD), f32)],
        compiler_params=params(58),
        cost_estimate=pl.CostEstimate(
            flops=100_000_000, bytes_accessed=300_000, transcendentals=0
        ),
        name="turn",
    )(
        mixer_up, orgrad, weight, *slot_tables, *numer, *mixed,
        *[proj for proj in projs for _ in range(2)], *projs, *tails, *tables,
    )


def window_back(proj, keys, vals, ups, out, number, allowed, held):
    start = number * BACK_QB
    span = slice(start, start + BACK_QB)
    band = slice(start, start + BACK_QB + WIN)
    query = proj[span, 2 * PD : 3 * PD]
    key = keys[band, :]
    prob = window_prob(query, key, allowed)
    up = ups[span, :]
    prob_grad = nt(up, vals[band, :])
    inner = jnp.sum(prob * prob_grad, -1, keepdims=True)
    score = (prob * (prob_grad - inner)).astype(bf16)
    out[span, 2 * PD : 3 * PD] = (nn(score, key) * HD ** (-0.5)).astype(bf16)
    dkey = tn(score, query) * HD ** (-0.5)
    dval = tn(prob.astype(bf16), up)
    for piece, new, more in ((3, dkey, held[0]), (4, dval, held[1])):
        cols = slice(piece * PD, (piece + 1) * PD)
        out[start : start + BACK_QB - WIN, cols] = new[WIN:BACK_QB].astype(bf16)
        out[start + BACK_QB - WIN : start + BACK_QB, cols] = (new[BACK_QB:] + more).astype(bf16)
    return dkey[:WIN], dval[:WIN]


def attend_back_kernel(
    spots, proj, tails, states, later, lent, ups, grads, table, rank, pick,
    out, rank_grad, right_grad, keys, vals, conv, flow
):
    rows = proj.shape[0]
    chunks = rows // BACK_CHUNK
    keys[0:WIN, :] = tails[0, 0:WIN]
    vals[0:WIN, :] = tails[0, WIN : 2 * WIN]
    conv[0:16, :] = tails[0, 2 * WIN : 2 * WIN + 16].astype(f32)
    keys[WIN:, :] = proj[:, 3 * PD : 4 * PD]
    vals[WIN:, :] = proj[:, 4 * PD : 5 * PD]
    conv[16:, :] = proj[:, 5 * PD : 6 * PD].astype(f32)
    tap = head_taps(spots, table)
    right = table.at[:, pl.ds(pl.multiple_of(HEAD_PAD * pl.program_id(0), PD), HEAD_PAD)]
    flow[rows:, :] = jnp.zeros((16, PD), f32)
    follow = whole_state(later[0])
    causal = causal_mask(BACK_CHUNK)
    first_mask, mask = window_masks(BACK_QB)
    held = (lent[0, 0:WIN].astype(f32), lent[0, WIN : 2 * WIN].astype(f32))
    for chunk in range(chunks - 1, -1, -1):
        at = chunk * BACK_CHUNK
        span = slice(at, at + BACK_CHUNK)
        base = proj[span, 0:PD]
        value = proj[span, PD : 2 * PD]
        grad = grads[span, :]
        picked = nn(base, pick[...])
        q_one, q_two, feat_q = features(picked, 0)
        k_one, k_two, feat_k = features(picked, 512)
        key_low = picked[:, 1024:1152].astype(bf16)
        query_high = picked[:, 1152:1280].astype(bf16)
        score = nt(base, key_low)
        weight = jnp.where(causal, 1.0 + score + 0.5 * score * score, 0.0).astype(bf16)
        slope = jnp.where(causal, nt(grad, value) * (1.0 + score), 0.0).astype(bf16)
        follow_round = follow.astype(bf16)
        q_up = nt(grad, states[0, chunk * (BACK_CHUNK // CHUNK)])
        k_up = nt(value, follow_round)
        inside = [q_up * q_two, q_up * q_one, k_up * k_two, k_up * k_one]
        inside = jnp.concatenate([part.astype(bf16) for part in inside], 1)
        low = nn(slope, key_low) + tn(slope, query_high) + nt(inside, pick[:, :1024])
        out[span, 0:PD] = low.astype(bf16)
        out[span, PD : 2 * PD] = (tn(weight, grad) + nn(feat_k, follow_round)).astype(bf16)
        if chunk:
            follow = follow + tn(feat_q, grad)
        gate = proj[span, 6 * PD : 7 * PD].astype(f32)
        up = ups[span, :].astype(f32)
        sig = jax.nn.sigmoid(gate)
        act = gate * sig
        flow[span, :] = up * act
        for number in range((at + BACK_CHUNK) // BACK_QB - 1, at // BACK_QB - 1, -1):
            held = window_back(
                proj, keys, vals, ups, out, number, mask if number else first_mask, held
            )
        slope_gate = sig + act * (1.0 - sig)
        out[span, 6 * PD : 7 * PD] = (up * conv_of(conv, tap, at, BACK_CHUNK) * slope_gate).astype(bf16)
    grad_in = tap[0:1] * flow[0:rows, :]
    for offset in range(1, KW):
        grad_in = grad_in + tap[offset : offset + 1] * flow[offset : offset + rows, :]
    out[:, 5 * PD : 6 * PD] = grad_in.astype(bf16)
    last = slice(rows - 16, rows)
    edge = grad_in[rows - 16 :, :] + lent[0, 2 * WIN : 2 * WIN + 16].astype(f32)
    out[last, 5 * PD : 6 * PD] = edge.astype(bf16)
    right_grad[...] = tn(rank[...], out[...]).astype(bf16)

    @pl.when(pl.program_id(0) == 0)
    def _():
        rank_grad[...] = nt(out[...], right[...])

    @pl.when(pl.program_id(0) > 0)
    def _():
        rank_grad[...] += nt(out[...], right[...])


def attend_back(spots, slot, proj, tails, states, later, lent, ups, grads, table, rank, tables):
    rows = proj.shape[0]
    number = slot % 2
    whole = lambda a: pl.BlockSpec(a.shape, lambda h: (0,) * a.ndim)
    head = pl.BlockSpec((rows, HEAD_PAD), lambda h: (0, h))
    edge = pl.BlockSpec((1, PACK - STATE, PD), lambda h: (2 * number + h, 0, 0))
    state = pl.BlockSpec((1, STATE, PD), lambda h: (2 * number + h, 0, 0))
    column = pl.BlockSpec((rows, PD), lambda h: (0, 2 * slot + h))
    return pl.pallas_call(
        functools.partial(attend_back_kernel, spots),
        grid=(2,),
        out_shape=(
            jax.ShapeDtypeStruct((rows, 2 * HEAD_PAD), bf16),
            jax.ShapeDtypeStruct((rows, R), f32),
            jax.ShapeDtypeStruct((R, 2 * HEAD_PAD), bf16),
        ),
        in_specs=[
            head,
            edge,
            pl.BlockSpec((1, rows // CHUNK, 256, PD), lambda h: (h, 0, 0, 0)),
            state,
            edge,
            column,
            column,
            whole(table),
            whole(rank),
        ]
        + [whole(t) for t in tables],
        out_specs=(
            head,
            pl.BlockSpec((rows, R), lambda h: (0, 0)),
            pl.BlockSpec((R, HEAD_PAD), lambda h: (0, h)),
        ),
        scratch_shapes=[
            pltpu.VMEM((rows + WIN, PD), bf16),
            pltpu.VMEM((rows + WIN, PD), bf16),
            pltpu.VMEM((rows + 16, PD), f32),
            pltpu.VMEM((rows + 16, PD), f32),
        ],
        compiler_params=params(48),
        cost_estimate=pl.CostEstimate(
            flops=100_000_000, bytes_accessed=300_000, transcendentals=0
        ),
        name="attend_back",
    )(proj, tails, states, later, lent, ups, grads, table, rank, *tables)


def first_back_kernel(*refs):
    grads = refs[0:4]
    rank_grad, left = refs[4:6]
    sources = refs[6:10]
    part, weight, sems = refs[10:]
    size = 2 * HEAD_PAD
    copies = [(sources[n], weight.at[size * n : size * (n + 1)]) for n in range(SLOTS)]
    begin = pl.program_id(0) == 0

    @pl.when(begin)
    def _():
        run_copies(copies, sems, 0)

    total = nn(rank_grad[0].astype(bf16), left[...])
    for slot in range(SLOTS):

        @pl.when(begin)
        def _():
            wait_copies(copies[slot : slot + 1], sems, slot)

        total = total + nn(grads[slot][0], weight[size * slot : size * (slot + 1), :])
    part[0] = total.astype(bf16)


def first_back(start, count, grads, rank_grad, left, sources):
    cores, _, size = grads[0].shape
    width = left.shape[1]
    whole = lambda a: pl.BlockSpec(a.shape, lambda i: (0,) * a.ndim)
    span = lambda cols: pl.BlockSpec((1, count, cols), lambda i: (i, start // count, 0))
    return pl.pallas_call(
        first_back_kernel,
        grid=(cores,),
        out_shape=jax.ShapeDtypeStruct((cores, count, width), bf16),
        in_specs=[span(size)] * 4 + [span(R), whole(left)] + [ANY] * len(sources),
        out_specs=pl.BlockSpec((1, count, width), lambda i: (i, 0, 0)),
        scratch_shapes=[pltpu.VMEM((SLOTS * size, width), bf16), pltpu.SemaphoreType.DMA((SLOTS,))],
        compiler_params=params(56),
        cost_estimate=pl.CostEstimate(
            flops=100_000_000, bytes_accessed=300_000, transcendentals=0
        ),
        name="first_back",
    )(*grads, rank_grad, left, *sources)


def norm_two_kernel(own, other, wide, gain, left, middle, second, rank):
    total = wide[...].astype(f32) + (own[...].astype(f32) + other[...].astype(f32))
    scale = lax.rsqrt(jnp.mean(total * total, -1, keepdims=True) + epsilon)
    rounded = (total * scale * gain[...]).astype(bf16)
    middle[...] = total
    second[...] = rounded
    rank[...] = nn(rounded, left[...]).astype(bf16)


def norm_two(own, other, wide, gain, left):
    rows, width = own.shape
    block = pl.BlockSpec((CHUNK, width), lambda i: (i, 0))
    whole = lambda a: pl.BlockSpec(a.shape, lambda i: (0,) * a.ndim)
    return pl.pallas_call(
        norm_two_kernel,
        grid=(rows // CHUNK,),
        out_shape=(
            jax.ShapeDtypeStruct((rows, width), f32),
            jax.ShapeDtypeStruct((rows, width), bf16),
            jax.ShapeDtypeStruct((rows, R), bf16),
        ),
        in_specs=[block, block, block, whole(gain), whole(left)],
        out_specs=(block, block, pl.BlockSpec((CHUNK, R), lambda i: (i, 0))),
        compiler_params=params(40),
        cost_estimate=pl.CostEstimate(
            flops=100_000_000, bytes_accessed=300_000, transcendentals=0
        ),
        name="norm_two",
    )(own, other, wide, gain, left)


def back_two_kernel(own, other, middle, upstream, gain, right, mixer_up, rgrad):
    vector = middle[...]
    scale = lax.rsqrt(jnp.mean(vector * vector, -1, keepdims=True) + epsilon)
    flow = gain[...] * (own[...].astype(f32) + other[...].astype(f32))
    inner = jnp.mean(vector * flow, -1, keepdims=True)
    total = upstream[...].astype(f32) + scale * flow - vector * (scale * scale * scale * inner)
    rounded = total.astype(bf16)
    mixer_up[...] = rounded
    rgrad[...] = nt(rounded, right[...]).astype(bf16)


def back_two(own, other, middle, upstream, gain, right):
    rows, width = own.shape
    block = pl.BlockSpec((CHUNK, width), lambda i: (i, 0))
    whole = lambda a: pl.BlockSpec(a.shape, lambda i: (0,) * a.ndim)
    return pl.pallas_call(
        back_two_kernel,
        grid=(rows // CHUNK,),
        out_shape=(
            jax.ShapeDtypeStruct((rows, width), bf16),
            jax.ShapeDtypeStruct((rows, R), bf16),
        ),
        in_specs=[block, block, block, block, whole(gain), whole(right)],
        out_specs=(block, pl.BlockSpec((CHUNK, R), lambda i: (i, 0))),
        compiler_params=params(40),
        cost_estimate=pl.CostEstimate(
            flops=100_000_000, bytes_accessed=300_000, transcendentals=0
        ),
        name="back_two",
    )(own, other, middle, upstream, gain, right)


def weighted(hot, parts):
    expert = pl.program_id(0)
    total = hot[expert, 0] * parts[0].astype(f32)
    for slot in range(1, SLOTS):
        total = total + hot[expert, slot] * parts[slot].astype(f32)
    return total


def by_core(flag, mine, other, base):
    lead = flag[0] > 0
    one, two = mine[:, :base], other[:, :base]
    return jnp.where(lead, one, two), jnp.where(lead, two, one)


def early_kernel(half, pad, hot, flag, mine, other, *outs):
    right, gate_left, down_right, out_left, gate_right, down_left = outs
    width = right.shape[2]
    base = 2 * PD + 3 * pad
    own, sibling = weighted(hot, mine), weighted(hot, other)
    for n, ref in enumerate((right, gate_left, down_right)):
        cols = slice(base + width * n, base + width * (n + 1))
        ref[0] = own[:, cols] + sibling[:, cols]
    cores = by_core(flag, own, sibling, base)
    out_left[0] = jnp.concatenate(
        [part[:, PD * h : PD * h + HD] for part in cores for h in range(2)], 1
    )
    for g in range(2):
        at = 2 * PD + pad * g
        gate_right[0, :, g, :] = jnp.concatenate([part[:, at : at + half] for part in cores], 1)
    at = 2 * PD + 2 * pad
    down_left[0] = jnp.concatenate([part[:, at : at + half] for part in cores], 1)


def late_kernel(hot, flag, mine, other, right, left):
    width = left.shape[2]
    base = 2 * HEAD_PAD
    own, sibling = weighted(hot, mine), weighted(hot, other)
    left[0] = own[:, base : base + width] + sibling[:, base : base + width]
    for core, part in enumerate(by_core(flag, own, sibling, base)):
        for head in range(2):
            at = HEAD_PAD * head
            right[0, :, 2 * core + head, :] = jnp.concatenate(
                [part[:, at + place_at : at + place_at + size] for _, size, place_at in HEAD_SEGMENTS], 1
            )


def tables_of(kernel, shapes, name, hot, flag, mine, other):
    whole = lambda a: pl.BlockSpec(a.shape, lambda e: (0,) * a.ndim)
    smem = pl.BlockSpec(memory_space=pltpu.SMEM)
    spot = lambda rank: lambda e: (e,) + (0,) * (rank - 1)
    return pl.pallas_call(
        kernel,
        grid=(NA,),
        out_shape=[jax.ShapeDtypeStruct((NA,) + shape, f32) for shape in shapes],
        in_specs=[smem, smem, whole(mine), whole(other)],
        out_specs=[pl.BlockSpec((1,) + shape, spot(len(shape) + 1)) for shape in shapes],
        compiler_params=params(40),
        cost_estimate=pl.CostEstimate(
            flops=100_000_000, bytes_accessed=300_000, transcendentals=0
        ),
        name=name,
    )(hot, flag, mine, other)


def swap_core(array):
    return lax.ppermute(array, "core", [(0, 1), (1, 0)])


def swap_chip(array, bit):
    count = lax.axis_size("chip")
    return lax.ppermute(array, "chip", [(i, i ^ bit) for i in range(count)])


def swap_tp(array, bit):
    return lax.ppermute(array, "tp", [(i, i ^ bit) for i in range(4)])


def both_cores(own):
    return order_cores(own, swap_core(own))


def order_cores(own, other):
    lead = lax.axis_index("core") == 0
    return jnp.concatenate([jnp.where(lead, own, other), jnp.where(lead, other, own)], 0)


def own_rows(array, core):
    half = array.shape[0] // 2
    return lax.dynamic_slice_in_dim(array, core * half, half, 0)


def hold_kernel(*refs):
    pass


def hold(*arrays, after=()):
    return pl.pallas_call(
        hold_kernel,
        out_shape=tuple(jax.ShapeDtypeStruct(a.shape, a.dtype) for a in arrays),
        in_specs=[ANY] * (len(arrays) + len(after)),
        out_specs=(ANY,) * len(arrays),
        input_output_aliases={i: i for i in range(len(arrays))},
        compiler_params=pltpu.CompilerParams(has_side_effects=True),
        name="hold",
    )(*arrays, *after)


def hop_xy(piece):
    return swap_chip(piece, 1), swap_chip(piece, 2)


def hop_diag(from_x, from_y, cut):
    return swap_chip(from_y[:cut], 1), swap_chip(from_x[cut:], 2)


def cross(array):
    return lax.ppermute(array, "tp", [(1, 2), (2, 1)])


def edge(array):
    return lax.ppermute(array, "tp", [(1, 0), (2, 3)])


def pick_inner(inner_array, edge_array):
    z = lax.axis_index("tp")
    return jnp.where((z == 1) | (z == 2), inner_array, edge_array)


def add_swapped(array, bit):
    other = swap_chip(array, bit)
    return (array.astype(f32) + other.astype(f32)).astype(array.dtype)


def add_rest(array):
    bit = 2
    while bit < lax.axis_size("chip"):
        array = add_swapped(array, bit)
        bit *= 2
    return array


def plane_parts(array):
    if lax.axis_size("chip") == 4:
        return [swap_chip(array, bit) for bit in (1, 2, 3)]
    return [add_rest(add_swapped(array, 1))]


def plane_sum(array, parts):
    if len(parts) == 1:
        return parts[0]
    total = array.astype(f32)
    for part in parts:
        total = total + part.astype(f32)
    return total.astype(array.dtype)


def swap_states(packed):
    if lax.axis_size("chip") == 4:
        return tuple(swap_chip(packed, bit) for bit in (1, 2, 3))
    return (lax.all_gather(packed, "chip"),)


def use_states(parts, backward):
    chip = lax.axis_index("chip")
    count = lax.axis_size("chip")
    if len(parts) > 1:
        total = 0.0
        for bit, part in zip((1, 2, 3), parts):
            other = chip ^ bit
            ahead = (other > chip) if backward else (other < chip)
            total = total + jnp.where(ahead, part[:, :STATE].astype(f32), 0.0)
        near = jnp.where(lax.rem(chip, 2) == (0 if backward else 1), parts[0], parts[2])
    else:
        index = jnp.arange(count, dtype=jnp.int32)
        ahead = (index > chip) if backward else (index < chip)
        states = parts[0][:, :, :STATE].astype(f32)
        total = jnp.sum(jnp.where(ahead[:, None, None, None], states, 0.0), 0)
        at = jnp.minimum(chip + 1, count - 1) if backward else jnp.maximum(chip - 1, 0)
        near = lax.dynamic_index_in_dim(parts[0], at, 0, False)
    inside = (chip < count - 1) if backward else (chip > 0)
    return total, jnp.where(inside, near[:, STATE:], 0.0).astype(bf16)


def copy_kernel(source, dest):
    dest[...] = source[...]


def copy_of(array):
    block = pl.BlockSpec((1,) + array.shape[1:], lambda i: (i, 0, 0))
    return pl.pallas_call(
        copy_kernel,
        grid=(array.shape[0],),
        out_shape=jax.ShapeDtypeStruct(array.shape, array.dtype),
        in_specs=[block],
        out_specs=block,
        compiler_params=params(32),
        cost_estimate=pl.CostEstimate(
            flops=100_000_000, bytes_accessed=300_000, transcendentals=0
        ),
        name="copy_of",
    )(array)


def stack_tp(parts):
    z = lax.axis_index("tp")
    result = jnp.zeros((SLOTS,) + parts[0].shape, parts[0].dtype)
    for slot, part in enumerate(parts):
        result = lax.dynamic_update_index_in_dim(result, part, z ^ slot, 0)
    return result


def pad_heads(table):
    lead = table.shape[:-2]
    heads = table.shape[-2]
    zero = [(0, 0)] * (len(lead) + 1)
    low = jnp.pad(table[..., : 2 * FD], zero + [(0, PD - 2 * FD)])
    high = table[..., 2 * FD :].reshape(lead + (heads, 6, HD))
    high = jnp.pad(high, zero + [(0, 0), (0, PD - HD)]).reshape(lead + (heads, 6 * PD))
    return jnp.concatenate([low, high], -1).reshape(lead + (heads * HEAD_PAD,))


def pad_last(table, size):
    return jnp.pad(table, [(0, 0)] * (table.ndim - 1) + [(0, size - table.shape[-1])])


def norm_rows(vector, gain_vector):
    row_scale = lax.rsqrt(jnp.mean(vector * vector, -1, keepdims=True) + epsilon)
    return (vector * row_scale * gain_vector, row_scale)


def norm_back(vector, row_scale, gain_vector, upstream):
    inner_mean = jnp.mean(vector * gain_vector * upstream, -1, keepdims=True)
    return (
        row_scale * gain_vector * upstream - vector * row_scale * row_scale * row_scale * inner_mean
    )


def body(
    block_input,
    gain_first,
    frozen_mixer_weight,
    conv_filter,
    frozen_output_weight,
    gain_second,
    frozen_gate_up_weight,
    frozen_down_weight,
    mixer_left,
    mixer_right,
    output_left,
    output_right,
    gateup_left,
    gateup_right,
    down_left,
    down_right,
    adapter_index,
    seq_lengths,
    out_cotangent,
):
    chip = lax.axis_index("chip")
    core = lax.axis_index("core")
    z = lax.axis_index("tp")
    y, x = place()
    sequences, length, width = block_input.shape
    rows = 2 * length
    heads_here = frozen_mixer_weight.shape[1]
    ff_here = frozen_down_weight.shape[0]
    half = ff_here // 2
    pad = (half + PD - 1) // PD * PD
    quarter = half // 2

    tables = (jnp.asarray(feature_tables(), bf16),)

    w_mix = jnp.transpose(frozen_mixer_weight, (1, 2, 0)).reshape(heads_here * HCOLS, width)
    w_gate = jnp.transpose(frozen_gate_up_weight, (1, 2, 0)).reshape(2 * ff_here, width)
    w_out = frozen_output_weight
    w_down = frozen_down_weight
    side = width // 2

    def cut(matrix, start, count):
        return lax.dynamic_slice(matrix, (start, x * side), (count, side))

    mixer_piece = jnp.concatenate(
        [
            cut(w_mix, 2 * HCOLS * core + HCOLS * y, HCOLS),
            cut(w_out, 2 * HD * core + HD * y, HD),
        ],
        0,
    )
    feed_piece = jnp.concatenate(
        [
            cut(w_gate, half * core + quarter * y, quarter),
            cut(w_gate, ff_here + half * core + quarter * y, quarter),
            cut(w_down, half * core + quarter * y, quarter),
        ],
        0,
    )
    slot_seq = z ^ jnp.arange(SLOTS, dtype=jnp.int32)
    slot_adapter = jnp.sum(
        jnp.where(slot_seq[:, None] == jnp.arange(SLOTS)[None, :], adapter_index[None, :], 0), 1
    )
    onehot = slot_adapter[:, None] == jnp.arange(NA, dtype=jnp.int32)[None, :]

    def select(table):
        return jnp.einsum(
            "se,e...->s...", onehot.astype(bf16), table, preferred_element_type=f32
        ).astype(bf16)

    mine = slot_adapter[0]
    my_mixer_left = lax.dynamic_index_in_dim(mixer_left, mine, 0, False)
    my_output_right = lax.dynamic_index_in_dim(output_right, mine, 0, False)
    my_gateup_left = lax.dynamic_index_in_dim(gateup_left, mine, 0, False)
    my_down_right = lax.dynamic_index_in_dim(down_right, mine, 0, False)
    right_table = pad_heads(
        select(lax.dynamic_slice_in_dim(mixer_right, 2 * core, 2, 2))
    )
    out_table = lax.dynamic_slice_in_dim(jnp.swapaxes(output_left, 1, 2), 2 * HD * core, 2 * HD, 2)
    out_table = pad_last(select(out_table).reshape(SLOTS, R, 2, HD), PD).reshape(SLOTS, R, 2 * PD)
    gate_table = lax.dynamic_slice_in_dim(gateup_right, half * core, half, 3)
    gate_table = pad_last(select(gate_table), pad).reshape(SLOTS, R, 2 * pad)
    down_table = lax.dynamic_slice_in_dim(jnp.swapaxes(down_left, 1, 2), half * core, half, 2)
    down_table = pad_last(select(down_table), pad)
    taps = lax.dynamic_slice_in_dim(conv_filter, 2 * HD * core, 2 * HD, 1)
    taps = pad_last(taps.reshape(KW, 2, HD), PD).reshape(KW, 2 * PD)
    taps = jnp.broadcast_to(jnp.pad(taps, ((0, R - KW), (0, 0))), (SLOTS, R, 2 * PD))
    packed = jnp.concatenate([right_table, out_table, gate_table, down_table, taps], 2)
    spots = Table(pad)

    gain_one = gain_first.astype(f32)
    gain_two = gain_second.astype(f32)[None, :]
    own_input = lax.dynamic_index_in_dim(block_input, z, 0, False)
    own_cotangent = lax.dynamic_index_in_dim(out_cotangent, z, 0, False)
    my_length = lax.dynamic_index_in_dim(seq_lengths, z, 0, False)
    upstream_own = jnp.where(
        (((chip * 2 + core) * length + jnp.arange(length, dtype=jnp.int32)) < my_length)[:, None],
        own_cotangent,
        0.0,
    ).astype(bf16)

    e_m, c_m = swap_tp(mixer_piece, 1), cross(mixer_piece)
    both_input = both_cores(own_input)
    first = norm_rows(both_input.astype(f32), gain_one)[0].astype(bf16)
    mixer_rank = nn(first, my_mixer_left).astype(bf16)
    upstream_other = swap_core(upstream_own)
    upstream_own, upstream_other, e_m, c_m, mixer_rank, packed, both_input = hold(
        upstream_own, upstream_other, e_m, c_m, mixer_rank, packed, both_input
    )

    projs, packs, wides = [], [], []
    borrowed, prior, mixed, numer, chunk_states = [None, None], [None, None], [], [], []
    slots = [packed[0], None, None, None]

    def attend_slot(slot):
        pair, n = slot // 2, slot % 2
        out = attend(spots, n, projs[slot], borrowed[pair], prior[pair], slots[slot], tables)
        for kept, value in zip((mixed, numer, chunk_states), out):
            kept.append(value)

    def project_slot(slot, refs):
        out = project(slot == 0, first, mixer_rank, slots[slot], tables, refs)
        for kept, value in zip((projs, packs, wides), out):
            kept.append(value)

    x1, y1 = hop_xy(e_m)
    c2_m, f_m = cross(e_m), edge(c_m)
    table1 = swap_tp(packed[1], 1)
    project_slot(0, (w_mix,))
    slot2 = pick_inner(c2_m, f_m)
    x1, y1, slot2, c2_m, c_m, packs[0], table1, feed_piece, packed = hold(
        x1, y1, slot2, c2_m, c_m, packs[0], table1, feed_piece, packed
    )
    slots[1] = table1
    d1 = hop_diag(x1, y1, M_CUT)
    x2, y2 = hop_xy(slot2)
    f2_m = edge(c2_m)
    table2, table3 = swap_tp(packed[2], 2), swap_tp(packed[3], 3)
    upstream = order_cores(upstream_own, upstream_other)
    down_rgrad = nt(upstream, my_down_right).astype(bf16)
    slot3 = pick_inner(c_m, f2_m)
    x2, y2, slot3, feed_piece, table2, table3, upstream, down_rgrad, *d1 = hold(
        x2, y2, slot3, feed_piece, table2, table3, upstream, down_rgrad, *d1
    )
    slots[2], slots[3] = table2, table3
    d2 = hop_diag(x2, y2, M_CUT)
    x3, y3 = hop_xy(slot3)
    e_f = swap_tp(feed_piece, 1)
    set1 = (e_m, x1, y1, *d1)
    project_slot(1, set1)
    x3, y3, e_f, packs[0], packs[1], *d2 = hold(x3, y3, e_f, packs[0], packs[1], *d2)
    d3 = hop_diag(x3, y3, M_CUT)
    c_f = cross(feed_piece)
    gathered = lax.all_gather(jnp.concatenate(packs[:2], 0), "chip")
    set2 = (slot2, x2, y2, *d2)
    project_slot(2, set2)
    prior[0], borrowed[0] = use_states((gathered,), False)
    d3_a, d3_b, c_f, packs[2], prior[0], borrowed[0] = hold(
        *d3, c_f, packs[2], prior[0], borrowed[0]
    )
    fx1, fy1 = hop_xy(e_f)
    c2_f, f_f = cross(e_f), edge(c_f)
    set3 = (slot3, x3, y3, d3_a, d3_b)
    project_slot(3, set3)
    fslot2 = pick_inner(c2_f, f_f)
    fx1, fy1, fslot2, c2_f, c_f, packs[2], packs[3] = hold(
        fx1, fy1, fslot2, c2_f, c_f, packs[2], packs[3]
    )
    crossing = swap_states(jnp.concatenate(packs[2:], 0))
    attend_slot(0)
    attend_slot(1)
    fd1 = hop_diag(fx1, fy1, feed_cut(quarter))
    mixed[0], mixed[1], fslot2, c2_f, fd1_a, fd1_b, *crossing = hold(
        mixed[0], mixed[1], fslot2, c2_f, *fd1, *crossing
    )
    fd1 = (fd1_a, fd1_b)
    fx2, fy2 = hop_xy(fslot2)
    f2_f = edge(c2_f)
    prior[1], borrowed[1] = use_states(crossing, False)
    attend_slot(2)
    attend_slot(3)
    fslot3 = pick_inner(c_f, f2_f)
    sets = list(set1) + list(set2) + list(set3)
    out_part, out_rank, out_weight = mix_out(spots, mixed, slots, my_output_right, [w_out] + sets)
    fx2, fy2, out_part, fslot3 = hold(fx2, fy2, out_part, fslot3)
    other_part = swap_core(out_part)
    middle, second, gate_rank = norm_two(out_part, other_part, both_input, gain_two, my_gateup_left)

    gateup_left_t = my_gateup_left.T

    def feed_slots(which, sources, carry):
        return feed(
            which,
            which[-1] == SLOTS - 1,
            half,
            spots,
            second,
            upstream,
            gate_rank,
            down_rgrad,
            my_down_right,
            gateup_left_t,
            [slots[k] for k in which],
            sources,
            carry,
        )

    fd2 = hop_diag(fx2, fy2, feed_cut(quarter))
    fx3, fy3 = hop_xy(fslot3)
    carry, gate_grads, down_grads = feed_slots(
        (0, 1), [(w_gate, w_down), (e_f, fx1, fy1, *fd1)], []
    )
    fx3, fy3, carry[2], *fd2 = hold(fx3, fy3, carry[2], *fd2)
    fd3 = hop_diag(fx3, fy3, feed_cut(quarter))
    carry, more_gates, more_downs = feed_slots((2,), [(fslot2, fx2, fy2, *fd2)], carry)
    gate_grads, down_grads = gate_grads + more_gates, down_grads + more_downs
    carry[2], *fd3 = hold(carry[2], *fd3)
    carry, more_gates, more_downs = feed_slots((3,), [(fslot3, fx3, fy3, *fd3)], carry)
    gate_grads, down_grads = gate_grads + more_gates, down_grads + more_downs
    down_part, back_part, ranks = carry
    other_back = swap_core(back_part)
    other_down = swap_core(own_rows(down_part, 1 - core))
    own_down = own_rows(down_part, core).astype(f32)
    own_output = (own_rows(middle, core) + (own_down + other_down.astype(f32))).astype(bf16)
    own_output, other_back = hold(own_output, other_back)
    block_output = lax.all_gather(own_output, "tp")
    mixer_up, output_rgrad = back_two(
        back_part, other_back, middle, upstream, gain_two, my_output_right
    )


    ups, grads, packed0, packed1, left_grads = turn(
        spots, mixer_up, output_rgrad, out_weight, slots, numer, mixed, projs, borrowed, tables
    )
    packed0, packed1, left_grads, ranks, out_rank = hold(
        packed0, packed1, left_grads, ranks, out_rank
    )
    crossing = swap_states(packed0)
    down_rank, gateup_rgrad = ranks[:, :R].astype(bf16), ranks[:, R:].astype(bf16)
    shared = jnp.stack(
        [
            tn(out_rank.astype(bf16), mixer_up),
            tn(gateup_rgrad, second),
            tn(down_rank, upstream),
        ]
    )
    owned = jnp.stack(
        [jnp.concatenate([left_grads[i], gate_grads[i], down_grads[i]], 1) for i in range(SLOTS)]
    )
    packed1, shared, owned, *crossing = hold(packed1, shared, owned, *crossing)
    backs = []

    def back_slots(pair, which, later, returned):
        for n in which:
            slot = 2 * pair + n
            backs.append(
                attend_back(
                    spots,
                    slot,
                    projs[slot],
                    borrowed[pair],
                    chunk_states[slot],
                    later,
                    returned,
                    ups,
                    grads,
                    slots[slot],
                    mixer_rank,
                    tables,
                )
            )

    def join(array, other):
        return (array.astype(f32) + other.astype(f32)).astype(array.dtype)

    def packs_of(owned, shared):
        flat = jnp.concatenate(list(shared), 1).astype(bf16)
        return [jnp.concatenate([owned[k], flat], 1) for k in range(SLOTS)]

    next_crossing = swap_states(packed1)
    back_slots(0, (0, 1), *use_states(crossing, True))
    early_rank = backs[0][1] + backs[1][1]
    shared_x, owned_x = swap_chip(shared, 1), swap_chip(owned, 1)
    early_rank, shared_x, owned_x, *crossing = hold(
        early_rank, shared_x, owned_x, *next_crossing
    )
    shared, owned = add_rest(join(shared, shared_x)), add_rest(join(owned, owned_x))
    later, returned = use_states(crossing, True)
    back_slots(1, (0,), later, returned)
    early_rank = early_rank + backs[2][1]
    early_rank, later, shared, owned = hold(early_rank, later, shared, owned)
    early = packs_of(owned, shared)
    early = [early[0]] + [swap_tp(early[bit], bit) for bit in (1, 2, 3)]
    back_slots(1, (1,), later, returned)
    rank_grad = early_rank + backs[3][1]
    rank_grad, *early = hold(rank_grad, *early)
    early = jnp.stack(early)
    early_other = swap_core(early)

    mixer_all = jnp.concatenate(
        [
            jnp.stack([back[2] for back in backs]),
            tn(rank_grad.astype(bf16), first)[None].astype(bf16),
        ],
        0,
    )
    mixer_x = plane_parts(mixer_all)
    proj_grads = [back[0].reshape(2, length, 2 * HEAD_PAD) for back in backs]
    left_t = my_mixer_left.T
    count_a = length // 2
    count_b = length - count_a
    rank_rows = rank_grad.reshape(2, length, R)
    part_a = first_back(0, count_a, proj_grads, rank_rows, left_t, wides)
    part_a, rank_rows, early, early_other, *mixer_x = hold(
        part_a, rank_rows, early, early_other, *mixer_x, after=(block_output,)
    )
    mixer_all = plane_sum(mixer_all, mixer_x)

    def finish(part, start, count):
        here = lax.dynamic_index_in_dim(part, core, 0, False)
        there = lax.dynamic_index_in_dim(part, 1 - core, 0, False)
        total = here.astype(f32) + swap_core(there).astype(f32)
        wide = own_input[start : start + count].astype(f32)
        scale_one = lax.rsqrt(jnp.mean(wide * wide, -1, keepdims=True) + epsilon)
        straight = lax.dynamic_slice_in_dim(
            mixer_up, core * length + start, count, 0
        ).astype(f32)
        return (straight + norm_back(wide, scale_one, gain_one, total)).astype(bf16)

    done_a = finish(part_a, 0, count_a)
    e_a, c_a = swap_tp(done_a, 1), cross(done_a)
    late = packs_of(mixer_all[:SLOTS], mixer_all[SLOTS:])
    late = [late[0]] + [swap_tp(late[bit], bit) for bit in (1, 2, 3)]
    part_b = first_back(count_a, count_b, proj_grads, rank_rows, left_t, wides)
    e_a, c_a, part_b, *late = hold(e_a, c_a, part_b, *late)
    late = jnp.stack(late)
    c2_a, f_a = cross(e_a), edge(c_a)
    done_b = finish(part_b, count_a, count_b)
    done_b, early, early_other, late, block_output = hold(
        done_b, early, early_other, late, block_output
    )
    block_output = copy_of(block_output)
    e_b, c_b = swap_tp(done_b, 1), cross(done_b)
    late_other = swap_core(late)
    hot = jnp.swapaxes(onehot, 0, 1).astype(f32)
    flag = jnp.reshape(core == 0, (1,)).astype(jnp.int32)
    early_tables = tables_of(
        functools.partial(early_kernel, half, pad),
        [(R, width)] * 3 + [(R, heads_here * HD), (R, 2, ff_here), (R, ff_here)],
        "early_tables",
        hot,
        flag,
        early,
        early_other,
    )
    (
        c2_a, f_a, e_b, c_b, late, late_other, done_a, done_b, e_a
    ) = hold(
        c2_a, f_a, e_b, c_b, late, late_other, done_a, done_b, e_a,
        after=(*early_tables, block_output),
    )
    f2_a, c2_b, f_b = edge(c2_a), cross(e_b), edge(c_b)

    input_grad = jnp.zeros(block_input.shape, bf16)

    def put(whole, part, slot, number):
        return lax.dynamic_update_slice(whole, part[None], (z ^ slot, number * count_a, 0))

    input_grad = put(input_grad, done_a, 0, 0)
    input_grad = put(input_grad, done_b, 0, 1)
    input_grad = put(input_grad, e_a, 1, 0)
    input_grad = put(input_grad, e_b, 1, 1)
    input_grad = put(input_grad, pick_inner(c2_a, f_a), 2, 0)
    grad_mixer_right, grad_mixer_left = tables_of(
        late_kernel,
        [(R, heads_here, HCOLS), (R, width)],
        "late_tables",
        hot,
        flag,
        late,
        late_other,
    )
    f2_a, c2_b, f_b, input_grad = hold(
        f2_a, c2_b, f_b, input_grad, after=(grad_mixer_right, grad_mixer_left)
    )
    f2_b = edge(c2_b)
    input_grad = put(input_grad, pick_inner(c_a, f2_a), 3, 0)
    input_grad = put(input_grad, pick_inner(c2_b, f_b), 2, 1)
    input_grad = put(input_grad, pick_inner(c_b, f2_b), 3, 1)
    grad_output_right, grad_gateup_left, grad_down_right = early_tables[:3]
    grad_output_left, grad_gateup_right, grad_down_left = early_tables[3:]
    return (
        block_output,
        input_grad,
        jnp.swapaxes(grad_mixer_left, 1, 2),
        grad_mixer_right,
        jnp.swapaxes(grad_output_left, 1, 2),
        grad_output_right,
        jnp.swapaxes(grad_gateup_left, 1, 2),
        grad_gateup_right,
        jnp.swapaxes(grad_down_left, 1, 2),
        grad_down_right,
    )


def solution(mesh):
    seq, tp = mesh.devices.shape
    fine = Mesh(mesh.devices.reshape(seq // 2, 2, tp), ("chip", "core", "tp"))
    where = ("chip", "core")
    return jax.shard_map(
        body,
        mesh=fine,
        in_specs=(
            P(None, where, None),
            P(),
            P(None, "tp", None),
            P(None, "tp"),
            P("tp", None),
            P(),
            P(None, None, "tp"),
            P("tp", None),
            P(),
            P(None, None, "tp", None),
            P(None, "tp", None),
            P(),
            P(),
            P(None, None, None, "tp"),
            P(None, "tp", None),
            P(),
            P(),
            P(),
            P(None, where, None),
        ),
        out_specs=(
            P(None, where, None),
            P(None, where, None),
            P(),
            P(None, None, "tp", None),
            P(None, "tp", None),
            P(),
            P(),
            P(None, None, None, "tp"),
            P(None, "tp", None),
            P(),
        ),
        check_vma=False,
    )
```

```python
import functools

import jax
import jax.numpy as jnp
import numpy as np
from jax import lax
from jax.experimental import pallas as pl
from jax.experimental.pallas import tpu as pltpu
from jax.sharding import Mesh
from jax.sharding import PartitionSpec as P

HD = 112
PD = 128
FD = 16
R = 16
NA = 8
KW = 3
WIN = 64
HCOLS = 704
SLOTS = 4
HEAD_PAD = 7 * PD
STATE = 160
CHUNK = 256
TURN = 1024
QB = 128
BACK_QB = 256
BACK_CHUNK = 512
ATT = 512
PACK = STATE + 2 * WIN + 32

epsilon = 1e-05
masked = -1e30
f32 = jnp.float32
bf16 = jnp.bfloat16
ANY = pl.BlockSpec(memory_space=pl.ANY)


def nn(a, b):
    return lax.dot_general(a, b, (((1,), (0,)), ((), ())), preferred_element_type=f32)


def nt(a, b):
    return lax.dot_general(a, b, (((1,), (1,)), ((), ())), preferred_element_type=f32)


def tn(a, b):
    return lax.dot_general(a, b, (((0,), (0,)), ((), ())), preferred_element_type=f32)


def feature_tables():
    leading, trailing = np.triu_indices(FD)
    pick = np.zeros((PD, 1280), np.float32)
    for base, row in ((0, 0), (512, FD)):
        pick[PD - 1, base] = 1.0
        pick[PD - 1, base + 256 : base + 256 + 1 + FD] = 1.0
        for i in range(FD):
            pick[row + i, base + 1 + i] = 0.5
        for n, (i, j) in enumerate(zip(leading, trailing)):
            pick[row + i, base + 1 + FD + n] = 0.25 if i == j and base == 0 else 0.5
            pick[row + j, base + 256 + 1 + FD + n] = 0.5
    for i in range(FD):
        pick[FD + i, 1024 + i] = 0.25
        pick[i, 1152 + FD + i] = 0.25
    return pick


HEAD_SEGMENTS = [(0, 2 * FD, 0)] + [(2 * FD + HD * i, HD, PD * (i + 1)) for i in range(6)]
M_ROWS = HCOLS + HD
M_CUT = 2 * FD + 3 * HD


def place():
    j = lax.rem(lax.axis_index("chip"), 4)
    return j // 2, lax.rem(j, 2)


def run_copies(copies, sems, start):
    for number, (src, dst) in enumerate(copies):
        copy = pltpu.make_async_copy(src, dst, sems.at[start + number])
        copy.start()


def wait_copies(copies, sems, start):
    for number, (src, dst) in enumerate(copies):
        pltpu.make_async_copy(src, dst, sems.at[start + number]).wait()


def spread_pieces(refs, cut, rows, dest, base, width, offset_of):
    y, x = place()
    z_ref, x_ref, y_ref, da_ref, db_ref = refs
    copies = []
    for kind, yy, xx in (("z", y, x), ("x", y, 1 - x), ("y", 1 - y, x), ("d", 1 - y, 1 - x)):
        cols = pl.ds(pl.multiple_of(xx * width, PD), width)
        for first, count in rows:
            spans = [(first, count)]
            if kind == "d" and first < cut < first + count:
                spans = [(first, cut - first), (cut, first + count - cut)]
            for row, size in spans:
                if kind == "d":
                    src = da_ref if row < cut else db_ref
                    src = src.at[pl.ds(row if row < cut else row - cut, size)]
                else:
                    src = {"z": z_ref, "x": x_ref, "y": y_ref}[kind].at[pl.ds(row, size)]
                start = pl.multiple_of(base + offset_of(row, yy), 16)
                copies.append((src, dest.at[pl.ds(start, size), cols]))
    return copies


def mixer_offset(row, yy):
    for first, count, at in HEAD_SEGMENTS:
        if first <= row < first + count:
            return yy * HEAD_PAD + at + row - first
    return None


MIXER_ROWS = [(first, count) for first, count, _ in HEAD_SEGMENTS]


def mixer_copies(refs, own, dest, base):
    if own:
        core = lax.axis_index("core")
        copies = []
        for head in range(2):
            for first, count, at in HEAD_SEGMENTS:
                src = pl.multiple_of(2 * HCOLS * core + HCOLS * head + first, 16)
                copies.append(
                    (refs[0].at[pl.ds(src, count)], dest.at[pl.ds(base + HEAD_PAD * head + at, count)])
                )
        return copies
    return spread_pieces(refs, M_CUT, MIXER_ROWS, dest, base, dest.shape[1] // 2, mixer_offset)


def mixer_pads(dest, base):
    for head in range(2):
        for first, count, at in HEAD_SEGMENTS:
            start = base + HEAD_PAD * head + at + count
            dest[start : start + PD - count] = jnp.zeros((PD - count, dest.shape[1]), bf16)


def output_copies(refs, own, dest, base):
    if own:
        core = lax.axis_index("core")
        return [
            (
                refs[0].at[pl.ds(pl.multiple_of(2 * HD * core + HD * head, 16), HD)],
                dest.at[pl.ds(base + PD * head, HD)],
            )
            for head in range(2)
        ]
    return spread_pieces(
        refs, M_CUT, [(HCOLS, HD)], dest, base, dest.shape[1] // 2, lambda row, yy: yy * PD + row - HCOLS
    )


def output_pads(dest, base):
    for head in range(2):
        start = base + PD * head + HD
        dest[start : start + PD - HD] = jnp.zeros((PD - HD, dest.shape[1]), bf16)


def feed_cut(quarter):
    return quarter + (quarter // 2 + 15) // 16 * 16


def feed_copies(refs, own, dest, half, pad):
    if own:
        core = lax.axis_index("core")
        wg, wd = refs
        spots = [(wg, 0, 0), (wg, 2 * half, pad), (wd, 0, 2 * pad)]
        return [
            (
                ref.at[pl.ds(pl.multiple_of(half * core + first, 16), half)],
                dest.at[pl.ds(at, half)],
            )
            for ref, first, at in spots
        ]
    quarter = half // 2

    def offset_of(row, yy):
        return row // quarter * pad + yy * quarter + row % quarter

    rows = [(quarter * i, quarter) for i in range(3)]
    return spread_pieces(
        refs, feed_cut(quarter), rows, dest, 0, dest.shape[1] // 2, offset_of
    )


def feed_pads(dest, half, pad):
    for i in range(3):
        dest[pad * i + half : pad * (i + 1)] = jnp.zeros((pad - half, dest.shape[1]), bf16)


def features(picked, at):
    one = picked[:, at : at + 256]
    two = picked[:, at + 256 : at + 512]
    return one, two, (one * two).astype(bf16)


class Table:
    def __init__(self, pad):
        sizes = (2 * HEAD_PAD, 2 * PD, 2 * pad, pad, 2 * PD)
        starts = np.cumsum((0,) + sizes)
        self.right, self.left, self.gate, self.down, self.taps = (
            slice(int(a), int(a) + n) for a, n in zip(starts, sizes)
        )
        self.edges = [int(a) for a in starts]


def params(mib, **more):
    return pltpu.CompilerParams(vmem_limit_bytes=mib * 2**20, **more)


def project_kernel(own, first, rank, table, pick, *rest):
    count = 1 if own else 5
    refs = rest[:count]
    proj, packed, weight, sems = rest[count:]
    copies = mixer_copies(refs, own, weight, 0)
    run_copies(copies, sems, 0)
    mixer_pads(weight, 0)
    wait_copies(copies, sems, 0)
    blocks = first.shape[0] // CHUNK
    for head in range(2):
        cols = pl.ds(HEAD_PAD * head, HEAD_PAD)

        def one(block, carry):
            rows = pl.ds(pl.multiple_of(block * CHUNK, CHUNK), CHUNK)
            result = nt(first[rows, :], weight[cols, :]) + nn(rank[rows, :], table[:, cols])
            rounded = result.astype(bf16)
            lane = lax.broadcasted_iota(jnp.int32, (CHUNK, PD), 1)
            base = jnp.where(lane == PD - 1, 1.0, result[:, :PD]).astype(bf16)
            proj[rows, cols] = rounded
            proj[rows, HEAD_PAD * head : HEAD_PAD * head + PD] = base
            _, _, feat = features(nn(base, pick[:, 512:1024]), 0)
            return carry + tn(feat, rounded[:, PD : 2 * PD])

        total = lax.fori_loop(0, blocks, one, jnp.zeros((256, PD), f32))
        packed[head, 0:STATE] = total[:STATE].astype(bf16)
        last = first.shape[0]
        at = HEAD_PAD * head
        packed[head, STATE : STATE + WIN] = proj[last - WIN :, at + 3 * PD : at + 4 * PD]
        packed[head, STATE + WIN : STATE + 2 * WIN] = proj[last - WIN :, at + 4 * PD : at + 5 * PD]
        packed[head, PACK - 32 : PACK - 16] = proj[last - 16 :, at + 5 * PD : at + 6 * PD]
        packed[head, PACK - 16 : PACK] = jnp.zeros((16, PD), bf16)


def project(own, first, rank, table, tables, refs):
    rows, width = first.shape
    vm = pl.BlockSpec(memory_space=pltpu.VMEM)
    return pl.pallas_call(
        functools.partial(project_kernel, own),
        out_shape=(
            jax.ShapeDtypeStruct((rows, 2 * HEAD_PAD), bf16),
            jax.ShapeDtypeStruct((2, PACK, PD), bf16),
            jax.ShapeDtypeStruct((2 * HEAD_PAD, width), bf16),
        ),
        in_specs=[vm] * 4 + [ANY] * len(refs),
        out_specs=(vm, vm, vm),
        scratch_shapes=[pltpu.SemaphoreType.DMA((40,))],
        compiler_params=params(48),
        cost_estimate=pl.CostEstimate(
            flops=100_000_000, bytes_accessed=300_000, transcendentals=0
        ),
        name="project",
    )(first, rank, table, *tables, *refs)


def window_masks(count):
    query = lax.broadcasted_iota(jnp.int32, (count, count + WIN), 0)
    key = lax.broadcasted_iota(jnp.int32, (count, count + WIN), 1)
    others = (key > query) & (key <= query + WIN)
    lead = jnp.where(lax.axis_index("chip") > 0, 0, WIN)
    return others & (key >= lead), others


def window_prob(query, keys, allowed):
    scores = nt(query, keys) * HD ** (-0.5)
    scores = jnp.where(allowed, scores, masked)
    largest = jnp.max(scores, -1, keepdims=True)
    expo = jnp.exp(scores - largest)
    return expo * (1.0 / jnp.sum(expo, -1, keepdims=True))


def causal_mask(size):
    row = lax.broadcasted_iota(jnp.int32, (size, size), 0)
    col = lax.broadcasted_iota(jnp.int32, (size, size), 1)
    return col <= row


def conv_of(conv, taps, start, count):
    result = taps[0:1] * conv[pl.ds(16 + start, count), :]
    for offset in range(1, KW):
        result = result + taps[offset : offset + 1] * conv[pl.ds(16 + start - offset, count), :]
    return result


def attend_kernel(spots, proj, tails, prior, table, pick, mixed, numer, states, keys, vals, conv):
    rows = proj.shape[0]
    keys[0:WIN, :] = tails[0, 0:WIN]
    vals[0:WIN, :] = tails[0, WIN : 2 * WIN]
    conv[0:16, :] = tails[0, 2 * WIN : 2 * WIN + 16].astype(f32)
    keys[WIN:, :] = proj[:, 3 * PD : 4 * PD]
    vals[WIN:, :] = proj[:, 4 * PD : 5 * PD]
    conv[16:, :] = proj[:, 5 * PD : 6 * PD].astype(f32)
    tap = head_taps(spots, table)
    state = whole_state(prior[0])
    causal = causal_mask(ATT)
    first_mask, mask = window_masks(QB)
    for chunk in range(rows // ATT):
        states[0, chunk] = state.astype(bf16)
        at = chunk * ATT
        span = slice(at, at + ATT)
        base = proj[span, 0:PD]
        value = proj[span, PD : 2 * PD]
        picked = nn(base, pick[:, :1152])
        _, _, feat_q = features(picked, 0)
        score = nt(base, picked[:, 1024:1152].astype(bf16))
        weight = jnp.where(causal, 1.0 + score + 0.5 * score * score, 0.0).astype(bf16)
        total = nn(weight, value) + nn(feat_q, state.astype(bf16))
        if at + ATT < rows:
            _, _, feat_k = features(picked, 512)
            state = state + tn(feat_k, value)
        parts = []
        for number in range(chunk * ATT // QB, (chunk + 1) * ATT // QB):
            query = proj[number * QB : (number + 1) * QB, 2 * PD : 3 * PD]
            allowed = mask if number else first_mask
            prob = window_prob(query, keys[number * QB : number * QB + QB + WIN, :], allowed)
            parts.append(nn(prob.astype(bf16), vals[number * QB : number * QB + QB + WIN, :]))
        window = jnp.concatenate(parts, 0)
        scale = lax.rsqrt(jnp.sum(total * total, -1, keepdims=True) * (1.0 / HD) + epsilon)
        gate = proj[span, 6 * PD : 7 * PD].astype(f32)
        branch = conv_of(conv, tap, at, ATT) * (gate * jax.nn.sigmoid(gate))
        mixed[span, :] = (total * scale + window + branch).astype(bf16)
        numer[span, :] = total.astype(bf16)


def whole_state(state):
    return jnp.concatenate([state, jnp.zeros((256 - STATE, PD), f32)], 0)


def head_taps(spots, table):
    start = pl.multiple_of(spots.taps.start + PD * pl.program_id(0), PD)
    return table[:, pl.ds(start, PD)].astype(f32)


def attend(spots, number, proj, tails, prior, table, tables):
    rows = proj.shape[0]
    whole = lambda a: pl.BlockSpec(a.shape, lambda h: (0,) * a.ndim)
    return pl.pallas_call(
        functools.partial(attend_kernel, spots),
        grid=(2,),
        out_shape=(
            jax.ShapeDtypeStruct((rows, 2 * PD), bf16),
            jax.ShapeDtypeStruct((rows, 2 * PD), bf16),
            jax.ShapeDtypeStruct((2, rows // ATT, 256, PD), bf16),
        ),
        in_specs=[
            pl.BlockSpec((rows, HEAD_PAD), lambda h: (0, h)),
            pl.BlockSpec((1, PACK - STATE, PD), lambda h: (2 * number + h, 0, 0)),
            pl.BlockSpec((1, STATE, PD), lambda h: (2 * number + h, 0, 0)),
            whole(table),
        ]
        + [whole(t) for t in tables],
        out_specs=(
            pl.BlockSpec((rows, PD), lambda h: (0, h)),
            pl.BlockSpec((rows, PD), lambda h: (0, h)),
            pl.BlockSpec((1, rows // ATT, 256, PD), lambda h: (h, 0, 0, 0)),
        ),
        scratch_shapes=[
            pltpu.VMEM((rows + WIN, PD), bf16),
            pltpu.VMEM((rows + WIN, PD), bf16),
            pltpu.VMEM((rows + 16, PD), f32),
        ],
        compiler_params=params(48),
        cost_estimate=pl.CostEstimate(
            flops=100_000_000, bytes_accessed=300_000, transcendentals=0
        ),
        name="attend",
    )(proj, tails, prior, table, *tables)


def mix_out_kernel(spots, *refs):
    mixed = refs[0:4]
    lefts = refs[4:8]
    right = refs[8]
    sources = refs[9 : 9 + 1 + 15]
    part, rank, kept, weight, sems = refs[25:]
    groups = []
    for slot in range(SLOTS):
        pieces = sources[0:1] if slot == 0 else sources[1 + 5 * (slot - 1) : 1 + 5 * slot]
        groups.append(output_copies(pieces, slot == 0, weight, 2 * PD * slot))

    @pl.when(pl.program_id(0) == 0)
    def _():
        for slot in range(SLOTS):
            run_copies(groups[slot], sems, 8 * slot)
            output_pads(weight, 2 * PD * slot)
        for slot in range(SLOTS):
            wait_copies(groups[slot], sems, 8 * slot)

    total = jnp.zeros(part.shape, f32)
    rank_sum = jnp.zeros((part.shape[0], R), f32)
    for slot in range(SLOTS):
        total = total + nn(mixed[slot][...], weight[2 * PD * slot : 2 * PD * (slot + 1), :])
        rank_sum = rank_sum + nt(mixed[slot][...], lefts[slot][:, spots.left])
    total = total + nn(rank_sum.astype(bf16), right[...])
    part[...] = total.astype(bf16)
    rank[...] = rank_sum
    rows = kept.shape[0]
    kept[...] = weight[pl.ds(pl.multiple_of(pl.program_id(0) * rows, rows), rows), :]


def mix_out(spots, mixed, lefts, right, sources):
    rows = mixed[0].shape[0]
    width = right.shape[1]
    block = CHUNK
    steps = rows // block
    whole = lambda a: pl.BlockSpec(a.shape, lambda i: (0,) * a.ndim)
    return pl.pallas_call(
        functools.partial(mix_out_kernel, spots),
        grid=(steps,),
        out_shape=(
            jax.ShapeDtypeStruct((rows, width), bf16),
            jax.ShapeDtypeStruct((rows, R), f32),
            jax.ShapeDtypeStruct((SLOTS * 2 * PD, width), bf16),
        ),
        in_specs=[pl.BlockSpec((block, 2 * PD), lambda i: (i, 0))] * 4
        + [whole(a) for a in lefts]
        + [whole(right)]
        + [ANY] * len(sources),
        out_specs=(
            pl.BlockSpec((block, width), lambda i: (i, 0)),
            pl.BlockSpec((block, R), lambda i: (i, 0)),
            pl.BlockSpec((SLOTS * 2 * PD // steps, width), lambda i: (i, 0)),
        ),
        scratch_shapes=[pltpu.VMEM((SLOTS * 2 * PD, width), bf16), pltpu.SemaphoreType.DMA((32,))],
        compiler_params=params(48),
        cost_estimate=pl.CostEstimate(
            flops=100_000_000, bytes_accessed=300_000, transcendentals=0
        ),
        name="mix_out",
    )(*mixed, *lefts, right, *sources)


def feed_kernel(slots, last, half, pad, spots, *refs):
    count = len(slots)
    fresh = slots[0] == 0
    second, grad, grank, rgrad, dright, gleft = refs[:6]
    tables, refs = refs[6 : 6 + count], refs[6 + count :]
    groups = []
    sources = []
    for slot in slots:
        size = 2 if slot == 0 else 5
        sources.append(refs[:size])
        refs = refs[size:]
    if not fresh:
        (down_in, back_in, ranks_in), refs = refs[:3], refs[3:]
    down_out, back_out, ranks_out = refs[:3]
    right_outs, left_outs = refs[3 : 3 + count], refs[3 + count : 3 + 2 * count]
    weights, sems, *sums = refs[3 + 2 * count :]
    right_grads, left_grads = sums[:count], sums[count:]
    for n, slot in enumerate(slots):
        part = weights.at[3 * pad * n : 3 * pad * (n + 1)]
        groups.append(feed_copies(sources[n], slot == 0, part, half, pad))
    begin = pl.program_id(0) == 0

    @pl.when(begin)
    def _():
        for n in range(count):
            run_copies(groups[n], sems, 16 * n)
        for n in range(count):
            feed_pads(weights.at[3 * pad * n : 3 * pad * (n + 1)], half, pad)
            right_grads[n][...] = jnp.zeros(right_grads[n].shape, f32)
            left_grads[n][...] = jnp.zeros(left_grads[n].shape, f32)

    down = jnp.zeros(down_out.shape, f32) if fresh else down_in[...]
    back = jnp.zeros(back_out.shape, f32) if fresh else back_in[...]
    down_rank = jnp.zeros((down.shape[0], R), f32) if fresh else ranks_in[:, :R]
    back_rank = jnp.zeros((down.shape[0], R), f32) if fresh else ranks_in[:, R:]
    for n in range(count):

        @pl.when(begin)
        def _():
            wait_copies(groups[n], sems, 16 * n)

        at = 3 * pad * n
        right, left = tables[n][:, spots.gate], tables[n][:, spots.down]
        gate_up = nt(second[...], weights[at : at + 2 * pad, :]) + nn(grank[...], right)
        gate, up = gate_up[:, :pad], gate_up[:, pad:]
        hidden_grad = nt(grad[...], weights[at + 2 * pad : at + 3 * pad, :]) + nn(rgrad[...], left)
        sig = jax.nn.sigmoid(gate)
        act = gate * sig
        hidden = (act * up).astype(bf16)
        gate_grad = hidden_grad * up * (sig * (1.0 + gate * (1.0 - sig)))
        both = jnp.concatenate([gate_grad.astype(bf16), (hidden_grad * act).astype(bf16)], 1)
        down = down + nn(hidden, weights[at + 2 * pad : at + 3 * pad, :])
        back = back + nn(both, weights[at : at + 2 * pad, :])
        down_rank = down_rank + nt(hidden, left)
        back_rank = back_rank + nt(both, right)
        right_grads[n][...] += tn(grank[...], both)
        left_grads[n][...] += tn(rgrad[...], hidden)
    ranks_out[:, :R] = down_rank
    ranks_out[:, R:] = back_rank
    if last:
        down = down + nn(down_rank.astype(bf16), dright[...])
        back = back + nn(back_rank.astype(bf16), gleft[...])
    down_out[...] = down.astype(down_out.dtype)
    back_out[...] = back.astype(back_out.dtype)

    @pl.when(pl.program_id(0) == pl.num_programs(0) - 1)
    def _():
        for out, total in zip(right_outs + left_outs, right_grads + left_grads):
            out[...] = total[...].astype(bf16)


def feed(slots, last, half, spots, second, grad, grank, rgrad, dright, gleft, tables, sources, carry):
    rows, width = second.shape
    pad = spots.down.stop - spots.down.start
    count = len(slots)
    block = CHUNK
    kind = bf16 if last else f32
    whole = lambda a: pl.BlockSpec(a.shape, lambda i: (0,) * a.ndim)
    wide = pl.BlockSpec((block, width), lambda i: (i, 0))
    thin = pl.BlockSpec((block, R), lambda i: (i, 0))
    pair = pl.BlockSpec((block, 2 * R), lambda i: (i, 0))
    flat = sum([list(s) for s in sources], [])
    out = pl.pallas_call(
        functools.partial(feed_kernel, slots, last, half, pad, spots),
        grid=(rows // block,),
        out_shape=(
            jax.ShapeDtypeStruct((rows, width), kind),
            jax.ShapeDtypeStruct((rows, width), kind),
            jax.ShapeDtypeStruct((rows, 2 * R), f32),
        )
        + (jax.ShapeDtypeStruct((R, 2 * pad), bf16),) * count
        + (jax.ShapeDtypeStruct((R, pad), bf16),) * count,
        in_specs=[wide, wide, thin, thin, whole(dright), whole(gleft)]
        + [whole(t) for t in tables]
        + [ANY] * len(flat)
        + ([wide, wide, pair] if carry else []),
        out_specs=(wide, wide, pair)
        + (pl.BlockSpec((R, 2 * pad), lambda i: (0, 0)),) * count
        + (pl.BlockSpec((R, pad), lambda i: (0, 0)),) * count,
        scratch_shapes=[
            pltpu.VMEM((3 * pad * count, width), bf16),
            pltpu.SemaphoreType.DMA((16 * count,)),
        ]
        + [pltpu.VMEM((R, 2 * pad), f32)] * count
        + [pltpu.VMEM((R, pad), f32)] * count,
        compiler_params=params(58),
        cost_estimate=pl.CostEstimate(
            flops=100_000_000, bytes_accessed=300_000, transcendentals=0
        ),
        name="feed",
    )(second, grad, grank, rgrad, dright, gleft, *tables, *flat, *carry)
    return list(out[:3]), list(out[3 : 3 + count]), list(out[3 + count :])


def turn_kernel(spots, *refs):
    mixer_up, orgrad, weight = refs[:3]
    tables, numers, mixeds, bases, heads, tails = (
        refs[3:7], refs[7:11], refs[11:15], refs[15:23], refs[23:27], refs[27:29]
    )
    pick = refs[29]
    up_out, grad_out, packs, left_out, total_state, left_sums = (
        refs[30], refs[31], refs[32:34], refs[34], refs[35], refs[36]
    )
    step = pl.program_id(0)

    @pl.when(step == 0)
    def _():
        total_state[...] = jnp.zeros(total_state.shape, f32)
        left_sums[...] = jnp.zeros(left_sums.shape, f32)

    both = nt(mixer_up[...], weight[...])
    for n in range(SLOTS):
        table = tables[n]
        flow = both[:, 2 * PD * n : 2 * PD * (n + 1)] + nn(orgrad[...], table[:, spots.left])
        left_sums[n] += tn(orgrad[...], mixeds[n][...])
        for head in range(2):
            cols = slice(PD * head, PD * (head + 1))
            wide = slice(PD * (2 * n + head), PD * (2 * n + head + 1))
            up = flow[:, cols]
            total = numers[n][:, cols].astype(f32)
            scale = lax.rsqrt(jnp.sum(total * total, -1, keepdims=True) * (1.0 / HD) + epsilon)
            inner = jnp.sum(total * up, -1, keepdims=True) * (1.0 / HD)
            grad = (scale * up - total * (scale * scale * scale * inner)).astype(bf16)
            up_out[:, wide] = up.astype(bf16)
            grad_out[:, wide] = grad
            _, _, feat = features(nn(bases[2 * n + head][...], pick[:, 0:512]), 0)
            total_state[2 * n + head] += tn(feat, grad)

    @pl.when(step == pl.num_programs(0) - 1)
    def _():
        for pair in range(2):
            packs[pair][:, 0:STATE, :] = total_state[4 * pair : 4 * pair + 4, :STATE, :].astype(bf16)
        left_out[...] = left_sums[...].astype(bf16)

    @pl.when(step == 0)
    def _():
        for n in range(SLOTS):
            for head in range(2):
                at = n % 2 * 2 + head
                rows = tails[n // 2].at[at]
                give_back(spots, tables[n], heads[n], rows, up_out, packs[n // 2].at[at], n, head)


def give_back(spots, table, rows, tails, up_out, lent, n, head):
    at = HEAD_PAD * head
    wide = slice(PD * (2 * n + head), PD * (2 * n + head + 1))
    query = rows[:, at + 2 * PD : at + 3 * PD]
    keys = jnp.concatenate([tails[0:WIN, :], rows[:, at + 3 * PD : at + 4 * PD]], 0)
    vals = jnp.concatenate([tails[WIN : 2 * WIN, :], rows[:, at + 4 * PD : at + 5 * PD]], 0)
    prob = window_prob(query, keys, window_masks(QB)[0])
    up = up_out[0:QB, wide]
    prob_grad = nt(up, vals)
    inner = jnp.sum(prob * prob_grad, -1, keepdims=True)
    score = (prob * (prob_grad - inner)).astype(bf16)
    lent[STATE : STATE + WIN, :] = (tn(score, query)[:WIN] * HD ** (-0.5)).astype(bf16)
    lent[STATE + WIN : STATE + 2 * WIN, :] = tn(prob.astype(bf16), up)[:WIN].astype(bf16)
    start = spots.taps.start + PD * head
    tap = table[:, start : start + PD].astype(f32)
    gate = rows[0:16, at + 6 * PD : at + 7 * PD].astype(f32)
    flow = up_out[0:16, wide].astype(f32) * (gate * jax.nn.sigmoid(gate))
    row0 = tap[2:3] * flow[0:1]
    row1 = tap[1:2] * flow[0:1] + tap[2:3] * flow[1:2]
    index = lax.broadcasted_iota(jnp.int32, (16, PD), 0)
    edge_rows = jnp.where(index == 14, row0, jnp.where(index == 15, row1, 0.0))
    lent[PACK - 32 : PACK - 16, :] = edge_rows.astype(bf16)
    lent[PACK - 16 : PACK, :] = jnp.zeros((16, PD), bf16)


def turn(spots, mixer_up, orgrad, weight, slot_tables, numer, mixed, projs, tails, tables):
    rows, width = mixer_up.shape
    whole = lambda a: pl.BlockSpec(a.shape, lambda i: (0,) * a.ndim)
    flat = lambda *shape: pl.BlockSpec(shape, lambda i: (0,) * len(shape))
    tall = lambda cols, at: pl.BlockSpec((TURN, cols), lambda i: (i, at))
    heads = 2 * SLOTS
    return pl.pallas_call(
        functools.partial(turn_kernel, spots),
        grid=(rows // TURN,),
        out_shape=(
            jax.ShapeDtypeStruct((rows, heads * PD), bf16),
            jax.ShapeDtypeStruct((rows, heads * PD), bf16),
            jax.ShapeDtypeStruct((4, PACK, PD), bf16),
            jax.ShapeDtypeStruct((4, PACK, PD), bf16),
            jax.ShapeDtypeStruct((SLOTS, R, 2 * PD), bf16),
        ),
        in_specs=[tall(width, 0), tall(R, 0), whole(weight)]
        + [whole(t) for t in slot_tables]
        + [tall(2 * PD, 0)] * 8
        + [tall(PD, 0), tall(PD, 7)] * SLOTS
        + [flat(QB, 2 * HEAD_PAD)] * SLOTS
        + [whole(t) for t in tails]
        + [whole(t) for t in tables],
        out_specs=(
            tall(heads * PD, 0),
            tall(heads * PD, 0),
            flat(4, PACK, PD),
            flat(4, PACK, PD),
            flat(SLOTS, R, 2 * PD),
        ),
        scratch_shapes=[pltpu.VMEM((heads, 256, PD), f32), pltpu.VMEM((SLOTS, R, 2 * PD), f32)],
        compiler_params=params(58),
        cost_estimate=pl.CostEstimate(
            flops=100_000_000, bytes_accessed=300_000, transcendentals=0
        ),
        name="turn",
    )(
        mixer_up, orgrad, weight, *slot_tables, *numer, *mixed,
        *[proj for proj in projs for _ in range(2)], *projs, *tails, *tables,
    )


def window_back(proj, keys, vals, ups, out, number, allowed, held):
    start = number * BACK_QB
    span = slice(start, start + BACK_QB)
    band = slice(start, start + BACK_QB + WIN)
    query = proj[span, 2 * PD : 3 * PD]
    key = keys[band, :]
    prob = window_prob(query, key, allowed)
    up = ups[span, :]
    prob_grad = nt(up, vals[band, :])
    inner = jnp.sum(prob * prob_grad, -1, keepdims=True)
    score = (prob * (prob_grad - inner)).astype(bf16)
    out[span, 2 * PD : 3 * PD] = (nn(score, key) * HD ** (-0.5)).astype(bf16)
    dkey = tn(score, query) * HD ** (-0.5)
    dval = tn(prob.astype(bf16), up)
    for piece, new, more in ((3, dkey, held[0]), (4, dval, held[1])):
        cols = slice(piece * PD, (piece + 1) * PD)
        out[start : start + BACK_QB - WIN, cols] = new[WIN:BACK_QB].astype(bf16)
        out[start + BACK_QB - WIN : start + BACK_QB, cols] = (new[BACK_QB:] + more).astype(bf16)
    return dkey[:WIN], dval[:WIN]


def attend_back_kernel(
    spots, proj, tails, states, later, lent, ups, grads, table, rank, pick,
    out, rank_grad, right_grad, keys, vals, conv, flow
):
    rows = proj.shape[0]
    chunks = rows // BACK_CHUNK
    keys[0:WIN, :] = tails[0, 0:WIN]
    vals[0:WIN, :] = tails[0, WIN : 2 * WIN]
    conv[0:16, :] = tails[0, 2 * WIN : 2 * WIN + 16].astype(f32)
    keys[WIN:, :] = proj[:, 3 * PD : 4 * PD]
    vals[WIN:, :] = proj[:, 4 * PD : 5 * PD]
    conv[16:, :] = proj[:, 5 * PD : 6 * PD].astype(f32)
    tap = head_taps(spots, table)
    right = table.at[:, pl.ds(pl.multiple_of(HEAD_PAD * pl.program_id(0), PD), HEAD_PAD)]
    flow[rows:, :] = jnp.zeros((16, PD), f32)
    follow = whole_state(later[0])
    causal = causal_mask(BACK_CHUNK)
    first_mask, mask = window_masks(BACK_QB)
    held = (lent[0, 0:WIN].astype(f32), lent[0, WIN : 2 * WIN].astype(f32))
    for chunk in range(chunks - 1, -1, -1):
        at = chunk * BACK_CHUNK
        span = slice(at, at + BACK_CHUNK)
        base = proj[span, 0:PD]
        value = proj[span, PD : 2 * PD]
        grad = grads[span, :]
        picked = nn(base, pick[...])
        q_one, q_two, feat_q = features(picked, 0)
        k_one, k_two, feat_k = features(picked, 512)
        key_low = picked[:, 1024:1152].astype(bf16)
        query_high = picked[:, 1152:1280].astype(bf16)
        score = nt(base, key_low)
        weight = jnp.where(causal, 1.0 + score + 0.5 * score * score, 0.0).astype(bf16)
        slope = jnp.where(causal, nt(grad, value) * (1.0 + score), 0.0).astype(bf16)
        follow_round = follow.astype(bf16)
        q_up = nt(grad, states[0, chunk * (BACK_CHUNK // ATT)])
        k_up = nt(value, follow_round)
        inside = [q_up * q_two, q_up * q_one, k_up * k_two, k_up * k_one]
        inside = jnp.concatenate([part.astype(bf16) for part in inside], 1)
        low = nn(slope, key_low) + tn(slope, query_high) + nt(inside, pick[:, :1024])
        out[span, 0:PD] = low.astype(bf16)
        out[span, PD : 2 * PD] = (tn(weight, grad) + nn(feat_k, follow_round)).astype(bf16)
        if chunk:
            follow = follow + tn(feat_q, grad)
        gate = proj[span, 6 * PD : 7 * PD].astype(f32)
        up = ups[span, :].astype(f32)
        sig = jax.nn.sigmoid(gate)
        act = gate * sig
        flow[span, :] = up * act
        for number in range((at + BACK_CHUNK) // BACK_QB - 1, at // BACK_QB - 1, -1):
            held = window_back(
                proj, keys, vals, ups, out, number, mask if number else first_mask, held
            )
        slope_gate = sig + act * (1.0 - sig)
        out[span, 6 * PD : 7 * PD] = (up * conv_of(conv, tap, at, BACK_CHUNK) * slope_gate).astype(bf16)
    grad_in = tap[0:1] * flow[0:rows, :]
    for offset in range(1, KW):
        grad_in = grad_in + tap[offset : offset + 1] * flow[offset : offset + rows, :]
    out[:, 5 * PD : 6 * PD] = grad_in.astype(bf16)
    last = slice(rows - 16, rows)
    edge = grad_in[rows - 16 :, :] + lent[0, 2 * WIN : 2 * WIN + 16].astype(f32)
    out[last, 5 * PD : 6 * PD] = edge.astype(bf16)
    right_grad[...] = tn(rank[...], out[...]).astype(bf16)

    @pl.when(pl.program_id(0) == 0)
    def _():
        rank_grad[...] = nt(out[...], right[...])

    @pl.when(pl.program_id(0) > 0)
    def _():
        rank_grad[...] += nt(out[...], right[...])


def attend_back(spots, slot, proj, tails, states, later, lent, ups, grads, table, rank, tables):
    rows = proj.shape[0]
    number = slot % 2
    whole = lambda a: pl.BlockSpec(a.shape, lambda h: (0,) * a.ndim)
    head = pl.BlockSpec((rows, HEAD_PAD), lambda h: (0, h))
    edge = pl.BlockSpec((1, PACK - STATE, PD), lambda h: (2 * number + h, 0, 0))
    state = pl.BlockSpec((1, STATE, PD), lambda h: (2 * number + h, 0, 0))
    column = pl.BlockSpec((rows, PD), lambda h: (0, 2 * slot + h))
    return pl.pallas_call(
        functools.partial(attend_back_kernel, spots),
        grid=(2,),
        out_shape=(
            jax.ShapeDtypeStruct((rows, 2 * HEAD_PAD), bf16),
            jax.ShapeDtypeStruct((rows, R), f32),
            jax.ShapeDtypeStruct((R, 2 * HEAD_PAD), bf16),
        ),
        in_specs=[
            head,
            edge,
            pl.BlockSpec((1, rows // ATT, 256, PD), lambda h: (h, 0, 0, 0)),
            state,
            edge,
            column,
            column,
            whole(table),
            whole(rank),
        ]
        + [whole(t) for t in tables],
        out_specs=(
            head,
            pl.BlockSpec((rows, R), lambda h: (0, 0)),
            pl.BlockSpec((R, HEAD_PAD), lambda h: (0, h)),
        ),
        scratch_shapes=[
            pltpu.VMEM((rows + WIN, PD), bf16),
            pltpu.VMEM((rows + WIN, PD), bf16),
            pltpu.VMEM((rows + 16, PD), f32),
            pltpu.VMEM((rows + 16, PD), f32),
        ],
        compiler_params=params(48),
        cost_estimate=pl.CostEstimate(
            flops=100_000_000, bytes_accessed=300_000, transcendentals=0
        ),
        name="attend_back",
    )(proj, tails, states, later, lent, ups, grads, table, rank, *tables)


def first_back_kernel(core, *refs):
    grads = refs[0:4]
    rank_grad, left = refs[4:6]
    sources = refs[6:10]
    own, sibling, weight, sems = refs[10:]
    size = 2 * HEAD_PAD
    copies = [(sources[n], weight.at[size * n : size * (n + 1)]) for n in range(SLOTS)]
    begin = pl.program_id(0) == 0

    @pl.when(begin)
    def _():
        run_copies(copies, sems, 0)

    total = nn(rank_grad[0].astype(bf16), left[...])
    for slot in range(SLOTS):

        @pl.when(begin)
        def _():
            wait_copies(copies[slot : slot + 1], sems, slot)

        total = total + nn(grads[slot][0], weight[size * slot : size * (slot + 1), :])

    @pl.when(begin)
    def _():
        own[...] = total.astype(bf16)

    @pl.when(jnp.logical_not(begin))
    def _():
        sibling[...] = total.astype(bf16)


def first_back(core, start, count, grads, rank_grad, left, sources):
    _, _, size = grads[0].shape
    width = left.shape[1]
    whole = lambda a: pl.BlockSpec(a.shape, lambda i, c: (0,) * a.ndim)
    span = lambda cols: pl.BlockSpec(
        (1, count, cols), lambda i, c: (lax.rem(c[0] + i, 2), start // count, 0)
    )
    flat = pl.BlockSpec((count, width), lambda i, c: (0, 0))
    return pl.pallas_call(
        first_back_kernel,
        out_shape=(jax.ShapeDtypeStruct((count, width), bf16),) * 2,
        grid_spec=pltpu.PrefetchScalarGridSpec(
            num_scalar_prefetch=1,
            grid=(2,),
            in_specs=[span(size)] * 4 + [span(R), whole(left)] + [ANY] * len(sources),
            out_specs=(flat, flat),
            scratch_shapes=[
                pltpu.VMEM((SLOTS * size, width), bf16),
                pltpu.SemaphoreType.DMA((SLOTS,)),
            ],
        ),
        compiler_params=params(56),
        cost_estimate=pl.CostEstimate(
            flops=100_000_000, bytes_accessed=300_000, transcendentals=0
        ),
        name="first_back",
    )(core, *grads, rank_grad, left, *sources)


def norm_two_kernel(own, other, wide, gain, left, middle, second, rank):
    total = wide[...].astype(f32) + (own[...].astype(f32) + other[...].astype(f32))
    scale = lax.rsqrt(jnp.mean(total * total, -1, keepdims=True) + epsilon)
    rounded = (total * scale * gain[...]).astype(bf16)
    middle[...] = total
    second[...] = rounded
    rank[...] = nn(rounded, left[...]).astype(bf16)


def norm_two(own, other, wide, gain, left):
    rows, width = own.shape
    block = pl.BlockSpec((CHUNK, width), lambda i: (i, 0))
    whole = lambda a: pl.BlockSpec(a.shape, lambda i: (0,) * a.ndim)
    return pl.pallas_call(
        norm_two_kernel,
        grid=(rows // CHUNK,),
        out_shape=(
            jax.ShapeDtypeStruct((rows, width), f32),
            jax.ShapeDtypeStruct((rows, width), bf16),
            jax.ShapeDtypeStruct((rows, R), bf16),
        ),
        in_specs=[block, block, block, whole(gain), whole(left)],
        out_specs=(block, block, pl.BlockSpec((CHUNK, R), lambda i: (i, 0))),
        compiler_params=params(40),
        cost_estimate=pl.CostEstimate(
            flops=100_000_000, bytes_accessed=300_000, transcendentals=0
        ),
        name="norm_two",
    )(own, other, wide, gain, left)


def back_two_kernel(own, other, middle, upstream, gain, right, mixer_up, rgrad):
    vector = middle[...]
    scale = lax.rsqrt(jnp.mean(vector * vector, -1, keepdims=True) + epsilon)
    flow = gain[...] * (own[...].astype(f32) + other[...].astype(f32))
    inner = jnp.mean(vector * flow, -1, keepdims=True)
    total = upstream[...].astype(f32) + scale * flow - vector * (scale * scale * scale * inner)
    rounded = total.astype(bf16)
    mixer_up[...] = rounded
    rgrad[...] = nt(rounded, right[...]).astype(bf16)


def back_two(own, other, middle, upstream, gain, right):
    rows, width = own.shape
    block = pl.BlockSpec((CHUNK, width), lambda i: (i, 0))
    whole = lambda a: pl.BlockSpec(a.shape, lambda i: (0,) * a.ndim)
    return pl.pallas_call(
        back_two_kernel,
        grid=(rows // CHUNK,),
        out_shape=(
            jax.ShapeDtypeStruct((rows, width), bf16),
            jax.ShapeDtypeStruct((rows, R), bf16),
        ),
        in_specs=[block, block, block, block, whole(gain), whole(right)],
        out_specs=(block, pl.BlockSpec((CHUNK, R), lambda i: (i, 0))),
        compiler_params=params(40),
        cost_estimate=pl.CostEstimate(
            flops=100_000_000, bytes_accessed=300_000, transcendentals=0
        ),
        name="back_two",
    )(own, other, middle, upstream, gain, right)


def weighted(hot, parts):
    expert = pl.program_id(0)
    total = hot[expert, 0] * parts[0].astype(f32)
    for slot in range(1, SLOTS):
        total = total + hot[expert, slot] * parts[slot].astype(f32)
    return total


def by_core(flag, mine, other, base):
    lead = flag[0] > 0
    one, two = mine[:, :base], other[:, :base]
    return jnp.where(lead, one, two), jnp.where(lead, two, one)


def early_kernel(half, pad, hot, flag, mine, other, *outs):
    right, gate_left, down_right, out_left, gate_right, down_left = outs
    width = right.shape[2]
    base = 2 * PD + 3 * pad
    own, sibling = weighted(hot, mine), weighted(hot, other)
    for n, ref in enumerate((right, gate_left, down_right)):
        cols = slice(base + width * n, base + width * (n + 1))
        ref[0] = own[:, cols] + sibling[:, cols]
    cores = by_core(flag, own, sibling, base)
    out_left[0] = jnp.concatenate(
        [part[:, PD * h : PD * h + HD] for part in cores for h in range(2)], 1
    )
    for g in range(2):
        at = 2 * PD + pad * g
        gate_right[0, :, g, :] = jnp.concatenate([part[:, at : at + half] for part in cores], 1)
    at = 2 * PD + 2 * pad
    down_left[0] = jnp.concatenate([part[:, at : at + half] for part in cores], 1)


def late_kernel(hot, flag, mine, other, right, left):
    width = left.shape[2]
    base = 2 * HEAD_PAD
    own, sibling = weighted(hot, mine), weighted(hot, other)
    left[0] = own[:, base : base + width] + sibling[:, base : base + width]
    for core, part in enumerate(by_core(flag, own, sibling, base)):
        for head in range(2):
            at = HEAD_PAD * head
            right[0, :, 2 * core + head, :] = jnp.concatenate(
                [part[:, at + place_at : at + place_at + size] for _, size, place_at in HEAD_SEGMENTS], 1
            )


def tables_of(kernel, shapes, name, hot, flag, mine, other):
    whole = lambda a: pl.BlockSpec(a.shape, lambda e: (0,) * a.ndim)
    smem = pl.BlockSpec(memory_space=pltpu.SMEM)
    spot = lambda rank: lambda e: (e,) + (0,) * (rank - 1)
    return pl.pallas_call(
        kernel,
        grid=(NA,),
        out_shape=[jax.ShapeDtypeStruct((NA,) + shape, f32) for shape in shapes],
        in_specs=[smem, smem, whole(mine), whole(other)],
        out_specs=[pl.BlockSpec((1,) + shape, spot(len(shape) + 1)) for shape in shapes],
        compiler_params=params(40),
        cost_estimate=pl.CostEstimate(
            flops=100_000_000, bytes_accessed=300_000, transcendentals=0
        ),
        name=name,
    )(hot, flag, mine, other)


def swap_core(array):
    return lax.ppermute(array, "core", [(0, 1), (1, 0)])


def swap_chip(array, bit):
    count = lax.axis_size("chip")
    return lax.ppermute(array, "chip", [(i, i ^ bit) for i in range(count)])


def swap_tp(array, bit):
    return lax.ppermute(array, "tp", [(i, i ^ bit) for i in range(4)])


def both_cores(own):
    return order_cores(own, swap_core(own))


def order_cores(own, other):
    lead = lax.axis_index("core") == 0
    return jnp.concatenate([jnp.where(lead, own, other), jnp.where(lead, other, own)], 0)


def own_rows(array, core):
    half = array.shape[0] // 2
    return lax.dynamic_slice_in_dim(array, core * half, half, 0)


def hold_kernel(*refs):
    pass


def hold(*arrays, after=()):
    return pl.pallas_call(
        hold_kernel,
        out_shape=tuple(jax.ShapeDtypeStruct(a.shape, a.dtype) for a in arrays),
        in_specs=[ANY] * (len(arrays) + len(after)),
        out_specs=(ANY,) * len(arrays),
        input_output_aliases={i: i for i in range(len(arrays))},
        compiler_params=pltpu.CompilerParams(has_side_effects=True),
        name="hold",
    )(*arrays, *after)


def hop_xy(piece):
    return swap_chip(piece, 1), swap_chip(piece, 2)


def hop_diag(from_x, from_y, cut):
    return swap_chip(from_y[:cut], 1), swap_chip(from_x[cut:], 2)


def cross(array):
    return lax.ppermute(array, "tp", [(1, 2), (2, 1)])


def edge(array):
    return lax.ppermute(array, "tp", [(1, 0), (2, 3)])


def pick_inner(inner_array, edge_array):
    z = lax.axis_index("tp")
    return jnp.where((z == 1) | (z == 2), inner_array, edge_array)


def add_swapped(array, bit):
    other = swap_chip(array, bit)
    return (array.astype(f32) + other.astype(f32)).astype(array.dtype)


def add_rest(array):
    bit = 2
    while bit < lax.axis_size("chip"):
        array = add_swapped(array, bit)
        bit *= 2
    return array


def plane_parts(array):
    if lax.axis_size("chip") == 4:
        return [swap_chip(array, bit) for bit in (1, 2, 3)]
    return [add_rest(add_swapped(array, 1))]


def plane_sum(array, parts):
    if len(parts) == 1:
        return parts[0]
    total = array.astype(f32)
    for part in parts:
        total = total + part.astype(f32)
    return total.astype(array.dtype)


def swap_states(packed):
    if lax.axis_size("chip") == 4:
        return tuple(swap_chip(packed, bit) for bit in (1, 2, 3))
    return (lax.all_gather(packed, "chip"),)


def use_states(parts, backward):
    chip = lax.axis_index("chip")
    count = lax.axis_size("chip")
    if len(parts) > 1:
        total = 0.0
        for bit, part in zip((1, 2, 3), parts):
            other = chip ^ bit
            ahead = (other > chip) if backward else (other < chip)
            total = total + jnp.where(ahead, part[:, :STATE].astype(f32), 0.0)
        near = jnp.where(lax.rem(chip, 2) == (0 if backward else 1), parts[0], parts[2])
    else:
        index = jnp.arange(count, dtype=jnp.int32)
        ahead = (index > chip) if backward else (index < chip)
        states = parts[0][:, :, :STATE].astype(f32)
        total = jnp.sum(jnp.where(ahead[:, None, None, None], states, 0.0), 0)
        at = jnp.minimum(chip + 1, count - 1) if backward else jnp.maximum(chip - 1, 0)
        near = lax.dynamic_index_in_dim(parts[0], at, 0, False)
    inside = (chip < count - 1) if backward else (chip > 0)
    return total, jnp.where(inside, near[:, STATE:], 0.0).astype(bf16)


def copy_kernel(source, dest):
    dest[...] = source[...]


def copy_of(array):
    block = pl.BlockSpec((1,) + array.shape[1:], lambda i: (i, 0, 0))
    return pl.pallas_call(
        copy_kernel,
        grid=(array.shape[0],),
        out_shape=jax.ShapeDtypeStruct(array.shape, array.dtype),
        in_specs=[block],
        out_specs=block,
        compiler_params=params(32),
        cost_estimate=pl.CostEstimate(
            flops=100_000_000, bytes_accessed=300_000, transcendentals=0
        ),
        name="copy_of",
    )(array)


def stack_tp(parts):
    z = lax.axis_index("tp")
    result = jnp.zeros((SLOTS,) + parts[0].shape, parts[0].dtype)
    for slot, part in enumerate(parts):
        result = lax.dynamic_update_index_in_dim(result, part, z ^ slot, 0)
    return result


def pad_heads(table):
    lead = table.shape[:-2]
    heads = table.shape[-2]
    zero = [(0, 0)] * (len(lead) + 1)
    low = jnp.pad(table[..., : 2 * FD], zero + [(0, PD - 2 * FD)])
    high = table[..., 2 * FD :].reshape(lead + (heads, 6, HD))
    high = jnp.pad(high, zero + [(0, 0), (0, PD - HD)]).reshape(lead + (heads, 6 * PD))
    return jnp.concatenate([low, high], -1).reshape(lead + (heads * HEAD_PAD,))


def pad_last(table, size):
    return jnp.pad(table, [(0, 0)] * (table.ndim - 1) + [(0, size - table.shape[-1])])


def norm_rows(vector, gain_vector):
    row_scale = lax.rsqrt(jnp.mean(vector * vector, -1, keepdims=True) + epsilon)
    return (vector * row_scale * gain_vector, row_scale)


def norm_back(vector, row_scale, gain_vector, upstream):
    inner_mean = jnp.mean(vector * gain_vector * upstream, -1, keepdims=True)
    return (
        row_scale * gain_vector * upstream - vector * row_scale * row_scale * row_scale * inner_mean
    )


def body(
    block_input,
    gain_first,
    frozen_mixer_weight,
    conv_filter,
    frozen_output_weight,
    gain_second,
    frozen_gate_up_weight,
    frozen_down_weight,
    mixer_left,
    mixer_right,
    output_left,
    output_right,
    gateup_left,
    gateup_right,
    down_left,
    down_right,
    adapter_index,
    seq_lengths,
    out_cotangent,
):
    chip = lax.axis_index("chip")
    core = lax.axis_index("core")
    z = lax.axis_index("tp")
    y, x = place()
    sequences, length, width = block_input.shape
    rows = 2 * length
    heads_here = frozen_mixer_weight.shape[1]
    ff_here = frozen_down_weight.shape[0]
    half = ff_here // 2
    pad = (half + PD - 1) // PD * PD
    quarter = half // 2

    tables = (jnp.asarray(feature_tables(), bf16),)

    w_mix = jnp.transpose(frozen_mixer_weight, (1, 2, 0)).reshape(heads_here * HCOLS, width)
    w_gate = jnp.transpose(frozen_gate_up_weight, (1, 2, 0)).reshape(2 * ff_here, width)
    w_out = frozen_output_weight
    w_down = frozen_down_weight
    side = width // 2

    def cut(matrix, start, count):
        return lax.dynamic_slice(matrix, (start, x * side), (count, side))

    mixer_piece = jnp.concatenate(
        [
            cut(w_mix, 2 * HCOLS * core + HCOLS * y, HCOLS),
            cut(w_out, 2 * HD * core + HD * y, HD),
        ],
        0,
    )
    feed_piece = jnp.concatenate(
        [
            cut(w_gate, half * core + quarter * y, quarter),
            cut(w_gate, ff_here + half * core + quarter * y, quarter),
            cut(w_down, half * core + quarter * y, quarter),
        ],
        0,
    )
    slot_seq = z ^ jnp.arange(SLOTS, dtype=jnp.int32)
    slot_adapter = jnp.sum(
        jnp.where(slot_seq[:, None] == jnp.arange(SLOTS)[None, :], adapter_index[None, :], 0), 1
    )
    onehot = slot_adapter[:, None] == jnp.arange(NA, dtype=jnp.int32)[None, :]

    def select(table):
        return jnp.einsum(
            "se,e...->s...", onehot.astype(bf16), table, preferred_element_type=f32
        ).astype(bf16)

    mine = slot_adapter[0]
    my_mixer_left = lax.dynamic_index_in_dim(mixer_left, mine, 0, False)
    my_output_right = lax.dynamic_index_in_dim(output_right, mine, 0, False)
    my_gateup_left = lax.dynamic_index_in_dim(gateup_left, mine, 0, False)
    my_down_right = lax.dynamic_index_in_dim(down_right, mine, 0, False)
    right_table = pad_heads(
        select(lax.dynamic_slice_in_dim(mixer_right, 2 * core, 2, 2))
    )
    out_table = lax.dynamic_slice_in_dim(jnp.swapaxes(output_left, 1, 2), 2 * HD * core, 2 * HD, 2)
    out_table = pad_last(select(out_table).reshape(SLOTS, R, 2, HD), PD).reshape(SLOTS, R, 2 * PD)
    gate_table = lax.dynamic_slice_in_dim(gateup_right, half * core, half, 3)
    gate_table = pad_last(select(gate_table), pad).reshape(SLOTS, R, 2 * pad)
    down_table = lax.dynamic_slice_in_dim(jnp.swapaxes(down_left, 1, 2), half * core, half, 2)
    down_table = pad_last(select(down_table), pad)
    taps = lax.dynamic_slice_in_dim(conv_filter, 2 * HD * core, 2 * HD, 1)
    taps = pad_last(taps.reshape(KW, 2, HD), PD).reshape(KW, 2 * PD)
    taps = jnp.broadcast_to(jnp.pad(taps, ((0, R - KW), (0, 0))), (SLOTS, R, 2 * PD))
    packed = jnp.concatenate([right_table, out_table, gate_table, down_table, taps], 2)
    spots = Table(pad)

    gain_one = gain_first.astype(f32)
    gain_two = gain_second.astype(f32)[None, :]
    own_input = lax.dynamic_index_in_dim(block_input, z, 0, False)
    own_cotangent = lax.dynamic_index_in_dim(out_cotangent, z, 0, False)
    my_length = lax.dynamic_index_in_dim(seq_lengths, z, 0, False)
    upstream_own = jnp.where(
        (((chip * 2 + core) * length + jnp.arange(length, dtype=jnp.int32)) < my_length)[:, None],
        own_cotangent,
        0.0,
    ).astype(bf16)

    e_m, c_m = swap_tp(mixer_piece, 1), cross(mixer_piece)
    both_input = both_cores(own_input)
    first = norm_rows(both_input.astype(f32), gain_one)[0].astype(bf16)
    mixer_rank = nn(first, my_mixer_left).astype(bf16)
    upstream_other = swap_core(upstream_own)
    upstream_own, upstream_other, e_m, c_m, mixer_rank, packed, both_input = hold(
        upstream_own, upstream_other, e_m, c_m, mixer_rank, packed, both_input
    )

    projs, packs, wides = [], [], []
    borrowed, prior, mixed, numer, chunk_states = [None, None], [None, None], [], [], []
    slots = [packed[0], None, None, None]

    def attend_slot(slot):
        pair, n = slot // 2, slot % 2
        out = attend(spots, n, projs[slot], borrowed[pair], prior[pair], slots[slot], tables)
        for kept, value in zip((mixed, numer, chunk_states), out):
            kept.append(value)

    def project_slot(slot, refs):
        out = project(slot == 0, first, mixer_rank, slots[slot], tables, refs)
        for kept, value in zip((projs, packs, wides), out):
            kept.append(value)

    x1, y1 = hop_xy(e_m)
    c2_m, f_m = cross(e_m), edge(c_m)
    table1 = swap_tp(packed[1], 1)
    project_slot(0, (w_mix,))
    slot2 = pick_inner(c2_m, f_m)
    x1, y1, slot2, c2_m, c_m, packs[0], table1, feed_piece, packed = hold(
        x1, y1, slot2, c2_m, c_m, packs[0], table1, feed_piece, packed
    )
    slots[1] = table1
    d1 = hop_diag(x1, y1, M_CUT)
    x2, y2 = hop_xy(slot2)
    f2_m = edge(c2_m)
    table2, table3 = swap_tp(packed[2], 2), swap_tp(packed[3], 3)
    upstream = order_cores(upstream_own, upstream_other)
    down_rgrad = nt(upstream, my_down_right).astype(bf16)
    slot3 = pick_inner(c_m, f2_m)
    x2, y2, slot3, feed_piece, table2, table3, upstream, down_rgrad, *d1 = hold(
        x2, y2, slot3, feed_piece, table2, table3, upstream, down_rgrad, *d1
    )
    slots[2], slots[3] = table2, table3
    d2 = hop_diag(x2, y2, M_CUT)
    x3, y3 = hop_xy(slot3)
    e_f = swap_tp(feed_piece, 1)
    set1 = (e_m, x1, y1, *d1)
    project_slot(1, set1)
    x3, y3, e_f, packs[0], packs[1], *d2 = hold(x3, y3, e_f, packs[0], packs[1], *d2)
    d3 = hop_diag(x3, y3, M_CUT)
    c_f = cross(feed_piece)
    gathered = lax.all_gather(jnp.concatenate(packs[:2], 0), "chip")
    set2 = (slot2, x2, y2, *d2)
    project_slot(2, set2)
    prior[0], borrowed[0] = use_states((gathered,), False)
    d3_a, d3_b, c_f, packs[2], prior[0], borrowed[0] = hold(
        *d3, c_f, packs[2], prior[0], borrowed[0]
    )
    fx1, fy1 = hop_xy(e_f)
    c2_f, f_f = cross(e_f), edge(c_f)
    set3 = (slot3, x3, y3, d3_a, d3_b)
    project_slot(3, set3)
    fslot2 = pick_inner(c2_f, f_f)
    fx1, fy1, fslot2, c2_f, c_f, packs[2], packs[3] = hold(
        fx1, fy1, fslot2, c2_f, c_f, packs[2], packs[3]
    )
    crossing = swap_states(jnp.concatenate(packs[2:], 0))
    attend_slot(0)
    attend_slot(1)
    fd1 = hop_diag(fx1, fy1, feed_cut(quarter))
    mixed[0], mixed[1], fslot2, c2_f, fd1_a, fd1_b, *crossing = hold(
        mixed[0], mixed[1], fslot2, c2_f, *fd1, *crossing
    )
    fd1 = (fd1_a, fd1_b)
    fx2, fy2 = hop_xy(fslot2)
    f2_f = edge(c2_f)
    prior[1], borrowed[1] = use_states(crossing, False)
    attend_slot(2)
    attend_slot(3)
    fslot3 = pick_inner(c_f, f2_f)
    sets = list(set1) + list(set2) + list(set3)
    out_part, out_rank, out_weight = mix_out(spots, mixed, slots, my_output_right, [w_out] + sets)
    fx2, fy2, out_part, fslot3 = hold(fx2, fy2, out_part, fslot3)
    other_part = swap_core(out_part)
    middle, second, gate_rank = norm_two(out_part, other_part, both_input, gain_two, my_gateup_left)

    gateup_left_t = my_gateup_left.T

    def feed_slots(which, sources, carry):
        return feed(
            which,
            which[-1] == SLOTS - 1,
            half,
            spots,
            second,
            upstream,
            gate_rank,
            down_rgrad,
            my_down_right,
            gateup_left_t,
            [slots[k] for k in which],
            sources,
            carry,
        )

    fd2 = hop_diag(fx2, fy2, feed_cut(quarter))
    fx3, fy3 = hop_xy(fslot3)
    carry, gate_grads, down_grads = feed_slots(
        (0, 1), [(w_gate, w_down), (e_f, fx1, fy1, *fd1)], []
    )
    fx3, fy3, carry[2], *fd2 = hold(fx3, fy3, carry[2], *fd2)
    fd3 = hop_diag(fx3, fy3, feed_cut(quarter))
    carry, more_gates, more_downs = feed_slots((2,), [(fslot2, fx2, fy2, *fd2)], carry)
    gate_grads, down_grads = gate_grads + more_gates, down_grads + more_downs
    carry[2], *fd3 = hold(carry[2], *fd3)
    carry, more_gates, more_downs = feed_slots((3,), [(fslot3, fx3, fy3, *fd3)], carry)
    gate_grads, down_grads = gate_grads + more_gates, down_grads + more_downs
    down_part, back_part, ranks = carry
    other_back = swap_core(back_part)
    other_down = swap_core(own_rows(down_part, 1 - core))
    own_down = own_rows(down_part, core).astype(f32)
    own_output = (own_rows(middle, core) + (own_down + other_down.astype(f32))).astype(bf16)
    own_output, other_back = hold(own_output, other_back)
    block_output = lax.all_gather(own_output, "tp")
    mixer_up, output_rgrad = back_two(
        back_part, other_back, middle, upstream, gain_two, my_output_right
    )


    ups, grads, packed0, packed1, left_grads = turn(
        spots, mixer_up, output_rgrad, out_weight, slots, numer, mixed, projs, borrowed, tables
    )
    packed0, packed1, left_grads, ranks, out_rank = hold(
        packed0, packed1, left_grads, ranks, out_rank
    )
    crossing = swap_states(packed0)
    down_rank, gateup_rgrad = ranks[:, :R].astype(bf16), ranks[:, R:].astype(bf16)
    shared = jnp.stack(
        [
            tn(out_rank.astype(bf16), mixer_up),
            tn(gateup_rgrad, second),
            tn(down_rank, upstream),
        ]
    )
    owned = jnp.stack(
        [jnp.concatenate([left_grads[i], gate_grads[i], down_grads[i]], 1) for i in range(SLOTS)]
    )
    packed1, shared, owned, *crossing = hold(packed1, shared, owned, *crossing)
    backs = []

    def back_slots(pair, which, later, returned):
        for n in which:
            slot = 2 * pair + n
            backs.append(
                attend_back(
                    spots,
                    slot,
                    projs[slot],
                    borrowed[pair],
                    chunk_states[slot],
                    later,
                    returned,
                    ups,
                    grads,
                    slots[slot],
                    mixer_rank,
                    tables,
                )
            )

    def join(array, other):
        return (array.astype(f32) + other.astype(f32)).astype(array.dtype)

    def packs_of(owned, shared):
        flat = jnp.concatenate(list(shared), 1).astype(bf16)
        return [jnp.concatenate([owned[k], flat], 1) for k in range(SLOTS)]

    next_crossing = swap_states(packed1)
    back_slots(0, (0, 1), *use_states(crossing, True))
    early_rank = backs[0][1] + backs[1][1]
    shared_x, owned_x = swap_chip(shared, 1), swap_chip(owned, 1)
    early_rank, shared_x, owned_x, *crossing = hold(
        early_rank, shared_x, owned_x, *next_crossing
    )
    shared, owned = add_rest(join(shared, shared_x)), add_rest(join(owned, owned_x))
    later, returned = use_states(crossing, True)
    back_slots(1, (0,), later, returned)
    early_rank = early_rank + backs[2][1]
    early_rank, later, shared, owned = hold(early_rank, later, shared, owned)
    early = packs_of(owned, shared)
    early = [early[0]] + [swap_tp(early[bit], bit) for bit in (1, 2, 3)]
    back_slots(1, (1,), later, returned)
    rank_grad = early_rank + backs[3][1]
    rank_grad, *early = hold(rank_grad, *early)
    early = jnp.stack(early)
    early_other = swap_core(early)

    mixer_all = jnp.concatenate(
        [
            jnp.stack([back[2] for back in backs]),
            tn(rank_grad.astype(bf16), first)[None].astype(bf16),
        ],
        0,
    )
    mixer_x = plane_parts(mixer_all)
    proj_grads = [back[0].reshape(2, length, 2 * HEAD_PAD) for back in backs]
    left_t = my_mixer_left.T
    count_a = length // 2
    count_b = length - count_a
    rank_rows = rank_grad.reshape(2, length, R)
    core_array = jnp.reshape(core, (1,)).astype(jnp.int32)
    here_a, there_a = first_back(core_array, 0, count_a, proj_grads, rank_rows, left_t, wides)
    here_a, there_a, rank_rows, early, early_other, *mixer_x = hold(
        here_a, there_a, rank_rows, early, early_other, *mixer_x, after=(block_output,)
    )
    mixer_all = plane_sum(mixer_all, mixer_x)

    def finish(here, there, start, count):
        total = here.astype(f32) + swap_core(there).astype(f32)
        wide = own_input[start : start + count].astype(f32)
        scale_one = lax.rsqrt(jnp.mean(wide * wide, -1, keepdims=True) + epsilon)
        straight = lax.dynamic_slice_in_dim(
            mixer_up, core * length + start, count, 0
        ).astype(f32)
        return (straight + norm_back(wide, scale_one, gain_one, total)).astype(bf16)

    done_a = finish(here_a, there_a, 0, count_a)
    e_a, c_a = swap_tp(done_a, 1), cross(done_a)
    late = packs_of(mixer_all[:SLOTS], mixer_all[SLOTS:])
    late = [late[0]] + [swap_tp(late[bit], bit) for bit in (1, 2, 3)]
    here_b, there_b = first_back(core_array, count_a, count_b, proj_grads, rank_rows, left_t, wides)
    e_a, c_a, here_b, there_b, *late = hold(e_a, c_a, here_b, there_b, *late)
    late = jnp.stack(late)
    c2_a, f_a = cross(e_a), edge(c_a)
    done_b = finish(here_b, there_b, count_a, count_b)
    done_b, early, early_other, late, block_output = hold(
        done_b, early, early_other, late, block_output
    )
    block_output = copy_of(block_output)
    e_b, c_b = swap_tp(done_b, 1), cross(done_b)
    late_other = swap_core(late)
    hot = jnp.swapaxes(onehot, 0, 1).astype(f32)
    flag = jnp.reshape(core == 0, (1,)).astype(jnp.int32)
    early_tables = tables_of(
        functools.partial(early_kernel, half, pad),
        [(R, width)] * 3 + [(R, heads_here * HD), (R, 2, ff_here), (R, ff_here)],
        "early_tables",
        hot,
        flag,
        early,
        early_other,
    )
    (
        c2_a, f_a, e_b, c_b, late, late_other, done_a, done_b, e_a
    ) = hold(
        c2_a, f_a, e_b, c_b, late, late_other, done_a, done_b, e_a,
        after=(*early_tables, block_output),
    )
    f2_a, c2_b, f_b = edge(c2_a), cross(e_b), edge(c_b)

    input_grad = jnp.zeros(block_input.shape, bf16)

    def put(whole, part, slot, number):
        return lax.dynamic_update_slice(whole, part[None], (z ^ slot, number * count_a, 0))

    input_grad = put(input_grad, done_a, 0, 0)
    input_grad = put(input_grad, done_b, 0, 1)
    input_grad = put(input_grad, e_a, 1, 0)
    input_grad = put(input_grad, e_b, 1, 1)
    input_grad = put(input_grad, pick_inner(c2_a, f_a), 2, 0)
    grad_mixer_right, grad_mixer_left = tables_of(
        late_kernel,
        [(R, heads_here, HCOLS), (R, width)],
        "late_tables",
        hot,
        flag,
        late,
        late_other,
    )
    f2_a, c2_b, f_b, input_grad = hold(
        f2_a, c2_b, f_b, input_grad, after=(grad_mixer_right, grad_mixer_left)
    )
    f2_b = edge(c2_b)
    input_grad = put(input_grad, pick_inner(c_a, f2_a), 3, 0)
    input_grad = put(input_grad, pick_inner(c2_b, f_b), 2, 1)
    input_grad = put(input_grad, pick_inner(c_b, f2_b), 3, 1)
    grad_output_right, grad_gateup_left, grad_down_right = early_tables[:3]
    grad_output_left, grad_gateup_right, grad_down_left = early_tables[3:]
    return (
        block_output,
        input_grad,
        jnp.swapaxes(grad_mixer_left, 1, 2),
        grad_mixer_right,
        jnp.swapaxes(grad_output_left, 1, 2),
        grad_output_right,
        jnp.swapaxes(grad_gateup_left, 1, 2),
        grad_gateup_right,
        jnp.swapaxes(grad_down_left, 1, 2),
        grad_down_right,
    )


def solution(mesh):
    seq, tp = mesh.devices.shape
    fine = Mesh(mesh.devices.reshape(seq // 2, 2, tp), ("chip", "core", "tp"))
    where = ("chip", "core")
    return jax.shard_map(
        body,
        mesh=fine,
        in_specs=(
            P(None, where, None),
            P(),
            P(None, "tp", None),
            P(None, "tp"),
            P("tp", None),
            P(),
            P(None, None, "tp"),
            P("tp", None),
            P(),
            P(None, None, "tp", None),
            P(None, "tp", None),
            P(),
            P(),
            P(None, None, None, "tp"),
            P(None, "tp", None),
            P(),
            P(),
            P(),
            P(None, where, None),
        ),
        out_specs=(
            P(None, where, None),
            P(None, where, None),
            P(),
            P(None, None, "tp", None),
            P(None, "tp", None),
            P(),
            P(),
            P(None, None, None, "tp"),
            P(None, "tp", None),
            P(),
        ),
        check_vma=False,
    )
```

```python
import functools

import jax
import jax.numpy as jnp
import numpy as np
from jax import lax
from jax.experimental import pallas as pl
from jax.experimental.pallas import tpu as pltpu
from jax.sharding import Mesh
from jax.sharding import PartitionSpec as P

HD = 112
PD = 128
FD = 16
R = 16
NA = 8
KW = 3
WIN = 64
HCOLS = 704
SLOTS = 4
HEAD_PAD = 7 * PD
STATE = 160
CHUNK = 256
TURN = 1024
WIDE = 512
QB = 128
BACK_QB = 256
BACK_CHUNK = 512
ATT = 512
PACK = STATE + 2 * WIN + 32

epsilon = 1e-05
masked = -1e30
f32 = jnp.float32
bf16 = jnp.bfloat16
ANY = pl.BlockSpec(memory_space=pl.ANY)


def nn(a, b):
    return lax.dot_general(a, b, (((1,), (0,)), ((), ())), preferred_element_type=f32)


def nt(a, b):
    return lax.dot_general(a, b, (((1,), (1,)), ((), ())), preferred_element_type=f32)


def tn(a, b):
    return lax.dot_general(a, b, (((0,), (0,)), ((), ())), preferred_element_type=f32)


def feature_tables():
    leading, trailing = np.triu_indices(FD)
    pick = np.zeros((PD, 1280), np.float32)
    for base, row in ((0, 0), (512, FD)):
        pick[PD - 1, base] = 1.0
        pick[PD - 1, base + 256 : base + 256 + 1 + FD] = 1.0
        for i in range(FD):
            pick[row + i, base + 1 + i] = 0.5
        for n, (i, j) in enumerate(zip(leading, trailing)):
            pick[row + i, base + 1 + FD + n] = 0.25 if i == j and base == 0 else 0.5
            pick[row + j, base + 256 + 1 + FD + n] = 0.5
    for i in range(FD):
        pick[FD + i, 1024 + i] = 0.25
        pick[i, 1152 + FD + i] = 0.25
    return pick


HEAD_SEGMENTS = [(0, 2 * FD, 0)] + [(2 * FD + HD * i, HD, PD * (i + 1)) for i in range(6)]
M_ROWS = HCOLS + HD
M_CUT = 2 * FD + 3 * HD


def place():
    j = lax.rem(lax.axis_index("chip"), 4)
    return j // 2, lax.rem(j, 2)


def run_copies(copies, sems, start):
    for number, (src, dst) in enumerate(copies):
        copy = pltpu.make_async_copy(src, dst, sems.at[start + number])
        copy.start()


def wait_copies(copies, sems, start):
    for number, (src, dst) in enumerate(copies):
        pltpu.make_async_copy(src, dst, sems.at[start + number]).wait()


def spread_pieces(refs, cut, rows, dest, base, width, offset_of):
    y, x = place()
    z_ref, x_ref, y_ref, da_ref, db_ref = refs
    copies = []
    for kind, yy, xx in (("z", y, x), ("x", y, 1 - x), ("y", 1 - y, x), ("d", 1 - y, 1 - x)):
        cols = pl.ds(pl.multiple_of(xx * width, PD), width)
        for first, count in rows:
            spans = [(first, count)]
            if kind == "d" and first < cut < first + count:
                spans = [(first, cut - first), (cut, first + count - cut)]
            for row, size in spans:
                if kind == "d":
                    src = da_ref if row < cut else db_ref
                    src = src.at[pl.ds(row if row < cut else row - cut, size)]
                else:
                    src = {"z": z_ref, "x": x_ref, "y": y_ref}[kind].at[pl.ds(row, size)]
                start = pl.multiple_of(base + offset_of(row, yy), 16)
                copies.append((src, dest.at[pl.ds(start, size), cols]))
    return copies


def mixer_offset(row, yy):
    for first, count, at in HEAD_SEGMENTS:
        if first <= row < first + count:
            return yy * HEAD_PAD + at + row - first
    return None


MIXER_ROWS = [(first, count) for first, count, _ in HEAD_SEGMENTS]


def mixer_copies(refs, own, dest, base):
    if own:
        core = lax.axis_index("core")
        copies = []
        for head in range(2):
            for first, count, at in HEAD_SEGMENTS:
                src = pl.multiple_of(2 * HCOLS * core + HCOLS * head + first, 16)
                copies.append(
                    (refs[0].at[pl.ds(src, count)], dest.at[pl.ds(base + HEAD_PAD * head + at, count)])
                )
        return copies
    return spread_pieces(refs, M_CUT, MIXER_ROWS, dest, base, dest.shape[1] // 2, mixer_offset)


def mixer_pads(dest, base):
    for head in range(2):
        for first, count, at in HEAD_SEGMENTS:
            start = base + HEAD_PAD * head + at + count
            dest[start : start + PD - count] = jnp.zeros((PD - count, dest.shape[1]), bf16)


def output_copies(refs, own, dest, base):
    if own:
        core = lax.axis_index("core")
        return [
            (
                refs[0].at[pl.ds(pl.multiple_of(2 * HD * core + HD * head, 16), HD)],
                dest.at[pl.ds(base + PD * head, HD)],
            )
            for head in range(2)
        ]
    return spread_pieces(
        refs, M_CUT, [(HCOLS, HD)], dest, base, dest.shape[1] // 2, lambda row, yy: yy * PD + row - HCOLS
    )


def output_pads(dest, base):
    for head in range(2):
        start = base + PD * head + HD
        dest[start : start + PD - HD] = jnp.zeros((PD - HD, dest.shape[1]), bf16)


def feed_cut(quarter):
    return quarter + (quarter // 2 + 15) // 16 * 16


def feed_copies(refs, own, dest, half, pad):
    if own:
        core = lax.axis_index("core")
        wg, wd = refs
        spots = [(wg, 0, 0), (wg, 2 * half, pad), (wd, 0, 2 * pad)]
        return [
            (
                ref.at[pl.ds(pl.multiple_of(half * core + first, 16), half)],
                dest.at[pl.ds(at, half)],
            )
            for ref, first, at in spots
        ]
    quarter = half // 2

    def offset_of(row, yy):
        return row // quarter * pad + yy * quarter + row % quarter

    rows = [(quarter * i, quarter) for i in range(3)]
    return spread_pieces(
        refs, feed_cut(quarter), rows, dest, 0, dest.shape[1] // 2, offset_of
    )


def feed_pads(dest, half, pad):
    for i in range(3):
        dest[pad * i + half : pad * (i + 1)] = jnp.zeros((pad - half, dest.shape[1]), bf16)


def features(picked, at):
    one = picked[:, at : at + 256]
    two = picked[:, at + 256 : at + 512]
    return one, two, (one * two).astype(bf16)


class Table:
    def __init__(self, pad):
        sizes = (2 * HEAD_PAD, 2 * PD, 2 * pad, pad, 2 * PD)
        starts = np.cumsum((0,) + sizes)
        self.right, self.left, self.gate, self.down, self.taps = (
            slice(int(a), int(a) + n) for a, n in zip(starts, sizes)
        )
        self.edges = [int(a) for a in starts]


def params(mib, **more):
    return pltpu.CompilerParams(vmem_limit_bytes=mib * 2**20, **more)


def project_kernel(own, first, rank, table, pick, *rest):
    count = 1 if own else 5
    refs = rest[:count]
    proj, packed, weight, sems = rest[count:]
    copies = mixer_copies(refs, own, weight, 0)
    run_copies(copies, sems, 0)
    mixer_pads(weight, 0)
    wait_copies(copies, sems, 0)
    blocks = first.shape[0] // CHUNK
    for head in range(2):
        cols = pl.ds(HEAD_PAD * head, HEAD_PAD)

        def one(block, carry):
            rows = pl.ds(pl.multiple_of(block * CHUNK, CHUNK), CHUNK)
            result = nt(first[rows, :], weight[cols, :]) + nn(rank[rows, :], table[:, cols])
            rounded = result.astype(bf16)
            lane = lax.broadcasted_iota(jnp.int32, (CHUNK, PD), 1)
            base = jnp.where(lane == PD - 1, 1.0, result[:, :PD]).astype(bf16)
            proj[rows, cols] = rounded
            proj[rows, HEAD_PAD * head : HEAD_PAD * head + PD] = base
            _, _, feat = features(nn(base, pick[:, 512:1024]), 0)
            return carry + tn(feat, rounded[:, PD : 2 * PD])

        total = lax.fori_loop(0, blocks, one, jnp.zeros((256, PD), f32))
        packed[head, 0:STATE] = total[:STATE].astype(bf16)
        last = first.shape[0]
        at = HEAD_PAD * head
        packed[head, STATE : STATE + WIN] = proj[last - WIN :, at + 3 * PD : at + 4 * PD]
        packed[head, STATE + WIN : STATE + 2 * WIN] = proj[last - WIN :, at + 4 * PD : at + 5 * PD]
        packed[head, PACK - 32 : PACK - 16] = proj[last - 16 :, at + 5 * PD : at + 6 * PD]
        packed[head, PACK - 16 : PACK] = jnp.zeros((16, PD), bf16)


def project(own, first, rank, table, tables, refs):
    rows, width = first.shape
    vm = pl.BlockSpec(memory_space=pltpu.VMEM)
    return pl.pallas_call(
        functools.partial(project_kernel, own),
        out_shape=(
            jax.ShapeDtypeStruct((rows, 2 * HEAD_PAD), bf16),
            jax.ShapeDtypeStruct((2, PACK, PD), bf16),
            jax.ShapeDtypeStruct((2 * HEAD_PAD, width), bf16),
        ),
        in_specs=[vm] * 4 + [ANY] * len(refs),
        out_specs=(vm, vm, vm),
        scratch_shapes=[pltpu.SemaphoreType.DMA((40,))],
        compiler_params=params(48),
        cost_estimate=pl.CostEstimate(
            flops=100_000_000, bytes_accessed=300_000, transcendentals=0
        ),
        name="project",
    )(first, rank, table, *tables, *refs)


def window_masks(count):
    query = lax.broadcasted_iota(jnp.int32, (count, count + WIN), 0)
    key = lax.broadcasted_iota(jnp.int32, (count, count + WIN), 1)
    others = (key > query) & (key <= query + WIN)
    lead = jnp.where(lax.axis_index("chip") > 0, 0, WIN)
    return others & (key >= lead), others


def window_prob(query, keys, allowed):
    scores = nt(query, keys) * HD ** (-0.5)
    scores = jnp.where(allowed, scores, masked)
    largest = jnp.max(scores, -1, keepdims=True)
    expo = jnp.exp(scores - largest)
    return expo * (1.0 / jnp.sum(expo, -1, keepdims=True))


def causal_mask(size):
    row = lax.broadcasted_iota(jnp.int32, (size, size), 0)
    col = lax.broadcasted_iota(jnp.int32, (size, size), 1)
    return col <= row


def conv_of(conv, taps, start, count):
    result = taps[0:1] * conv[pl.ds(16 + start, count), :]
    for offset in range(1, KW):
        result = result + taps[offset : offset + 1] * conv[pl.ds(16 + start - offset, count), :]
    return result


def attend_kernel(spots, proj, tails, prior, table, pick, mixed, numer, states, keys, vals, conv):
    rows = proj.shape[0]
    keys[0:WIN, :] = tails[0, 0:WIN]
    vals[0:WIN, :] = tails[0, WIN : 2 * WIN]
    conv[0:16, :] = tails[0, 2 * WIN : 2 * WIN + 16].astype(f32)
    keys[WIN:, :] = proj[:, 3 * PD : 4 * PD]
    vals[WIN:, :] = proj[:, 4 * PD : 5 * PD]
    conv[16:, :] = proj[:, 5 * PD : 6 * PD].astype(f32)
    tap = head_taps(spots, table)
    state = whole_state(prior[0])
    causal = causal_mask(ATT)
    first_mask, mask = window_masks(QB)
    for chunk in range(rows // ATT):
        states[0, chunk] = state.astype(bf16)
        at = chunk * ATT
        span = slice(at, at + ATT)
        base = proj[span, 0:PD]
        value = proj[span, PD : 2 * PD]
        picked = nn(base, pick[:, :1152])
        _, _, feat_q = features(picked, 0)
        score = nt(base, picked[:, 1024:1152].astype(bf16))
        weight = jnp.where(causal, 1.0 + score + 0.5 * score * score, 0.0).astype(bf16)
        total = nn(weight, value) + nn(feat_q, state.astype(bf16))
        if at + ATT < rows:
            _, _, feat_k = features(picked, 512)
            state = state + tn(feat_k, value)
        parts = []
        for number in range(chunk * ATT // QB, (chunk + 1) * ATT // QB):
            query = proj[number * QB : (number + 1) * QB, 2 * PD : 3 * PD]
            allowed = mask if number else first_mask
            prob = window_prob(query, keys[number * QB : number * QB + QB + WIN, :], allowed)
            parts.append(nn(prob.astype(bf16), vals[number * QB : number * QB + QB + WIN, :]))
        window = jnp.concatenate(parts, 0)
        scale = lax.rsqrt(jnp.sum(total * total, -1, keepdims=True) * (1.0 / HD) + epsilon)
        gate = proj[span, 6 * PD : 7 * PD].astype(f32)
        branch = conv_of(conv, tap, at, ATT) * (gate * jax.nn.sigmoid(gate))
        mixed[span, :] = (total * scale + window + branch).astype(bf16)
        numer[span, :] = total.astype(bf16)


def whole_state(state):
    return jnp.concatenate([state, jnp.zeros((256 - STATE, PD), f32)], 0)


def head_taps(spots, table):
    start = pl.multiple_of(spots.taps.start + PD * pl.program_id(0), PD)
    return table[:, pl.ds(start, PD)].astype(f32)


def attend(spots, number, proj, tails, prior, table, tables):
    rows = proj.shape[0]
    whole = lambda a: pl.BlockSpec(a.shape, lambda h: (0,) * a.ndim)
    return pl.pallas_call(
        functools.partial(attend_kernel, spots),
        grid=(2,),
        out_shape=(
            jax.ShapeDtypeStruct((rows, 2 * PD), bf16),
            jax.ShapeDtypeStruct((rows, 2 * PD), bf16),
            jax.ShapeDtypeStruct((2, rows // ATT, 256, PD), bf16),
        ),
        in_specs=[
            pl.BlockSpec((rows, HEAD_PAD), lambda h: (0, h)),
            pl.BlockSpec((1, PACK - STATE, PD), lambda h: (2 * number + h, 0, 0)),
            pl.BlockSpec((1, STATE, PD), lambda h: (2 * number + h, 0, 0)),
            whole(table),
        ]
        + [whole(t) for t in tables],
        out_specs=(
            pl.BlockSpec((rows, PD), lambda h: (0, h)),
            pl.BlockSpec((rows, PD), lambda h: (0, h)),
            pl.BlockSpec((1, rows // ATT, 256, PD), lambda h: (h, 0, 0, 0)),
        ),
        scratch_shapes=[
            pltpu.VMEM((rows + WIN, PD), bf16),
            pltpu.VMEM((rows + WIN, PD), bf16),
            pltpu.VMEM((rows + 16, PD), f32),
        ],
        compiler_params=params(48),
        cost_estimate=pl.CostEstimate(
            flops=100_000_000, bytes_accessed=300_000, transcendentals=0
        ),
        name="attend",
    )(proj, tails, prior, table, *tables)


def mix_out_kernel(spots, *refs):
    mixed = refs[0:4]
    lefts = refs[4:8]
    right = refs[8]
    sources = refs[9 : 9 + 1 + 15]
    part, rank, kept, weight, sems = refs[25:]
    groups = []
    for slot in range(SLOTS):
        pieces = sources[0:1] if slot == 0 else sources[1 + 5 * (slot - 1) : 1 + 5 * slot]
        groups.append(output_copies(pieces, slot == 0, weight, 2 * PD * slot))

    @pl.when(pl.program_id(0) == 0)
    def _():
        for slot in range(SLOTS):
            run_copies(groups[slot], sems, 8 * slot)
            output_pads(weight, 2 * PD * slot)
        for slot in range(SLOTS):
            wait_copies(groups[slot], sems, 8 * slot)

    total = jnp.zeros(part.shape, f32)
    rank_sum = jnp.zeros((part.shape[0], R), f32)
    for slot in range(SLOTS):
        total = total + nn(mixed[slot][...], weight[2 * PD * slot : 2 * PD * (slot + 1), :])
        rank_sum = rank_sum + nt(mixed[slot][...], lefts[slot][:, spots.left])
    total = total + nn(rank_sum.astype(bf16), right[...])
    part[...] = total.astype(bf16)
    rank[...] = rank_sum
    rows = kept.shape[0]
    kept[...] = weight[pl.ds(pl.multiple_of(pl.program_id(0) * rows, rows), rows), :]


def mix_out(spots, mixed, lefts, right, sources):
    rows = mixed[0].shape[0]
    width = right.shape[1]
    block = CHUNK
    steps = rows // block
    whole = lambda a: pl.BlockSpec(a.shape, lambda i: (0,) * a.ndim)
    return pl.pallas_call(
        functools.partial(mix_out_kernel, spots),
        grid=(steps,),
        out_shape=(
            jax.ShapeDtypeStruct((rows, width), bf16),
            jax.ShapeDtypeStruct((rows, R), f32),
            jax.ShapeDtypeStruct((SLOTS * 2 * PD, width), bf16),
        ),
        in_specs=[pl.BlockSpec((block, 2 * PD), lambda i: (i, 0))] * 4
        + [whole(a) for a in lefts]
        + [whole(right)]
        + [ANY] * len(sources),
        out_specs=(
            pl.BlockSpec((block, width), lambda i: (i, 0)),
            pl.BlockSpec((block, R), lambda i: (i, 0)),
            pl.BlockSpec((SLOTS * 2 * PD // steps, width), lambda i: (i, 0)),
        ),
        scratch_shapes=[pltpu.VMEM((SLOTS * 2 * PD, width), bf16), pltpu.SemaphoreType.DMA((32,))],
        compiler_params=params(48),
        cost_estimate=pl.CostEstimate(
            flops=100_000_000, bytes_accessed=300_000, transcendentals=0
        ),
        name="mix_out",
    )(*mixed, *lefts, right, *sources)


def feed_kernel(slots, last, half, pad, spots, *refs):
    count = len(slots)
    fresh = slots[0] == 0
    second, grad, grank, rgrad, dright, gleft = refs[:6]
    tables, refs = refs[6 : 6 + count], refs[6 + count :]
    groups = []
    sources = []
    for slot in slots:
        size = 2 if slot == 0 else 5
        sources.append(refs[:size])
        refs = refs[size:]
    if not fresh:
        (down_in, back_in, ranks_in), refs = refs[:3], refs[3:]
    down_out, back_out, ranks_out = refs[:3]
    right_outs, left_outs = refs[3 : 3 + count], refs[3 + count : 3 + 2 * count]
    weights, sems, *sums = refs[3 + 2 * count :]
    right_grads, left_grads = sums[:count], sums[count:]
    for n, slot in enumerate(slots):
        part = weights.at[3 * pad * n : 3 * pad * (n + 1)]
        groups.append(feed_copies(sources[n], slot == 0, part, half, pad))
    begin = pl.program_id(0) == 0

    @pl.when(begin)
    def _():
        for n in range(count):
            run_copies(groups[n], sems, 16 * n)
        for n in range(count):
            feed_pads(weights.at[3 * pad * n : 3 * pad * (n + 1)], half, pad)
            right_grads[n][...] = jnp.zeros(right_grads[n].shape, f32)
            left_grads[n][...] = jnp.zeros(left_grads[n].shape, f32)

    down = jnp.zeros(down_out.shape, f32) if fresh else down_in[...]
    back = jnp.zeros(back_out.shape, f32) if fresh else back_in[...]
    down_rank = jnp.zeros((down.shape[0], R), f32) if fresh else ranks_in[:, :R]
    back_rank = jnp.zeros((down.shape[0], R), f32) if fresh else ranks_in[:, R:]
    for n in range(count):

        @pl.when(begin)
        def _():
            wait_copies(groups[n], sems, 16 * n)

        at = 3 * pad * n
        right, left = tables[n][:, spots.gate], tables[n][:, spots.down]
        gate_up = nt(second[...], weights[at : at + 2 * pad, :]) + nn(grank[...], right)
        gate, up = gate_up[:, :pad], gate_up[:, pad:]
        hidden_grad = nt(grad[...], weights[at + 2 * pad : at + 3 * pad, :]) + nn(rgrad[...], left)
        sig = jax.nn.sigmoid(gate)
        act = gate * sig
        hidden = (act * up).astype(bf16)
        gate_grad = hidden_grad * up * (sig * (1.0 + gate * (1.0 - sig)))
        both = jnp.concatenate([gate_grad.astype(bf16), (hidden_grad * act).astype(bf16)], 1)
        down = down + nn(hidden, weights[at + 2 * pad : at + 3 * pad, :])
        back = back + nn(both, weights[at : at + 2 * pad, :])
        down_rank = down_rank + nt(hidden, left)
        back_rank = back_rank + nt(both, right)
        right_grads[n][...] += tn(grank[...], both)
        left_grads[n][...] += tn(rgrad[...], hidden)
    ranks_out[:, :R] = down_rank
    ranks_out[:, R:] = back_rank
    if last:
        down = down + nn(down_rank.astype(bf16), dright[...])
        back = back + nn(back_rank.astype(bf16), gleft[...])
    down_out[...] = down.astype(down_out.dtype)
    back_out[...] = back.astype(back_out.dtype)

    @pl.when(pl.program_id(0) == pl.num_programs(0) - 1)
    def _():
        for out, total in zip(right_outs + left_outs, right_grads + left_grads):
            out[...] = total[...].astype(bf16)


def feed(slots, last, half, spots, second, grad, grank, rgrad, dright, gleft, tables, sources, carry):
    rows, width = second.shape
    pad = spots.down.stop - spots.down.start
    count = len(slots)
    block = CHUNK
    kind = bf16 if last else f32
    whole = lambda a: pl.BlockSpec(a.shape, lambda i: (0,) * a.ndim)
    wide = pl.BlockSpec((block, width), lambda i: (i, 0))
    thin = pl.BlockSpec((block, R), lambda i: (i, 0))
    pair = pl.BlockSpec((block, 2 * R), lambda i: (i, 0))
    flat = sum([list(s) for s in sources], [])
    out = pl.pallas_call(
        functools.partial(feed_kernel, slots, last, half, pad, spots),
        grid=(rows // block,),
        out_shape=(
            jax.ShapeDtypeStruct((rows, width), kind),
            jax.ShapeDtypeStruct((rows, width), kind),
            jax.ShapeDtypeStruct((rows, 2 * R), f32),
        )
        + (jax.ShapeDtypeStruct((R, 2 * pad), bf16),) * count
        + (jax.ShapeDtypeStruct((R, pad), bf16),) * count,
        in_specs=[wide, wide, thin, thin, whole(dright), whole(gleft)]
        + [whole(t) for t in tables]
        + [ANY] * len(flat)
        + ([wide, wide, pair] if carry else []),
        out_specs=(wide, wide, pair)
        + (pl.BlockSpec((R, 2 * pad), lambda i: (0, 0)),) * count
        + (pl.BlockSpec((R, pad), lambda i: (0, 0)),) * count,
        scratch_shapes=[
            pltpu.VMEM((3 * pad * count, width), bf16),
            pltpu.SemaphoreType.DMA((16 * count,)),
        ]
        + [pltpu.VMEM((R, 2 * pad), f32)] * count
        + [pltpu.VMEM((R, pad), f32)] * count,
        compiler_params=params(58),
        cost_estimate=pl.CostEstimate(
            flops=100_000_000, bytes_accessed=300_000, transcendentals=0
        ),
        name="feed",
    )(second, grad, grank, rgrad, dright, gleft, *tables, *flat, *carry)
    return list(out[:3]), list(out[3 : 3 + count]), list(out[3 + count :])


def turn_kernel(spots, *refs):
    mixer_up, orgrad, weight = refs[:3]
    tables, numers, mixeds, bases, heads, tails = (
        refs[3:7], refs[7:11], refs[11:15], refs[15:23], refs[23:27], refs[27:29]
    )
    pick = refs[29]
    up_out, grad_out, packs, left_out, total_state, left_sums = (
        refs[30], refs[31], refs[32:34], refs[34], refs[35], refs[36]
    )
    step = pl.program_id(0)

    @pl.when(step == 0)
    def _():
        total_state[...] = jnp.zeros(total_state.shape, f32)
        left_sums[...] = jnp.zeros(left_sums.shape, f32)

    both = nt(mixer_up[...], weight[...])
    for n in range(SLOTS):
        table = tables[n]
        flow = both[:, 2 * PD * n : 2 * PD * (n + 1)] + nn(orgrad[...], table[:, spots.left])
        left_sums[n] += tn(orgrad[...], mixeds[n][...])
        for head in range(2):
            cols = slice(PD * head, PD * (head + 1))
            wide = slice(PD * (2 * n + head), PD * (2 * n + head + 1))
            up = flow[:, cols]
            total = numers[n][:, cols].astype(f32)
            scale = lax.rsqrt(jnp.sum(total * total, -1, keepdims=True) * (1.0 / HD) + epsilon)
            inner = jnp.sum(total * up, -1, keepdims=True) * (1.0 / HD)
            grad = (scale * up - total * (scale * scale * scale * inner)).astype(bf16)
            up_out[:, wide] = up.astype(bf16)
            grad_out[:, wide] = grad
            _, _, feat = features(nn(bases[2 * n + head][...], pick[:, 0:512]), 0)
            total_state[2 * n + head] += tn(feat, grad)

    @pl.when(step == pl.num_programs(0) - 1)
    def _():
        for pair in range(2):
            packs[pair][:, 0:STATE, :] = total_state[4 * pair : 4 * pair + 4, :STATE, :].astype(bf16)
        left_out[...] = left_sums[...].astype(bf16)

    @pl.when(step == 0)
    def _():
        for n in range(SLOTS):
            for head in range(2):
                at = n % 2 * 2 + head
                rows = tails[n // 2].at[at]
                give_back(spots, tables[n], heads[n], rows, up_out, packs[n // 2].at[at], n, head)


def give_back(spots, table, rows, tails, up_out, lent, n, head):
    at = HEAD_PAD * head
    wide = slice(PD * (2 * n + head), PD * (2 * n + head + 1))
    query = rows[:, at + 2 * PD : at + 3 * PD]
    keys = jnp.concatenate([tails[0:WIN, :], rows[:, at + 3 * PD : at + 4 * PD]], 0)
    vals = jnp.concatenate([tails[WIN : 2 * WIN, :], rows[:, at + 4 * PD : at + 5 * PD]], 0)
    prob = window_prob(query, keys, window_masks(QB)[0])
    up = up_out[0:QB, wide]
    prob_grad = nt(up, vals)
    inner = jnp.sum(prob * prob_grad, -1, keepdims=True)
    score = (prob * (prob_grad - inner)).astype(bf16)
    lent[STATE : STATE + WIN, :] = (tn(score, query)[:WIN] * HD ** (-0.5)).astype(bf16)
    lent[STATE + WIN : STATE + 2 * WIN, :] = tn(prob.astype(bf16), up)[:WIN].astype(bf16)
    start = spots.taps.start + PD * head
    tap = table[:, start : start + PD].astype(f32)
    gate = rows[0:16, at + 6 * PD : at + 7 * PD].astype(f32)
    flow = up_out[0:16, wide].astype(f32) * (gate * jax.nn.sigmoid(gate))
    row0 = tap[2:3] * flow[0:1]
    row1 = tap[1:2] * flow[0:1] + tap[2:3] * flow[1:2]
    index = lax.broadcasted_iota(jnp.int32, (16, PD), 0)
    edge_rows = jnp.where(index == 14, row0, jnp.where(index == 15, row1, 0.0))
    lent[PACK - 32 : PACK - 16, :] = edge_rows.astype(bf16)
    lent[PACK - 16 : PACK, :] = jnp.zeros((16, PD), bf16)


def turn(spots, mixer_up, orgrad, weight, slot_tables, numer, mixed, projs, tails, tables):
    rows, width = mixer_up.shape
    whole = lambda a: pl.BlockSpec(a.shape, lambda i: (0,) * a.ndim)
    flat = lambda *shape: pl.BlockSpec(shape, lambda i: (0,) * len(shape))
    tall = lambda cols, at: pl.BlockSpec((TURN, cols), lambda i: (i, at))
    heads = 2 * SLOTS
    return pl.pallas_call(
        functools.partial(turn_kernel, spots),
        grid=(rows // TURN,),
        out_shape=(
            jax.ShapeDtypeStruct((rows, heads * PD), bf16),
            jax.ShapeDtypeStruct((rows, heads * PD), bf16),
            jax.ShapeDtypeStruct((4, PACK, PD), bf16),
            jax.ShapeDtypeStruct((4, PACK, PD), bf16),
            jax.ShapeDtypeStruct((SLOTS, R, 2 * PD), bf16),
        ),
        in_specs=[tall(width, 0), tall(R, 0), whole(weight)]
        + [whole(t) for t in slot_tables]
        + [tall(2 * PD, 0)] * 8
        + [tall(PD, 0), tall(PD, 7)] * SLOTS
        + [flat(QB, 2 * HEAD_PAD)] * SLOTS
        + [whole(t) for t in tails]
        + [whole(t) for t in tables],
        out_specs=(
            tall(heads * PD, 0),
            tall(heads * PD, 0),
            flat(4, PACK, PD),
            flat(4, PACK, PD),
            flat(SLOTS, R, 2 * PD),
        ),
        scratch_shapes=[pltpu.VMEM((heads, 256, PD), f32), pltpu.VMEM((SLOTS, R, 2 * PD), f32)],
        compiler_params=params(58),
        cost_estimate=pl.CostEstimate(
            flops=100_000_000, bytes_accessed=300_000, transcendentals=0
        ),
        name="turn",
    )(
        mixer_up, orgrad, weight, *slot_tables, *numer, *mixed,
        *[proj for proj in projs for _ in range(2)], *projs, *tails, *tables,
    )


def window_back(proj, keys, vals, ups, out, number, allowed, held):
    start = number * BACK_QB
    span = slice(start, start + BACK_QB)
    band = slice(start, start + BACK_QB + WIN)
    query = proj[span, 2 * PD : 3 * PD]
    key = keys[band, :]
    prob = window_prob(query, key, allowed)
    up = ups[span, :]
    prob_grad = nt(up, vals[band, :])
    inner = jnp.sum(prob * prob_grad, -1, keepdims=True)
    score = (prob * (prob_grad - inner)).astype(bf16)
    out[span, 2 * PD : 3 * PD] = (nn(score, key) * HD ** (-0.5)).astype(bf16)
    dkey = tn(score, query) * HD ** (-0.5)
    dval = tn(prob.astype(bf16), up)
    for piece, new, more in ((3, dkey, held[0]), (4, dval, held[1])):
        cols = slice(piece * PD, (piece + 1) * PD)
        out[start : start + BACK_QB - WIN, cols] = new[WIN:BACK_QB].astype(bf16)
        out[start + BACK_QB - WIN : start + BACK_QB, cols] = (new[BACK_QB:] + more).astype(bf16)
    return dkey[:WIN], dval[:WIN]


def attend_back_kernel(
    spots, proj, tails, states, later, lent, ups, grads, table, rank, pick,
    out, rank_grad, right_grad, keys, vals, conv, flow
):
    rows = proj.shape[0]
    chunks = rows // BACK_CHUNK
    keys[0:WIN, :] = tails[0, 0:WIN]
    vals[0:WIN, :] = tails[0, WIN : 2 * WIN]
    conv[0:16, :] = tails[0, 2 * WIN : 2 * WIN + 16].astype(f32)
    keys[WIN:, :] = proj[:, 3 * PD : 4 * PD]
    vals[WIN:, :] = proj[:, 4 * PD : 5 * PD]
    conv[16:, :] = proj[:, 5 * PD : 6 * PD].astype(f32)
    tap = head_taps(spots, table)
    right = table.at[:, pl.ds(pl.multiple_of(HEAD_PAD * pl.program_id(0), PD), HEAD_PAD)]
    flow[rows:, :] = jnp.zeros((16, PD), f32)
    follow = whole_state(later[0])
    causal = causal_mask(BACK_CHUNK)
    first_mask, mask = window_masks(BACK_QB)
    held = (lent[0, 0:WIN].astype(f32), lent[0, WIN : 2 * WIN].astype(f32))
    for chunk in range(chunks - 1, -1, -1):
        at = chunk * BACK_CHUNK
        span = slice(at, at + BACK_CHUNK)
        base = proj[span, 0:PD]
        value = proj[span, PD : 2 * PD]
        grad = grads[span, :]
        picked = nn(base, pick[...])
        q_one, q_two, feat_q = features(picked, 0)
        k_one, k_two, feat_k = features(picked, 512)
        key_low = picked[:, 1024:1152].astype(bf16)
        query_high = picked[:, 1152:1280].astype(bf16)
        score = nt(base, key_low)
        weight = jnp.where(causal, 1.0 + score + 0.5 * score * score, 0.0).astype(bf16)
        slope = jnp.where(causal, nt(grad, value) * (1.0 + score), 0.0).astype(bf16)
        follow_round = follow.astype(bf16)
        q_up = nt(grad, states[0, chunk * (BACK_CHUNK // ATT)])
        k_up = nt(value, follow_round)
        inside = [q_up * q_two, q_up * q_one, k_up * k_two, k_up * k_one]
        inside = jnp.concatenate([part.astype(bf16) for part in inside], 1)
        low = nn(slope, key_low) + tn(slope, query_high) + nt(inside, pick[:, :1024])
        out[span, 0:PD] = low.astype(bf16)
        out[span, PD : 2 * PD] = (tn(weight, grad) + nn(feat_k, follow_round)).astype(bf16)
        if chunk:
            follow = follow + tn(feat_q, grad)
        gate = proj[span, 6 * PD : 7 * PD].astype(f32)
        up = ups[span, :].astype(f32)
        sig = jax.nn.sigmoid(gate)
        act = gate * sig
        flow[span, :] = up * act
        for number in range((at + BACK_CHUNK) // BACK_QB - 1, at // BACK_QB - 1, -1):
            held = window_back(
                proj, keys, vals, ups, out, number, mask if number else first_mask, held
            )
        slope_gate = sig + act * (1.0 - sig)
        out[span, 6 * PD : 7 * PD] = (up * conv_of(conv, tap, at, BACK_CHUNK) * slope_gate).astype(bf16)
    grad_in = tap[0:1] * flow[0:rows, :]
    for offset in range(1, KW):
        grad_in = grad_in + tap[offset : offset + 1] * flow[offset : offset + rows, :]
    out[:, 5 * PD : 6 * PD] = grad_in.astype(bf16)
    last = slice(rows - 16, rows)
    edge = grad_in[rows - 16 :, :] + lent[0, 2 * WIN : 2 * WIN + 16].astype(f32)
    out[last, 5 * PD : 6 * PD] = edge.astype(bf16)
    right_grad[...] = tn(rank[...], out[...]).astype(bf16)

    @pl.when(pl.program_id(0) == 0)
    def _():
        rank_grad[...] = nt(out[...], right[...])

    @pl.when(pl.program_id(0) > 0)
    def _():
        rank_grad[...] += nt(out[...], right[...])


def attend_back(spots, slot, proj, tails, states, later, lent, ups, grads, table, rank, tables):
    rows = proj.shape[0]
    number = slot % 2
    whole = lambda a: pl.BlockSpec(a.shape, lambda h: (0,) * a.ndim)
    head = pl.BlockSpec((rows, HEAD_PAD), lambda h: (0, h))
    edge = pl.BlockSpec((1, PACK - STATE, PD), lambda h: (2 * number + h, 0, 0))
    state = pl.BlockSpec((1, STATE, PD), lambda h: (2 * number + h, 0, 0))
    column = pl.BlockSpec((rows, PD), lambda h: (0, 2 * slot + h))
    return pl.pallas_call(
        functools.partial(attend_back_kernel, spots),
        grid=(2,),
        out_shape=(
            jax.ShapeDtypeStruct((rows, 2 * HEAD_PAD), bf16),
            jax.ShapeDtypeStruct((rows, R), f32),
            jax.ShapeDtypeStruct((R, 2 * HEAD_PAD), bf16),
        ),
        in_specs=[
            head,
            edge,
            pl.BlockSpec((1, rows // ATT, 256, PD), lambda h: (h, 0, 0, 0)),
            state,
            edge,
            column,
            column,
            whole(table),
            whole(rank),
        ]
        + [whole(t) for t in tables],
        out_specs=(
            head,
            pl.BlockSpec((rows, R), lambda h: (0, 0)),
            pl.BlockSpec((R, HEAD_PAD), lambda h: (0, h)),
        ),
        scratch_shapes=[
            pltpu.VMEM((rows + WIN, PD), bf16),
            pltpu.VMEM((rows + WIN, PD), bf16),
            pltpu.VMEM((rows + 16, PD), f32),
            pltpu.VMEM((rows + 16, PD), f32),
        ],
        compiler_params=params(48),
        cost_estimate=pl.CostEstimate(
            flops=100_000_000, bytes_accessed=300_000, transcendentals=0
        ),
        name="attend_back",
    )(proj, tails, states, later, lent, ups, grads, table, rank, *tables)


def first_back_kernel(core, *refs):
    grads = refs[0:4]
    rank_grad, left = refs[4:6]
    sources = refs[6:10]
    own, sibling, weight, sems = refs[10:]
    size = 2 * HEAD_PAD
    copies = [(sources[n], weight.at[size * n : size * (n + 1)]) for n in range(SLOTS)]
    begin = pl.program_id(0) == 0

    @pl.when(begin)
    def _():
        run_copies(copies, sems, 0)

    total = nn(rank_grad[0].astype(bf16), left[...])
    for slot in range(SLOTS):

        @pl.when(begin)
        def _():
            wait_copies(copies[slot : slot + 1], sems, slot)

        total = total + nn(grads[slot][0], weight[size * slot : size * (slot + 1), :])

    @pl.when(begin)
    def _():
        own[...] = total.astype(bf16)

    @pl.when(jnp.logical_not(begin))
    def _():
        sibling[...] = total.astype(bf16)


def first_back(core, start, count, grads, rank_grad, left, sources):
    _, _, size = grads[0].shape
    width = left.shape[1]
    whole = lambda a: pl.BlockSpec(a.shape, lambda i, c: (0,) * a.ndim)
    span = lambda cols: pl.BlockSpec(
        (1, count, cols), lambda i, c: (lax.rem(c[0] + i, 2), start // count, 0)
    )
    flat = pl.BlockSpec((count, width), lambda i, c: (0, 0))
    return pl.pallas_call(
        first_back_kernel,
        out_shape=(jax.ShapeDtypeStruct((count, width), bf16),) * 2,
        grid_spec=pltpu.PrefetchScalarGridSpec(
            num_scalar_prefetch=1,
            grid=(2,),
            in_specs=[span(size)] * 4 + [span(R), whole(left)] + [ANY] * len(sources),
            out_specs=(flat, flat),
            scratch_shapes=[
                pltpu.VMEM((SLOTS * size, width), bf16),
                pltpu.SemaphoreType.DMA((SLOTS,)),
            ],
        ),
        compiler_params=params(56),
        cost_estimate=pl.CostEstimate(
            flops=100_000_000, bytes_accessed=300_000, transcendentals=0
        ),
        name="first_back",
    )(core, *grads, rank_grad, left, *sources)


def norm_two_kernel(own, other, wide, gain, left, middle, second, rank):
    total = wide[...].astype(f32) + (own[...].astype(f32) + other[...].astype(f32))
    scale = lax.rsqrt(jnp.mean(total * total, -1, keepdims=True) + epsilon)
    rounded = (total * scale * gain[...]).astype(bf16)
    middle[...] = total
    second[...] = rounded
    rank[...] = nn(rounded, left[...]).astype(bf16)


def norm_two(own, other, wide, gain, left):
    rows, width = own.shape
    block = pl.BlockSpec((WIDE, width), lambda i: (i, 0))
    whole = lambda a: pl.BlockSpec(a.shape, lambda i: (0,) * a.ndim)
    return pl.pallas_call(
        norm_two_kernel,
        grid=(rows // WIDE,),
        out_shape=(
            jax.ShapeDtypeStruct((rows, width), f32),
            jax.ShapeDtypeStruct((rows, width), bf16),
            jax.ShapeDtypeStruct((rows, R), bf16),
        ),
        in_specs=[block, block, block, whole(gain), whole(left)],
        out_specs=(block, block, pl.BlockSpec((WIDE, R), lambda i: (i, 0))),
        compiler_params=params(40),
        cost_estimate=pl.CostEstimate(
            flops=100_000_000, bytes_accessed=300_000, transcendentals=0
        ),
        name="norm_two",
    )(own, other, wide, gain, left)


def back_two_kernel(own, other, middle, upstream, gain, right, mixer_up, rgrad):
    vector = middle[...]
    scale = lax.rsqrt(jnp.mean(vector * vector, -1, keepdims=True) + epsilon)
    flow = gain[...] * (own[...].astype(f32) + other[...].astype(f32))
    inner = jnp.mean(vector * flow, -1, keepdims=True)
    total = upstream[...].astype(f32) + scale * flow - vector * (scale * scale * scale * inner)
    rounded = total.astype(bf16)
    mixer_up[...] = rounded
    rgrad[...] = nt(rounded, right[...]).astype(bf16)


def back_two(own, other, middle, upstream, gain, right):
    rows, width = own.shape
    block = pl.BlockSpec((CHUNK, width), lambda i: (i, 0))
    whole = lambda a: pl.BlockSpec(a.shape, lambda i: (0,) * a.ndim)
    return pl.pallas_call(
        back_two_kernel,
        grid=(rows // CHUNK,),
        out_shape=(
            jax.ShapeDtypeStruct((rows, width), bf16),
            jax.ShapeDtypeStruct((rows, R), bf16),
        ),
        in_specs=[block, block, block, block, whole(gain), whole(right)],
        out_specs=(block, pl.BlockSpec((CHUNK, R), lambda i: (i, 0))),
        compiler_params=params(40),
        cost_estimate=pl.CostEstimate(
            flops=100_000_000, bytes_accessed=300_000, transcendentals=0
        ),
        name="back_two",
    )(own, other, middle, upstream, gain, right)


def weighted(hot, parts):
    expert = pl.program_id(0)
    total = hot[expert, 0] * parts[0].astype(f32)
    for slot in range(1, SLOTS):
        total = total + hot[expert, slot] * parts[slot].astype(f32)
    return total


def by_core(flag, mine, other, base):
    lead = flag[0] > 0
    one, two = mine[:, :base], other[:, :base]
    return jnp.where(lead, one, two), jnp.where(lead, two, one)


def early_kernel(half, pad, hot, flag, mine, other, *outs):
    right, gate_left, down_right, out_left, gate_right, down_left = outs
    width = right.shape[2]
    base = 2 * PD + 3 * pad
    own, sibling = weighted(hot, mine), weighted(hot, other)
    for n, ref in enumerate((right, gate_left, down_right)):
        cols = slice(base + width * n, base + width * (n + 1))
        ref[0] = own[:, cols] + sibling[:, cols]
    cores = by_core(flag, own, sibling, base)
    out_left[0] = jnp.concatenate(
        [part[:, PD * h : PD * h + HD] for part in cores for h in range(2)], 1
    )
    for g in range(2):
        at = 2 * PD + pad * g
        gate_right[0, :, g, :] = jnp.concatenate([part[:, at : at + half] for part in cores], 1)
    at = 2 * PD + 2 * pad
    down_left[0] = jnp.concatenate([part[:, at : at + half] for part in cores], 1)


def late_kernel(hot, flag, mine, other, right, left):
    width = left.shape[2]
    base = 2 * HEAD_PAD
    own, sibling = weighted(hot, mine), weighted(hot, other)
    left[0] = own[:, base : base + width] + sibling[:, base : base + width]
    for core, part in enumerate(by_core(flag, own, sibling, base)):
        for head in range(2):
            at = HEAD_PAD * head
            right[0, :, 2 * core + head, :] = jnp.concatenate(
                [part[:, at + place_at : at + place_at + size] for _, size, place_at in HEAD_SEGMENTS], 1
            )


def tables_of(kernel, shapes, name, hot, flag, mine, other):
    whole = lambda a: pl.BlockSpec(a.shape, lambda e: (0,) * a.ndim)
    smem = pl.BlockSpec(memory_space=pltpu.SMEM)
    spot = lambda rank: lambda e: (e,) + (0,) * (rank - 1)
    return pl.pallas_call(
        kernel,
        grid=(NA,),
        out_shape=[jax.ShapeDtypeStruct((NA,) + shape, f32) for shape in shapes],
        in_specs=[smem, smem, whole(mine), whole(other)],
        out_specs=[pl.BlockSpec((1,) + shape, spot(len(shape) + 1)) for shape in shapes],
        compiler_params=params(40),
        cost_estimate=pl.CostEstimate(
            flops=100_000_000, bytes_accessed=300_000, transcendentals=0
        ),
        name=name,
    )(hot, flag, mine, other)


def swap_core(array):
    return lax.ppermute(array, "core", [(0, 1), (1, 0)])


def swap_chip(array, bit):
    count = lax.axis_size("chip")
    return lax.ppermute(array, "chip", [(i, i ^ bit) for i in range(count)])


def swap_tp(array, bit):
    return lax.ppermute(array, "tp", [(i, i ^ bit) for i in range(4)])


def both_cores(own):
    return order_cores(own, swap_core(own))


def order_cores(own, other):
    lead = lax.axis_index("core") == 0
    return jnp.concatenate([jnp.where(lead, own, other), jnp.where(lead, other, own)], 0)


def own_rows(array, core):
    half = array.shape[0] // 2
    return lax.dynamic_slice_in_dim(array, core * half, half, 0)


def hold_kernel(*refs):
    pass


def hold(*arrays, after=()):
    return pl.pallas_call(
        hold_kernel,
        out_shape=tuple(jax.ShapeDtypeStruct(a.shape, a.dtype) for a in arrays),
        in_specs=[ANY] * (len(arrays) + len(after)),
        out_specs=(ANY,) * len(arrays),
        input_output_aliases={i: i for i in range(len(arrays))},
        compiler_params=pltpu.CompilerParams(has_side_effects=True),
        name="hold",
    )(*arrays, *after)


def hop_xy(piece):
    return swap_chip(piece, 1), swap_chip(piece, 2)


def hop_diag(from_x, from_y, cut):
    return swap_chip(from_y[:cut], 1), swap_chip(from_x[cut:], 2)


def cross(array):
    return lax.ppermute(array, "tp", [(1, 2), (2, 1)])


def edge(array):
    return lax.ppermute(array, "tp", [(1, 0), (2, 3)])


def pick_inner(inner_array, edge_array):
    z = lax.axis_index("tp")
    return jnp.where((z == 1) | (z == 2), inner_array, edge_array)


def add_swapped(array, bit):
    other = swap_chip(array, bit)
    return (array.astype(f32) + other.astype(f32)).astype(array.dtype)


def add_rest(array):
    bit = 2
    while bit < lax.axis_size("chip"):
        array = add_swapped(array, bit)
        bit *= 2
    return array


def plane_parts(array):
    if lax.axis_size("chip") == 4:
        return [swap_chip(array, bit) for bit in (1, 2, 3)]
    return [add_rest(add_swapped(array, 1))]


def plane_sum(array, parts):
    if len(parts) == 1:
        return parts[0]
    total = array.astype(f32)
    for part in parts:
        total = total + part.astype(f32)
    return total.astype(array.dtype)


def swap_states(packed):
    if lax.axis_size("chip") == 4:
        return tuple(swap_chip(packed, bit) for bit in (1, 2, 3))
    return (lax.all_gather(packed, "chip"),)


def use_states(parts, backward):
    chip = lax.axis_index("chip")
    count = lax.axis_size("chip")
    if len(parts) > 1:
        total = 0.0
        for bit, part in zip((1, 2, 3), parts):
            other = chip ^ bit
            ahead = (other > chip) if backward else (other < chip)
            total = total + jnp.where(ahead, part[:, :STATE].astype(f32), 0.0)
        near = jnp.where(lax.rem(chip, 2) == (0 if backward else 1), parts[0], parts[2])
    else:
        index = jnp.arange(count, dtype=jnp.int32)
        ahead = (index > chip) if backward else (index < chip)
        states = parts[0][:, :, :STATE].astype(f32)
        total = jnp.sum(jnp.where(ahead[:, None, None, None], states, 0.0), 0)
        at = jnp.minimum(chip + 1, count - 1) if backward else jnp.maximum(chip - 1, 0)
        near = lax.dynamic_index_in_dim(parts[0], at, 0, False)
    inside = (chip < count - 1) if backward else (chip > 0)
    return total, jnp.where(inside, near[:, STATE:], 0.0).astype(bf16)


def copy_kernel(source, dest):
    dest[...] = source[...]


def copy_of(array):
    block = pl.BlockSpec((1,) + array.shape[1:], lambda i: (i, 0, 0))
    return pl.pallas_call(
        copy_kernel,
        grid=(array.shape[0],),
        out_shape=jax.ShapeDtypeStruct(array.shape, array.dtype),
        in_specs=[block],
        out_specs=block,
        compiler_params=params(32),
        cost_estimate=pl.CostEstimate(
            flops=100_000_000, bytes_accessed=300_000, transcendentals=0
        ),
        name="copy_of",
    )(array)


def stack_tp(parts):
    z = lax.axis_index("tp")
    result = jnp.zeros((SLOTS,) + parts[0].shape, parts[0].dtype)
    for slot, part in enumerate(parts):
        result = lax.dynamic_update_index_in_dim(result, part, z ^ slot, 0)
    return result


def pad_heads(table):
    lead = table.shape[:-2]
    heads = table.shape[-2]
    zero = [(0, 0)] * (len(lead) + 1)
    low = jnp.pad(table[..., : 2 * FD], zero + [(0, PD - 2 * FD)])
    high = table[..., 2 * FD :].reshape(lead + (heads, 6, HD))
    high = jnp.pad(high, zero + [(0, 0), (0, PD - HD)]).reshape(lead + (heads, 6 * PD))
    return jnp.concatenate([low, high], -1).reshape(lead + (heads * HEAD_PAD,))


def pad_last(table, size):
    return jnp.pad(table, [(0, 0)] * (table.ndim - 1) + [(0, size - table.shape[-1])])


def norm_rows(vector, gain_vector):
    row_scale = lax.rsqrt(jnp.mean(vector * vector, -1, keepdims=True) + epsilon)
    return (vector * row_scale * gain_vector, row_scale)


def norm_back(vector, row_scale, gain_vector, upstream):
    inner_mean = jnp.mean(vector * gain_vector * upstream, -1, keepdims=True)
    return (
        row_scale * gain_vector * upstream - vector * row_scale * row_scale * row_scale * inner_mean
    )


def body(
    block_input,
    gain_first,
    frozen_mixer_weight,
    conv_filter,
    frozen_output_weight,
    gain_second,
    frozen_gate_up_weight,
    frozen_down_weight,
    mixer_left,
    mixer_right,
    output_left,
    output_right,
    gateup_left,
    gateup_right,
    down_left,
    down_right,
    adapter_index,
    seq_lengths,
    out_cotangent,
):
    chip = lax.axis_index("chip")
    core = lax.axis_index("core")
    z = lax.axis_index("tp")
    y, x = place()
    sequences, length, width = block_input.shape
    rows = 2 * length
    heads_here = frozen_mixer_weight.shape[1]
    ff_here = frozen_down_weight.shape[0]
    half = ff_here // 2
    pad = (half + PD - 1) // PD * PD
    quarter = half // 2

    tables = (jnp.asarray(feature_tables(), bf16),)

    w_mix = jnp.transpose(frozen_mixer_weight, (1, 2, 0)).reshape(heads_here * HCOLS, width)
    w_gate = jnp.transpose(frozen_gate_up_weight, (1, 2, 0)).reshape(2 * ff_here, width)
    w_out = frozen_output_weight
    w_down = frozen_down_weight
    side = width // 2

    def cut(matrix, start, count):
        return lax.dynamic_slice(matrix, (start, x * side), (count, side))

    mixer_piece = jnp.concatenate(
        [
            cut(w_mix, 2 * HCOLS * core + HCOLS * y, HCOLS),
            cut(w_out, 2 * HD * core + HD * y, HD),
        ],
        0,
    )
    feed_piece = jnp.concatenate(
        [
            cut(w_gate, half * core + quarter * y, quarter),
            cut(w_gate, ff_here + half * core + quarter * y, quarter),
            cut(w_down, half * core + quarter * y, quarter),
        ],
        0,
    )
    slot_seq = z ^ jnp.arange(SLOTS, dtype=jnp.int32)
    slot_adapter = jnp.sum(
        jnp.where(slot_seq[:, None] == jnp.arange(SLOTS)[None, :], adapter_index[None, :], 0), 1
    )
    onehot = slot_adapter[:, None] == jnp.arange(NA, dtype=jnp.int32)[None, :]

    def select(table):
        return jnp.einsum(
            "se,e...->s...", onehot.astype(bf16), table, preferred_element_type=f32
        ).astype(bf16)

    mine = slot_adapter[0]
    my_mixer_left = lax.dynamic_index_in_dim(mixer_left, mine, 0, False)
    my_output_right = lax.dynamic_index_in_dim(output_right, mine, 0, False)
    my_gateup_left = lax.dynamic_index_in_dim(gateup_left, mine, 0, False)
    my_down_right = lax.dynamic_index_in_dim(down_right, mine, 0, False)
    right_table = pad_heads(
        select(lax.dynamic_slice_in_dim(mixer_right, 2 * core, 2, 2))
    )
    out_table = lax.dynamic_slice_in_dim(jnp.swapaxes(output_left, 1, 2), 2 * HD * core, 2 * HD, 2)
    out_table = pad_last(select(out_table).reshape(SLOTS, R, 2, HD), PD).reshape(SLOTS, R, 2 * PD)
    gate_table = lax.dynamic_slice_in_dim(gateup_right, half * core, half, 3)
    gate_table = pad_last(select(gate_table), pad).reshape(SLOTS, R, 2 * pad)
    down_table = lax.dynamic_slice_in_dim(jnp.swapaxes(down_left, 1, 2), half * core, half, 2)
    down_table = pad_last(select(down_table), pad)
    taps = lax.dynamic_slice_in_dim(conv_filter, 2 * HD * core, 2 * HD, 1)
    taps = pad_last(taps.reshape(KW, 2, HD), PD).reshape(KW, 2 * PD)
    taps = jnp.broadcast_to(jnp.pad(taps, ((0, R - KW), (0, 0))), (SLOTS, R, 2 * PD))
    packed = jnp.concatenate([right_table, out_table, gate_table, down_table, taps], 2)
    spots = Table(pad)

    gain_one = gain_first.astype(f32)
    gain_two = gain_second.astype(f32)[None, :]
    own_input = lax.dynamic_index_in_dim(block_input, z, 0, False)
    own_cotangent = lax.dynamic_index_in_dim(out_cotangent, z, 0, False)
    my_length = lax.dynamic_index_in_dim(seq_lengths, z, 0, False)
    upstream_own = jnp.where(
        (((chip * 2 + core) * length + jnp.arange(length, dtype=jnp.int32)) < my_length)[:, None],
        own_cotangent,
        0.0,
    ).astype(bf16)

    e_m, c_m = swap_tp(mixer_piece, 1), cross(mixer_piece)
    both_input = both_cores(own_input)
    first = norm_rows(both_input.astype(f32), gain_one)[0].astype(bf16)
    mixer_rank = nn(first, my_mixer_left).astype(bf16)
    upstream_other = swap_core(upstream_own)
    upstream_own, upstream_other, e_m, c_m, mixer_rank, packed, both_input = hold(
        upstream_own, upstream_other, e_m, c_m, mixer_rank, packed, both_input
    )

    projs, packs, wides = [], [], []
    borrowed, prior, mixed, numer, chunk_states = [None, None], [None, None], [], [], []
    slots = [packed[0], None, None, None]

    def attend_slot(slot):
        pair, n = slot // 2, slot % 2
        out = attend(spots, n, projs[slot], borrowed[pair], prior[pair], slots[slot], tables)
        for kept, value in zip((mixed, numer, chunk_states), out):
            kept.append(value)

    def project_slot(slot, refs):
        out = project(slot == 0, first, mixer_rank, slots[slot], tables, refs)
        for kept, value in zip((projs, packs, wides), out):
            kept.append(value)

    x1, y1 = hop_xy(e_m)
    c2_m, f_m = cross(e_m), edge(c_m)
    table1 = swap_tp(packed[1], 1)
    project_slot(0, (w_mix,))
    slot2 = pick_inner(c2_m, f_m)
    x1, y1, slot2, c2_m, c_m, packs[0], table1, feed_piece, packed = hold(
        x1, y1, slot2, c2_m, c_m, packs[0], table1, feed_piece, packed
    )
    slots[1] = table1
    d1 = hop_diag(x1, y1, M_CUT)
    x2, y2 = hop_xy(slot2)
    f2_m = edge(c2_m)
    table2, table3 = swap_tp(packed[2], 2), swap_tp(packed[3], 3)
    upstream = order_cores(upstream_own, upstream_other)
    down_rgrad = nt(upstream, my_down_right).astype(bf16)
    slot3 = pick_inner(c_m, f2_m)
    x2, y2, slot3, feed_piece, table2, table3, upstream, down_rgrad, *d1 = hold(
        x2, y2, slot3, feed_piece, table2, table3, upstream, down_rgrad, *d1
    )
    slots[2], slots[3] = table2, table3
    d2 = hop_diag(x2, y2, M_CUT)
    x3, y3 = hop_xy(slot3)
    e_f = swap_tp(feed_piece, 1)
    set1 = (e_m, x1, y1, *d1)
    project_slot(1, set1)
    x3, y3, e_f, packs[0], packs[1], *d2 = hold(x3, y3, e_f, packs[0], packs[1], *d2)
    d3 = hop_diag(x3, y3, M_CUT)
    c_f = cross(feed_piece)
    gathered = lax.all_gather(jnp.concatenate(packs[:2], 0), "chip")
    set2 = (slot2, x2, y2, *d2)
    project_slot(2, set2)
    prior[0], borrowed[0] = use_states((gathered,), False)
    d3_a, d3_b, c_f, packs[2], prior[0], borrowed[0] = hold(
        *d3, c_f, packs[2], prior[0], borrowed[0]
    )
    fx1, fy1 = hop_xy(e_f)
    c2_f, f_f = cross(e_f), edge(c_f)
    set3 = (slot3, x3, y3, d3_a, d3_b)
    project_slot(3, set3)
    fslot2 = pick_inner(c2_f, f_f)
    fx1, fy1, fslot2, c2_f, c_f, packs[2], packs[3] = hold(
        fx1, fy1, fslot2, c2_f, c_f, packs[2], packs[3]
    )
    crossing = swap_states(jnp.concatenate(packs[2:], 0))
    attend_slot(0)
    attend_slot(1)
    fd1 = hop_diag(fx1, fy1, feed_cut(quarter))
    mixed[0], mixed[1], fslot2, c2_f, fd1_a, fd1_b, *crossing = hold(
        mixed[0], mixed[1], fslot2, c2_f, *fd1, *crossing
    )
    fd1 = (fd1_a, fd1_b)
    fx2, fy2 = hop_xy(fslot2)
    f2_f = edge(c2_f)
    prior[1], borrowed[1] = use_states(crossing, False)
    attend_slot(2)
    attend_slot(3)
    fslot3 = pick_inner(c_f, f2_f)
    sets = list(set1) + list(set2) + list(set3)
    out_part, out_rank, out_weight = mix_out(spots, mixed, slots, my_output_right, [w_out] + sets)
    fx2, fy2, out_part, fslot3 = hold(fx2, fy2, out_part, fslot3)
    other_part = swap_core(out_part)
    middle, second, gate_rank = norm_two(out_part, other_part, both_input, gain_two, my_gateup_left)

    gateup_left_t = my_gateup_left.T

    def feed_slots(which, sources, carry):
        return feed(
            which,
            which[-1] == SLOTS - 1,
            half,
            spots,
            second,
            upstream,
            gate_rank,
            down_rgrad,
            my_down_right,
            gateup_left_t,
            [slots[k] for k in which],
            sources,
            carry,
        )

    fd2 = hop_diag(fx2, fy2, feed_cut(quarter))
    fx3, fy3 = hop_xy(fslot3)
    carry, gate_grads, down_grads = feed_slots(
        (0, 1), [(w_gate, w_down), (e_f, fx1, fy1, *fd1)], []
    )
    fx3, fy3, carry[2], *fd2 = hold(fx3, fy3, carry[2], *fd2)
    fd3 = hop_diag(fx3, fy3, feed_cut(quarter))
    carry, more_gates, more_downs = feed_slots((2,), [(fslot2, fx2, fy2, *fd2)], carry)
    gate_grads, down_grads = gate_grads + more_gates, down_grads + more_downs
    carry[2], *fd3 = hold(carry[2], *fd3)
    carry, more_gates, more_downs = feed_slots((3,), [(fslot3, fx3, fy3, *fd3)], carry)
    gate_grads, down_grads = gate_grads + more_gates, down_grads + more_downs
    down_part, back_part, ranks = carry
    other_back = swap_core(back_part)
    other_down = swap_core(own_rows(down_part, 1 - core))
    own_down = own_rows(down_part, core).astype(f32)
    own_output = (own_rows(middle, core) + (own_down + other_down.astype(f32))).astype(bf16)
    own_output, other_back = hold(own_output, other_back)
    block_output = lax.all_gather(own_output, "tp")
    mixer_up, output_rgrad = back_two(
        back_part, other_back, middle, upstream, gain_two, my_output_right
    )


    ups, grads, packed0, packed1, left_grads = turn(
        spots, mixer_up, output_rgrad, out_weight, slots, numer, mixed, projs, borrowed, tables
    )
    packed0, packed1, left_grads, ranks, out_rank = hold(
        packed0, packed1, left_grads, ranks, out_rank
    )
    crossing = swap_states(packed0)
    down_rank, gateup_rgrad = ranks[:, :R].astype(bf16), ranks[:, R:].astype(bf16)
    shared = jnp.stack(
        [
            tn(out_rank.astype(bf16), mixer_up),
            tn(gateup_rgrad, second),
            tn(down_rank, upstream),
        ]
    )
    owned = jnp.stack(
        [jnp.concatenate([left_grads[i], gate_grads[i], down_grads[i]], 1) for i in range(SLOTS)]
    )
    packed1, shared, owned, *crossing = hold(packed1, shared, owned, *crossing)
    backs = []

    def back_slots(pair, which, later, returned):
        for n in which:
            slot = 2 * pair + n
            backs.append(
                attend_back(
                    spots,
                    slot,
                    projs[slot],
                    borrowed[pair],
                    chunk_states[slot],
                    later,
                    returned,
                    ups,
                    grads,
                    slots[slot],
                    mixer_rank,
                    tables,
                )
            )

    def join(array, other):
        return (array.astype(f32) + other.astype(f32)).astype(array.dtype)

    def packs_of(owned, shared):
        flat = jnp.concatenate(list(shared), 1).astype(bf16)
        return [jnp.concatenate([owned[k], flat], 1) for k in range(SLOTS)]

    next_crossing = swap_states(packed1)
    back_slots(0, (0, 1), *use_states(crossing, True))
    early_rank = backs[0][1] + backs[1][1]
    shared_x, owned_x = swap_chip(shared, 1), swap_chip(owned, 1)
    early_rank, shared_x, owned_x, *crossing = hold(
        early_rank, shared_x, owned_x, *next_crossing
    )
    shared, owned = add_rest(join(shared, shared_x)), add_rest(join(owned, owned_x))
    later, returned = use_states(crossing, True)
    back_slots(1, (0,), later, returned)
    early_rank = early_rank + backs[2][1]
    early_rank, later, shared, owned = hold(early_rank, later, shared, owned)
    early = packs_of(owned, shared)
    early = [early[0]] + [swap_tp(early[bit], bit) for bit in (1, 2, 3)]
    back_slots(1, (1,), later, returned)
    rank_grad = early_rank + backs[3][1]
    rank_grad, *early = hold(rank_grad, *early)
    early = jnp.stack(early)
    early_other = swap_core(early)

    mixer_all = jnp.concatenate(
        [
            jnp.stack([back[2] for back in backs]),
            tn(rank_grad.astype(bf16), first)[None].astype(bf16),
        ],
        0,
    )
    mixer_x = plane_parts(mixer_all)
    proj_grads = [back[0].reshape(2, length, 2 * HEAD_PAD) for back in backs]
    left_t = my_mixer_left.T
    count_a = length // 2
    count_b = length - count_a
    rank_rows = rank_grad.reshape(2, length, R)
    core_array = jnp.reshape(core, (1,)).astype(jnp.int32)
    here_a, there_a = first_back(core_array, 0, count_a, proj_grads, rank_rows, left_t, wides)
    here_a, there_a, rank_rows, early, early_other, *mixer_x = hold(
        here_a, there_a, rank_rows, early, early_other, *mixer_x, after=(block_output,)
    )
    mixer_all = plane_sum(mixer_all, mixer_x)

    def finish(here, there, start, count):
        total = here.astype(f32) + swap_core(there).astype(f32)
        wide = own_input[start : start + count].astype(f32)
        scale_one = lax.rsqrt(jnp.mean(wide * wide, -1, keepdims=True) + epsilon)
        straight = lax.dynamic_slice_in_dim(
            mixer_up, core * length + start, count, 0
        ).astype(f32)
        return (straight + norm_back(wide, scale_one, gain_one, total)).astype(bf16)

    done_a = finish(here_a, there_a, 0, count_a)
    e_a, c_a = swap_tp(done_a, 1), cross(done_a)
    late = packs_of(mixer_all[:SLOTS], mixer_all[SLOTS:])
    late = [late[0]] + [swap_tp(late[bit], bit) for bit in (1, 2, 3)]
    here_b, there_b = first_back(core_array, count_a, count_b, proj_grads, rank_rows, left_t, wides)
    e_a, c_a, here_b, there_b, *late = hold(e_a, c_a, here_b, there_b, *late)
    late = jnp.stack(late)
    c2_a, f_a = cross(e_a), edge(c_a)
    done_b = finish(here_b, there_b, count_a, count_b)
    done_b, early, early_other, late, block_output = hold(
        done_b, early, early_other, late, block_output
    )
    block_output = copy_of(block_output)
    e_b, c_b = swap_tp(done_b, 1), cross(done_b)
    late_other = swap_core(late)
    hot = jnp.swapaxes(onehot, 0, 1).astype(f32)
    flag = jnp.reshape(core == 0, (1,)).astype(jnp.int32)
    early_tables = tables_of(
        functools.partial(early_kernel, half, pad),
        [(R, width)] * 3 + [(R, heads_here * HD), (R, 2, ff_here), (R, ff_here)],
        "early_tables",
        hot,
        flag,
        early,
        early_other,
    )
    (
        c2_a, f_a, e_b, c_b, late, late_other, done_a, done_b, e_a
    ) = hold(
        c2_a, f_a, e_b, c_b, late, late_other, done_a, done_b, e_a,
        after=(*early_tables, block_output),
    )
    f2_a, c2_b, f_b = edge(c2_a), cross(e_b), edge(c_b)

    input_grad = jnp.zeros(block_input.shape, bf16)

    def put(whole, part, slot, number):
        return lax.dynamic_update_slice(whole, part[None], (z ^ slot, number * count_a, 0))

    input_grad = put(input_grad, done_a, 0, 0)
    input_grad = put(input_grad, done_b, 0, 1)
    input_grad = put(input_grad, e_a, 1, 0)
    input_grad = put(input_grad, e_b, 1, 1)
    input_grad = put(input_grad, pick_inner(c2_a, f_a), 2, 0)
    grad_mixer_right, grad_mixer_left = tables_of(
        late_kernel,
        [(R, heads_here, HCOLS), (R, width)],
        "late_tables",
        hot,
        flag,
        late,
        late_other,
    )
    f2_a, c2_b, f_b, input_grad = hold(
        f2_a, c2_b, f_b, input_grad, after=(grad_mixer_right, grad_mixer_left)
    )
    f2_b = edge(c2_b)
    input_grad = put(input_grad, pick_inner(c_a, f2_a), 3, 0)
    input_grad = put(input_grad, pick_inner(c2_b, f_b), 2, 1)
    input_grad = put(input_grad, pick_inner(c_b, f2_b), 3, 1)
    grad_output_right, grad_gateup_left, grad_down_right = early_tables[:3]
    grad_output_left, grad_gateup_right, grad_down_left = early_tables[3:]
    return (
        block_output,
        input_grad,
        jnp.swapaxes(grad_mixer_left, 1, 2),
        grad_mixer_right,
        jnp.swapaxes(grad_output_left, 1, 2),
        grad_output_right,
        jnp.swapaxes(grad_gateup_left, 1, 2),
        grad_gateup_right,
        jnp.swapaxes(grad_down_left, 1, 2),
        grad_down_right,
    )


def solution(mesh):
    seq, tp = mesh.devices.shape
    fine = Mesh(mesh.devices.reshape(seq // 2, 2, tp), ("chip", "core", "tp"))
    where = ("chip", "core")
    return jax.shard_map(
        body,
        mesh=fine,
        in_specs=(
            P(None, where, None),
            P(),
            P(None, "tp", None),
            P(None, "tp"),
            P("tp", None),
            P(),
            P(None, None, "tp"),
            P("tp", None),
            P(),
            P(None, None, "tp", None),
            P(None, "tp", None),
            P(),
            P(),
            P(None, None, None, "tp"),
            P(None, "tp", None),
            P(),
            P(),
            P(),
            P(None, where, None),
        ),
        out_specs=(
            P(None, where, None),
            P(None, where, None),
            P(),
            P(None, None, "tp", None),
            P(None, "tp", None),
            P(),
            P(),
            P(None, None, None, "tp"),
            P(None, "tp", None),
            P(),
        ),
        check_vma=False,
    )
```
